32 devices in a mesh: img: 4 (over z), row: 8 (over y, x, core).
Axes of the slice: x: 2, y: 2, z: 4, core: 2. Of those that a mesh axis runs over, the one named last changes fastest.
Arguments:
- patches: bfloat16 [4, 64, 56, 256], P('img', 'row'), may hold values from -6 to 6
- cotangent: bfloat16 [4, 64, 56, 256], P('img', 'row'), may hold values from -6 to 6
- image_sizes: int32 [4, 2], P('img'), may hold values from 28 to 64, as said below
- weights: float32 [32, 32768], P(('img', 'row')), may hold values from -8 to 8
- first_moment: float32 [32, 32768], P(('img', 'row')), may hold values from -14336 to 14336
- second_moment: float32 [32, 32768], P(('img', 'row')), may hold values from 0 to 28672
- weight_ema: float32 [32, 32768], P(('img', 'row')), may hold values from -8 to 8
- vectors: float32 [25, 256], replicated, may hold values from -2 to 2
- vec_first: float32 [25, 256], replicated, may hold values from -14336 to 14336
- vec_second: float32 [25, 256], replicated, may hold values from 0 to 57344
- vec_ema: float32 [25, 256], replicated, may hold values from -2 to 2
- basis_narrow: float32 [8, 256, 256], replicated, may hold values from -0.375 to 0.375
- basis_pair: float32 [512, 512], replicated, may hold values from -0.25 to 0.25
- basis_wide: float32 [3, 1024, 1024], replicated, may hold values from -0.1875 to 0.1875
Outputs:
- layer_out: bfloat16 [4, 64, 56, 256], P('img', 'row')
- grad_input: float32 [4, 64, 56, 256], P('img', 'row')
- new_weights: float32 [32, 32768], P(('img', 'row'))
- new_first: float32 [32, 32768], P(('img', 'row'))
- new_second: float32 [32, 32768], P(('img', 'row'))
- new_ema: float32 [32, 32768], P(('img', 'row'))
- new_vectors: float32 [25, 256], replicated
- new_vec_first: float32 [25, 256], replicated
- new_vec_second: float32 [25, 256], replicated
- new_vec_ema: float32 [25, 256], replicated
The draws below stay inside these ranges and needn't reach their ends.
Inputs may be any that keep to these rules, and one draw needn't show every extreme that they name: `image_sizes`: column 0 is an image's height in cells, from 57 to 64; column 1 its width, from 28 to 56; in every draw some image has height 64 and width 56.
All inputs are finite; a program needn't handle non-finite values.
Results may differ from the reference program's by a relative error of at most 0.014.
The reference program's roundings to bfloat16 on the way count: a program that leaves them out, or rounds other values in their place, can miss the bound.
Values may be sent and summed in bfloat16 or wider, within the bound.
No kernel may reach another device: no remote copies, remote signals or barrier semaphores. Data moves between devices by JAX's collectives and lax.ppermute only.
A program may use at most 192 MiB of HBM per device.

```python
import jax
import jax.numpy as jnp
from jax import lax

D = 256
HEADS = 8
FF = 1024
R = 8
W = 56
STEP = 5
IMGS = 4
H = 64
KEYS = 896
SHARDS = 32
PER = 32768
VROWS = 25
TOKENS_ALL = 14336


def segment_row(factors):
    dims = ((D, D), (D, 2 * D), (D, D), (D, FF), (FF, D), (4 * D, D))
    pieces = [jnp.full((dim_rows * dim_cols // SHARDS,), factor, jnp.float32) for (dim_rows, dim_cols), factor in zip(dims, factors)]
    return jnp.concatenate(pieces)


def weight_scales():
    return segment_row((2.0 * D ** (-0.5), D ** (-0.5), (0.02 * KEYS / D) ** 0.5, D ** (-0.5), FF ** (-0.5), (4.0 * D) ** (-0.5)))


def gradient_scales():
    root_tokens = (1.0 * TOKENS_ALL) ** 0.5
    return segment_row((0.1 * root_tokens, 0.1 * root_tokens, 0.1 * root_tokens, 0.5 * root_tokens, 0.5 * root_tokens, 0.05 * root_tokens))


def vector_law(key):
    noise = jax.random.truncated_normal(key, -3.0, 3.0, (VROWS, D), jnp.float32)
    row_index = jnp.arange(VROWS)
    is_gain = (row_index == 10) | (row_index == 14) | (row_index == 18)
    spread = jnp.where(is_gain, 0.2, 0.3)
    centre = jnp.where(is_gain, 1.0, 0.0)
    return centre[:, None] + spread[:, None] * noise


def draw_image_sizes(key, part):
    key = jax.random.fold_in(key, 11)
    key_height, key_width, key_chosen = jax.random.split(key, 3)
    heights = jax.random.randint(key_height, (IMGS,), H - R + 1, H + 1)
    widths = jax.random.randint(key_width, (IMGS,), W // 2, W + 1)
    chosen = jax.random.randint(key_chosen, (), 0, IMGS)
    picked = jnp.arange(IMGS) == chosen
    heights = jnp.where(picked, H, heights)
    widths = jnp.where(picked, W, widths)
    return jnp.stack([heights, widths], axis=1).astype(jnp.int32)


def draw_weights(key, part):
    key = jax.random.fold_in(key, 1)
    noise = jax.random.truncated_normal(key, -4.0, 4.0, (SHARDS, PER), jnp.float32)
    return noise * weight_scales()[None, :]


def draw_weight_ema(key, part):
    key = jax.random.fold_in(key, 2)
    noise = jax.random.truncated_normal(key, -4.0, 4.0, (SHARDS, PER), jnp.float32)
    return noise * weight_scales()[None, :]


def draw_first_moment(key, part):
    key = jax.random.fold_in(key, 3)
    noise = jax.random.truncated_normal(key, -3.0, 3.0, (SHARDS, PER), jnp.float32)
    return noise * gradient_scales()[None, :]


def draw_second_moment(key, part):
    key = jax.random.fold_in(key, 4)
    factor = jnp.exp(jax.random.uniform(key, (SHARDS, PER), jnp.float32, 0.0, 1.3862944))
    scales = gradient_scales()
    return factor * (scales * scales)[None, :]


def draw_vectors(key, part):
    key = jax.random.fold_in(key, 5)
    return vector_law(key)


def draw_vec_ema(key, part):
    key = jax.random.fold_in(key, 6)
    return vector_law(key)


def draw_vec_first(key, part):
    key = jax.random.fold_in(key, 7)
    noise = jax.random.truncated_normal(key, -3.0, 3.0, (VROWS, D), jnp.float32)
    return noise * (1.0 * TOKENS_ALL) ** 0.5


def draw_vec_second(key, part):
    key = jax.random.fold_in(key, 8)
    factor = jnp.exp(jax.random.uniform(key, (VROWS, D), jnp.float32, 0.0, 1.3862944))
    return factor * (1.0 * TOKENS_ALL)


def shard_levels(rng, shape, cuts, low, top_value):
    def one(dim, shards_of):
        steps = jax.random.uniform(jax.random.fold_in(jax.random.fold_in(rng, 6), dim), (shards_of,), jnp.float32, low / len(cuts), top_value / len(cuts))
        return jnp.repeat(jnp.exp(steps), shape[dim] // shards_of).reshape((-1,) + (1,) * (len(shape) - dim - 1))

    factor_of = one(*cuts[0])
    for cut in cuts[1:]:
        factor_of = factor_of * one(*cut)
    return factor_of


def scatter_about(key, extent, scale, most, cuts=(), kind=jnp.bfloat16):
    values = scale * jax.random.normal(key, extent, jnp.float32)
    if cuts:
        values = values * shard_levels(key, extent, cuts, -0.22, 0.18)
    return jnp.clip(values, -most, most).astype(kind)


def setup_inputs(seed: int = 0) -> dict:
    streams_of = jax.random.split(jax.random.key(seed), 15)
    patches = scatter_about(streams_of[0], (IMGS, H, W, D), 1.0, 6.0, ((0, 4), (1, 8)))
    cotangent = scatter_about(streams_of[1], (IMGS, H, W, D), 1.0, 6.0, ((0, 4), (1, 8)))
    image_sizes = draw_image_sizes(jax.random.fold_in(streams_of[14], 71), 0)
    weights = draw_weights(jax.random.fold_in(streams_of[14], 71), 0)
    first_moment = draw_first_moment(jax.random.fold_in(streams_of[14], 71), 0)
    second_moment = draw_second_moment(jax.random.fold_in(streams_of[14], 71), 0)
    weight_ema = draw_weight_ema(jax.random.fold_in(streams_of[14], 71), 0)
    vectors = draw_vectors(jax.random.fold_in(streams_of[14], 71), 0)
    vec_first = draw_vec_first(jax.random.fold_in(streams_of[14], 71), 0)
    vec_second = draw_vec_second(jax.random.fold_in(streams_of[14], 71), 0)
    vec_ema = draw_vec_ema(jax.random.fold_in(streams_of[14], 71), 0)
    basis_narrow = scatter_about(streams_of[11], (8, D, D), D ** -0.5, 0.375, (), jnp.float32)
    basis_pair = scatter_about(streams_of[12], (2 * D, 2 * D), (2 * D) ** -0.5, 0.25, (), jnp.float32)
    basis_wide = scatter_about(streams_of[13], (3, FF, FF), FF ** -0.5, 0.1875, (), jnp.float32)
    return {"patches": patches, "cotangent": cotangent, "image_sizes": image_sizes, "weights": weights, "first_moment": first_moment, "second_moment": second_moment, "weight_ema": weight_ema, "vectors": vectors, "vec_first": vec_first, "vec_second": vec_second, "vec_ema": vec_ema, "basis_narrow": basis_narrow, "basis_pair": basis_pair, "basis_wide": basis_wide}


NORM_EPS = 1e-05
ADAM_EPS = 1e-08
BETA = 0.5
WEIGHT_DECAY = 0.05
EMA_KEEP = 0.75
VECTOR_RATE = 0.06
MATRIX_RATES = (0.04, 0.02, 0.25, 0.02, 0.01, 0.01)
HIGH = lax.Precision.HIGHEST

@jax.custom_vjp
def low(v):
    return lax.optimization_barrier(v.astype(jnp.bfloat16)).astype(jnp.float32)

@jax.custom_vjp
def low_back(v):
    return v

def low_keep(v):
    return (low(v), None)

def low_pass(kept, grad):
    return (grad,)

def back_keep(v):
    return (v, None)

def back_low(kept, grad):
    return (low(grad),)
low.defvjp(low_keep, low_pass)
low_back.defvjp(back_keep, back_low)

def matmul(left_side, right_side):
    return jnp.dot(left_side, right_side, precision=HIGH, preferred_element_type=jnp.float32)

def layer_norm(values, gain, shift):
    centred = values - lax.optimization_barrier(jnp.mean(values, axis=-1, keepdims=True))
    inverse = lax.rsqrt(lax.optimization_barrier(jnp.mean(centred * centred, axis=-1, keepdims=True)) + NORM_EPS)
    return centred * inverse * gain + shift

def peg_mix(padded, peg_taps, peg_bias):
    framed = jnp.pad(padded, ((0, 0), (1, 1), (0, 0)))
    cell_rows = padded.shape[0] - 2
    cell_cols = padded.shape[1]
    mixed_sum = padded[1:-1] + peg_bias
    for tap_index in range(9):
        row_shift = tap_index // 3
        col_shift = tap_index % 3
        mixed_sum = mixed_sum + peg_taps[tap_index] * framed[row_shift:row_shift + cell_rows, col_shift:col_shift + cell_cols]
    return mixed_sum

def matrix_shapes(model_width, hidden_width):
    return ((model_width, model_width), (model_width, 2 * model_width), (model_width, model_width), (model_width, hidden_width), (hidden_width, model_width), (4 * model_width, model_width))

def basis_pairs(narrow, paired, wide):
    return ((narrow[0], narrow[1]), (narrow[2], paired), (narrow[3], narrow[4]), (narrow[5], wide[0]), (wide[1], narrow[6]), (wide[2], narrow[7]))

def unpack_matrices(packed):
    shard_count = packed.shape[0]
    matrices = []
    column_start = 0
    for dim_rows, dim_cols in matrix_shapes(D, FF):
        shard_span = dim_rows * dim_cols // shard_count
        matrices.append(packed[:, column_start:column_start + shard_span].reshape(dim_rows, dim_cols))
        column_start = column_start + shard_span
    return matrices

def pack_rows(matrices, shard_count):
    return jnp.concatenate([matrix.reshape(shard_count, -1) for matrix in matrices], axis=1)

def image_forward(tokens, image_height, image_width, params, vectors):
    w_query, w_keyval, w_out, w_up, w_down, w_reduce = [low(matrix) for matrix in params]
    rows_all, cell_cols, model_width = tokens.shape
    head_width = model_width // HEADS
    padded = jnp.pad(tokens, ((1, 1), (0, 0), (0, 0)))
    mixed_in = peg_mix(padded, vectors[0:9], vectors[9])
    normed = low(layer_norm(mixed_in, vectors[10], vectors[11]))
    flat_normed = normed.reshape(-1, model_width)
    queries = low_back(low(matmul(flat_normed, w_query) + vectors[12]))
    cell_rows = jnp.arange(rows_all, dtype=jnp.int32)
    cell_index = jnp.arange(cell_cols, dtype=jnp.int32)
    inside = (cell_rows[:, None] < image_height) & (cell_index[None, :] < image_width)
    masked = normed * inside[:, :, None].astype(jnp.float32)
    blocks = masked.reshape(rows_all // 2, 2, cell_cols // 2, 2, model_width).transpose(0, 2, 1, 3, 4).reshape(-1, 4 * model_width)
    reduced = low_back(matmul(blocks, w_reduce) + vectors[13])
    red_norm = low(layer_norm(reduced, vectors[14], vectors[15]))
    projected = matmul(red_norm, w_keyval)
    all_keys = low(projected[:, :model_width])
    all_values = low(projected[:, model_width:] + vectors[16])
    key_rows = jnp.arange(rows_all // 2, dtype=jnp.int32)
    key_cols = jnp.arange(cell_cols // 2, dtype=jnp.int32)
    key_inside = ((2 * key_rows[:, None] < image_height) & (2 * key_cols[None, :] < image_width)).reshape(-1)
    key_heads = all_keys.reshape(-1, HEADS, head_width)
    value_heads = all_values.reshape(-1, HEADS, head_width)
    query_blocks = queries.reshape(-1, R * W, HEADS, head_width)

    def attend(query_block):
        scores = low_back(jnp.einsum('qhd,khd->hqk', query_block, key_heads, precision=HIGH) * head_width ** (-0.5))
        scores = jnp.where(key_inside[None, None, :], scores, -1e+30)
        row_top = lax.optimization_barrier(jnp.max(scores, axis=2, keepdims=True))
        exponent = jnp.exp(scores - row_top)
        softmax_rows = low(exponent / lax.optimization_barrier(jnp.sum(exponent, axis=2, keepdims=True)))
        return jnp.einsum('hqk,khd->qhd', softmax_rows, value_heads, precision=HIGH)
    attended = lax.map(jax.checkpoint(attend), query_blocks)
    attended = low_back(low(attended.reshape(-1, model_width)))
    residual = mixed_in.reshape(-1, model_width) + low_back(matmul(attended, w_out) + vectors[17])
    second_in = low(layer_norm(residual, vectors[18], vectors[19]))
    up_input = low_back(matmul(second_in, w_up) + vectors[21:].reshape(-1))
    activated = low(jax.nn.gelu(up_input, approximate=False))
    return residual + matmul(activated, w_down) + vectors[20]

def reference(patches, cotangent, image_sizes, weights, first_moment, second_moment, weight_ema, vectors, vec_first, vec_second, vec_ema, basis_narrow, basis_pair, basis_wide):
    shard_count = weights.shape[0]
    params = tuple(unpack_matrices(weights))

    def one_image(totals, inputs):
        image_cells, image_cot, image_size = inputs

        def forward(cell_values, param_values, vector_values):
            return image_forward(cell_values, image_size[0], image_size[1], param_values, vector_values)
        result, pull_back = jax.vjp(forward, image_cells.astype(jnp.float32), params, vectors)
        grad_cells, grad_params, grad_vectors = pull_back(image_cot.astype(jnp.float32).reshape(-1, D))
        totals = (tuple((total + grad for total, grad in zip(totals[0], grad_params))), totals[1] + grad_vectors)
        return (totals, (result.reshape(image_cells.shape).astype(jnp.bfloat16), grad_cells))
    initial = (tuple((jnp.zeros_like(matrix) for matrix in params)), jnp.zeros_like(vectors))
    (grads, vec_grads), (layer_out, grad_input) = lax.scan(one_image, initial, (patches, cotangent, image_sizes))
    bases = basis_pairs(basis_narrow, basis_pair, basis_wide)
    correction = 1.0 - BETA ** STEP
    firsts = unpack_matrices(first_moment)
    seconds = unpack_matrices(second_moment)
    averages = unpack_matrices(weight_ema)
    new_mats, new_firsts, new_seconds, new_avgs = ([], [], [], [])
    for matrix_index in range(6):
        basis_left, basis_right = bases[matrix_index]
        rotated = matmul(matmul(basis_left.T, grads[matrix_index]), basis_right)
        moment = BETA * firsts[matrix_index] + (1.0 - BETA) * rotated
        square = BETA * seconds[matrix_index] + (1.0 - BETA) * rotated * rotated
        direction = moment / correction / (jnp.sqrt(square / correction) + ADAM_EPS)
        turned = matmul(matmul(basis_left, direction), basis_right.T)
        updated = params[matrix_index] - MATRIX_RATES[matrix_index] * (turned + WEIGHT_DECAY * params[matrix_index])
        new_mats.append(updated)
        new_firsts.append(moment)
        new_seconds.append(square)
        new_avgs.append(EMA_KEEP * averages[matrix_index] + (1.0 - EMA_KEEP) * updated)
    vec_moment = BETA * vec_first + (1.0 - BETA) * vec_grads
    vec_square = BETA * vec_second + (1.0 - BETA) * vec_grads * vec_grads
    vec_direction = vec_moment / correction / (jnp.sqrt(vec_square / correction) + ADAM_EPS)
    new_vectors = vectors - VECTOR_RATE * vec_direction
    new_vec_ema = EMA_KEEP * vec_ema + (1.0 - EMA_KEEP) * new_vectors
    return (layer_out, grad_input, pack_rows(new_mats, shard_count), pack_rows(new_firsts, shard_count), pack_rows(new_seconds, shard_count), pack_rows(new_avgs, shard_count), new_vectors, vec_moment, vec_square, new_vec_ema)
```

```python
from functools import partial

import jax
import jax.numpy as jnp
from jax import lax
from jax.sharding import PartitionSpec as P

HEADS = 8
FF = 1024
STEP = 5


NORM_EPS = 1e-05
ADAM_EPS = 1e-08
BETA = 0.5
WEIGHT_DECAY = 0.05
EMA_KEEP = 0.75
VECTOR_RATE = 0.06
MATRIX_RATES = (0.04, 0.02, 0.25, 0.02, 0.01, 0.01)
HIGH = lax.Precision.HIGHEST


import functools
import math
from jax.experimental import pallas as pl
from jax.experimental.pallas import tpu as pltpu
LOG2E = math.log2(math.e)
f32 = jnp.float32
bf16 = jnp.bfloat16


def contract(a, b, ca, cb, **kw):
    return lax.dot_general(
        a, b, (((ca,), (cb,)), ((), ())), preferred_element_type=f32, **kw
    )


def over_heads(body, heads, unroll):
    if unroll:
        for head in range(heads):
            body(head)
    else:

        def step(head, carry):
            body(head)
            return carry

        lax.fori_loop(0, heads, step, 0)


def head_columns(head):
    group = head // 4
    if isinstance(head, int):
        return slice(group * 128, group * 128 + 128)
    return pl.ds(pl.multiple_of(group * 128, 128), 128)


def head_rows(head, base=0):
    if isinstance(head, int):
        return slice(base + head * 32, base + head * 32 + 32)
    return pl.ds(pl.multiple_of(base + head * 32, 32), 32)


def attend_kernel(step, unroll, q_ref, k_ref, v_ref, mask_ref, o_ref, log_ref):
    tokens = q_ref.shape[0]
    scale = 32**-0.5 * LOG2E
    lane = lax.broadcasted_iota(jnp.int32, (1, 128), 1) // 32
    mask = mask_ref[...]

    def one_head(head):
        cols = head_columns(head)
        mine = lane == head % 4
        keys = jnp.where(mine, k_ref[:, cols], 0)
        values = jnp.where(mine, v_ref[:, cols], 0)

        def block(start):
            rows = pl.ds(start, step)
            scores = contract(q_ref[rows, cols], keys, 1, 1) * scale + mask
            top = jnp.max(scores, axis=1, keepdims=True)
            exponent = jnp.exp2(scores - top)
            total = jnp.sum(exponent, axis=1, keepdims=True)
            probs = (exponent * (1.0 / total)).astype(bf16)
            out = contract(probs, values, 1, 0)
            o_ref[rows, cols] = jnp.where(mine, out, o_ref[rows, cols])
            log_ref[head, rows, :] = jnp.broadcast_to(top + jnp.log2(total), (step, 128))

        over_blocks(block, tokens, step)

    over_heads(one_head, HEADS, unroll)


def over_blocks(block, tokens, step):
    if tokens == step:
        block(0)
    else:

        def go(index, carry):
            block(pl.multiple_of(index * step, step))
            return carry

        lax.fori_loop(0, tokens // step, go, 0)


def attend(q, k, v, mask):
    tokens, width = q.shape
    unroll = k.shape[0] <= 1024
    return pl.pallas_call(
        functools.partial(attend_kernel, tokens if unroll else 64, unroll),
        out_shape=(
            jax.ShapeDtypeStruct((tokens, width), f32),
            jax.ShapeDtypeStruct((HEADS, tokens, 128), f32),
        ),
        compiler_params=pltpu.CompilerParams(vmem_limit_bytes=40 * 2**20),
        name="attend",
    )(q, k, v, mask)


def attend_back_kernel(
    step, unroll, q_ref, k_ref, v_ref, mask_ref, o_ref, log_ref, g_ref, dq_ref, dkv_ref, ps, dss, qt, gt
):
    tokens, width = q_ref.shape
    scale = 32**-0.5
    lane = lax.broadcasted_iota(jnp.int32, (1, 128), 1) // 32
    mask = mask_ref[...]
    qt[...] = q_ref[...].astype(f32).T.astype(bf16)
    gt[...] = g_ref[...].astype(f32).T.astype(bf16)

    def one_head(head):
        cols = head_columns(head)
        mine = lane == head % 4
        keys = jnp.where(mine, k_ref[:, cols], 0)
        values = jnp.where(mine, v_ref[:, cols], 0)

        def block(start):
            rows = pl.ds(start, step)
            grad = g_ref[rows, cols]
            inner = jnp.sum(
                jnp.where(mine, grad.astype(f32) * o_ref[rows, cols], 0.0), axis=1, keepdims=True
            )
            scores = contract(q_ref[rows, cols], keys, 1, 1)
            probs = jnp.exp2(scores * (scale * LOG2E) + mask - log_ref[head, rows, 0:1])
            grad_scores = (probs * (contract(grad, values, 1, 1) - inner)).astype(bf16)
            ps[rows, :] = probs.astype(bf16)
            dss[rows, :] = grad_scores
            out = contract(grad_scores, keys, 1, 0) * scale
            dq_ref[rows, cols] = jnp.where(mine, out, dq_ref[rows, cols])

        over_blocks(block, tokens, step)
        dkv_ref[head_rows(head), :] = contract(qt[head_rows(head), :], dss[...], 1, 0) * scale
        dkv_ref[head_rows(head, width), :] = contract(gt[head_rows(head), :], ps[...], 1, 0)

    over_heads(one_head, HEADS, unroll)


def attend_back(q, k, v, mask, o, log, grad):
    tokens, width = q.shape
    keys = k.shape[0]
    unroll = keys <= 1024
    return pl.pallas_call(
        functools.partial(attend_back_kernel, tokens if unroll else 64, unroll),
        out_shape=(
            jax.ShapeDtypeStruct((tokens, width), f32),
            jax.ShapeDtypeStruct((2 * width, keys), f32),
        ),
        scratch_shapes=[
            pltpu.VMEM((tokens, keys), bf16),
            pltpu.VMEM((tokens, keys), bf16),
            pltpu.VMEM((width, tokens), bf16),
            pltpu.VMEM((width, tokens), bf16),
        ],
        compiler_params=pltpu.CompilerParams(vmem_limit_bytes=56 * 2**20),
        name="attend_back",
    )(q, k, v, mask, o, log, grad)


def extended(cells, sides, width):
    for axis, dim in sides:
        count = lax.axis_size(axis)
        ends = count - 1
        head = lax.slice_in_dim(cells, 0, width, axis=dim)
        tail = lax.slice_in_dim(cells, cells.shape[dim] - width, cells.shape[dim], axis=dim)
        cells = jnp.concatenate(
            [
                lax.ppermute(tail, axis, [(i, (i + 1) % count) for i in range(ends)]),
                cells,
                lax.ppermute(head, axis, [((i + 1) % count, i) for i in range(ends)]),
            ],
            axis=dim,
        )
    return cells


def layer_norm(values, gain, shift):
    centred = values - jnp.mean(values, axis=-1, keepdims=True)
    inverse = lax.rsqrt(jnp.mean(centred * centred, axis=-1, keepdims=True) + NORM_EPS)
    return centred * inverse * gain + shift


def peg_mix(padded, peg_taps, peg_bias):
    framed = jnp.pad(padded, ((0, 0), (1, 1), (0, 0)))
    cell_rows = padded.shape[0] - 2
    cell_cols = padded.shape[1]
    mixed_sum = padded[1:-1] + peg_bias
    for tap_index in range(9):
        row_shift = tap_index // 3
        col_shift = tap_index % 3
        mixed_sum = (
            mixed_sum
            + peg_taps[tap_index]
            * framed[row_shift : row_shift + cell_rows, col_shift : col_shift + cell_cols]
        )
    return mixed_sum


def matrix_shapes(model_width, hidden_width):
    return (
        (model_width, model_width),
        (model_width, 2 * model_width),
        (model_width, model_width),
        (model_width, hidden_width),
        (hidden_width, model_width),
        (4 * model_width, model_width),
    )


def basis_pairs(narrow, paired, wide):
    return (
        (narrow[0], narrow[1]),
        (narrow[2], paired),
        (narrow[3], narrow[4]),
        (narrow[5], wide[0]),
        (wide[1], narrow[6]),
        (wide[2], narrow[7]),
    )


def low_dot(left_side, right_side):
    return jnp.dot(left_side, right_side, preferred_element_type=jnp.float32)


def high_dot(left_side, right_side):
    return jnp.dot(left_side, right_side, precision=HIGH, preferred_element_type=jnp.float32)


def on_device(
    patches,
    cotangent,
    image_sizes,
    weights,
    first_moment,
    second_moment,
    weight_ema,
    vectors,
    vec_first,
    vec_second,
    vec_ema,
    basis_narrow,
    basis_pair,
    basis_wide,
):
    patch_tile = patches[0]
    tile_rows, tile_cols, model_width = patch_tile.shape
    token_count = tile_rows * tile_cols
    shard_count = lax.axis_size(("img", "row"))
    shard_rank = lax.axis_index(("img", "row"))
    tile_count = lax.axis_size("row")
    tile_rank = lax.axis_index("row")
    head_width = model_width // HEADS
    score_scale = head_width ** (-0.5)
    matrix_dims = matrix_shapes(model_width, FF)
    shard_spans = [dim_rows * dim_cols // shard_count for dim_rows, dim_cols in matrix_dims]
    gathered = lax.all_gather(weights.astype(jnp.bfloat16), ("img", "row"), axis=0, tiled=True)
    matrices = []
    column_start = 0
    for (dim_rows, dim_cols), shard_span in zip(matrix_dims, shard_spans):
        matrices.append(
            gathered[:, column_start : column_start + shard_span].reshape(dim_rows, dim_cols)
        )
        column_start = column_start + shard_span
    w_query, w_keyval, w_out, w_up, w_down, w_reduce = matrices
    peg_taps = vectors[0:9]
    peg_bias = vectors[9]
    gain_one, shift_one = (vectors[10], vectors[11])
    query_bias, reduce_bias = (vectors[12], vectors[13])
    gain_red, shift_red = (vectors[14], vectors[15])
    value_bias, out_bias = (vectors[16], vectors[17])
    gain_two, shift_two = (vectors[18], vectors[19])
    down_bias = vectors[20]
    up_bias = vectors[21:].reshape(-1)
    image_height = image_sizes[0, 0]
    image_width = image_sizes[0, 1]
    cell_rows = tile_rank * tile_rows + jnp.arange(tile_rows, dtype=jnp.int32)
    cell_index = jnp.arange(tile_cols, dtype=jnp.int32)
    inside = (cell_rows[:, None] < image_height) & (cell_index[None, :] < image_width)
    key_rows = jnp.arange(tile_count * tile_rows // 2, dtype=jnp.int32)
    key_cols = jnp.arange(tile_cols // 2, dtype=jnp.int32)
    key_inside = (
        (2 * key_rows[:, None] < image_height) & (2 * key_cols[None, :] < image_width)
    ).reshape(-1)
    padded = extended(patch_tile, (("row", 0),), 1).astype(jnp.float32)
    mixed_in = peg_mix(padded, peg_taps, peg_bias)
    normed = layer_norm(mixed_in, gain_one, shift_one).astype(jnp.bfloat16)
    flat_normed = normed.reshape(token_count, model_width)
    queries = (low_dot(flat_normed, w_query) + query_bias).astype(jnp.bfloat16)
    masked = normed * inside[:, :, None].astype(jnp.bfloat16)
    blocks = (
        masked.reshape(tile_rows // 2, 2, tile_cols // 2, 2, model_width)
        .transpose(0, 2, 1, 3, 4)
        .reshape(-1, 4 * model_width)
    )
    reduced = low_dot(blocks, w_reduce) + reduce_bias
    red_norm = layer_norm(reduced, gain_red, shift_red).astype(jnp.bfloat16)
    projected = low_dot(red_norm, w_keyval)
    own_keys = projected[:, :model_width].astype(jnp.bfloat16)
    own_values = (projected[:, model_width:] + value_bias).astype(jnp.bfloat16)
    all_keys, all_values = (
        lax.all_gather(own_keys, "row", axis=0, tiled=True),
        lax.all_gather(own_values, "row", axis=0, tiled=True),
    )
    key_mask = jnp.where(key_inside, 0.0, -1e30).astype(f32)[None, :]
    o32, logs = attend(queries, all_keys, all_values, key_mask)
    attended = o32.astype(jnp.bfloat16)
    residual = mixed_in.reshape(token_count, model_width) + (low_dot(attended, w_out) + out_bias)
    second_in = layer_norm(residual, gain_two, shift_two).astype(jnp.bfloat16)
    up_input = low_dot(second_in, w_up) + up_bias
    activated = jax.nn.gelu(up_input, approximate=False).astype(jnp.bfloat16)
    result = residual + low_dot(activated, w_down) + down_bias
    layer_out = result.astype(jnp.bfloat16).reshape(1, tile_rows, tile_cols, model_width)
    grad_out = cotangent[0].reshape(token_count, model_width)
    grad_result = grad_out.astype(jnp.float32)
    g_down = jnp.einsum("tf,td->fd", activated, grad_out, preferred_element_type=jnp.float32)
    g_down_bias = jnp.sum(grad_result, axis=0)
    grad_act = jnp.einsum("td,fd->tf", grad_out, w_down, preferred_element_type=jnp.float32)
    ignored, gelu_pull = jax.vjp(partial(jax.nn.gelu, approximate=False), up_input)
    grad_upper = gelu_pull(grad_act)[0].astype(jnp.bfloat16)
    g_up = jnp.einsum("td,tf->df", second_in, grad_upper, preferred_element_type=jnp.float32)
    g_up_bias = jnp.sum(grad_upper.astype(jnp.float32), axis=0)
    grad_second = jnp.einsum("tf,df->td", grad_upper, w_up, preferred_element_type=jnp.float32)
    ignored, second_pull = jax.vjp(layer_norm, residual, gain_two, shift_two)
    grad_resid, g_gain_two, g_shift_two = second_pull(grad_second)
    grad_resid = grad_resid + grad_result
    grad_branch = grad_resid.astype(jnp.bfloat16)
    g_out = jnp.einsum("td,te->de", attended, grad_branch, preferred_element_type=jnp.float32)
    g_out_bias = jnp.sum(grad_branch.astype(jnp.float32), axis=0)
    grad_att = jnp.einsum(
        "te,de->td", grad_branch, w_out, preferred_element_type=jnp.float32
    ).astype(jnp.bfloat16)
    dq32, dkv_t = attend_back(queries, all_keys, all_values, key_mask, o32, logs, grad_att)
    grad_query = dq32.astype(jnp.bfloat16)
    grad_keys_all = dkv_t[:model_width].T
    grad_vals_all = dkv_t[model_width:].T
    keyval_wide = w_keyval.astype(jnp.float32)
    own_grad_keys, own_grad_vals = (
        lax.psum_scatter(grad_keys_all, "row", scatter_dimension=0, tiled=True),
        lax.psum_scatter(grad_vals_all, "row", scatter_dimension=0, tiled=True),
    )
    grad_keyval = jnp.concatenate([own_grad_keys, own_grad_vals], axis=1)
    g_keyval = high_dot(red_norm.astype(jnp.float32).T, grad_keyval)
    g_value_bias = jnp.sum(own_grad_vals, axis=0)
    grad_red_norm = high_dot(grad_keyval, keyval_wide.T)
    g_query = jnp.einsum("td,te->de", flat_normed, grad_query, preferred_element_type=jnp.float32)
    g_query_bias = jnp.sum(grad_query.astype(jnp.float32), axis=0)
    ignored, reduced_pull = jax.vjp(layer_norm, reduced, gain_red, shift_red)
    grad_reduced_full, g_gain_red, g_shift_red = reduced_pull(grad_red_norm)
    grad_reduced = grad_reduced_full.astype(jnp.bfloat16)
    g_reduce = jnp.einsum("kc,kd->cd", blocks, grad_reduced, preferred_element_type=jnp.float32)
    g_reduce_bias = jnp.sum(grad_reduced.astype(jnp.float32), axis=0)
    grad_blocks = jnp.einsum(
        "kd,cd->kc", grad_reduced, w_reduce, preferred_element_type=jnp.float32
    )
    grad_masked = (
        grad_blocks.reshape(tile_rows // 2, tile_cols // 2, 2, 2, model_width)
        .transpose(0, 2, 1, 3, 4)
        .reshape(tile_rows, tile_cols, model_width)
    )
    grad_from_query = jnp.einsum(
        "te,de->td", grad_query, w_query, preferred_element_type=jnp.float32
    )
    grad_normed = grad_from_query.reshape(tile_rows, tile_cols, model_width) + grad_masked * inside[
        :, :, None
    ].astype(jnp.float32)
    ignored, first_pull = jax.vjp(layer_norm, mixed_in, gain_one, shift_one)
    grad_mixed, g_gain_one, g_shift_one = first_pull(grad_normed)
    grad_mixed = grad_mixed + grad_resid.reshape(tile_rows, tile_cols, model_width)
    framed = jnp.pad(padded, ((0, 0), (1, 1), (0, 0)))
    g_peg_bias = jnp.sum(grad_mixed, axis=(0, 1))
    tap_grads = []
    for tap_index in range(9):
        row_shift = tap_index // 3
        col_shift = tap_index % 3
        tap_grads.append(
            jnp.sum(
                framed[row_shift : row_shift + tile_rows, col_shift : col_shift + tile_cols]
                * grad_mixed,
                axis=(0, 1),
            )
        )
    grad_frame = extended(grad_mixed.astype(jnp.bfloat16), (("row", 0),), 1).astype(
        grad_mixed.dtype
    )
    grad_frame = jnp.pad(grad_frame, ((0, 0), (1, 1), (0, 0)))
    grad_input = grad_mixed
    for tap_index in range(9):
        row_shift = 2 - tap_index // 3
        col_shift = 2 - tap_index % 3
        grad_input = (
            grad_input
            + peg_taps[tap_index]
            * grad_frame[row_shift : row_shift + tile_rows, col_shift : col_shift + tile_cols]
        )
    grad_input = grad_input.reshape(1, tile_rows, tile_cols, model_width)
    vec_grads = jnp.concatenate(
        [
            jnp.stack(tap_grads),
            jnp.stack(
                [
                    g_peg_bias,
                    g_gain_one,
                    g_shift_one,
                    g_query_bias,
                    g_reduce_bias,
                    g_gain_red,
                    g_shift_red,
                    g_value_bias,
                    g_out_bias,
                    g_gain_two,
                    g_shift_two,
                    g_down_bias,
                ]
            ),
            g_up_bias.reshape(-1, model_width),
        ],
        axis=0,
    )
    vec_total = lax.psum(vec_grads, ("img", "row"))
    bases = basis_pairs(basis_narrow, basis_pair, basis_wide)
    local_grads = (g_query, g_keyval, g_out, g_up, g_down, g_reduce)
    rotated_terms = []
    for local_grad, (basis_left, basis_right) in zip(local_grads, bases):
        rotated_terms.append(
            high_dot(high_dot(basis_left.T, local_grad), basis_right).reshape(shard_count, -1)
        )
    summed = (
        lax.psum_scatter(rotated_terms[0], ("img", "row"), scatter_dimension=0, tiled=True),
        lax.psum_scatter(rotated_terms[1], ("img", "row"), scatter_dimension=0, tiled=True),
        lax.psum_scatter(rotated_terms[2], ("img", "row"), scatter_dimension=0, tiled=True),
        lax.psum_scatter(rotated_terms[3], ("img", "row"), scatter_dimension=0, tiled=True),
        lax.psum_scatter(rotated_terms[4], ("img", "row"), scatter_dimension=0, tiled=True),
        lax.psum_scatter(rotated_terms[5], ("img", "row"), scatter_dimension=0, tiled=True),
    )
    rotated = jnp.concatenate(summed, axis=1)
    correction = 1.0 - BETA**STEP
    new_first = BETA * first_moment + (1.0 - BETA) * rotated
    new_second = BETA * second_moment + (1.0 - BETA) * rotated * rotated
    direction = new_first / correction / (jnp.sqrt(new_second / correction) + ADAM_EPS)
    all_steps = lax.all_gather(direction, ("img", "row"), axis=0, tiled=True)
    turned_rows = []
    column_start = 0
    for (dim_rows, dim_cols), shard_span, (basis_left, basis_right) in zip(
        matrix_dims, shard_spans, bases
    ):
        step_matrix = all_steps[:, column_start : column_start + shard_span].reshape(
            dim_rows, dim_cols
        )
        rows_count = max(1, shard_span // dim_cols)
        entry_first = shard_rank * shard_span
        left_rows = lax.dynamic_slice_in_dim(basis_left, entry_first // dim_cols, rows_count, 0)
        turned = high_dot(high_dot(left_rows, step_matrix), basis_right.T).reshape(-1)
        turned_rows.append(turned.reshape(1, shard_span))
        column_start = column_start + shard_span
    turned_all = jnp.concatenate(turned_rows, axis=1)
    rate_row = jnp.concatenate(
        [
            jnp.full((shard_span,), rate_value, jnp.float32)
            for shard_span, rate_value in zip(shard_spans, MATRIX_RATES)
        ]
    )
    new_weights = weights - rate_row[None, :] * (turned_all + WEIGHT_DECAY * weights)
    new_ema = EMA_KEEP * weight_ema + (1.0 - EMA_KEEP) * new_weights
    vec_moment = BETA * vec_first + (1.0 - BETA) * vec_total
    vec_square = BETA * vec_second + (1.0 - BETA) * vec_total * vec_total
    vec_direction = vec_moment / correction / (jnp.sqrt(vec_square / correction) + ADAM_EPS)
    new_vectors = vectors - VECTOR_RATE * vec_direction
    new_vec_ema = EMA_KEEP * vec_ema + (1.0 - EMA_KEEP) * new_vectors
    return (
        layer_out,
        grad_input,
        new_weights,
        new_first,
        new_second,
        new_ema,
        new_vectors,
        vec_moment,
        vec_square,
        new_vec_ema,
    )


def solution(mesh):
    placed = (
        P("img", "row", None, None),
        P("img", "row", None, None),
        P("img", None),
        P(("img", "row"), None),
        P(("img", "row"), None),
        P(("img", "row"), None),
        P(("img", "row"), None),
        P(),
        P(),
        P(),
        P(),
        P(),
        P(),
        P(),
    )
    return jax.shard_map(
        on_device,
        mesh=mesh,
        in_specs=placed,
        out_specs=(
            P("img", "row", None, None),
            P("img", "row", None, None),
            P(("img", "row"), None),
            P(("img", "row"), None),
            P(("img", "row"), None),
            P(("img", "row"), None),
            P(),
            P(),
            P(),
            P(),
        ),
        check_vma=False,
    )
```

```python
import functools
import math

import jax
import jax.numpy as jnp
from jax import lax
from jax.experimental import pallas as pl
from jax.experimental.pallas import tpu as pltpu
from jax.sharding import PartitionSpec as P

HEADS = 8
FF = 1024
STEP = 5

NORM_EPS = 1e-05
ADAM_EPS = 1e-08
BETA = 0.5
WEIGHT_DECAY = 0.05
EMA_KEEP = 0.75
VECTOR_RATE = 0.06
MATRIX_RATES = (0.04, 0.02, 0.25, 0.02, 0.01, 0.01)
CORRECTION = 1.0 - BETA**STEP
LOG2E = math.log2(math.e)
f32 = jnp.float32
bf16 = jnp.bfloat16
LATE = (5, 1, 0, 2)
EARLY = (3, 4)


def matrix_shapes(width, hidden):
    return (
        (width, width),
        (width, 2 * width),
        (width, width),
        (width, hidden),
        (hidden, width),
        (4 * width, width),
    )


def contract(a, b, ca, cb, **kw):
    return lax.dot_general(
        a, b, (((ca,), (cb,)), ((), ())), preferred_element_type=f32, **kw
    )


def swap(x, axis, step):
    count = lax.axis_size(axis)
    return lax.ppermute(x, axis, [(i, i ^ step) for i in range(count)])


def row_groups():
    left = lax.axis_size("row") // 2
    groups, stride = [(1, 2)], 2
    while left > 1:
        size = 4 if left % 4 == 0 else 2
        groups.append((stride, size))
        left //= size
        stride *= size
    return groups


def gather_group(x, axis, stride, size):
    return jnp.stack([x] + [swap(x, axis, j * stride) for j in range(1, size)])


def gather_rows(x):
    groups = row_groups()
    for stride, size in groups[1:] + groups[:1]:
        x = gather_group(x, "row", stride, size)
    return x


def gather_all(x):
    return gather_rows(gather_group(x, "img", 1, lax.axis_size("img")))


def pair_sum(terms):
    while len(terms) > 1:
        terms = [a + b for a, b in zip(terms[::2], terms[1::2])]
    return terms[0]


def total_all(x):
    groups = [("row", stride, size) for stride, size in row_groups()]
    for axis, stride, size in groups + [("img", 1, lax.axis_size("img"))]:
        x = pair_sum([x] + [swap(x, axis, j * stride) for j in range(1, size)])
    return x


def rel_digits():
    groups = row_groups()
    return [groups[0]] + groups[1:][::-1]


def rel_rows():
    rel = jnp.zeros((1,), jnp.int32)
    for stride, size in rel_digits():
        rel = (rel[:, None] + stride * jnp.arange(size, dtype=jnp.int32)[None, :]).reshape(-1)
    return lax.axis_index("row") ^ rel


def source(block):
    sizes = lax.axis_size("img")
    img, rest = block % sizes, block // sizes
    rel = 0
    for stride, size in reversed(rel_digits()):
        rel = rel + (rest % size) * stride
        rest = rest // size
    row = lax.axis_index("row") ^ rel
    return (lax.axis_index("img") ^ img) * lax.axis_size("row") + row


def device_count():
    return lax.axis_size("img") * lax.axis_size("row")


def run(name, body, outs, args, scratch=(), mib=40, scalars=(), flops=0, moved=0):
    specs = [
        pl.BlockSpec(memory_space=pltpu.SMEM) if index in scalars else pl.BlockSpec(memory_space=pltpu.VMEM)
        for index in range(len(args))
    ]
    return pl.pallas_call(
        body,
        out_shape=tuple(jax.ShapeDtypeStruct(shape, dtype) for shape, dtype in outs),
        in_specs=specs,
        out_specs=tuple(pl.BlockSpec(memory_space=pltpu.VMEM) for _ in outs),
        scratch_shapes=[pltpu.VMEM(shape, dtype) for shape, dtype in scratch],
        compiler_params=pltpu.CompilerParams(vmem_limit_bytes=mib * 2**20),
        cost_estimate=pl.CostEstimate(flops=flops, bytes_accessed=moved, transcendentals=0),
        name=name,
    )(*args)


def each_block(count, body):
    if count <= 32:
        for index in range(count):
            body(index)
    else:

        def step(index, carry):
            body(index)
            return carry

        lax.fori_loop(0, count, step, 0)


def put_rows(ref, start, cols, value):
    count = value.shape[0]
    if count % 8 == 0:
        ref[pl.ds(pl.multiple_of(start, 8), count), cols] = value
    else:
        for row in range(count):
            ref[pl.ds(start + row, 1), cols] = value[row : row + 1]


def get_rows(ref, start, count, cols):
    if count % 8 == 0:
        return ref[pl.ds(pl.multiple_of(start, 8), count), cols]
    return jnp.concatenate([ref[pl.ds(start + row, 1), cols] for row in range(count)], axis=0)


def layout(width, group):
    dims = matrix_shapes(width, FF)
    found, start = [], 0
    for j in group:
        rows = dims[j][0] // device_count()
        blocks = dims[j][1] // width
        found.append((j, start, rows, blocks))
        start += rows * blocks
    return found, start


def packed_starts(width):
    dims = matrix_shapes(width, FF)
    starts, start = [], 0
    for m, n in dims:
        starts.append(start)
        start += m * n // device_count()
    return starts


def spread(block, parts, mats, start_of):
    for (j, first, rows, blocks), ref in zip(parts, mats):
        for col in range(blocks):
            piece = block[first + col * rows : first + (col + 1) * rows]
            put_rows(ref, start_of * rows, slice(col * 256, col * 256 + 256), piece)


def collect(out_ref, index, parts, mats, start_of):
    for (j, first, rows, blocks), ref in zip(parts, mats):
        for col in range(blocks):
            piece = get_rows(ref, start_of * rows, rows, slice(col * 256, col * 256 + 256))
            out_ref[index, first + col * rows : first + (col + 1) * rows, :] = piece


def norm_parts(values):
    centred = values - jnp.mean(values, axis=-1, keepdims=True)
    inverse = lax.rsqrt(jnp.mean(centred * centred, axis=-1, keepdims=True) + NORM_EPS)
    return centred * inverse, inverse


def norm_back(grad, unit, inverse, gain):
    grad_unit = grad * gain
    back = grad_unit - jnp.mean(grad_unit, axis=-1, keepdims=True)
    back = back - unit * jnp.mean(grad_unit * unit, axis=-1, keepdims=True)
    gain_sum = jnp.sum(grad * unit, axis=0, keepdims=True)
    return back * inverse, gain_sum, jnp.sum(grad, axis=0, keepdims=True)


def turned(value):
    return value.astype(f32).T.astype(bf16)


def col_sum(value):
    return jnp.sum(value, axis=0, keepdims=True)


def pack_kernel(width, w_ref, late_ref, early_ref, chunk):
    to_chunk(w_ref, chunk, width)
    split = late_ref.shape[0]
    late_ref[...] = chunk[0:split, :].astype(bf16)
    early_ref[...] = chunk[split:, :].astype(bf16)


def to_chunk(flat_ref, out_ref, width):
    dims, starts, base = matrix_shapes(width, FF), packed_starts(width), 0
    for group in (LATE, EARLY):
        parts, count = layout(width, group)
        for j, first, rows, blocks in parts:
            for col in range(blocks):
                for row in range(rows):
                    at = starts[j] + row * dims[j][1] + col * width
                    place = base + first + col * rows + row
                    out_ref[place : place + 1, :] = flat_ref[0:1, at : at + width]
        base += count


def from_chunk(values, base, group, out_ref, width):
    dims, starts = matrix_shapes(width, FF), packed_starts(width)
    parts, _ = layout(width, group)
    for j, first, rows, blocks in parts:
        for col in range(blocks):
            for row in range(rows):
                at = starts[j] + row * dims[j][1] + col * width
                place = base + first + col * rows + row
                out_ref[0:1, at : at + width] = values[place : place + 1, :]


def moments_kernel(width, *refs):
    for index in range(4):
        to_chunk(refs[index], refs[4 + index], width)


def bases_kernel(
    narrow_ref, pair_ref, wide_ref, narrow_out, turned_out, pair_out, wide_out, own_narrow, own_wide, tall
):
    count = device_count()
    rank = lax.axis_index("img") * lax.axis_size("row") + lax.axis_index("row")
    narrow_out[...] = narrow_ref[...].astype(bf16)
    pair_out[...] = pair_ref[...].astype(bf16)
    wide_out[...] = wide_ref[...].astype(bf16)
    for index, j in enumerate((0, 2, 3, 5)):
        turned_out[index] = narrow_ref[j].T.astype(bf16)
    for out_ref, source_ref, picks in ((own_narrow, narrow_ref, (0, 2, 3, 5)), (own_wide, wide_ref, (1, 2))):
        size = source_ref.shape[1]
        rows = size // count
        pad = 8 if rows < 8 else rows
        for index, j in enumerate(picks):
            mine = get_rows(source_ref.at[j], rank * rows, rows, slice(None))
            if rows < pad:
                mine = jnp.concatenate([mine, jnp.zeros((pad - rows, size), f32)], axis=0)
            lanes = 128
            if pad < lanes:
                mine = jnp.concatenate([mine, jnp.zeros((lanes - pad, size), f32)], axis=0)
            tall[0:size, :] = mine.T

            def body(block):
                put_rows(tall, size + block * rows, slice(None), get_rows(tall, source(block) * rows, rows, slice(None)))

            each_block(count, body)
            out_ref[index] = tall[size : 2 * size, :].T[0 : out_ref.shape[1]]


def unpack_kernel(groups, *refs):
    pieces, outs, mats = refs[:groups], refs[groups : groups + 4], refs[groups + 4 :]
    parts, _ = layout(256, LATE)
    done = 0
    for piece in pieces:
        count = piece.shape[0]

        def body(block, piece=piece, done=done):
            spread(piece[block].astype(f32), parts, mats, source(block + done))

        each_block(count, body)
        done += count
    for out_ref, ref in zip(outs, mats):
        out_ref[...] = ref[...].astype(bf16)


def shifted_frame(frame_ref, tile_ref, up_ref, down_ref):
    rows, cols, width = frame_ref.shape[0] - 2, 56, 256
    frame_ref[...] = jnp.zeros_like(frame_ref)
    frame_ref[0, 8 : 8 + cols, :] = up_ref[...].astype(f32)[-cols:]
    frame_ref[1 : 1 + rows, 8 : 8 + cols, :] = tile_ref[...].astype(f32).reshape(rows, cols, width)
    frame_ref[rows + 1, 8 : 8 + cols, :] = down_ref[...].astype(f32)[:cols]
    return [frame_ref[:, 7 + shift : 7 + shift + cols, :] for shift in range(3)]


def front_kernel(tile_ref, up_ref, down_ref, vec_ref, x0_ref, h1_ref, frame):
    rows = frame.shape[0] - 2
    moved = shifted_frame(frame, tile_ref, up_ref, down_ref)
    total = moved[1][1:-1] + vec_ref[9:10, :]
    for tap in range(9):
        total = total + vec_ref[tap : tap + 1, :] * moved[tap % 3][tap // 3 : tap // 3 + rows]
    x0 = total.reshape(x0_ref.shape)
    x0_ref[...] = x0
    unit, _ = norm_parts(x0)
    h1_ref[...] = (unit * vec_ref[10:11, :] + vec_ref[11:12, :]).astype(bf16)


def picked_cells(shape, cell_axis, size_ref, corner, tile_rows, cols):
    half = cols // 2
    key_shape = tuple(1 if axis == cell_axis else n for axis, n in enumerate(shape))
    key = lax.broadcasted_iota(jnp.int32, key_shape, 1 - cell_axis)
    row = jnp.zeros_like(key)
    for step in range(1, tile_rows // 2):
        row = row + (key >= step * half).astype(jnp.int32)
    col = 2 * (key - row * half) + corner % 2
    row = 2 * row + corner // 2
    inside = (row + lax.axis_index("row") * tile_rows < size_ref[0, 0]) & (col < size_ref[0, 1])
    target = jnp.where(inside, row * cols + col, -1)
    cell = lax.broadcasted_iota(jnp.int32, shape, cell_axis)
    return (cell == target).astype(f32).astype(bf16)


def keys_kernel(tile_rows, cols, size_ref, h1_ref, vec_ref, reduce_ref, keyval_ref, blocks_ref, c_ref, kn_ref, kv_ref):
    keys = c_ref.shape[0]
    for corner in range(4):
        pick = picked_cells((keys, h1_ref.shape[0]), 1, size_ref, corner, tile_rows, cols)
        blocks_ref[:, corner * 256 : corner * 256 + 256] = contract(pick, h1_ref[...], 1, 0).astype(bf16)
    c = contract(blocks_ref[...], reduce_ref[...], 1, 0) + vec_ref[13:14, :]
    c_ref[...] = c
    unit, _ = norm_parts(c)
    kn = (unit * vec_ref[14:15, :] + vec_ref[15:16, :]).astype(bf16)
    kn_ref[...] = kn
    kv = contract(kn, keyval_ref[...], 1, 0)
    kv_ref[:, 0:256] = kv[:, 0:256].astype(bf16)
    kv_ref[:, 256:512] = (kv[:, 256:512] + vec_ref[16:17, :]).astype(bf16)


def over_heads(body, heads, unroll):
    if unroll:
        for head in range(heads):
            body(head)
    else:

        def step(head, carry):
            body(head)
            return carry

        lax.fori_loop(0, heads, step, 0)


def over_blocks(block, tokens, step):
    if tokens == step:
        block(0)
    else:

        def go(index, carry):
            block(pl.multiple_of(index * step, step))
            return carry

        lax.fori_loop(0, tokens // step, go, 0)


def head_columns(head):
    group = head // 4
    if isinstance(head, int):
        return slice(group * 128, group * 128 + 128)
    return pl.ds(pl.multiple_of(group * 128, 128), 128)


def head_rows(head, base=0):
    if isinstance(head, int):
        return slice(base + head * 32, base + head * 32 + 32)
    return pl.ds(pl.multiple_of(base + head * 32, 32), 32)


def attend_kernel(
    step, unroll, h1_ref, query_ref, vec_ref, near_ref, far_ref, mask_ref, q_ref, k_ref, v_ref, o_ref, log_ref
):
    tokens = h1_ref.shape[0]
    half = near_ref.shape[0]
    for start, ref in ((0, near_ref), (half, far_ref)):
        k_ref[start : start + half, :] = ref[:, 0:256]
        v_ref[start : start + half, :] = ref[:, 256:512]
    q_ref[...] = (contract(h1_ref[...], query_ref[...], 1, 0) + vec_ref[12:13, :]).astype(bf16)
    scale = 32**-0.5 * LOG2E
    lane = lax.broadcasted_iota(jnp.int32, (1, 128), 1)
    mask = mask_ref[...]

    def one_head(head):
        cols = head_columns(head)
        mine = lane // 32 == head % 4
        keys = jnp.where(mine, k_ref[:, cols], 0)
        values = jnp.where(mine, v_ref[:, cols], 0)

        def block(start):
            rows = pl.ds(start, step)
            scores = contract(q_ref[rows, cols], keys, 1, 1) * scale + mask
            top = jnp.max(scores, axis=1, keepdims=True)
            exponent = jnp.exp2(scores - top)
            total = jnp.sum(exponent, axis=1, keepdims=True)
            probs = (exponent * (1.0 / total)).astype(bf16)
            out = contract(probs, values, 1, 0)
            o_ref[rows, cols] = jnp.where(mine, out, o_ref[rows, cols])
            log_ref[rows, :] = jnp.where(lane == head, top + jnp.log2(total), log_ref[rows, :])

        over_blocks(block, tokens, step)

    over_heads(one_head, HEADS, unroll)


def feed_kernel(
    o_ref, x0_ref, out_ref, early_ref, vec_ref, dy_ref, y_ref, do_ref, dx1_ref, up_grad, down_grad, out_grad, sums_ref,
    up_ref, down_ref, up_wide, down_wide,
):
    parts, _ = layout(256, EARLY)

    def body(block):
        spread(early_ref[block].astype(f32), parts, (up_wide, down_wide), block)

    each_block(early_ref.shape[0], body)
    up_ref[...] = up_wide[...].astype(bf16)
    down_ref[...] = down_wide[...].astype(bf16)
    o = o_ref[...].astype(bf16)
    x1 = x0_ref[...] + (contract(o, out_ref[...], 1, 0) + vec_ref[17:18, :])
    unit, inverse = norm_parts(x1)
    h2 = (unit * vec_ref[18:19, :] + vec_ref[19:20, :]).astype(bf16)
    dy_low = dy_ref[...]
    dy = dy_low.astype(f32)
    dyt = turned(dy_low)
    h2t = turned(h2)
    y = x1 + vec_ref[20:21, :]
    dh2 = jnp.zeros_like(y)
    for col in range(FF // 256):
        cols = slice(col * 256, col * 256 + 256)
        u = contract(h2, up_ref[:, cols], 1, 0) + vec_ref[21 + col : 22 + col, :]
        phi_sum = 0.5 * (1.0 + lax.erf(u * (2.0**-0.5)))
        density = jnp.exp(-0.5 * u * u) * ((2.0 * math.pi) ** -0.5)
        g = (u * phi_sum).astype(bf16)
        y = y + contract(g, down_ref[cols, :], 1, 0)
        down_grad[:, cols] = contract(dyt, g, 1, 0)
        du = (contract(dy_low, down_ref[cols, :], 1, 1) * (phi_sum + u * density)).astype(bf16)
        up_grad[:, cols] = contract(h2t, du, 1, 0)
        sums_ref[21 + col : 22 + col, :] = col_sum(du.astype(f32))
        dh2 = dh2 + contract(du, up_ref[:, cols], 1, 1)
    y_ref[...] = y.astype(bf16)
    back, gain_sum, bias_sum = norm_back(dh2, unit, inverse, vec_ref[18:19, :])
    dx1 = dy + back
    dx1_ref[...] = dx1
    da = dx1.astype(bf16)
    do_ref[...] = contract(da, out_ref[...], 1, 1).astype(bf16)
    out_grad[...] = contract(turned(o), da, 1, 0)
    sums_ref[0:17, :] = jnp.zeros((17, 256), f32)
    sums_ref[17:18, :] = col_sum(da.astype(f32))
    sums_ref[18:19, :] = gain_sum
    sums_ref[19:20, :] = bias_sum
    sums_ref[20:21, :] = col_sum(dy)


def rotate(left_turned, grad, right):
    half = contract(left_turned, grad.astype(bf16), 1, 0).astype(bf16)
    return contract(half, right, 1, 0)


def rotate_turned(grad_turned, left, right):
    half = contract(grad_turned.astype(bf16), left, 1, 0).astype(bf16)
    return contract(turned(half), right, 1, 0)


def share_out(keep_ref, send_ref, parts, mats):
    half = keep_ref.shape[0]
    for ref, base in ((keep_ref, 0), (send_ref, half)):

        def body(block, ref=ref, base=base):
            collect(ref, block, parts, mats, source(block + base))

        each_block(half, body)


def early_turn_kernel(up_grad, down_grad, turned_ref, narrow_ref, wide_ref, keep_ref, send_ref, up, down):
    up[...] = rotate(turned_ref[3], up_grad[...], wide_ref[0])
    down[...] = rotate_turned(down_grad[...], wide_ref[1], narrow_ref[6])
    share_out(keep_ref, send_ref, layout(256, EARLY)[0], (up, down))


def attend_back_kernel(
    step, unroll, q_ref, k_ref, v_ref, mask_ref, o_ref, log_ref, g_ref, h1_ref,
    dq_ref, keep_ref, send_ref, query_grad, bias_ref, dq_wide, dkv, ps, dss, qt, gt,
):
    tokens, width = q_ref.shape
    scale = 32**-0.5
    lane = lax.broadcasted_iota(jnp.int32, (1, 128), 1)
    mask = mask_ref[...]
    qt[...] = turned(q_ref[...])
    gt[...] = turned(g_ref[...])

    def one_head(head):
        cols = head_columns(head)
        mine = lane // 32 == head % 4
        keys = jnp.where(mine, k_ref[:, cols], 0)
        values = jnp.where(mine, v_ref[:, cols], 0)

        def block(start):
            rows = pl.ds(start, step)
            grad = g_ref[rows, cols]
            inner = jnp.sum(jnp.where(mine, grad.astype(f32) * o_ref[rows, cols], 0.0), axis=1, keepdims=True)
            if isinstance(head, int):
                log = log_ref[rows, head : head + 1]
            else:
                log = jnp.sum(jnp.where(lane == head, log_ref[rows, :], 0.0), axis=1, keepdims=True)
            scores = contract(q_ref[rows, cols], keys, 1, 1)
            probs = jnp.exp2(scores * (scale * LOG2E) + mask - log)
            grad_scores = (probs * (contract(grad, values, 1, 1) - inner)).astype(bf16)
            ps[rows, :] = probs.astype(bf16)
            dss[rows, :] = grad_scores
            out = contract(grad_scores, keys, 1, 0) * scale
            dq_wide[rows, cols] = jnp.where(mine, out, dq_wide[rows, cols])

        over_blocks(block, tokens, step)
        dkv[head_rows(head), :] = contract(qt[head_rows(head), :], dss[...], 1, 0) * scale
        dkv[head_rows(head, width), :] = contract(gt[head_rows(head), :], ps[...], 1, 0)

    over_heads(one_head, HEADS, unroll)
    dq = dq_wide[...].astype(bf16)
    dq_ref[...] = dq
    bias_ref[...] = col_sum(dq.astype(f32))
    half = keep_ref.shape[0]
    keep_ref[...] = dkv[:, 0:half].T
    send_ref[...] = dkv[:, half:].T
    query_grad[...] = contract(turned(h1_ref[...]), dq, 1, 0)


def split_kernel(count, terms, *refs):
    total = refs[0][...].astype(f32)
    for ref in refs[1:terms]:
        total = total + ref[...].astype(f32)
    rows = total.shape[0] // count
    refs[terms][...] = total[:rows]
    for index in range(1, count):
        refs[terms + index][...] = total[index * rows : (index + 1) * rows].astype(bf16)


def split_sum(terms, count):
    rows = terms[0].shape[0] // count
    tail = terms[0].shape[1:]
    outs = [((rows,) + tail, f32)] + [((rows,) + tail, bf16)] * (count - 1)
    return run("split_sum", functools.partial(split_kernel, count, len(terms)), outs, terms, mib=30)


def scatter_sum(keep, send, groups):
    terms = [keep, swap(send, "row", 1)]
    for axis, stride, size in groups:
        parts = split_sum(terms, size)
        terms = [parts[0]] + [swap(parts[j], axis, j * stride) for j in range(1, size)]
    return terms


def row_parts():
    return [("row", stride, size) for stride, size in rel_digits()[1:]]


def side_by_side(x, groups):
    for axis, stride, size in groups:
        x = jnp.concatenate([x] + [swap(x, axis, j * stride) for j in range(1, size)], axis=0)
    return x


def middle_turn_kernel(query_grad, out_grad, turned_ref, narrow_ref, query_ref, out_ref):
    query_ref[...] = rotate(turned_ref[0], query_grad[...], narrow_ref[1])
    out_ref[...] = rotate(turned_ref[2], out_grad[...], narrow_ref[4])


def keys_back_kernel(
    terms, *refs
):
    (kn_ref, c_ref, vec_ref, keyval_ref, blocks_ref, turned_ref, narrow_ref, pair_ref, wide_ref, query, out,
     keep_ref, send_ref, dc_ref, sums_ref, reduce, keyval) = refs[terms:]
    dkv = refs[0][...]
    for ref in refs[1:terms]:
        dkv = dkv + ref[...].astype(f32)
    high = dkv.astype(bf16)
    rest = (dkv - high.astype(f32)).astype(bf16)
    dkn = contract(high, keyval_ref[...], 1, 1) + contract(rest, keyval_ref[...], 1, 1)
    unit, inverse = norm_parts(c_ref[...])
    back, gain_sum, bias_sum = norm_back(dkn, unit, inverse, vec_ref[14:15, :])
    dc = back.astype(bf16)
    dc_ref[...] = dc
    knt = turned(kn_ref[...])
    keyval[...] = rotate(turned_ref[1], contract(knt, high, 1, 0) + contract(knt, rest, 1, 0), pair_ref[...])
    reduce[...] = rotate_turned(contract(turned(dc), blocks_ref[...], 1, 0), wide_ref[2], narrow_ref[7])
    share_out(keep_ref, send_ref, layout(256, LATE)[0], (reduce, keyval, query, out))
    sums_ref[0:1, :] = col_sum(dc.astype(f32))
    sums_ref[1:2, :] = gain_sum
    sums_ref[2:3, :] = bias_sum
    sums_ref[3:4, :] = col_sum(dkv[:, 256:512])


def cells_back_kernel(
    tile_rows, cols, size_ref, dq_ref, dc_ref, query_ref, reduce_ref, x0_ref, dx1_ref, vec_ref, tile_ref, up_ref, down_ref,
    feed_sums, key_sums, query_sum, dx0_ref, head_ref, tail_ref, sums_ref, frame,
):
    tokens = x0_ref.shape[0]
    dh1 = contract(dq_ref[...], query_ref[...], 1, 1)
    for corner in range(4):
        pick = picked_cells((tokens, dc_ref.shape[0]), 0, size_ref, corner, tile_rows, cols)
        placed = contract(pick, dc_ref[...], 1, 0).astype(bf16)
        dh1 = dh1 + contract(placed, reduce_ref[corner * 256 : corner * 256 + 256, :], 1, 1)
    unit, inverse = norm_parts(x0_ref[...])
    back, gain_sum, bias_sum = norm_back(dh1, unit, inverse, vec_ref[10:11, :])
    dx0 = dx1_ref[...] + back
    dx0_ref[...] = dx0
    head_ref[...] = dx0[0:64].astype(bf16)
    tail_ref[...] = dx0[tokens - 64 :].astype(bf16)
    sums_ref[...] = feed_sums[...]
    moved = shifted_frame(frame, tile_ref, up_ref, down_ref)
    grid = dx0.reshape(tile_rows, cols, 256)
    for tap in range(9):
        product = moved[tap % 3][tap // 3 : tap // 3 + tile_rows] * grid
        sums_ref[tap : tap + 1, :] = col_sum(product.reshape(tokens, 256))
    sums_ref[9:10, :] = col_sum(dx0)
    sums_ref[10:11, :] = gain_sum
    sums_ref[11:12, :] = bias_sum
    sums_ref[12:13, :] = query_sum[...]
    sums_ref[13:17, :] = key_sums[...]


def input_grad_kernel(tile_rows, dx0_ref, up_ref, down_ref, vec_ref, out_ref, frame):
    moved = shifted_frame(frame, dx0_ref, up_ref, down_ref)
    total = moved[1][1:-1]
    for tap in range(9):
        down, right = 2 - tap // 3, 2 - tap % 3
        total = total + vec_ref[tap : tap + 1, :] * moved[right][down : down + tile_rows]
    out_ref[...] = total.reshape(out_ref.shape)


def adam_kernel(base, terms, *refs):
    first_ref, second_ref, moment_ref, square_ref, step_ref = refs[terms:]
    total = refs[0][...]
    for ref in refs[1:terms]:
        total = total + ref[...].astype(f32)
    rows = total.shape[0]
    moment = BETA * first_ref[base : base + rows, :] + (1.0 - BETA) * total
    square = BETA * second_ref[base : base + rows, :] + (1.0 - BETA) * total * total
    moment_ref[...] = moment
    square_ref[...] = square
    step = moment * (1.0 / CORRECTION) / (jnp.sqrt(square * (1.0 / CORRECTION)) + ADAM_EPS)
    step_ref[...] = step.astype(bf16)


def finish_kernel(
    width, late_near, late_far, early_near, early_far, own_narrow, own_wide, narrow_ref, pair_ref, wide_ref,
    weights_ref, ema_ref, late_first, late_second, early_first, early_second,
    weights_out, ema_out, first_out, second_out, chunk,
):
    rights = {
        0: narrow_ref.at[1], 1: pair_ref, 2: narrow_ref.at[4], 3: wide_ref.at[0], 4: narrow_ref.at[6], 5: narrow_ref.at[7]
    }
    lefts = {0: (own_narrow, 0), 1: (own_narrow, 1), 2: (own_narrow, 2), 3: (own_narrow, 3), 4: (own_wide, 0), 5: (own_wide, 1)}
    base = 0
    for group, near, far in ((LATE, late_near, late_far), (EARLY, early_near, early_far)):
        parts, count = layout(width, group)
        blocks_near = near[...].astype(f32)
        blocks_far = far[...].astype(f32)
        for j, first, rows, blocks in parts:
            left_ref, index = lefts[j]
            left = left_ref[index].astype(bf16)
            half = left.shape[1] // 2
            sides = []
            for col in range(blocks):
                at = slice(first + col * rows, first + (col + 1) * rows)
                near_part = blocks_near[:, at, :].reshape(half, width).astype(bf16)
                far_part = blocks_far[:, at, :].reshape(half, width).astype(bf16)
                sides.append(contract(left[:, 0:half], near_part, 1, 0) + contract(left[:, half:], far_part, 1, 0))
            side = sides[0] if blocks == 1 else jnp.concatenate(sides, axis=1)
            full = contract(side.astype(bf16), rights[j][...], 1, 1)
            for col in range(blocks):
                at = slice(base + first + col * rows, base + first + (col + 1) * rows)
                old = weights_ref[at, :]
                piece = full[0:rows, col * width : (col + 1) * width]
                chunk[at, :] = old - MATRIX_RATES[j] * (piece + WEIGHT_DECAY * old)
        base += count
    from_chunk(chunk, 0, LATE, weights_out, width)
    split = layout(width, LATE)[1]
    from_chunk(chunk, split, EARLY, weights_out, width)
    chunk[...] = EMA_KEEP * ema_ref[...] + (1.0 - EMA_KEEP) * chunk[...]
    from_chunk(chunk, 0, LATE, ema_out, width)
    from_chunk(chunk, split, EARLY, ema_out, width)
    for late, early, out in ((late_first, early_first, first_out), (late_second, early_second, second_out)):
        from_chunk(late, 0, LATE, out, width)
        from_chunk(early, 0, EARLY, out, width)


def vector_kernel(total_ref, vec_ref, first_ref, second_ref, ema_ref, vec_out, first_out, second_out, ema_out):
    total = total_ref[...]
    moment = BETA * first_ref[...] + (1.0 - BETA) * total
    square = BETA * second_ref[...] + (1.0 - BETA) * total * total
    first_out[...] = moment
    second_out[...] = square
    step = moment * (1.0 / CORRECTION) / (jnp.sqrt(square * (1.0 / CORRECTION)) + ADAM_EPS)
    new = vec_ref[...] - VECTOR_RATE * step
    vec_out[...] = new
    ema_out[...] = EMA_KEEP * ema_ref[...] + (1.0 - EMA_KEEP) * new


def on_device(
    patches,
    cotangent,
    image_sizes,
    weights,
    first_moment,
    second_moment,
    weight_ema,
    vectors,
    vec_first,
    vec_second,
    vec_ema,
    basis_narrow,
    basis_pair,
    basis_wide,
):
    _, rows, cols, width = patches.shape
    tokens = rows * cols
    shards = device_count()
    tile = patches.reshape(tokens, width)
    dy = cotangent.reshape(tokens, width)
    per = weights.shape[1]
    late_rows, early_rows = layout(width, LATE)[1], layout(width, EARLY)[1]
    chunk = late_rows + early_rows
    ranks = lax.axis_size("row")
    own_keys = tokens // 4
    keys = own_keys * ranks
    frame = ((rows + 2, cols + 16, width), f32)
    img_part = ("img", 1, lax.axis_size("img"))
    xy_parts = row_parts()

    def border(head, tail):
        up = lax.ppermute(tail, "row", [(i, i + 1) for i in range(ranks - 1)])
        return up, lax.ppermute(head, "row", [(i + 1, i) for i in range(ranks - 1)])

    late, early = run(
        "pack",
        functools.partial(pack_kernel, width),
        [((late_rows, width), bf16), ((early_rows, width), bf16)],
        [weights],
        scratch=[((chunk, width), f32)],
        mib=8,
    )
    up_halo, down_halo = border(tile[:64], tile[tokens - 64 :])
    late_near = side_by_side(late[None], [img_part] + xy_parts[::-1])
    late_far = swap(late_near, "row", 1)
    early_all = lax.all_gather(early, ("img", "row"), axis=0, tiled=False)

    x0, h1 = run(
        "front",
        front_kernel,
        [((tokens, width), f32), ((tokens, width), bf16)],
        [tile, up_halo, down_halo, vectors],
        scratch=[frame],
        mib=16,
    )
    w_reduce, w_keyval, w_query, w_out = run(
        "unpack",
        functools.partial(unpack_kernel, 2),
        [((4 * width, width), bf16), ((width, 2 * width), bf16), ((width, width), bf16), ((width, width), bf16)],
        [late_near, late_far],
        scratch=[((4 * width, width), f32), ((width, 2 * width), f32), ((width, width), f32), ((width, width), f32)],
        mib=16,
    )
    blocks, c, kn, own_kv = run(
        "keys",
        functools.partial(keys_kernel, rows, cols),
        [((own_keys, 4 * width), bf16), ((own_keys, width), f32), ((own_keys, width), bf16), ((own_keys, 2 * width), bf16)],
        [image_sizes, h1, vectors, w_reduce, w_keyval],
        scalars=(0,),
        mib=16,
    )
    kv_near = side_by_side(own_kv, xy_parts[::-1])
    kv_far = swap(kv_near, "row", 1)

    rounded = run(
        "bases",
        bases_kernel,
        [
            ((8, width, width), bf16),
            ((4, width, width), bf16),
            ((2 * width, 2 * width), bf16),
            ((3, FF, FF), bf16),
            ((4, 16, width), f32),
            ((2, max(16, FF // shards), FF), f32),
        ],
        [basis_narrow, basis_pair, basis_wide],
        scratch=[((2 * FF, 128), f32)],
        mib=48,
    )
    narrow, narrow_turned, pair, wide, own_narrow, own_wide = rounded
    old_chunk, ema_chunk, first_chunk, second_chunk = run(
        "moments",
        functools.partial(moments_kernel, width),
        [((chunk, width), f32)] * 4,
        [weights, weight_ema, first_moment, second_moment],
        mib=8,
    )

    height, across = image_sizes[0, 0], image_sizes[0, 1]
    key_row = rel_rows()[:, None, None] * (rows // 2) + jnp.arange(rows // 2)[None, :, None]
    key_col = jnp.arange(cols // 2)[None, None, :]
    allowed = (2 * key_row < height) & (2 * key_col < across)
    mask = jnp.where(allowed, 0.0, -1e30).astype(f32).reshape(1, -1)

    unroll = keys <= 1024
    step = tokens if unroll else 32
    q, k, v, o, log = run(
        "attend",
        functools.partial(attend_kernel, step, unroll),
        [((tokens, width), bf16), ((keys, width), bf16), ((keys, width), bf16), ((tokens, width), f32), ((tokens, 128), f32)],
        [h1, w_query, vectors, kv_near, kv_far, mask],
        mib=44,
        flops=4 * tokens * keys * width * 8,
    )
    y, do, dx1, up_grad, down_grad, out_grad, feed_sums = run(
        "feed",
        feed_kernel,
        [
            ((tokens, width), bf16),
            ((tokens, width), bf16),
            ((tokens, width), f32),
            ((width, FF), f32),
            ((width, FF), f32),
            ((width, width), f32),
            ((25, width), f32),
        ],
        [o, x0, w_out, early_all, vectors, dy],
        scratch=[((width, FF), bf16), ((FF, width), bf16), ((width, FF), f32), ((FF, width), f32)],
        mib=40,
        flops=12 * tokens * FF * width,
    )
    half = (shards // 2, early_rows, width)
    early_keep, early_send = run(
        "early_turn",
        early_turn_kernel,
        [(half, f32), (half, f32)],
        [up_grad, down_grad, narrow_turned, narrow, wide],
        scratch=[((width, FF), f32), ((FF, width), f32)],
        mib=32,
        flops=4 * FF * FF * width,
    )
    early_terms = scatter_sum(early_keep, early_send, xy_parts + [img_part])

    dq, dkv_keep, dkv_send, query_grad, query_sum = run(
        "attend_back",
        functools.partial(attend_back_kernel, step, unroll),
        [
            ((tokens, width), bf16),
            ((keys // 2, 2 * width), f32),
            ((keys // 2, 2 * width), f32),
            ((width, width), f32),
            ((1, width), f32),
        ],
        [q, k, v, mask, o, log, do, h1],
        scratch=[
            ((tokens, width), f32),
            ((2 * width, keys), f32),
            ((tokens, keys), bf16),
            ((tokens, keys), bf16),
            ((width, tokens), bf16),
            ((width, tokens), bf16),
        ],
        mib=44 if unroll else 60,
        flops=10 * tokens * keys * width * 8,
    )
    dkv_terms = scatter_sum(dkv_keep, dkv_send, xy_parts)
    query_turn, out_turn = run(
        "middle_turn",
        middle_turn_kernel,
        [((width, width), f32), ((width, width), f32)],
        [query_grad, out_grad, narrow_turned, narrow],
        mib=12,
        flops=8 * width**3,
    )
    half = (shards // 2, late_rows, width)
    late_keep, late_send, dc, key_sums = run(
        "keys_back",
        functools.partial(keys_back_kernel, len(dkv_terms)),
        [(half, f32), (half, f32), ((own_keys, width), bf16), ((4, width), f32)],
        list(dkv_terms)
        + [kn, c, vectors, w_keyval, blocks, narrow_turned, narrow, pair, wide, query_turn, out_turn],
        scratch=[((4 * width, width), f32), ((width, 2 * width), f32)],
        mib=36,
        flops=2 * FF * FF * width,
    )
    late_terms = scatter_sum(late_keep, late_send, xy_parts + [img_part])
    dx0, head, tail, vec_grads = run(
        "cells_back",
        functools.partial(cells_back_kernel, rows, cols),
        [((tokens, width), f32), ((64, width), bf16), ((64, width), bf16), ((25, width), f32)],
        [image_sizes, dq, dc, w_query, w_reduce, x0, dx1, vectors, tile, up_halo, down_halo, feed_sums, key_sums, query_sum],
        scratch=[frame],
        scalars=(0,),
        mib=24,
        flops=10 * tokens * width * width,
    )
    grad_up, grad_down = border(head, tail)
    (grad_input,) = run(
        "input_grad",
        functools.partial(input_grad_kernel, rows),
        [((tokens, width), f32)],
        [dx0, grad_up, grad_down, vectors],
        scratch=[frame],
        mib=16,
    )

    def adam(terms, base, count):
        return run(
            "adam",
            functools.partial(adam_kernel, base, len(terms)),
            [((count, width), f32), ((count, width), f32), ((count, width), bf16)],
            list(terms) + [first_chunk, second_chunk],
            mib=8,
        )

    flat_terms = [t.reshape(early_rows, width) for t in early_terms]
    early_first, early_second, early_step = adam(flat_terms, late_rows, early_rows)
    flat_terms = [t.reshape(late_rows, width) for t in late_terms]
    late_first, late_second, late_step = adam(flat_terms, 0, late_rows)
    early_near = side_by_side(early_step[None], [img_part] + xy_parts[::-1])
    early_far = swap(early_near, "row", 1)
    step_near = side_by_side(late_step[None], [img_part] + xy_parts[::-1])
    step_far = swap(step_near, "row", 1)

    vec_total = total_all(vec_grads)
    new_vectors, vec_moment, vec_square, new_vec_ema = run(
        "vector_step",
        vector_kernel,
        [(vectors.shape, f32)] * 4,
        [vec_total, vectors, vec_first, vec_second, vec_ema],
        mib=4,
    )
    new_weights, new_ema, new_first, new_second = run(
        "finish",
        functools.partial(finish_kernel, width),
        [((1, per), f32)] * 4,
        [
            step_near, step_far, early_near, early_far, own_narrow, own_wide, narrow, pair, wide,
            old_chunk, ema_chunk, late_first, late_second, early_first, early_second,
        ],
        scratch=[((chunk, width), f32)],
        mib=40,
    )
    return (
        y.reshape(patches.shape),
        grad_input.reshape(patches.shape),
        new_weights,
        new_first,
        new_second,
        new_ema,
        new_vectors,
        vec_moment,
        vec_square,
        new_vec_ema,
    )


def solution(mesh):
    tiles = P("img", "row", None, None)
    packed = P(("img", "row"), None)
    return jax.shard_map(
        on_device,
        mesh=mesh,
        in_specs=(tiles, tiles, P("img", None)) + (packed,) * 4 + (P(),) * 7,
        out_specs=(tiles, tiles) + (packed,) * 4 + (P(),) * 4,
        check_vma=False,
    )
```

```python
import functools
import math

import jax
import jax.numpy as jnp
from jax import lax
from jax.experimental import pallas as pl
from jax.experimental.pallas import tpu as pltpu
from jax.sharding import PartitionSpec as P

HEADS = 8
FF = 1024
STEP = 5

NORM_EPS = 1e-05
ADAM_EPS = 1e-08
BETA = 0.5
WEIGHT_DECAY = 0.05
EMA_KEEP = 0.75
VECTOR_RATE = 0.06
MATRIX_RATES = (0.04, 0.02, 0.25, 0.02, 0.01, 0.01)
CORRECTION = 1.0 - BETA**STEP
LOG2E = math.log2(math.e)
f32 = jnp.float32
bf16 = jnp.bfloat16
LATE = (5, 1, 0, 2)
EARLY = (3, 4)


def matrix_shapes(width, hidden):
    return (
        (width, width),
        (width, 2 * width),
        (width, width),
        (width, hidden),
        (hidden, width),
        (4 * width, width),
    )


def contract(a, b, ca, cb, **kw):
    return lax.dot_general(
        a, b, (((ca,), (cb,)), ((), ())), preferred_element_type=f32, **kw
    )


def swap(x, axis, step):
    count = lax.axis_size(axis)
    return lax.ppermute(x, axis, [(i, i ^ step) for i in range(count)])


def row_groups():
    left = lax.axis_size("row") // 2
    groups, stride = [(1, 2)], 2
    while left > 1:
        size = 4 if left % 4 == 0 else 2
        groups.append((stride, size))
        left //= size
        stride *= size
    return groups


def rel_digits():
    groups = row_groups()
    return [groups[0]] + groups[1:][::-1]


def source(block):
    sizes = lax.axis_size("img")
    img, rest = block % sizes, block // sizes
    rel = 0
    for stride, size in reversed(rel_digits()):
        rel = rel + (rest % size) * stride
        rest = rest // size
    row = lax.axis_index("row") ^ rel
    return (lax.axis_index("img") ^ img) * lax.axis_size("row") + row


def device_count():
    return lax.axis_size("img") * lax.axis_size("row")


def run(name, body, outs, args, scratch=(), mib=6, scalars=(), micros=1.0, after=(), raw=(), sems=0):
    count = len(args)

    def without(*refs):
        body(*refs[:count], *refs[count + len(after) :])

    space = {index: pltpu.SMEM for index in scalars} | {index: pl.ANY for index in raw}
    specs = [pl.BlockSpec(memory_space=space.get(index, pltpu.VMEM)) for index in range(count)]
    return pl.pallas_call(
        without,
        out_shape=tuple(jax.ShapeDtypeStruct(shape, dtype) for shape, dtype in outs),
        in_specs=specs + [pl.BlockSpec(memory_space=pl.ANY)] * len(after),
        out_specs=tuple(pl.BlockSpec(memory_space=pltpu.VMEM) for _ in outs),
        scratch_shapes=[pltpu.VMEM(shape, dtype) for shape, dtype in scratch]
        + ([pltpu.SemaphoreType.DMA((sems,))] if sems else []),
        compiler_params=pltpu.CompilerParams(vmem_limit_bytes=mib * 2**20),
        cost_estimate=pl.CostEstimate(flops=0, bytes_accessed=int(micros * 3.6e6), transcendentals=0),
        name=name,
    )(*args, *after)


def each_block(count, body):
    if count <= 32:
        for index in range(count):
            body(index)
    else:

        def step(index, carry):
            body(index)
            return carry

        lax.fori_loop(0, count, step, 0)


def put_rows(ref, start, cols, value):
    count = value.shape[0]
    if count % 8 == 0:
        ref[pl.ds(pl.multiple_of(start, 8), count), cols] = value
    else:
        for row in range(count):
            ref[pl.ds(start + row, 1), cols] = value[row : row + 1]


def get_rows(ref, start, count, cols):
    if count % 8 == 0:
        return ref[pl.ds(pl.multiple_of(start, 8), count), cols]
    return jnp.concatenate([ref[pl.ds(start + row, 1), cols] for row in range(count)], axis=0)


def layout(width, group):
    dims = matrix_shapes(width, FF)
    found, start = [], 0
    for j in group:
        rows = dims[j][0] // device_count()
        blocks = dims[j][1] // width
        found.append((j, start, rows, blocks))
        start += rows * blocks
    return found, start


def packed_starts(width):
    dims = matrix_shapes(width, FF)
    starts, start = [], 0
    for m, n in dims:
        starts.append(start)
        start += m * n // device_count()
    return starts


def spread(block, parts, mats, start_of):
    for (j, first, rows, blocks), ref in zip(parts, mats):
        for col in range(blocks):
            piece = block[first + col * rows : first + (col + 1) * rows]
            put_rows(ref, start_of * rows, slice(col * 256, col * 256 + 256), piece)


def collect(out_ref, index, parts, mats, start_of):
    for (j, first, rows, blocks), ref in zip(parts, mats):
        for col in range(blocks):
            piece = get_rows(ref, start_of * rows, rows, slice(col * 256, col * 256 + 256))
            out_ref[index, first + col * rows : first + (col + 1) * rows, :] = piece


def norm_parts(values):
    centred = values - jnp.mean(values, axis=-1, keepdims=True)
    inverse = lax.rsqrt(jnp.mean(centred * centred, axis=-1, keepdims=True) + NORM_EPS)
    return centred * inverse, inverse


def norm_back(grad, unit, inverse, gain):
    grad_unit = grad * gain
    back = grad_unit - jnp.mean(grad_unit, axis=-1, keepdims=True)
    back = back - unit * jnp.mean(grad_unit * unit, axis=-1, keepdims=True)
    gain_sum = jnp.sum(grad * unit, axis=0, keepdims=True)
    return back * inverse, gain_sum, jnp.sum(grad, axis=0, keepdims=True)


def turned(value):
    return value.astype(f32).T.astype(bf16)


def col_sum(value):
    return jnp.sum(value, axis=0, keepdims=True)


def pack_kernel(width, w_ref, out_ref, chunk):
    to_chunk(w_ref, chunk, width)
    out_ref[...] = chunk[...].astype(bf16)


def to_chunk(flat_ref, out_ref, width):
    dims, starts, base = matrix_shapes(width, FF), packed_starts(width), 0
    for group in (LATE, EARLY):
        parts, count = layout(width, group)
        for j, first, rows, blocks in parts:
            for col in range(blocks):
                for row in range(rows):
                    at = starts[j] + row * dims[j][1] + col * width
                    place = base + first + col * rows + row
                    out_ref[place : place + 1, :] = flat_ref[0:1, at : at + width]
        base += count


def from_chunk(values, base, group, out_ref, width):
    dims, starts = matrix_shapes(width, FF), packed_starts(width)
    parts, _ = layout(width, group)
    for j, first, rows, blocks in parts:
        for col in range(blocks):
            for row in range(rows):
                at = starts[j] + row * dims[j][1] + col * width
                place = base + first + col * rows + row
                out_ref[0:1, at : at + width] = values[place : place + 1, :]


def moments_kernel(width, *refs):
    for index in range(4):
        to_chunk(refs[index], refs[4 + index], width)


def own_rows(matrix_ref, out_ref, tall):
    count = device_count()
    rank = lax.axis_index("img") * lax.axis_size("row") + lax.axis_index("row")
    size = matrix_ref.shape[0]
    rows = size // count
    place = lax.broadcasted_iota(jnp.int32, (128, 1), 0)
    place = jnp.where(place < rows, place + rank * rows, -1)
    pick = (lax.broadcasted_iota(jnp.int32, (128, size), 1) == place).astype(f32).astype(bf16)
    tall[0:size, :] = contract(pick, matrix_ref[...], 1, 0).T

    def body(block):
        put_rows(tall, size + block * rows, slice(None), get_rows(tall, source(block) * rows, rows, slice(None)))

    each_block(count, body)
    out_ref[...] = tall[size : 2 * size, :].T[0 : out_ref.shape[0]]


def small_bases_kernel(narrow_ref, pair_ref, narrow_out, turned_out, pair_out, own_ref, tall):
    narrow_out[...] = narrow_ref[...].astype(bf16)
    pair_out[...] = pair_ref[...].astype(bf16)
    for index, j in enumerate((0, 2, 3, 5)):
        turned_out[index] = narrow_ref[j].T.astype(bf16)
        own_rows(narrow_out.at[j], own_ref.at[index], tall)


def wide_bases_kernel(wide_ref, wide_out, own_ref, tall, buffer, sems):
    count, size = wide_ref.shape[0], wide_ref.shape[1]
    rows, depth = buffer.shape[1], buffer.shape[0]
    each = size // rows
    total = count * each

    def copy(index):
        at = wide_ref.at[index // each, pl.ds(index % each * rows, rows)]
        return pltpu.make_async_copy(at, buffer.at[index % depth], sems.at[index % depth])

    for index in range(depth):
        copy(index).start()
    for index in range(total):
        copy(index).wait()
        first = index % each * rows
        wide_out[index // each, first : first + rows, :] = buffer[index % depth].astype(bf16)
        if index + depth < total:
            copy(index + depth).start()
    for index in range(2):
        own_rows(wide_out.at[index + 1], own_ref.at[index], tall)


def stack_kernel(split, *refs):
    count = len(refs) - 2
    for index in range(count):
        refs[count][index] = refs[index][0:split, :]
        refs[count + 1][index] = refs[index][split:, :]


def unpack(pieces, group, mats):
    parts, _ = layout(256, group)
    wanted = [(part, ref) for part, ref in zip(parts, mats) if ref is not None]
    done = 0
    for piece in pieces:

        def body(block, piece=piece, done=done):
            spread(piece[block].astype(f32), [p for p, _ in wanted], [r for _, r in wanted], source(block + done))

        each_block(piece.shape[0], body)
        done += piece.shape[0]


def shifted_frame(frame_ref, tile_ref, up_ref, down_ref):
    rows, cols, width = frame_ref.shape[0] - 2, 56, 256
    frame_ref[...] = jnp.zeros_like(frame_ref)
    frame_ref[0, 8 : 8 + cols, :] = up_ref[...].astype(f32)[-cols:]
    frame_ref[1 : 1 + rows, 8 : 8 + cols, :] = tile_ref[...].astype(f32).reshape(rows, cols, width)
    frame_ref[rows + 1, 8 : 8 + cols, :] = down_ref[...].astype(f32)[:cols]
    return [frame_ref[:, 7 + shift : 7 + shift + cols, :] for shift in range(3)]


def front_kernel(tile_rows, cols, size_ref, tile_ref, up_ref, down_ref, vec_ref, x0_ref, h1_ref, mask_ref, vec_out, frame):
    rows = frame.shape[0] - 2
    vec_out[...] = vec_ref[...]
    moved = shifted_frame(frame, tile_ref, up_ref, down_ref)
    total = moved[1][1:-1] + vec_ref[9:10, :]
    for tap in range(9):
        total = total + vec_ref[tap : tap + 1, :] * moved[tap % 3][tap // 3 : tap // 3 + rows]
    x0 = total.reshape(x0_ref.shape)
    x0_ref[...] = x0
    unit, _ = norm_parts(x0)
    h1_ref[...] = (unit * vec_ref[10:11, :] + vec_ref[11:12, :]).astype(bf16)
    half = cols // 2
    own = tile_rows // 2 * half
    key = lax.broadcasted_iota(jnp.int32, mask_ref.shape, 1)
    block = jnp.zeros_like(key)
    for start in range(own, mask_ref.shape[1], own):
        block = block + (key >= start).astype(jnp.int32)
    key = key - block * own
    row = jnp.zeros_like(key)
    for start in range(half, own, half):
        row = row + (key >= start).astype(jnp.int32)
    col = key - row * half
    rel = jnp.zeros_like(key)
    for stride, size in reversed(rel_digits()):
        rel = rel + (block & (size - 1)) * stride
        block = block >> (size.bit_length() - 1)
    row = row + (rel ^ lax.axis_index("row")) * (tile_rows // 2)
    inside = (2 * row < size_ref[0, 0]) & (2 * col < size_ref[0, 1])
    mask_ref[...] = jnp.where(inside, 0.0, -1e30)


def picked_cells(shape, cell_axis, size_ref, corner, tile_rows, cols):
    half = cols // 2
    key_shape = tuple(1 if axis == cell_axis else n for axis, n in enumerate(shape))
    key = lax.broadcasted_iota(jnp.int32, key_shape, 1 - cell_axis)
    row = jnp.zeros_like(key)
    for step in range(1, tile_rows // 2):
        row = row + (key >= step * half).astype(jnp.int32)
    col = 2 * (key - row * half) + corner % 2
    row = 2 * row + corner // 2
    inside = (row + lax.axis_index("row") * tile_rows < size_ref[0, 0]) & (col < size_ref[0, 1])
    target = jnp.where(inside, row * cols + col, -1)
    cell = lax.broadcasted_iota(jnp.int32, shape, cell_axis)
    return (cell == target).astype(f32).astype(bf16)


def keys_kernel(
    tile_rows, cols, size_ref, h1_ref, vec_ref, near_ref, far_ref,
    reduce_ref, keyval_ref, query_ref, out_ref, blocks_ref, c_ref, kn_ref, kv_ref,
    reduce_wide, keyval_wide, query_wide, out_wide,
):
    unpack((near_ref, far_ref), LATE, (reduce_wide, keyval_wide, query_wide, out_wide))
    reduce_ref[...] = reduce_wide[...].astype(bf16)
    keyval_ref[...] = keyval_wide[...].astype(bf16)
    query_ref[...] = query_wide[...].astype(bf16)
    out_ref[...] = out_wide[...].astype(bf16)
    keys = c_ref.shape[0]
    for corner in range(4):
        pick = picked_cells((keys, h1_ref.shape[0]), 1, size_ref, corner, tile_rows, cols)
        blocks_ref[:, corner * 256 : corner * 256 + 256] = contract(pick, h1_ref[...], 1, 0).astype(bf16)
    c = contract(blocks_ref[...], reduce_ref[...], 1, 0) + vec_ref[13:14, :]
    c_ref[...] = c
    unit, _ = norm_parts(c)
    kn = (unit * vec_ref[14:15, :] + vec_ref[15:16, :]).astype(bf16)
    kn_ref[...] = kn
    kv = contract(kn, keyval_ref[...], 1, 0)
    kv_ref[:, 0:256] = kv[:, 0:256].astype(bf16)
    kv_ref[:, 256:512] = (kv[:, 256:512] + vec_ref[16:17, :]).astype(bf16)


def over_heads(body, first, last, unroll):
    if unroll:
        for head in range(first, last):
            body(head)
    else:

        def step(head, carry):
            body(head)
            return carry

        lax.fori_loop(first, last, step, 0)


def over_blocks(block, tokens, step):
    if tokens == step:
        block(0)
    else:

        def go(index, carry):
            block(pl.multiple_of(index * step, step))
            return carry

        lax.fori_loop(0, tokens // step, go, 0)


def head_columns(head):
    group = head // 4
    if isinstance(head, int):
        return slice(group * 128, group * 128 + 128)
    return pl.ds(pl.multiple_of(group * 128, 128), 128)


def head_rows(head, base=0):
    if isinstance(head, int):
        return slice(base + head * 32, base + head * 32 + 32)
    return pl.ds(pl.multiple_of(base + head * 32, 32), 32)


def attend_kernel(
    step, unroll, h1_ref, query_ref, vec_ref, near_ref, far_ref, mask_ref, q_ref, k_ref, v_ref, o_ref, log_ref
):
    tokens = h1_ref.shape[0]
    half = near_ref.shape[0]
    for start, ref in ((0, near_ref), (half, far_ref)):
        k_ref[start : start + half, :] = ref[:, 0:256]
        v_ref[start : start + half, :] = ref[:, 256:512]
    q_ref[...] = (contract(h1_ref[...], query_ref[...], 1, 0) + vec_ref[12:13, :]).astype(bf16)
    scale = 32**-0.5 * LOG2E
    lane = lax.broadcasted_iota(jnp.int32, (1, 128), 1)
    mask = mask_ref[...]

    def one_head(head):
        cols = head_columns(head)
        mine = lane // 32 == head % 4
        keys = jnp.where(mine, k_ref[:, cols], 0)
        values = jnp.where(mine, v_ref[:, cols], 0)

        def block(start):
            rows = pl.ds(start, step)
            scores = contract(q_ref[rows, cols], keys, 1, 1) * scale + mask
            top = jnp.max(scores, axis=1, keepdims=True)
            exponent = jnp.exp2(scores - top)
            total = jnp.sum(exponent, axis=1, keepdims=True)
            probs = (exponent * (1.0 / total)).astype(bf16)
            out = contract(probs, values, 1, 0)
            o_ref[rows, cols] = jnp.where(mine, out, o_ref[rows, cols])
            log_ref[rows, :] = jnp.where(lane == head, top + jnp.log2(total), log_ref[rows, :])

        over_blocks(block, tokens, step)

    over_heads(one_head, 0, HEADS, unroll)


def feed_kernel(
    o_ref, x0_ref, out_ref, near_ref, far_ref, vec_ref, dy_ref,
    y_ref, do_ref, dx1_ref, up_grad, down_grad, out_grad, sums_ref, up_ref, down_ref, up_wide, down_wide,
):
    unpack((near_ref, far_ref), EARLY, (up_wide, down_wide))
    up_ref[...] = up_wide[...].astype(bf16)
    down_ref[...] = down_wide[...].astype(bf16)
    o = o_ref[...].astype(bf16)
    x1 = x0_ref[...] + (contract(o, out_ref[...], 1, 0) + vec_ref[17:18, :])
    unit, inverse = norm_parts(x1)
    h2 = (unit * vec_ref[18:19, :] + vec_ref[19:20, :]).astype(bf16)
    dy_low = dy_ref[...]
    dy = dy_low.astype(f32)
    dyt = turned(dy_low)
    h2t = turned(h2)
    y = x1 + vec_ref[20:21, :]
    dh2 = jnp.zeros_like(y)
    for col in range(FF // 256):
        cols = slice(col * 256, col * 256 + 256)
        u = contract(h2, up_ref[:, cols], 1, 0) + vec_ref[21 + col : 22 + col, :]
        phi_sum = 0.5 * (1.0 + lax.erf(u * (2.0**-0.5)))
        density = jnp.exp(-0.5 * u * u) * ((2.0 * math.pi) ** -0.5)
        g = (u * phi_sum).astype(bf16)
        y = y + contract(g, down_ref[cols, :], 1, 0)
        down_grad[:, cols] = contract(dyt, g, 1, 0)
        du = (contract(dy_low, down_ref[cols, :], 1, 1) * (phi_sum + u * density)).astype(bf16)
        up_grad[:, cols] = contract(h2t, du, 1, 0)
        sums_ref[21 + col : 22 + col, :] = col_sum(du.astype(f32))
        dh2 = dh2 + contract(du, up_ref[:, cols], 1, 1)
    y_ref[...] = y.astype(bf16)
    back, gain_sum, bias_sum = norm_back(dh2, unit, inverse, vec_ref[18:19, :])
    dx1 = dy + back
    dx1_ref[...] = dx1
    da = dx1.astype(bf16)
    do_ref[...] = contract(da, out_ref[...], 1, 1).astype(bf16)
    out_grad[...] = contract(turned(o), da, 1, 0)
    sums_ref[0:17, :] = jnp.zeros((17, 256), f32)
    sums_ref[17:18, :] = col_sum(da.astype(f32))
    sums_ref[18:19, :] = gain_sum
    sums_ref[19:20, :] = bias_sum
    sums_ref[20:21, :] = col_sum(dy)


def rotate(left_turned, grad, right):
    half = contract(left_turned, grad.astype(bf16), 1, 0).astype(bf16)
    return contract(half, right, 1, 0)


def rotate_turned(grad_turned, left, right):
    half = contract(grad_turned.astype(bf16), left, 1, 0).astype(bf16)
    return contract(turned(half), right, 1, 0)


def share_out(keep_ref, send_ref, parts, mats):
    half = keep_ref.shape[0]
    for ref, base in ((keep_ref, 0), (send_ref, half)):

        def body(block, ref=ref, base=base):
            collect(ref, block, parts, mats, source(block + base))

        each_block(half, body)


def early_turn_kernel(up_grad, down_grad, turned_ref, narrow_ref, wide_ref, keep_ref, send_ref, up, down):
    up[...] = rotate(turned_ref[3], up_grad[...], wide_ref[0])
    down[...] = rotate_turned(down_grad[...], wide_ref[1], narrow_ref[6])
    share_out(keep_ref, send_ref, layout(256, EARLY)[0], (up, down))


def middle_turn_kernel(query_left, query_right, out_grad, turned_ref, narrow_ref, query_ref, out_ref):
    query_grad = jnp.concatenate([query_left[...], query_right[...]], axis=1)
    query_ref[...] = rotate(turned_ref[0], query_grad, narrow_ref[1])
    out_ref[...] = rotate(turned_ref[2], out_grad[...], narrow_ref[4])


def attend_back_kernel(
    step, unroll, group, q_ref, k_ref, v_ref, mask_ref, o_ref, log_ref, g_ref, h1_ref,
    dq_ref, keep_ref, send_ref, query_grad, bias_ref, dq_wide, dkv, ps, dss, qt, gt,
):
    tokens = q_ref.shape[0]
    scale = 32**-0.5
    lane = lax.broadcasted_iota(jnp.int32, (1, 128), 1)
    mask = mask_ref[...]
    cols = slice(group * 128, group * 128 + 128)
    qt[...] = turned(q_ref[:, cols])
    gt[...] = turned(g_ref[:, cols])

    def one_head(head):
        mine = lane // 32 == head
        keys = jnp.where(mine, k_ref[:, cols], 0)
        values = jnp.where(mine, v_ref[:, cols], 0)

        def block(start):
            rows = pl.ds(start, step)
            grad = g_ref[rows, cols]
            inner = jnp.sum(jnp.where(mine, grad.astype(f32) * o_ref[rows, cols], 0.0), axis=1, keepdims=True)
            if isinstance(head, int):
                log = log_ref[rows, group * 4 + head : group * 4 + head + 1]
            else:
                log = jnp.sum(jnp.where(lane == head + group * 4, log_ref[rows, :], 0.0), axis=1, keepdims=True)
            scores = contract(q_ref[rows, cols], keys, 1, 1)
            probs = jnp.exp2(scores * (scale * LOG2E) + mask - log)
            grad_scores = (probs * (contract(grad, values, 1, 1) - inner)).astype(bf16)
            ps[rows, :] = probs.astype(bf16)
            dss[rows, :] = grad_scores
            out = contract(grad_scores, keys, 1, 0) * scale
            dq_wide[rows, :] = jnp.where(mine, out, dq_wide[rows, :])

        over_blocks(block, tokens, step)
        dkv[head_rows(head), :] = contract(qt[head_rows(head), :], dss[...], 1, 0) * scale
        dkv[head_rows(head, 128), :] = contract(gt[head_rows(head), :], ps[...], 1, 0)

    over_heads(one_head, 0, 4, unroll)
    dq = dq_wide[...].astype(bf16)
    dq_ref[...] = dq
    bias_ref[...] = col_sum(dq.astype(f32))
    half = keep_ref.shape[0]
    keep_ref[...] = dkv[:, 0:half].T
    send_ref[...] = dkv[:, half:].T
    query_grad[...] = contract(turned(h1_ref[...]), dq, 1, 0)


def total_of(refs):
    total = refs[0][...]
    for ref in refs[1:]:
        total = total + ref[...].astype(f32)
    return total


def split_kernel(count, terms, *refs):
    total = total_of(refs[:terms])
    rows = total.shape[0] // count
    refs[terms][...] = total[:rows]
    for index in range(1, count):
        refs[terms + index][...] = total[index * rows : (index + 1) * rows].astype(bf16)


def split_sum(terms, count, after=()):
    rows = terms[0].shape[0] // count
    tail = terms[0].shape[1:]
    outs = [((rows,) + tail, f32)] + [((rows,) + tail, bf16)] * (count - 1)
    return run("split_sum", functools.partial(split_kernel, count, len(terms)), outs, terms, micros=0.6, after=after)


def split_heads_kernel(count, left_keep, left_got, right_keep, right_got, *outs):
    rows = outs[0].shape[0]
    for index in range(count):
        at = slice(index * rows, (index + 1) * rows)
        left = left_keep[at, :] + left_got[at, :]
        right = right_keep[at, :] + right_got[at, :]
        parts = (left[:, 0:128], right[:, 0:128], left[:, 128:256], right[:, 128:256])
        for place, part in enumerate(parts):
            cols = slice(place * 128, place * 128 + 128)
            outs[index][:, cols] = part if index == 0 else part.astype(bf16)


def pair_total(values):
    while len(values) > 1:
        values = [a + b for a, b in zip(values[::2], values[1::2])]
    return values[0]


def two_parts(value):
    high = value.astype(bf16)
    return high, (value - high.astype(f32)).astype(bf16)


def split_with_vectors_kernel(count, terms, first, *refs):
    vec_terms = 2 if first else 1
    keep_ref, vec_ref = refs[terms + vec_terms], refs[terms + vec_terms + 1]
    sends = refs[terms + vec_terms + 2 :]
    if first:
        total = total_of(refs[:terms])
        vec = refs[terms][...] + refs[terms + 1][...]
    else:
        rows = refs[0].shape[0]
        total = refs[0][...]
        for ref in refs[1:terms]:
            total = total + ref[0:rows, :].astype(f32)
        vec = pair_total([refs[terms][...]] + [vector_part(ref, rows) for ref in refs[1:terms]])
    rows = total.shape[0] // count
    keep_ref[...] = total[:rows]
    high, rest = two_parts(vec)
    vec_ref[...] = high.astype(f32) + rest.astype(f32)
    for index, ref in enumerate(sends, 1):
        ref[0:rows, :] = total[index * rows : (index + 1) * rows].astype(bf16)
        ref[rows : rows + 32, :] = high
        ref[rows + 32 : rows + 64, :] = rest


def vector_part(ref, rows):
    return ref[rows : rows + 32, :].astype(f32) + ref[rows + 32 : rows + 64, :].astype(f32)


def split_with_vectors(terms, vec_terms, count, first, after=()):
    rows = terms[0].shape[0] // count
    width = terms[0].shape[1]
    outs = [((rows, width), f32), ((32, width), f32)] + [((rows + 64, width), bf16)] * (count - 1)
    body = functools.partial(split_with_vectors_kernel, count, len(terms), first)
    return run("split_with_vectors", body, outs, list(terms) + list(vec_terms), micros=0.6, after=after)


def row_parts():
    return [("row", stride, size) for stride, size in rel_digits()[1:]]


def one_by_one(groups):
    return [(axis, stride << bit, 2) for axis, stride, size in groups for bit in reversed(range(size.bit_length() - 1))]


def side_by_side(x, groups):
    for axis, stride, size in groups:
        x = jnp.concatenate([x] + [swap(x, axis, j * stride) for j in range(1, size)], axis=0)
    return x


def keys_back_kernel(
    terms, *refs
):
    (kn_ref, c_ref, vec_ref, keyval_ref, blocks_ref, turned_ref, narrow_ref, pair_ref, wide_ref, query, out,
     keep_ref, send_ref, dc_ref, sums_ref, reduce, keyval) = refs[terms:]
    dkv = total_of(refs[:terms])
    high, rest = two_parts(dkv)
    dkn = contract(high, keyval_ref[...], 1, 1) + contract(rest, keyval_ref[...], 1, 1)
    unit, inverse = norm_parts(c_ref[...])
    back, gain_sum, bias_sum = norm_back(dkn, unit, inverse, vec_ref[14:15, :])
    dc = back.astype(bf16)
    dc_ref[...] = dc
    knt = turned(kn_ref[...])
    keyval[...] = rotate(turned_ref[1], contract(knt, high, 1, 0) + contract(knt, rest, 1, 0), pair_ref[...])
    reduce[...] = rotate_turned(contract(turned(dc), blocks_ref[...], 1, 0), wide_ref[2], narrow_ref[7])
    share_out(keep_ref, send_ref, layout(256, LATE)[0], (reduce, keyval, query, out))
    sums_ref[0:1, :] = col_sum(dc.astype(f32))
    sums_ref[1:2, :] = gain_sum
    sums_ref[2:3, :] = bias_sum
    sums_ref[3:4, :] = col_sum(dkv[:, 256:512])


def cells_back_kernel(
    tile_rows, cols, size_ref, dq_left, dq_right, dc_ref, query_ref, reduce_ref, x0_ref, dx1_ref, vec_ref, tile_ref, up_ref, down_ref,
    feed_sums, key_sums, left_sum, right_sum, dx0_ref, head_ref, tail_ref, sums_ref, frame,
):
    tokens = x0_ref.shape[0]
    dh1 = contract(dq_left[...], query_ref[:, 0:128], 1, 1) + contract(dq_right[...], query_ref[:, 128:256], 1, 1)
    for corner in range(4):
        pick = picked_cells((tokens, dc_ref.shape[0]), 0, size_ref, corner, tile_rows, cols)
        placed = contract(pick, dc_ref[...], 1, 0).astype(bf16)
        dh1 = dh1 + contract(placed, reduce_ref[corner * 256 : corner * 256 + 256, :], 1, 1)
    unit, inverse = norm_parts(x0_ref[...])
    back, gain_sum, bias_sum = norm_back(dh1, unit, inverse, vec_ref[10:11, :])
    dx0 = dx1_ref[...] + back
    dx0_ref[...] = dx0
    head_ref[...] = dx0[0:64].astype(bf16)
    tail_ref[...] = dx0[tokens - 64 :].astype(bf16)
    sums_ref[0:25, :] = feed_sums[...]
    sums_ref[25:32, :] = jnp.zeros((7, 256), f32)
    moved = shifted_frame(frame, tile_ref, up_ref, down_ref)
    grid = dx0.reshape(tile_rows, cols, 256)
    for tap in range(9):
        product = moved[tap % 3][tap // 3 : tap // 3 + tile_rows] * grid
        sums_ref[tap : tap + 1, :] = col_sum(product.reshape(tokens, 256))
    sums_ref[9:10, :] = col_sum(dx0)
    sums_ref[10:11, :] = gain_sum
    sums_ref[11:12, :] = bias_sum
    sums_ref[12:13, 0:128] = left_sum[...]
    sums_ref[12:13, 128:256] = right_sum[...]
    sums_ref[13:17, :] = key_sums[...]


def input_grad_kernel(tile_rows, dx0_ref, up_ref, down_ref, vec_ref, out_ref, frame):
    moved = shifted_frame(frame, dx0_ref, up_ref, down_ref)
    total = moved[1][1:-1]
    for tap in range(9):
        down, right = 2 - tap // 3, 2 - tap % 3
        total = total + vec_ref[tap : tap + 1, :] * moved[right][down : down + tile_rows]
    out_ref[...] = total.reshape(out_ref.shape)


def moments_of(total, first, second, moment_ref, square_ref):
    moment = BETA * first + (1.0 - BETA) * total
    square = BETA * second + (1.0 - BETA) * total * total
    moment_ref[...] = moment
    square_ref[...] = square
    return moment * (1.0 / CORRECTION) / (jnp.sqrt(square * (1.0 / CORRECTION)) + ADAM_EPS)


def adam_kernel(base, terms, *refs):
    first_ref, second_ref, moment_ref, square_ref, step_ref = refs[terms:]
    total = total_of(refs[:terms])
    at = slice(base, base + total.shape[0])
    step_ref[...] = moments_of(total, first_ref[at, :], second_ref[at, :], moment_ref, square_ref).astype(bf16)


def late_adam_kernel(terms, *refs):
    (own_vec, first_ref, second_ref, vec_ref, vec_first, vec_second, vec_ema,
     moment_ref, square_ref, step_ref, vec_out, vec_first_out, vec_second_out, vec_ema_out) = refs[terms:]
    rows = refs[0].shape[0]
    total = refs[0][...]
    for ref in refs[1:terms]:
        total = total + ref[0:rows, :].astype(f32)
    step_ref[...] = moments_of(total, first_ref[0:rows, :], second_ref[0:rows, :], moment_ref, square_ref).astype(bf16)
    vec = pair_total([own_vec[...]] + [vector_part(ref, rows) for ref in refs[1:terms]])
    vec = vec[0 : vec_ref.shape[0]]
    new = vec_ref[...] - VECTOR_RATE * moments_of(vec, vec_first[...], vec_second[...], vec_first_out, vec_second_out)
    vec_out[...] = new
    vec_ema_out[...] = EMA_KEEP * vec_ema[...] + (1.0 - EMA_KEEP) * new


def step_sides(group, width, refs, own_narrow, own_wide, second):
    lefts = {0: (own_narrow, 0), 1: (own_narrow, 1), 2: (own_narrow, 2), 3: (own_narrow, 3), 4: (own_wide, 0), 5: (own_wide, 1)}
    found = []
    values = refs[...].astype(f32)
    for j, first, rows, blocks in layout(width, group)[0]:
        left_ref, index = lefts[j]
        half = left_ref.shape[2] // 2
        left = left_ref[index][:, half * second : half * (second + 1)].astype(bf16)
        sides = []
        for col in range(blocks):
            part = values[:, first + col * rows : first + (col + 1) * rows, :]
            sides.append(contract(left, part.reshape(half, width).astype(bf16), 1, 0))
        found.append(sides[0] if blocks == 1 else jnp.concatenate(sides, axis=1))
    return found


def right_of(j, narrow_ref, pair_ref, wide_ref):
    return {0: narrow_ref.at[1], 1: pair_ref, 2: narrow_ref.at[4], 3: wide_ref.at[0], 4: narrow_ref.at[6], 5: narrow_ref.at[7]}[j][...]


def update_rows(group, width, base, sides, rights, weights_ref, chunk):
    for (j, first, rows, blocks), side in zip(layout(width, group)[0], sides):
        full = contract(side.astype(bf16), right_of(j, *rights), 1, 1)
        for col in range(blocks):
            start = first + col * rows
            old = weights_ref[base + start : base + start + rows, :]
            piece = full[0:rows, col * width : (col + 1) * width]
            chunk[start : start + rows, :] = old - MATRIX_RATES[j] * (piece + WEIGHT_DECAY * old)


def early_finish_kernel(
    width, late_near, early_near, early_far, own_narrow, own_wide, narrow_ref, pair_ref, wide_ref,
    weights_ref, late_first, late_second, early_first, early_second,
    new_ref, first_out, second_out, *late_sides,
):
    near = step_sides(EARLY, width, early_near, own_narrow, own_wide, 0)
    far = step_sides(EARLY, width, early_far, own_narrow, own_wide, 1)
    sides = [a + b for a, b in zip(near, far)]
    base = layout(width, LATE)[1]
    update_rows(EARLY, width, base, sides, (narrow_ref, pair_ref, wide_ref), weights_ref, new_ref)
    for late, early, out in ((late_first, early_first, first_out), (late_second, early_second, second_out)):
        from_chunk(late, 0, LATE, out, width)
        from_chunk(early, 0, EARLY, out, width)
    for ref, side in zip(late_sides, step_sides(LATE, width, late_near, own_narrow, own_wide, 0)):
        ref[...] = side


def finish_kernel(
    width, late_far, reduce_side, keyval_side, query_side, out_side, early_new, own_narrow, own_wide, narrow_ref, pair_ref, wide_ref,
    weights_ref, ema_ref, weights_out, ema_out, chunk,
):
    far = step_sides(LATE, width, late_far, own_narrow, own_wide, 1)
    near = (reduce_side, keyval_side, query_side, out_side)
    sides = [a[...] + b for a, b in zip(near, far)]
    split = layout(width, LATE)[1]
    update_rows(LATE, width, 0, sides, (narrow_ref, pair_ref, wide_ref), weights_ref, chunk)
    chunk[split:, :] = early_new[...]
    from_chunk(chunk, 0, LATE, weights_out, width)
    from_chunk(chunk, split, EARLY, weights_out, width)
    chunk[...] = EMA_KEEP * ema_ref[...] + (1.0 - EMA_KEEP) * chunk[...]
    from_chunk(chunk, 0, LATE, ema_out, width)
    from_chunk(chunk, split, EARLY, ema_out, width)


def on_device(
    patches,
    cotangent,
    image_sizes,
    weights,
    first_moment,
    second_moment,
    weight_ema,
    vectors,
    vec_first,
    vec_second,
    vec_ema,
    basis_narrow,
    basis_pair,
    basis_wide,
):
    _, rows, cols, width = patches.shape
    tokens = rows * cols
    shards = device_count()
    tile = patches.reshape(tokens, width)
    dy = cotangent.reshape(tokens, width)
    per = weights.shape[1]
    late_rows, early_rows = layout(width, LATE)[1], layout(width, EARLY)[1]
    chunk = late_rows + early_rows
    ranks = lax.axis_size("row")
    own_keys = tokens // 4
    keys = own_keys * ranks
    frame = ((rows + 2, cols + 16, width), f32)
    img_part = ("img", 1, lax.axis_size("img"))
    xy_parts = row_parts()

    def border(head, tail):
        up = lax.ppermute(tail, "row", [(i, i + 1) for i in range(ranks - 1)])
        return up, lax.ppermute(head, "row", [(i + 1, i) for i in range(ranks - 1)])

    gather_groups = xy_parts[::-1]
    lines = lax.axis_size("img")

    (packed,) = run(
        "pack",
        functools.partial(pack_kernel, width),
        [((chunk, width), bf16)],
        [weights],
        scratch=[((chunk, width), f32)],
    )
    up_halo, down_halo = border(tile[:64], tile[tokens - 64 :])
    slices = [packed] + [swap(packed, "img", j) for j in range(1, lines)]
    old_chunk, ema_chunk, first_chunk, second_chunk = run(
        "moments",
        functools.partial(moments_kernel, width),
        [((chunk, width), f32)] * 4,
        [weights, weight_ema, first_moment, second_moment],
        after=[packed],
    )
    narrow, narrow_turned, pair, own_narrow = run(
        "small_bases",
        small_bases_kernel,
        [((8, width, width), bf16), ((4, width, width), bf16), ((2 * width, 2 * width), bf16), ((4, 16, width), f32)],
        [basis_narrow, basis_pair],
        scratch=[((2 * width, 128), f32)],
        micros=1.5,
        after=[packed],
    )
    x0, h1, mask, vec = run(
        "front",
        functools.partial(front_kernel, rows, cols),
        [((tokens, width), f32), ((tokens, width), bf16), ((1, keys), f32), (vectors.shape, f32)],
        [image_sizes, tile, up_halo, down_halo, vectors],
        scratch=[frame],
        scalars=(0,),
        micros=1.3,
    )
    late_line, early_line = run(
        "stack",
        functools.partial(stack_kernel, late_rows),
        [((lines, late_rows, width), bf16), ((lines, early_rows, width), bf16)],
        slices,
        micros=0.4,
        after=[own_narrow, ema_chunk, vec],
    )
    late_near = side_by_side(late_line, gather_groups)
    late_far = swap(late_near, "row", 1)
    early_near = side_by_side(early_line, one_by_one(xy_parts)[::-1])
    early_far = swap(early_near, "row", 1)
    wide, own_wide = run(
        "wide_bases",
        wide_bases_kernel,
        [((3, FF, FF), bf16), ((2, max(16, FF // shards), FF), f32)],
        [basis_wide],
        scratch=[((2 * FF, 128), f32), ((4, width, FF), f32)],
        micros=5.0,
        mib=8,
        raw=(0,),
        sems=4,
        after=[late_line],
    )
    w_reduce, w_keyval, w_query, w_out, blocks, c, kn, own_kv = run(
        "keys",
        functools.partial(keys_kernel, rows, cols),
        [
            ((4 * width, width), bf16),
            ((width, 2 * width), bf16),
            ((width, width), bf16),
            ((width, width), bf16),
            ((own_keys, 4 * width), bf16),
            ((own_keys, width), f32),
            ((own_keys, width), bf16),
            ((own_keys, 2 * width), bf16),
        ],
        [image_sizes, h1, vec, late_near, late_far],
        scratch=[((4 * width, width), f32), ((width, 2 * width), f32), ((width, width), f32), ((width, width), f32)],
        scalars=(0,),
        micros=1.5,
        after=[own_wide],
    )
    kv_near = side_by_side(own_kv, gather_groups)
    kv_far = swap(kv_near, "row", 1)

    unroll = keys <= 1024
    step = tokens if unroll else 32
    q, k, v, o, log = run(
        "attend",
        functools.partial(attend_kernel, step, unroll),
        [((tokens, width), bf16), ((keys, width), bf16), ((keys, width), bf16), ((tokens, width), f32), ((tokens, 128), f32)],
        [h1, w_query, vec, kv_near, kv_far, mask],
        mib=8 if unroll else 44,
        micros=8.0,
    )
    y, do, dx1, up_grad, down_grad, out_grad, feed_sums = run(
        "feed",
        feed_kernel,
        [
            ((tokens, width), bf16),
            ((tokens, width), bf16),
            ((tokens, width), f32),
            ((width, FF), f32),
            ((width, FF), f32),
            ((width, width), f32),
            (vectors.shape, f32),
        ],
        [o, x0, w_out, early_near, early_far, vec, dy],
        scratch=[((width, FF), bf16), ((FF, width), bf16), ((width, FF), f32), ((FF, width), f32)],
        mib=12,
        micros=3.5,
    )
    half = (shards // 2, early_rows, width)
    early_keep, early_send = run(
        "early_turn",
        early_turn_kernel,
        [(half, f32), (half, f32)],
        [up_grad, down_grad, narrow_turned, narrow, wide],
        scratch=[((width, FF), f32), ((FF, width), f32)],
        mib=10,
        micros=2.0,
    )

    def back(group, after):
        return run(
            "attend_back",
            functools.partial(attend_back_kernel, step, unroll, group),
            [
                ((tokens, 128), bf16),
                ((keys // 2, width), f32),
                ((keys // 2, width), f32),
                ((width, 128), f32),
                ((1, 128), f32),
            ],
            [q, k, v, mask, o, log, do, h1],
            scratch=[
                ((tokens, 128), f32),
                ((width, keys), f32),
                ((tokens, keys), bf16),
                ((tokens, keys), bf16),
                ((128, tokens), bf16),
                ((128, tokens), bf16),
            ],
            mib=14 if unroll else 60,
            micros=5.0,
            after=after,
        )

    pairs = one_by_one(xy_parts + [img_part])
    dq_left, left_keep, left_send, query_left, left_sum = back(0, [early_keep])
    early_terms = [early_keep, swap(early_send, "row", 1)]
    early_keep, early_send = split_sum(early_terms, 2, after=[query_left])
    early_terms = [early_keep, swap(early_send, *pairs[0][:2])]
    left_got = swap(left_send, "row", 1)
    dq_right, right_keep, right_send, query_right, right_sum = back(1, [early_keep])
    right_got = swap(right_send, "row", 1)
    dkv_keep, *dkv_sends = run(
        "split_heads",
        functools.partial(split_heads_kernel, xy_parts[0][2]),
        [((keys // 2 // xy_parts[0][2], 2 * width), f32)]
        + [((keys // 2 // xy_parts[0][2], 2 * width), bf16)] * (xy_parts[0][2] - 1),
        [left_keep, left_got, right_keep, right_got],
        micros=0.8,
    )
    axis, stride, size = xy_parts[0]
    dkv_terms = [dkv_keep] + [swap(x, axis, j * stride) for j, x in enumerate(dkv_sends, 1)]
    for axis, stride, size in xy_parts[1:]:
        keep, *sends = split_sum(dkv_terms, size)
        dkv_terms = [keep] + [swap(x, axis, j * stride) for j, x in enumerate(sends, 1)]
    query_turn, out_turn = run(
        "middle_turn",
        middle_turn_kernel,
        [((width, width), f32), ((width, width), f32)],
        [query_left, query_right, out_grad, narrow_turned, narrow],
        micros=0.7,
    )
    early_keep, early_send = split_sum(early_terms, 2, after=[query_turn])
    early_terms = [early_keep, swap(early_send, *pairs[1][:2])]
    half = (shards // 2, late_rows, width)
    late_keep, late_send, dc, key_sums = run(
        "keys_back",
        functools.partial(keys_back_kernel, len(dkv_terms)),
        [(half, f32), (half, f32), ((own_keys, width), bf16), ((4, width), f32)],
        list(dkv_terms) + [kn, c, vec, w_keyval, blocks, narrow_turned, narrow, pair, wide, query_turn, out_turn],
        scratch=[((4 * width, width), f32), ((width, 2 * width), f32)],
        micros=2.0,
        after=[early_keep],
    )
    late_got = swap(late_send, "row", 1)
    dx0, head, tail, vec_grads = run(
        "cells_back",
        functools.partial(cells_back_kernel, rows, cols),
        [((tokens, width), f32), ((64, width), bf16), ((64, width), bf16), ((32, width), f32)],
        [
            image_sizes, dq_left, dq_right, dc, w_query, w_reduce, x0, dx1, vec, tile, up_halo, down_halo,
            feed_sums, key_sums, left_sum, right_sum,
        ],
        scratch=[frame],
        scalars=(0,),
        micros=2.0,
    )
    vec_terms = [vec_grads, swap(vec_grads, "row", 1)]
    grad_up, grad_down = border(head, tail)
    late_terms = [late_keep.reshape(-1, width), late_got.reshape(-1, width)]
    waits = [[early_keep], [grad_up, grad_down]]
    for index, (axis, stride, size) in enumerate(xy_parts + [img_part]):
        if index + 2 < len(pairs):
            early_keep, early_send = split_sum(early_terms, 2, after=[dc] if index == 0 else [late_keep])
            early_terms = [early_keep, swap(early_send, *pairs[index + 2][:2])]
            waits[0] = [early_keep]
        late_keep, own_vec, *sends = split_with_vectors(
            late_terms, vec_terms, size, index == 0, waits[0] if index == 0 else waits[0] + waits[1]
        )
        late_terms = [late_keep] + [swap(x, axis, j * stride) for j, x in enumerate(sends, 1)]
        vec_terms = [own_vec]
    for axis, stride, _ in pairs[2 + len(xy_parts) + 1 :]:
        early_keep, early_send = split_sum(early_terms, 2)
        early_terms = [early_keep, swap(early_send, axis, stride)]
    early_first, early_second, early_step = run(
        "adam",
        functools.partial(adam_kernel, late_rows, 2),
        [((early_rows, width), f32), ((early_rows, width), f32), ((early_rows, width), bf16)],
        [t.reshape(early_rows, width) for t in early_terms] + [first_chunk, second_chunk],
        micros=0.6,
    )
    steps_line = side_by_side(early_step[None], one_by_one([img_part])[::-1])
    (grad_input,) = run(
        "input_grad",
        functools.partial(input_grad_kernel, rows),
        [((tokens, width), f32)],
        [dx0, grad_up, grad_down, vec],
        scratch=[frame],
        micros=1.5,
        after=[late_keep],
    )
    late_first, late_second, late_step, new_vectors, vec_moment, vec_square, new_vec_ema = run(
        "late_adam",
        functools.partial(late_adam_kernel, len(late_terms)),
        [((late_rows, width), f32), ((late_rows, width), f32), ((late_rows, width), bf16)] + [(vectors.shape, f32)] * 4,
        late_terms + [own_vec, first_chunk, second_chunk, vec, vec_first, vec_second, vec_ema],
        micros=0.8,
        after=[early_step, grad_input],
    )
    step_near = side_by_side(late_step[None], [img_part] + gather_groups)
    step_far = swap(step_near, "row", 1)
    steps_near = side_by_side(steps_line, one_by_one(xy_parts)[::-1])
    steps_far = swap(steps_near, "row", 1)

    early_new, new_first, new_second, *late_sides = run(
        "early_finish",
        functools.partial(early_finish_kernel, width),
        [((early_rows, width), f32), ((1, per), f32), ((1, per), f32)]
        + [((own_wide.shape[1], width), f32)]
        + [((own_narrow.shape[1], cols_of * width), f32) for cols_of in (2, 1, 1)],
        [
            step_near, steps_near, steps_far, own_narrow, own_wide, narrow, pair, wide,
            old_chunk, late_first, late_second, early_first, early_second,
        ],
        micros=2.0,
    )
    new_weights, new_ema = run(
        "finish",
        functools.partial(finish_kernel, width),
        [((1, per), f32)] * 2,
        [step_far, *late_sides, early_new, own_narrow, own_wide, narrow, pair, wide, old_chunk, ema_chunk],
        scratch=[((chunk, width), f32)],
        micros=1.5,
        after=[new_first],
    )
    return (
        y.reshape(patches.shape),
        grad_input.reshape(patches.shape),
        new_weights,
        new_first,
        new_second,
        new_ema,
        new_vectors,
        vec_moment,
        vec_square,
        new_vec_ema,
    )


def solution(mesh):
    tiles = P("img", "row", None, None)
    packed = P(("img", "row"), None)
    return jax.shard_map(
        on_device,
        mesh=mesh,
        in_specs=(tiles, tiles, P("img", None)) + (packed,) * 4 + (P(),) * 7,
        out_specs=(tiles, tiles) + (packed,) * 4 + (P(),) * 4,
        check_vma=False,
    )
```

```python
import functools
import math

import jax
import jax.numpy as jnp
from jax import lax
from jax.experimental import pallas as pl
from jax.experimental.pallas import tpu as pltpu
from jax.sharding import PartitionSpec as P

HEADS = 8
FF = 1024
STEP = 5

NORM_EPS = 1e-05
ADAM_EPS = 1e-08
BETA = 0.5
WEIGHT_DECAY = 0.05
EMA_KEEP = 0.75
VECTOR_RATE = 0.06
MATRIX_RATES = (0.04, 0.02, 0.25, 0.02, 0.01, 0.01)
CORRECTION = 1.0 - BETA**STEP
LOG2E = math.log2(math.e)
f32 = jnp.float32
bf16 = jnp.bfloat16
LATE = (5, 1, 0, 2)
EARLY = (3, 4)


def matrix_shapes(width, hidden):
    return (
        (width, width),
        (width, 2 * width),
        (width, width),
        (width, hidden),
        (hidden, width),
        (4 * width, width),
    )


def contract(a, b, ca, cb, **kw):
    return lax.dot_general(
        a, b, (((ca,), (cb,)), ((), ())), preferred_element_type=f32, **kw
    )


def swap(x, axis, step):
    count = lax.axis_size(axis)
    return lax.ppermute(x, axis, [(i, i ^ step) for i in range(count)])


def row_groups():
    left = lax.axis_size("row") // 2
    groups, stride = [(1, 2)], 2
    while left > 1:
        size = 4 if left % 4 == 0 else 2
        groups.append((stride, size))
        left //= size
        stride *= size
    return groups


def rel_digits():
    groups = row_groups()
    return [groups[0]] + groups[1:][::-1]


def source(block):
    sizes = lax.axis_size("img")
    img, rest = block % sizes, block // sizes
    rel = 0
    for stride, size in reversed(rel_digits()):
        rel = rel + (rest % size) * stride
        rest = rest // size
    row = lax.axis_index("row") ^ rel
    return (lax.axis_index("img") ^ img) * lax.axis_size("row") + row


def device_count():
    return lax.axis_size("img") * lax.axis_size("row")


def run(name, body, outs, args, scratch=(), mib=6, scalars=(), micros=1.0, after=(), raw=(), sems=0):
    count = len(args)

    def without(*refs):
        body(*refs[:count], *refs[count + len(after) :])

    space = {index: pltpu.SMEM for index in scalars} | {index: pltpu.HBM for index in raw}
    specs = [pl.BlockSpec(memory_space=space.get(index, pltpu.VMEM)) for index in range(count)]
    return pl.pallas_call(
        without,
        out_shape=tuple(jax.ShapeDtypeStruct(shape, dtype) for shape, dtype in outs),
        in_specs=specs + [pl.BlockSpec(memory_space=pl.ANY)] * len(after),
        out_specs=tuple(pl.BlockSpec(memory_space=pltpu.VMEM) for _ in outs),
        scratch_shapes=[pltpu.VMEM(shape, dtype) for shape, dtype in scratch]
        + ([pltpu.SemaphoreType.DMA((sems,))] if sems else []),
        compiler_params=pltpu.CompilerParams(vmem_limit_bytes=mib * 2**20),
        cost_estimate=pl.CostEstimate(flops=0, bytes_accessed=int(micros * 3.6e6), transcendentals=0),
        name=name,
    )(*args, *after)


def each_block(count, body):
    if count <= 32:
        for index in range(count):
            body(index)
    else:

        def step(index, carry):
            body(index)
            return carry

        lax.fori_loop(0, count, step, 0)


def put_rows(ref, start, cols, value):
    count = value.shape[0]
    if count % 8 == 0:
        ref[pl.ds(pl.multiple_of(start, 8), count), cols] = value
    else:
        for row in range(count):
            ref[pl.ds(start + row, 1), cols] = value[row : row + 1]


def get_rows(ref, start, count, cols):
    if count % 8 == 0:
        return ref[pl.ds(pl.multiple_of(start, 8), count), cols]
    return jnp.concatenate([ref[pl.ds(start + row, 1), cols] for row in range(count)], axis=0)


def layout(width, group):
    dims = matrix_shapes(width, FF)
    found, start = [], 0
    for j in group:
        rows = dims[j][0] // device_count()
        blocks = dims[j][1] // width
        found.append((j, start, rows, blocks))
        start += rows * blocks
    return found, start


def packed_starts(width):
    dims = matrix_shapes(width, FF)
    starts, start = [], 0
    for m, n in dims:
        starts.append(start)
        start += m * n // device_count()
    return starts


def spread(block, parts, mats, start_of):
    for (j, first, rows, blocks), ref in zip(parts, mats):
        for col in range(blocks):
            piece = block[first + col * rows : first + (col + 1) * rows]
            put_rows(ref, start_of * rows, slice(col * 256, col * 256 + 256), piece)


def collect(out_ref, index, parts, mats, start_of):
    for (j, first, rows, blocks), ref in zip(parts, mats):
        for col in range(blocks):
            piece = get_rows(ref, start_of * rows, rows, slice(col * 256, col * 256 + 256))
            out_ref[index, first + col * rows : first + (col + 1) * rows, :] = piece


def norm_parts(values):
    centred = values - jnp.mean(values, axis=-1, keepdims=True)
    inverse = lax.rsqrt(jnp.mean(centred * centred, axis=-1, keepdims=True) + NORM_EPS)
    return centred * inverse, inverse


def norm_back(grad, unit, inverse, gain):
    grad_unit = grad * gain
    back = grad_unit - jnp.mean(grad_unit, axis=-1, keepdims=True)
    back = back - unit * jnp.mean(grad_unit * unit, axis=-1, keepdims=True)
    gain_sum = jnp.sum(grad * unit, axis=0, keepdims=True)
    return back * inverse, gain_sum, jnp.sum(grad, axis=0, keepdims=True)


def turned(value):
    return value.astype(f32).T.astype(bf16)


def col_sum(value):
    return jnp.sum(value, axis=0, keepdims=True)


def pack_kernel(width, w_ref, out_ref, chunk):
    to_chunk(w_ref, chunk, width)
    out_ref[...] = chunk[...].astype(bf16)


def to_chunk(flat_ref, out_ref, width, index=0):
    dims, starts, base = matrix_shapes(width, FF), packed_starts(width), 0
    for group in (LATE, EARLY):
        parts, count = layout(width, group)
        for j, first, rows, blocks in parts:
            for col in range(blocks):
                for row in range(rows):
                    at = starts[j] + row * dims[j][1] + col * width
                    place = base + first + col * rows + row
                    out_ref[place : place + 1, :] = flat_ref[index : index + 1, at : at + width]
        base += count


def from_chunk(values, base, group, out_ref, width):
    dims, starts = matrix_shapes(width, FF), packed_starts(width)
    parts, _ = layout(width, group)
    for j, first, rows, blocks in parts:
        for col in range(blocks):
            for row in range(rows):
                at = starts[j] + row * dims[j][1] + col * width
                place = base + first + col * rows + row
                out_ref[0:1, at : at + width] = values[place : place + 1, :]


def moments_kernel(width, rows_ref, *outs):
    for index, ref in enumerate(outs):
        to_chunk(rows_ref, ref, width, index)


def own_rows(matrix_ref, out_ref, tall):
    count = device_count()
    rank = lax.axis_index("img") * lax.axis_size("row") + lax.axis_index("row")
    size = matrix_ref.shape[0]
    rows = size // count
    place = lax.broadcasted_iota(jnp.int32, (128, 1), 0)
    place = jnp.where(place < rows, place + rank * rows, -1)
    pick = (lax.broadcasted_iota(jnp.int32, (128, size), 1) == place).astype(f32).astype(bf16)
    tall[0:size, :] = contract(pick, matrix_ref[...], 1, 0).T

    def body(block):
        put_rows(tall, size + block * rows, slice(None), get_rows(tall, source(block) * rows, rows, slice(None)))

    each_block(count, body)
    out_ref[...] = tall[size : 2 * size, :].T[0 : out_ref.shape[0]]


def narrow_bases_kernel(narrow_ref, pair_ref, narrow_out, turned_out, pair_out, own_ref, tall):
    narrow_out[...] = narrow_ref[...].astype(bf16)
    pair_out[...] = pair_ref[...].astype(bf16)
    for index, j in enumerate((0, 2, 3, 5)):
        turned_out[index] = narrow_ref[j].T.astype(bf16)
        own_rows(narrow_out.at[j], own_ref.at[index], tall)


def wide_bases_kernel(wide_ref, wide_out, own_ref, tall, buffer, sems):
    count, size = wide_ref.shape[0], wide_ref.shape[1]
    rows, depth = buffer.shape[1], buffer.shape[0]
    each = size // rows
    total = count * each

    def copy(index):
        at = wide_ref.at[index // each, pl.ds(index % each * rows, rows)]
        return pltpu.make_async_copy(at, buffer.at[index % depth], sems.at[index % depth])

    for index in range(depth):
        copy(index).start()
    for index in range(total):
        copy(index).wait()
        first = index % each * rows
        wide_out[index // each, first : first + rows, :] = buffer[index % depth].astype(bf16)
        if index + depth < total:
            copy(index + depth).start()
    for index in range(2):
        own_rows(wide_out.at[index + 1], own_ref.at[index], tall)


def join_kernel(*refs):
    start = 0
    for ref in refs[:-1]:
        refs[-1][start : start + ref.shape[0]] = ref[...]
        start += ref.shape[0]


def join(pieces, after=()):
    shape = (sum(x.shape[0] for x in pieces),) + pieces[0].shape[1:]
    return run("join", join_kernel, [(shape, pieces[0].dtype)], list(pieces), micros=0.4, after=after)[0]


def unpack(pieces, group, mats, base=0):
    parts = [(j, first + base, rows, blocks) for j, first, rows, blocks in layout(256, group)[0]]
    done = 0
    for piece in pieces:

        def body(block, piece=piece, done=done):
            spread(piece[block].astype(f32), parts, mats, source(block + done))

        each_block(piece.shape[0], body)
        done += piece.shape[0]


def shifted_frame(frame_ref, tile_ref, up_ref, down_ref):
    rows, cols, width = frame_ref.shape[0] - 2, 56, 256
    frame_ref[...] = jnp.zeros_like(frame_ref)
    frame_ref[0, 8 : 8 + cols, :] = up_ref[...].astype(f32)[-cols:]
    frame_ref[1 : 1 + rows, 8 : 8 + cols, :] = tile_ref[...].astype(f32).reshape(rows, cols, width)
    frame_ref[rows + 1, 8 : 8 + cols, :] = down_ref[...].astype(f32)[:cols]
    return [frame_ref[:, 7 + shift : 7 + shift + cols, :] for shift in range(3)]


def front_kernel(tile_rows, cols, size_ref, tile_ref, up_ref, down_ref, vec_ref, x0_ref, h1_ref, mask_ref, vec_out, size_out, frame):
    rows = frame.shape[0] - 2
    vec_out[...] = vec_ref[...]
    size_out[...] = jnp.where(lax.broadcasted_iota(jnp.int32, size_out.shape, 0) == 0, size_ref[0, 0], size_ref[0, 1])
    moved = shifted_frame(frame, tile_ref, up_ref, down_ref)
    total = moved[1][1:-1] + vec_ref[9:10, :]
    for tap in range(9):
        total = total + vec_ref[tap : tap + 1, :] * moved[tap % 3][tap // 3 : tap // 3 + rows]
    x0 = total.reshape(x0_ref.shape)
    x0_ref[...] = x0
    unit, _ = norm_parts(x0)
    h1_ref[...] = (unit * vec_ref[10:11, :] + vec_ref[11:12, :]).astype(bf16)
    half = cols // 2
    own = tile_rows // 2 * half
    key = lax.broadcasted_iota(jnp.int32, mask_ref.shape, 1)
    block = jnp.zeros_like(key)
    for start in range(own, mask_ref.shape[1], own):
        block = block + (key >= start).astype(jnp.int32)
    key = key - block * own
    row = jnp.zeros_like(key)
    for start in range(half, own, half):
        row = row + (key >= start).astype(jnp.int32)
    col = key - row * half
    rel = jnp.zeros_like(key)
    for stride, size in reversed(rel_digits()):
        rel = rel + (block & (size - 1)) * stride
        block = block >> (size.bit_length() - 1)
    row = row + (rel ^ lax.axis_index("row")) * (tile_rows // 2)
    inside = (2 * row < size_ref[0, 0]) & (2 * col < size_ref[0, 1])
    mask_ref[...] = jnp.where(inside, 0.0, -1e30)


def picked_cells(shape, cell_axis, size_ref, corner, tile_rows, cols):
    half = cols // 2
    key_shape = tuple(1 if axis == cell_axis else n for axis, n in enumerate(shape))
    key = lax.broadcasted_iota(jnp.int32, key_shape, 1 - cell_axis)
    row = jnp.zeros_like(key)
    for step in range(1, tile_rows // 2):
        row = row + (key >= step * half).astype(jnp.int32)
    col = 2 * (key - row * half) + corner % 2
    row = 2 * row + corner // 2
    inside = (row + lax.axis_index("row") * tile_rows < size_ref[0:1, 0:1]) & (col < size_ref[1:2, 0:1])
    target = jnp.where(inside, row * cols + col, -1)
    cell = lax.broadcasted_iota(jnp.int32, shape, cell_axis)
    return (cell == target).astype(f32).astype(bf16)


def keys_kernel(
    tile_rows, cols, size_ref, h1_ref, vec_ref, near_ref, far_ref,
    reduce_ref, keyval_ref, query_ref, out_ref, blocks_ref, c_ref, kn_ref, kv_ref,
    reduce_wide, keyval_wide, query_wide, out_wide,
):
    unpack((near_ref, far_ref), LATE, (reduce_wide, keyval_wide, query_wide, out_wide))
    reduce_ref[...] = reduce_wide[...].astype(bf16)
    keyval_ref[...] = keyval_wide[...].astype(bf16)
    query_ref[...] = query_wide[...].astype(bf16)
    out_ref[...] = out_wide[...].astype(bf16)
    keys = c_ref.shape[0]
    for corner in range(4):
        pick = picked_cells((keys, h1_ref.shape[0]), 1, size_ref, corner, tile_rows, cols)
        blocks_ref[:, corner * 256 : corner * 256 + 256] = contract(pick, h1_ref[...], 1, 0).astype(bf16)
    c = contract(blocks_ref[...], reduce_ref[...], 1, 0) + vec_ref[13:14, :]
    c_ref[...] = c
    unit, _ = norm_parts(c)
    kn = (unit * vec_ref[14:15, :] + vec_ref[15:16, :]).astype(bf16)
    kn_ref[...] = kn
    kv = contract(kn, keyval_ref[...], 1, 0)
    kv_ref[:, 0:256] = kv[:, 0:256].astype(bf16)
    kv_ref[:, 256:512] = (kv[:, 256:512] + vec_ref[16:17, :]).astype(bf16)


def over_heads(body, first, last, unroll):
    if unroll:
        for head in range(first, last):
            body(head)
    else:

        def step(head, carry):
            body(head)
            return carry

        lax.fori_loop(first, last, step, 0)


def over_blocks(block, tokens, step):
    if tokens == step:
        block(0)
    else:

        def go(index, carry):
            block(pl.multiple_of(index * step, step))
            return carry

        lax.fori_loop(0, tokens // step, go, 0)


def head_columns(head):
    group = head // 4
    if isinstance(head, int):
        return slice(group * 128, group * 128 + 128)
    return pl.ds(pl.multiple_of(group * 128, 128), 128)


def head_rows(head, base=0):
    if isinstance(head, int):
        return slice(base + head * 32, base + head * 32 + 32)
    return pl.ds(pl.multiple_of(base + head * 32, 32), 32)


def attend_kernel(
    step, unroll, h1_ref, query_ref, vec_ref, near_ref, far_ref, mask_ref, q_ref, k_ref, v_ref, o_ref, log_ref
):
    tokens = h1_ref.shape[0]
    half = near_ref.shape[0]
    for start, ref in ((0, near_ref), (half, far_ref)):
        k_ref[start : start + half, :] = ref[:, 0:256]
        v_ref[start : start + half, :] = ref[:, 256:512]
    q_ref[...] = (contract(h1_ref[...], query_ref[...], 1, 0) + vec_ref[12:13, :]).astype(bf16)
    scale = 32**-0.5 * LOG2E
    lane = lax.broadcasted_iota(jnp.int32, (1, 128), 1)
    mask = mask_ref[...]

    def one_head(head):
        cols = head_columns(head)
        mine = lane // 32 == head % 4
        keys = jnp.where(mine, k_ref[:, cols], 0)
        values = jnp.where(mine, v_ref[:, cols], 0)

        def block(start):
            rows = pl.ds(start, step)
            scores = contract(q_ref[rows, cols], keys, 1, 1) * scale + mask
            top = jnp.max(scores, axis=1, keepdims=True)
            exponent = jnp.exp2(scores - top)
            total = jnp.sum(exponent, axis=1, keepdims=True)
            probs = (exponent * (1.0 / total)).astype(bf16)
            out = contract(probs, values, 1, 0)
            o_ref[rows, cols] = jnp.where(mine, out, o_ref[rows, cols])
            log_ref[rows, :] = jnp.where(lane == head, top + jnp.log2(total), log_ref[rows, :])

        over_blocks(block, tokens, step)

    over_heads(one_head, 0, HEADS, unroll)


def feed_kernel(
    o_ref, x0_ref, out_ref, near_ref, far_ref, vec_ref, dy_ref,
    y_ref, do_ref, dx1_ref, up_grad, down_grad, out_grad, sums_ref, up_ref, down_ref, up_wide, down_wide,
):
    unpack((near_ref, far_ref), EARLY, (up_wide, down_wide), layout(256, LATE)[1])
    up_ref[...] = up_wide[...].astype(bf16)
    down_ref[...] = down_wide[...].astype(bf16)
    o = o_ref[...].astype(bf16)
    x1 = x0_ref[...] + (contract(o, out_ref[...], 1, 0) + vec_ref[17:18, :])
    unit, inverse = norm_parts(x1)
    h2 = (unit * vec_ref[18:19, :] + vec_ref[19:20, :]).astype(bf16)
    dy_low = dy_ref[...]
    dy = dy_low.astype(f32)
    dyt = turned(dy_low)
    h2t = turned(h2)
    y = x1 + vec_ref[20:21, :]
    dh2 = jnp.zeros_like(y)
    for col in range(FF // 256):
        cols = slice(col * 256, col * 256 + 256)
        u = contract(h2, up_ref[:, cols], 1, 0) + vec_ref[21 + col : 22 + col, :]
        phi_sum = 0.5 * (1.0 + lax.erf(u * (2.0**-0.5)))
        density = jnp.exp(-0.5 * u * u) * ((2.0 * math.pi) ** -0.5)
        g = (u * phi_sum).astype(bf16)
        y = y + contract(g, down_ref[cols, :], 1, 0)
        down_grad[:, cols] = contract(dyt, g, 1, 0)
        du = (contract(dy_low, down_ref[cols, :], 1, 1) * (phi_sum + u * density)).astype(bf16)
        up_grad[:, cols] = contract(h2t, du, 1, 0)
        sums_ref[21 + col : 22 + col, :] = col_sum(du.astype(f32))
        dh2 = dh2 + contract(du, up_ref[:, cols], 1, 1)
    y_ref[...] = y.astype(bf16)
    back, gain_sum, bias_sum = norm_back(dh2, unit, inverse, vec_ref[18:19, :])
    dx1 = dy + back
    dx1_ref[...] = dx1
    da = dx1.astype(bf16)
    do_ref[...] = contract(da, out_ref[...], 1, 1).astype(bf16)
    out_grad[...] = contract(turned(o), da, 1, 0)
    sums_ref[0:17, :] = jnp.zeros((17, 256), f32)
    sums_ref[17:18, :] = col_sum(da.astype(f32))
    sums_ref[18:19, :] = gain_sum
    sums_ref[19:20, :] = bias_sum
    sums_ref[20:21, :] = col_sum(dy)


def rotate(left_turned, grad, right):
    half = contract(left_turned, grad.astype(bf16), 1, 0).astype(bf16)
    return contract(half, right, 1, 0)


def rotate_turned(grad_turned, left, right):
    half = contract(grad_turned.astype(bf16), left, 1, 0).astype(bf16)
    return contract(turned(half), right, 1, 0)


def share_out(keep_ref, send_ref, parts, mats):
    half = keep_ref.shape[0]
    for ref, base in ((keep_ref, 0), (send_ref, half)):

        def body(block, ref=ref, base=base):
            collect(ref, block, parts, mats, source(block + base))

        each_block(half, body)


def early_turn_kernel(up_grad, down_grad, turned_ref, narrow_ref, wide_ref, keep_ref, send_ref, up, down):
    up[...] = rotate(turned_ref[3], up_grad[...], wide_ref[0])
    down[...] = rotate_turned(down_grad[...], wide_ref[1], narrow_ref[6])
    share_out(keep_ref, send_ref, layout(256, EARLY)[0], (up, down))


def middle_turn_kernel(query_left, query_right, out_grad, turned_ref, narrow_ref, query_ref, out_ref):
    query_grad = jnp.concatenate([query_left[...], query_right[...]], axis=1)
    query_ref[...] = rotate(turned_ref[0], query_grad, narrow_ref[1])
    out_ref[...] = rotate(turned_ref[2], out_grad[...], narrow_ref[4])


def attend_back_kernel(
    step, unroll, group, q_ref, k_ref, v_ref, mask_ref, o_ref, log_ref, g_ref, h1_ref,
    dq_ref, keep_ref, send_ref, query_grad, bias_ref, dq_wide, dkv, ps, dss, qt, gt,
):
    tokens = q_ref.shape[0]
    scale = 32**-0.5
    lane = lax.broadcasted_iota(jnp.int32, (1, 128), 1)
    mask = mask_ref[...]
    cols = slice(group * 128, group * 128 + 128)
    qt[...] = turned(q_ref[:, cols])
    gt[...] = turned(g_ref[:, cols])

    def one_head(head):
        mine = lane // 32 == head
        keys = jnp.where(mine, k_ref[:, cols], 0)
        values = jnp.where(mine, v_ref[:, cols], 0)

        def block(start):
            rows = pl.ds(start, step)
            grad = g_ref[rows, cols]
            inner = jnp.sum(jnp.where(mine, grad.astype(f32) * o_ref[rows, cols], 0.0), axis=1, keepdims=True)
            if isinstance(head, int):
                log = log_ref[rows, group * 4 + head : group * 4 + head + 1]
            else:
                log = jnp.sum(jnp.where(lane == head + group * 4, log_ref[rows, :], 0.0), axis=1, keepdims=True)
            scores = contract(q_ref[rows, cols], keys, 1, 1)
            probs = jnp.exp2(scores * (scale * LOG2E) + mask - log)
            grad_scores = (probs * (contract(grad, values, 1, 1) - inner)).astype(bf16)
            ps[rows, :] = probs.astype(bf16)
            dss[rows, :] = grad_scores
            out = contract(grad_scores, keys, 1, 0) * scale
            dq_wide[rows, :] = jnp.where(mine, out, dq_wide[rows, :])

        over_blocks(block, tokens, step)
        dkv[head_rows(head), :] = contract(qt[head_rows(head), :], dss[...], 1, 0) * scale
        dkv[head_rows(head, 128), :] = contract(gt[head_rows(head), :], ps[...], 1, 0)

    over_heads(one_head, 0, 4, unroll)
    dq = dq_wide[...].astype(bf16)
    dq_ref[...] = dq
    bias_ref[...] = col_sum(dq.astype(f32))
    half = keep_ref.shape[0]
    keep_ref[...] = dkv[:, 0:half].T
    send_ref[...] = dkv[:, half:].T
    query_grad[...] = contract(turned(h1_ref[...]), dq, 1, 0)


def total_of(refs):
    total = refs[0][...]
    for ref in refs[1:]:
        total = total + ref[...].astype(f32)
    return total


def split_kernel(count, terms, *refs):
    total = total_of(refs[:terms])
    rows = total.shape[0] // count
    refs[terms][...] = total[:rows]
    for index in range(1, count):
        refs[terms + index][...] = total[index * rows : (index + 1) * rows].astype(bf16)


def split_sum(terms, count, after=()):
    rows = terms[0].shape[0] // count
    tail = terms[0].shape[1:]
    outs = [((rows,) + tail, f32)] + [((rows,) + tail, bf16)] * (count - 1)
    return run("split_sum", functools.partial(split_kernel, count, len(terms)), outs, terms, micros=0.6, after=after)


def split_heads_kernel(count, left_keep, left_got, right_keep, right_got, *outs):
    rows = outs[0].shape[0]
    for index in range(count):
        at = slice(index * rows, (index + 1) * rows)
        left = left_keep[at, :] + left_got[at, :]
        right = right_keep[at, :] + right_got[at, :]
        parts = (left[:, 0:128], right[:, 0:128], left[:, 128:256], right[:, 128:256])
        for place, part in enumerate(parts):
            cols = slice(place * 128, place * 128 + 128)
            outs[index][:, cols] = part if index == 0 else part.astype(bf16)


def pair_total(values):
    while len(values) > 1:
        values = [a + b for a, b in zip(values[::2], values[1::2])]
    return values[0]


def two_parts(value):
    high = value.astype(bf16)
    return high, (value - high.astype(f32)).astype(bf16)


def split_with_vectors_kernel(count, terms, first, *refs):
    vec_terms = 2 if first else 1
    keep_ref, vec_ref = refs[terms + vec_terms], refs[terms + vec_terms + 1]
    sends = refs[terms + vec_terms + 2 :]
    if first:
        total = total_of(refs[:terms])
        vec = refs[terms][...] + refs[terms + 1][...]
    else:
        rows = refs[0].shape[0]
        total = refs[0][...]
        for ref in refs[1:terms]:
            total = total + ref[0:rows, :].astype(f32)
        vec = pair_total([refs[terms][...]] + [vector_part(ref, rows) for ref in refs[1:terms]])
    rows = total.shape[0] // count
    keep_ref[...] = total[:rows]
    high, rest = two_parts(vec)
    vec_ref[...] = high.astype(f32) + rest.astype(f32)
    for index, ref in enumerate(sends, 1):
        ref[0:rows, :] = total[index * rows : (index + 1) * rows].astype(bf16)
        ref[rows : rows + 32, :] = high
        ref[rows + 32 : rows + 64, :] = rest


def vector_part(ref, rows):
    return ref[rows : rows + 32, :].astype(f32) + ref[rows + 32 : rows + 64, :].astype(f32)


def split_with_vectors(terms, vec_terms, count, first, after=()):
    rows = terms[0].shape[0] // count
    width = terms[0].shape[1]
    outs = [((rows, width), f32), ((32, width), f32)] + [((rows + 64, width), bf16)] * (count - 1)
    body = functools.partial(split_with_vectors_kernel, count, len(terms), first)
    return run("split_with_vectors", body, outs, list(terms) + list(vec_terms), micros=0.6, after=after)


def row_parts():
    return [("row", stride, size) for stride, size in rel_digits()[1:]]


def one_by_one(groups):
    return [(axis, stride << bit, 2) for axis, stride, size in groups for bit in reversed(range(size.bit_length() - 1))]


def side_by_side(x, groups):
    for axis, stride, size in groups:
        x = jnp.concatenate([x] + [swap(x, axis, j * stride) for j in range(1, size)], axis=0)
    return x


def keys_back_kernel(
    terms, *refs
):
    (kn_ref, c_ref, vec_ref, keyval_ref, blocks_ref, turned_ref, narrow_ref, pair_ref, wide_ref, query, out,
     keep_ref, send_ref, dc_ref, sums_ref, reduce, keyval) = refs[terms:]
    dkv = total_of(refs[:terms])
    high, rest = two_parts(dkv)
    dkn = contract(high, keyval_ref[...], 1, 1) + contract(rest, keyval_ref[...], 1, 1)
    unit, inverse = norm_parts(c_ref[...])
    back, gain_sum, bias_sum = norm_back(dkn, unit, inverse, vec_ref[14:15, :])
    dc = back.astype(bf16)
    dc_ref[...] = dc
    knt = turned(kn_ref[...])
    keyval[...] = rotate(turned_ref[1], contract(knt, high, 1, 0) + contract(knt, rest, 1, 0), pair_ref[...])
    reduce[...] = rotate_turned(contract(turned(dc), blocks_ref[...], 1, 0), wide_ref[2], narrow_ref[7])
    share_out(keep_ref, send_ref, layout(256, LATE)[0], (reduce, keyval, query, out))
    sums_ref[0:1, :] = col_sum(dc.astype(f32))
    sums_ref[1:2, :] = gain_sum
    sums_ref[2:3, :] = bias_sum
    sums_ref[3:4, :] = col_sum(dkv[:, 256:512])


def cells_back_kernel(
    tile_rows, cols, size_ref, dq_left, dq_right, dc_ref, query_ref, reduce_ref, x0_ref, dx1_ref, vec_ref, tile_ref, up_ref, down_ref,
    feed_sums, key_sums, left_sum, right_sum, dx0_ref, head_ref, tail_ref, sums_ref, frame,
):
    tokens = x0_ref.shape[0]
    dh1 = contract(dq_left[...], query_ref[:, 0:128], 1, 1) + contract(dq_right[...], query_ref[:, 128:256], 1, 1)
    for corner in range(4):
        pick = picked_cells((tokens, dc_ref.shape[0]), 0, size_ref, corner, tile_rows, cols)
        placed = contract(pick, dc_ref[...], 1, 0).astype(bf16)
        dh1 = dh1 + contract(placed, reduce_ref[corner * 256 : corner * 256 + 256, :], 1, 1)
    unit, inverse = norm_parts(x0_ref[...])
    back, gain_sum, bias_sum = norm_back(dh1, unit, inverse, vec_ref[10:11, :])
    dx0 = dx1_ref[...] + back
    dx0_ref[...] = dx0
    head_ref[...] = dx0[0:64].astype(bf16)
    tail_ref[...] = dx0[tokens - 64 :].astype(bf16)
    sums_ref[0:25, :] = feed_sums[...]
    sums_ref[25:32, :] = jnp.zeros((7, 256), f32)
    moved = shifted_frame(frame, tile_ref, up_ref, down_ref)
    grid = dx0.reshape(tile_rows, cols, 256)
    for tap in range(9):
        product = moved[tap % 3][tap // 3 : tap // 3 + tile_rows] * grid
        sums_ref[tap : tap + 1, :] = col_sum(product.reshape(tokens, 256))
    sums_ref[9:10, :] = col_sum(dx0)
    sums_ref[10:11, :] = gain_sum
    sums_ref[11:12, :] = bias_sum
    sums_ref[12:13, 0:128] = left_sum[...]
    sums_ref[12:13, 128:256] = right_sum[...]
    sums_ref[13:17, :] = key_sums[...]


def input_grad_kernel(tile_rows, dx0_ref, up_ref, down_ref, vec_ref, out_ref, frame):
    moved = shifted_frame(frame, dx0_ref, up_ref, down_ref)
    total = moved[1][1:-1]
    for tap in range(9):
        down, right = 2 - tap // 3, 2 - tap % 3
        total = total + vec_ref[tap : tap + 1, :] * moved[right][down : down + tile_rows]
    out_ref[...] = total.reshape(out_ref.shape)


def moments_of(total, first, second, moment_ref, square_ref):
    moment = BETA * first + (1.0 - BETA) * total
    square = BETA * second + (1.0 - BETA) * total * total
    moment_ref[...] = moment
    square_ref[...] = square
    return moment * (1.0 / CORRECTION) / (jnp.sqrt(square * (1.0 / CORRECTION)) + ADAM_EPS)


def adam_kernel(base, terms, *refs):
    first_ref, second_ref, moment_ref, square_ref, step_ref = refs[terms:]
    total = total_of(refs[:terms])
    at = slice(base, base + total.shape[0])
    step_ref[...] = moments_of(total, first_ref[at, :], second_ref[at, :], moment_ref, square_ref).astype(bf16)


def late_adam_kernel(terms, *refs):
    (own_vec, first_ref, second_ref, vec_ref, vec_first, vec_second, vec_ema,
     moment_ref, square_ref, step_ref, vec_out, vec_first_out, vec_second_out, vec_ema_out) = refs[terms:]
    rows = refs[0].shape[0]
    total = refs[0][...]
    for ref in refs[1:terms]:
        total = total + ref[0:rows, :].astype(f32)
    step_ref[...] = moments_of(total, first_ref[0:rows, :], second_ref[0:rows, :], moment_ref, square_ref).astype(bf16)
    vec = pair_total([own_vec[...]] + [vector_part(ref, rows) for ref in refs[1:terms]])
    vec = vec[0 : vec_ref.shape[0]]
    new = vec_ref[...] - VECTOR_RATE * moments_of(vec, vec_first[...], vec_second[...], vec_first_out, vec_second_out)
    vec_out[...] = new
    vec_ema_out[...] = EMA_KEEP * vec_ema[...] + (1.0 - EMA_KEEP) * new


def step_sides(group, width, refs, own_narrow, own_wide, second):
    lefts = {0: (own_narrow, 0), 1: (own_narrow, 1), 2: (own_narrow, 2), 3: (own_narrow, 3), 4: (own_wide, 0), 5: (own_wide, 1)}
    found = []
    values = refs[...].astype(f32)
    for j, first, rows, blocks in layout(width, group)[0]:
        left_ref, index = lefts[j]
        half = left_ref.shape[2] // 2
        left = left_ref[index][:, half * second : half * (second + 1)].astype(bf16)
        sides = []
        for col in range(blocks):
            part = values[:, first + col * rows : first + (col + 1) * rows, :]
            sides.append(contract(left, part.reshape(half, width).astype(bf16), 1, 0))
        found.append(sides[0] if blocks == 1 else jnp.concatenate(sides, axis=1))
    return found


def right_of(j, narrow_ref, pair_ref, wide_ref):
    return {0: narrow_ref.at[1], 1: pair_ref, 2: narrow_ref.at[4], 3: wide_ref.at[0], 4: narrow_ref.at[6], 5: narrow_ref.at[7]}[j][...]


def update_rows(group, width, base, sides, rights, weights_ref, chunk):
    for (j, first, rows, blocks), side in zip(layout(width, group)[0], sides):
        full = contract(side.astype(bf16), right_of(j, *rights), 1, 1)
        for col in range(blocks):
            start = first + col * rows
            old = weights_ref[base + start : base + start + rows, :]
            piece = full[0:rows, col * width : (col + 1) * width]
            chunk[start : start + rows, :] = old - MATRIX_RATES[j] * (piece + WEIGHT_DECAY * old)


def early_finish_kernel(
    width, late_near, early_near, early_far, own_narrow, own_wide, narrow_ref, pair_ref, wide_ref,
    weights_ref, late_first, late_second, early_first, early_second,
    new_ref, first_out, second_out, *late_sides,
):
    near = step_sides(EARLY, width, early_near, own_narrow, own_wide, 0)
    far = step_sides(EARLY, width, early_far, own_narrow, own_wide, 1)
    sides = [a + b for a, b in zip(near, far)]
    base = layout(width, LATE)[1]
    update_rows(EARLY, width, base, sides, (narrow_ref, pair_ref, wide_ref), weights_ref, new_ref)
    for late, early, out in ((late_first, early_first, first_out), (late_second, early_second, second_out)):
        from_chunk(late, 0, LATE, out, width)
        from_chunk(early, 0, EARLY, out, width)
    for ref, side in zip(late_sides, step_sides(LATE, width, late_near, own_narrow, own_wide, 0)):
        ref[...] = side


def finish_kernel(
    width, late_far, reduce_side, keyval_side, query_side, out_side, early_new, own_narrow, own_wide, narrow_ref, pair_ref, wide_ref,
    weights_ref, ema_ref, weights_out, ema_out, chunk,
):
    far = step_sides(LATE, width, late_far, own_narrow, own_wide, 1)
    near = (reduce_side, keyval_side, query_side, out_side)
    sides = [a[...] + b for a, b in zip(near, far)]
    split = layout(width, LATE)[1]
    update_rows(LATE, width, 0, sides, (narrow_ref, pair_ref, wide_ref), weights_ref, chunk)
    chunk[split:, :] = early_new[...]
    from_chunk(chunk, 0, LATE, weights_out, width)
    from_chunk(chunk, split, EARLY, weights_out, width)
    chunk[...] = EMA_KEEP * ema_ref[...] + (1.0 - EMA_KEEP) * chunk[...]
    from_chunk(chunk, 0, LATE, ema_out, width)
    from_chunk(chunk, split, EARLY, ema_out, width)


def on_device(
    patches,
    cotangent,
    image_sizes,
    weights,
    first_moment,
    second_moment,
    weight_ema,
    vectors,
    vec_first,
    vec_second,
    vec_ema,
    basis_narrow,
    basis_pair,
    basis_wide,
):
    _, rows, cols, width = patches.shape
    tokens = rows * cols
    shards = device_count()
    tile = patches.reshape(tokens, width)
    dy = cotangent.reshape(tokens, width)
    per = weights.shape[1]
    late_rows, early_rows = layout(width, LATE)[1], layout(width, EARLY)[1]
    chunk = late_rows + early_rows
    ranks = lax.axis_size("row")
    own_keys = tokens // 4
    keys = own_keys * ranks
    frame = ((rows + 2, cols + 16, width), f32)
    img_part = ("img", 1, lax.axis_size("img"))
    xy_parts = row_parts()

    def border(head, tail):
        up = lax.ppermute(tail, "row", [(i, i + 1) for i in range(ranks - 1)])
        return up, lax.ppermute(head, "row", [(i + 1, i) for i in range(ranks - 1)])

    gather_groups = xy_parts[::-1]
    lines = lax.axis_size("img")

    (packed,) = run(
        "pack",
        functools.partial(pack_kernel, width),
        [((chunk, width), bf16)],
        [weights],
        scratch=[((chunk, width), f32)],
    )
    line = join([packed[None]] + [swap(packed, "img", j)[None] for j in range(1, lines)])
    up_halo, down_halo = border(tile[:64], tile[tokens - 64 :])
    x0, h1, mask, vec, sizes = run(
        "front",
        functools.partial(front_kernel, rows, cols),
        [((tokens, width), f32), ((tokens, width), bf16), ((1, keys), f32), (vectors.shape, f32), ((8, 128), jnp.int32)],
        [image_sizes, tile, up_halo, down_halo, vectors],
        scratch=[frame],
        scalars=(0,),
        micros=1.3,
        after=[line],
    )
    wide, own_wide = run(
        "wide_bases",
        wide_bases_kernel,
        [((3, FF, FF), bf16), ((2, max(16, FF // shards), FF), f32)],
        [basis_wide],
        scratch=[((2 * FF, 128), f32), ((12, width, FF), f32)],
        micros=6.0,
        mib=48,
        raw=(0,),
        sems=12,
        after=[line],
    )
    all_near = line
    for axis, stride, size in gather_groups:
        pieces = [all_near] + [swap(all_near, axis, j * stride) for j in range(1, size)]
        all_near = join(pieces, after=[own_wide, vec])
    all_far = swap(all_near, "row", 1)
    w_reduce, w_keyval, w_query, w_out, blocks, c, kn, own_kv = run(
        "keys",
        functools.partial(keys_kernel, rows, cols),
        [
            ((4 * width, width), bf16),
            ((width, 2 * width), bf16),
            ((width, width), bf16),
            ((width, width), bf16),
            ((own_keys, 4 * width), bf16),
            ((own_keys, width), f32),
            ((own_keys, width), bf16),
            ((own_keys, 2 * width), bf16),
        ],
        [sizes, h1, vec, all_near, all_far],
        scratch=[((4 * width, width), f32), ((width, 2 * width), f32), ((width, width), f32), ((width, width), f32)],
        micros=1.5,
    )
    narrow, narrow_turned, pair, own_narrow = run(
        "narrow_bases",
        narrow_bases_kernel,
        [((8, width, width), bf16), ((4, width, width), bf16), ((2 * width, 2 * width), bf16), ((4, 16, width), f32)],
        [basis_narrow, basis_pair],
        scratch=[((2 * width, 128), f32)],
        micros=1.5,
        after=[own_kv],
    )
    kv_near = side_by_side(own_kv, gather_groups)
    kv_far = swap(kv_near, "row", 1)

    unroll = keys <= 1024
    step = tokens if unroll else 32
    q, k, v, o, log = run(
        "attend",
        functools.partial(attend_kernel, step, unroll),
        [((tokens, width), bf16), ((keys, width), bf16), ((keys, width), bf16), ((tokens, width), f32), ((tokens, 128), f32)],
        [h1, w_query, vec, kv_near, kv_far, mask],
        mib=8 if unroll else 44,
        micros=8.0,
        after=[own_narrow],
    )
    y, do, dx1, up_grad, down_grad, out_grad, feed_sums = run(
        "feed",
        feed_kernel,
        [
            ((tokens, width), bf16),
            ((tokens, width), bf16),
            ((tokens, width), f32),
            ((width, FF), f32),
            ((width, FF), f32),
            ((width, width), f32),
            (vectors.shape, f32),
        ],
        [o, x0, w_out, all_near, all_far, vec, dy],
        scratch=[((width, FF), bf16), ((FF, width), bf16), ((width, FF), f32), ((FF, width), f32)],
        mib=12,
        micros=3.5,
    )
    half = (shards // 2, early_rows, width)
    early_keep, early_send = run(
        "early_turn",
        early_turn_kernel,
        [(half, f32), (half, f32)],
        [up_grad, down_grad, narrow_turned, narrow, wide],
        scratch=[((width, FF), f32), ((FF, width), f32)],
        mib=10,
        micros=2.0,
    )

    def back(group, after):
        return run(
            "attend_back",
            functools.partial(attend_back_kernel, step, unroll, group),
            [
                ((tokens, 128), bf16),
                ((keys // 2, width), f32),
                ((keys // 2, width), f32),
                ((width, 128), f32),
                ((1, 128), f32),
            ],
            [q, k, v, mask, o, log, do, h1],
            scratch=[
                ((tokens, 128), f32),
                ((width, keys), f32),
                ((tokens, keys), bf16),
                ((tokens, keys), bf16),
                ((128, tokens), bf16),
                ((128, tokens), bf16),
            ],
            mib=14 if unroll else 60,
            micros=5.0,
            after=after,
        )

    pairs = one_by_one(xy_parts + [img_part])
    place = 0

    def early_pair(after=()):
        nonlocal early_terms, place
        keep, send = split_sum(early_terms, 2, after=after)
        early_terms = [keep, swap(send, *pairs[place][:2])]
        place += 1
        return keep

    early_terms = [early_keep, swap(early_send, "row", 1)]
    dq_left, left_keep, left_send, query_left, left_sum = back(0, [early_keep])
    token = early_pair([query_left])
    left_got = swap(left_send, "row", 1)
    dq_right, right_keep, right_send, query_right, right_sum = back(1, [token])
    right_got = swap(right_send, "row", 1)
    axis, stride, size = xy_parts[0]
    dkv_keep, *dkv_sends = run(
        "split_heads",
        functools.partial(split_heads_kernel, size),
        [((keys // 2 // size, 2 * width), f32)] + [((keys // 2 // size, 2 * width), bf16)] * (size - 1),
        [left_keep, left_got, right_keep, right_got],
        micros=0.8,
    )
    token = early_pair([dkv_keep])
    old_chunk, ema_chunk, first_chunk, second_chunk = run(
        "moments",
        functools.partial(moments_kernel, width),
        [((chunk, width), f32)] * 4,
        [jnp.concatenate([weights, weight_ema, first_moment, second_moment], axis=0)],
        after=[dkv_keep],
    )
    dkv_terms = [dkv_keep] + [swap(x, axis, j * stride) for j, x in enumerate(dkv_sends, 1)]
    for axis, stride, size in xy_parts[1:]:
        keep, *sends = split_sum(dkv_terms, size)
        dkv_terms = [keep] + [swap(x, axis, j * stride) for j, x in enumerate(sends, 1)]
    query_turn, out_turn = run(
        "middle_turn",
        middle_turn_kernel,
        [((width, width), f32), ((width, width), f32)],
        [query_left, query_right, out_grad, narrow_turned, narrow],
        micros=0.7,
        after=[dkv_keep],
    )
    half = (shards // 2, late_rows, width)
    late_keep, late_send, dc, key_sums = run(
        "keys_back",
        functools.partial(keys_back_kernel, len(dkv_terms)),
        [(half, f32), (half, f32), ((own_keys, width), bf16), ((4, width), f32)],
        list(dkv_terms) + [kn, c, vec, w_keyval, blocks, narrow_turned, narrow, pair, wide, query_turn, out_turn],
        scratch=[((4 * width, width), f32), ((width, 2 * width), f32)],
        micros=2.0,
        after=[token, old_chunk],
    )
    late_got = swap(late_send, "row", 1)
    token = early_pair([dc])
    dx0, head, tail, vec_grads = run(
        "cells_back",
        functools.partial(cells_back_kernel, rows, cols),
        [((tokens, width), f32), ((64, width), bf16), ((64, width), bf16), ((32, width), f32)],
        [
            sizes, dq_left, dq_right, dc, w_query, w_reduce, x0, dx1, vec, tile, up_halo, down_halo,
            feed_sums, key_sums, left_sum, right_sum,
        ],
        scratch=[frame],
        micros=2.0,
        after=[token],
    )
    vec_terms = [vec_grads, swap(vec_grads, "row", 1)]
    grad_up, grad_down = border(head, tail)
    while place < len(pairs):
        token = early_pair()
    late_terms = [late_keep.reshape(-1, width), late_got.reshape(-1, width)]

    def late_stage(part, first, after):
        nonlocal late_terms, vec_terms
        axis, stride, size = part
        keep, own_vec, *sends = split_with_vectors(late_terms, vec_terms, size, first, after)
        late_terms = [keep] + [swap(x, axis, j * stride) for j, x in enumerate(sends, 1)]
        vec_terms = [own_vec]
        return keep

    token = late_stage(xy_parts[0], True, [token])
    early_first, early_second, early_step = run(
        "adam",
        functools.partial(adam_kernel, late_rows, 2),
        [((early_rows, width), f32), ((early_rows, width), f32), ((early_rows, width), bf16)],
        [t.reshape(early_rows, width) for t in early_terms] + [first_chunk, second_chunk],
        micros=0.6,
        after=[token],
    )
    for part in xy_parts[1:]:
        late_stage(part, False, [])
    steps_pairs = one_by_one(xy_parts + [img_part])[::-1]
    steps = early_step[None]

    def steps_pair(after=()):
        nonlocal steps
        axis, stride, _ = steps_pairs.pop(0)
        steps = join([steps, swap(steps, axis, stride)], after)
        return steps

    token = late_stage(img_part, False, [steps_pair()])
    (grad_input,) = run(
        "input_grad",
        functools.partial(input_grad_kernel, rows),
        [((tokens, width), f32)],
        [dx0, grad_up, grad_down, vec],
        scratch=[frame],
        micros=1.5,
        after=[token],
    )
    late_first, late_second, late_step, new_vectors, vec_moment, vec_square, new_vec_ema = run(
        "late_adam",
        functools.partial(late_adam_kernel, len(late_terms)),
        [((late_rows, width), f32), ((late_rows, width), f32), ((late_rows, width), bf16)] + [(vectors.shape, f32)] * 4,
        late_terms + vec_terms + [first_chunk, second_chunk, vec, vec_first, vec_second, vec_ema],
        micros=0.8,
        after=[steps_pair(), grad_input],
    )
    step_near = late_step[None]
    after = [late_step]
    for axis, stride, size in [img_part] + gather_groups:
        pieces = [step_near] + [swap(step_near, axis, j * stride) for j in range(1, size)]
        step_near = join(pieces, [steps_pair(after)] if steps_pairs else [])
        after = [step_near]
    while steps_pairs:
        steps_pair()
    step_far = swap(step_near, "row", 1)
    steps_near, steps_far = steps, swap(steps, "row", 1)

    early_new, new_first, new_second, *late_sides = run(
        "early_finish",
        functools.partial(early_finish_kernel, width),
        [((early_rows, width), f32), ((1, per), f32), ((1, per), f32)]
        + [((own_wide.shape[1], width), f32)]
        + [((own_narrow.shape[1], cols_of * width), f32) for cols_of in (2, 1, 1)],
        [
            step_near, steps_near, steps_far, own_narrow, own_wide, narrow, pair, wide,
            old_chunk, late_first, late_second, early_first, early_second,
        ],
        micros=2.0,
    )
    new_weights, new_ema = run(
        "finish",
        functools.partial(finish_kernel, width),
        [((1, per), f32)] * 2,
        [step_far, *late_sides, early_new, own_narrow, own_wide, narrow, pair, wide, old_chunk, ema_chunk],
        scratch=[((chunk, width), f32)],
        micros=1.5,
    )
    return (
        y.reshape(patches.shape),
        grad_input.reshape(patches.shape),
        new_weights,
        new_first,
        new_second,
        new_ema,
        new_vectors,
        vec_moment,
        vec_square,
        new_vec_ema,
    )


def solution(mesh):
    tiles = P("img", "row", None, None)
    packed = P(("img", "row"), None)
    return jax.shard_map(
        on_device,
        mesh=mesh,
        in_specs=(tiles, tiles, P("img", None)) + (packed,) * 4 + (P(),) * 7,
        out_specs=(tiles, tiles) + (packed,) * 4 + (P(),) * 4,
        check_vma=False,
    )
```

```python
import functools
import math

import jax
import jax.numpy as jnp
from jax import lax
from jax.experimental import pallas as pl
from jax.experimental.pallas import tpu as pltpu
from jax.sharding import PartitionSpec as P

HEADS = 8
FF = 1024
STEP = 5

NORM_EPS = 1e-05
ADAM_EPS = 1e-08
BETA = 0.5
WEIGHT_DECAY = 0.05
EMA_KEEP = 0.75
VECTOR_RATE = 0.06
MATRIX_RATES = (0.04, 0.02, 0.25, 0.02, 0.01, 0.01)
CORRECTION = 1.0 - BETA**STEP
LOG2E = math.log2(math.e)
f32 = jnp.float32
bf16 = jnp.bfloat16
LATE = (5, 1, 0, 2)
EARLY = (3, 4)


def matrix_shapes(width, hidden):
    return (
        (width, width),
        (width, 2 * width),
        (width, width),
        (width, hidden),
        (hidden, width),
        (4 * width, width),
    )


def contract(a, b, ca, cb, **kw):
    return lax.dot_general(
        a, b, (((ca,), (cb,)), ((), ())), preferred_element_type=f32, **kw
    )


def swap(x, axis, step):
    count = lax.axis_size(axis)
    return lax.ppermute(x, axis, [(i, i ^ step) for i in range(count)])


def row_groups():
    left = lax.axis_size("row") // 2
    groups, stride = [(1, 2)], 2
    while left > 1:
        size = 4 if left % 4 == 0 else 2
        groups.append((stride, size))
        left //= size
        stride *= size
    return groups


def rel_digits():
    groups = row_groups()
    return [groups[0]] + groups[1:][::-1]


def source(block):
    sizes = lax.axis_size("img")
    img, rest = block % sizes, block // sizes
    rel = 0
    for stride, size in reversed(rel_digits()):
        rel = rel + (rest % size) * stride
        rest = rest // size
    row = lax.axis_index("row") ^ rel
    return (lax.axis_index("img") ^ img) * lax.axis_size("row") + row


def device_count():
    return lax.axis_size("img") * lax.axis_size("row")


def run(name, body, outs, args, scratch=(), mib=6, scalars=(), micros=1.0, after=(), raw=(), sems=0):
    count = len(args)

    def without(*refs):
        body(*refs[:count], *refs[count + len(after) :])

    space = {index: pltpu.SMEM for index in scalars} | {index: pltpu.HBM for index in raw}
    specs = [pl.BlockSpec(memory_space=space.get(index, pltpu.VMEM)) for index in range(count)]
    return pl.pallas_call(
        without,
        out_shape=tuple(jax.ShapeDtypeStruct(shape, dtype) for shape, dtype in outs),
        in_specs=specs + [pl.BlockSpec(memory_space=pl.ANY)] * len(after),
        out_specs=tuple(pl.BlockSpec(memory_space=pltpu.VMEM) for _ in outs),
        scratch_shapes=[pltpu.VMEM(shape, dtype) for shape, dtype in scratch]
        + ([pltpu.SemaphoreType.DMA((sems,))] if sems else []),
        compiler_params=pltpu.CompilerParams(vmem_limit_bytes=mib * 2**20),
        cost_estimate=pl.CostEstimate(flops=0, bytes_accessed=int(micros * 3.6e6), transcendentals=0),
        name=name,
    )(*args, *after)


def each_block(count, body):
    if count <= 32:
        for index in range(count):
            body(index)
    else:

        def step(index, carry):
            body(index)
            return carry

        lax.fori_loop(0, count, step, 0)


def put_rows(ref, start, cols, value):
    count = value.shape[0]
    if count % 8 == 0:
        ref[pl.ds(pl.multiple_of(start, 8), count), cols] = value
    else:
        for row in range(count):
            ref[pl.ds(start + row, 1), cols] = value[row : row + 1]


def get_rows(ref, start, count, cols):
    if count % 8 == 0:
        return ref[pl.ds(pl.multiple_of(start, 8), count), cols]
    return jnp.concatenate([ref[pl.ds(start + row, 1), cols] for row in range(count)], axis=0)


def layout(width, group):
    dims = matrix_shapes(width, FF)
    found, start = [], 0
    for j in group:
        rows = dims[j][0] // device_count()
        blocks = dims[j][1] // width
        found.append((j, start, rows, blocks))
        start += rows * blocks
    return found, start


def packed_starts(width):
    dims = matrix_shapes(width, FF)
    starts, start = [], 0
    for m, n in dims:
        starts.append(start)
        start += m * n // device_count()
    return starts


def spread(block, parts, mats, start_of):
    for (j, first, rows, blocks), ref in zip(parts, mats):
        for col in range(blocks):
            piece = block[first + col * rows : first + (col + 1) * rows]
            put_rows(ref, start_of * rows, slice(col * 256, col * 256 + 256), piece)


def collect(out_ref, index, parts, mats, start_of):
    for (j, first, rows, blocks), ref in zip(parts, mats):
        for col in range(blocks):
            piece = get_rows(ref, start_of * rows, rows, slice(col * 256, col * 256 + 256))
            out_ref[index, first + col * rows : first + (col + 1) * rows, :] = piece


def norm_parts(values):
    centred = values - jnp.mean(values, axis=-1, keepdims=True)
    inverse = lax.rsqrt(jnp.mean(centred * centred, axis=-1, keepdims=True) + NORM_EPS)
    return centred * inverse, inverse


def norm_back(grad, unit, inverse, gain):
    grad_unit = grad * gain
    back = grad_unit - jnp.mean(grad_unit, axis=-1, keepdims=True)
    back = back - unit * jnp.mean(grad_unit * unit, axis=-1, keepdims=True)
    gain_sum = jnp.sum(grad * unit, axis=0, keepdims=True)
    return back * inverse, gain_sum, jnp.sum(grad, axis=0, keepdims=True)


def turned(value):
    return value.astype(f32).T.astype(bf16)


def col_sum(value):
    return jnp.sum(value, axis=0, keepdims=True)


def pack_kernel(width, w_ref, out_ref, chunk):
    to_chunk(w_ref, chunk, width)
    out_ref[...] = chunk[...].astype(bf16)


def to_chunk(flat_ref, out_ref, width, index=0):
    dims, starts, base = matrix_shapes(width, FF), packed_starts(width), 0
    for group in (LATE, EARLY):
        parts, count = layout(width, group)
        for j, first, rows, blocks in parts:
            for col in range(blocks):
                for row in range(rows):
                    at = starts[j] + row * dims[j][1] + col * width
                    place = base + first + col * rows + row
                    out_ref[place : place + 1, :] = flat_ref[index : index + 1, at : at + width]
        base += count


def from_chunk(values, out_ref, width):
    dims, starts = matrix_shapes(width, FF), packed_starts(width)
    for j, first, rows, blocks in both_groups(width):
        for col in range(blocks):
            for row in range(rows):
                at = starts[j] + row * dims[j][1] + col * width
                place = first + col * rows + row
                out_ref[0:1, at : at + width] = values[place : place + 1, :]


def moments_kernel(width, rows_ref, *outs):
    for index, ref in enumerate(outs):
        to_chunk(rows_ref, ref, width, index)


def own_rows(matrix_ref, out_ref, tall):
    count = device_count()
    rank = lax.axis_index("img") * lax.axis_size("row") + lax.axis_index("row")
    size = matrix_ref.shape[0]
    rows, pad = size // count, out_ref.shape[0] // 2
    place = lax.broadcasted_iota(jnp.int32, (128, 1), 0)
    mine = jnp.where(place < rows, place + rank * rows, -1)
    other = place - pad
    other = jnp.where((other >= 0) & (other < rows), other + (rank ^ 1) * rows, mine)
    pick = (lax.broadcasted_iota(jnp.int32, (128, size), 1) == other).astype(f32).astype(bf16)
    tall[0:size, :] = contract(pick, matrix_ref[...], 1, 0).T

    def body(block):
        put_rows(tall, size + block * rows, slice(None), get_rows(tall, source(block) * rows, rows, slice(None)))

    each_block(count, body)
    out_ref[...] = tall[size : 2 * size, :].T[0 : out_ref.shape[0]]


def narrow_bases_kernel(narrow_ref, pair_ref, narrow_out, turned_out, pair_out, own_ref, tall):
    narrow_out[...] = narrow_ref[...].astype(bf16)
    pair_out[...] = pair_ref[...].astype(bf16)
    for index, j in enumerate((0, 2, 3, 5)):
        turned_out[index] = narrow_ref[j].T.astype(bf16)
        own_rows(narrow_out.at[j], own_ref.at[index], tall)


def own_wide_kernel(wide_ref, own_ref, tall):
    for index in range(2):
        own_rows(wide_ref.at[index + 1], own_ref.at[index], tall)


def wide_bases_kernel(wide_ref, wide_out, token, buffer, sems):
    count, size = wide_ref.shape[0], wide_ref.shape[1]
    rows, depth = buffer.shape[1], buffer.shape[0]
    each = size // rows
    total = count * each

    def copy(index):
        at = wide_ref.at[index // each, pl.ds(index % each * rows, rows)]
        return pltpu.make_async_copy(at, buffer.at[index % depth], sems.at[index % depth])

    for index in range(depth):
        copy(index).start()
    for index in range(total):
        copy(index).wait()
        first = index % each * rows
        wide_out[index // each, first : first + rows, :] = buffer[index % depth].astype(bf16)
        if index + depth < total:
            copy(index + depth).start()
    token[...] = jnp.zeros_like(token)


def join_kernel(*refs):
    start = 0
    for ref in refs[:-1]:
        refs[-1][start : start + ref.shape[0]] = ref[...]
        start += ref.shape[0]


def join(pieces, after=()):
    shape = (sum(x.shape[0] for x in pieces),) + pieces[0].shape[1:]
    return run("join", join_kernel, [(shape, pieces[0].dtype)], list(pieces), micros=0.4, after=after)[0]


def unpack(pieces, group, mats, base=0):
    parts = [(j, first + base, rows, blocks) for j, first, rows, blocks in layout(256, group)[0]]
    done = 0
    for piece in pieces:

        def body(block, piece=piece, done=done):
            spread(piece[block].astype(f32), parts, mats, source(block + done))

        each_block(piece.shape[0], body)
        done += piece.shape[0]


def shifted_frame(frame_ref, tile_ref, up_ref, down_ref):
    rows, cols, width = frame_ref.shape[0] - 2, 56, 256
    frame_ref[...] = jnp.zeros_like(frame_ref)
    frame_ref[0, 8 : 8 + cols, :] = up_ref[...].astype(f32)[-cols:]
    frame_ref[1 : 1 + rows, 8 : 8 + cols, :] = tile_ref[...].astype(f32).reshape(rows, cols, width)
    frame_ref[rows + 1, 8 : 8 + cols, :] = down_ref[...].astype(f32)[:cols]
    return [frame_ref[:, 7 + shift : 7 + shift + cols, :] for shift in range(3)]


def front_kernel(tile_rows, cols, size_ref, tile_ref, up_ref, down_ref, vec_ref, x0_ref, h1_ref, mask_ref, vec_out, size_out, frame):
    rows = frame.shape[0] - 2
    vec_out[...] = vec_ref[...]
    size_out[...] = jnp.where(lax.broadcasted_iota(jnp.int32, size_out.shape, 0) == 0, size_ref[0, 0], size_ref[0, 1])
    moved = shifted_frame(frame, tile_ref, up_ref, down_ref)
    total = moved[1][1:-1] + vec_ref[9:10, :]
    for tap in range(9):
        total = total + vec_ref[tap : tap + 1, :] * moved[tap % 3][tap // 3 : tap // 3 + rows]
    x0 = total.reshape(x0_ref.shape)
    x0_ref[...] = x0
    unit, _ = norm_parts(x0)
    h1_ref[...] = (unit * vec_ref[10:11, :] + vec_ref[11:12, :]).astype(bf16)
    half = cols // 2
    own = tile_rows // 2 * half
    key = lax.broadcasted_iota(jnp.int32, mask_ref.shape, 1)
    block = jnp.zeros_like(key)
    for start in range(own, mask_ref.shape[1], own):
        block = block + (key >= start).astype(jnp.int32)
    key = key - block * own
    row = jnp.zeros_like(key)
    for start in range(half, own, half):
        row = row + (key >= start).astype(jnp.int32)
    col = key - row * half
    rel = jnp.zeros_like(key)
    for stride, size in reversed(rel_digits()):
        rel = rel + (block & (size - 1)) * stride
        block = block >> (size.bit_length() - 1)
    row = row + (rel ^ lax.axis_index("row")) * (tile_rows // 2)
    inside = (2 * row < size_ref[0, 0]) & (2 * col < size_ref[0, 1])
    mask_ref[...] = jnp.where(inside, 0.0, -1e30)


def picked_cells(shape, cell_axis, size_ref, corner, tile_rows, cols):
    half = cols // 2
    key_shape = tuple(1 if axis == cell_axis else n for axis, n in enumerate(shape))
    key = lax.broadcasted_iota(jnp.int32, key_shape, 1 - cell_axis)
    row = jnp.zeros_like(key)
    for step in range(1, tile_rows // 2):
        row = row + (key >= step * half).astype(jnp.int32)
    col = 2 * (key - row * half) + corner % 2
    row = 2 * row + corner // 2
    inside = (row + lax.axis_index("row") * tile_rows < size_ref[0:1, 0:1]) & (col < size_ref[1:2, 0:1])
    target = jnp.where(inside, row * cols + col, -1)
    cell = lax.broadcasted_iota(jnp.int32, shape, cell_axis)
    return (cell == target).astype(f32).astype(bf16)


def keys_kernel(
    tile_rows, cols, size_ref, h1_ref, vec_ref, near_ref, far_ref,
    reduce_ref, keyval_ref, query_ref, out_ref, blocks_ref, c_ref, kn_ref, kv_ref,
    reduce_wide, keyval_wide, query_wide, out_wide,
):
    unpack((near_ref, far_ref), LATE, (reduce_wide, keyval_wide, query_wide, out_wide))
    reduce_ref[...] = reduce_wide[...].astype(bf16)
    keyval_ref[...] = keyval_wide[...].astype(bf16)
    query_ref[...] = query_wide[...].astype(bf16)
    out_ref[...] = out_wide[...].astype(bf16)
    keys = c_ref.shape[0]
    for corner in range(4):
        pick = picked_cells((keys, h1_ref.shape[0]), 1, size_ref, corner, tile_rows, cols)
        blocks_ref[:, corner * 256 : corner * 256 + 256] = contract(pick, h1_ref[...], 1, 0).astype(bf16)
    c = contract(blocks_ref[...], reduce_ref[...], 1, 0) + vec_ref[13:14, :]
    c_ref[...] = c
    unit, _ = norm_parts(c)
    kn = (unit * vec_ref[14:15, :] + vec_ref[15:16, :]).astype(bf16)
    kn_ref[...] = kn
    kv = contract(kn, keyval_ref[...], 1, 0)
    kv_ref[:, 0:256] = kv[:, 0:256].astype(bf16)
    kv_ref[:, 256:512] = (kv[:, 256:512] + vec_ref[16:17, :]).astype(bf16)


def over_heads(body, first, last, unroll):
    if unroll:
        for head in range(first, last):
            body(head)
    else:

        def step(head, carry):
            body(head)
            return carry

        lax.fori_loop(first, last, step, 0)


def over_blocks(block, tokens, step):
    if tokens == step:
        block(0)
    else:

        def go(index, carry):
            block(pl.multiple_of(index * step, step))
            return carry

        lax.fori_loop(0, tokens // step, go, 0)


def head_columns(head):
    group = head // 4
    if isinstance(head, int):
        return slice(group * 128, group * 128 + 128)
    return pl.ds(pl.multiple_of(group * 128, 128), 128)


def head_rows(head, base=0):
    if isinstance(head, int):
        return slice(base + head * 32, base + head * 32 + 32)
    return pl.ds(pl.multiple_of(base + head * 32, 32), 32)


def attend_kernel(
    step, unroll, h1_ref, query_ref, vec_ref, near_ref, far_ref, mask_ref, q_ref, k_ref, v_ref, o_ref, log_ref
):
    tokens = h1_ref.shape[0]
    half = near_ref.shape[0]
    for start, ref in ((0, near_ref), (half, far_ref)):
        k_ref[start : start + half, :] = ref[:, 0:256]
        v_ref[start : start + half, :] = ref[:, 256:512]
    q_ref[...] = (contract(h1_ref[...], query_ref[...], 1, 0) + vec_ref[12:13, :]).astype(bf16)
    scale = 32**-0.5 * LOG2E
    lane = lax.broadcasted_iota(jnp.int32, (1, 128), 1)
    mask = mask_ref[...]

    def one_head(head):
        cols = head_columns(head)
        mine = lane // 32 == head % 4
        keys = jnp.where(mine, k_ref[:, cols], 0)
        values = jnp.where(mine, v_ref[:, cols], 0)

        def block(start):
            rows = pl.ds(start, step)
            scores = contract(q_ref[rows, cols], keys, 1, 1) * scale + mask
            top = jnp.max(scores, axis=1, keepdims=True)
            exponent = jnp.exp2(scores - top)
            total = jnp.sum(exponent, axis=1, keepdims=True)
            probs = (exponent * (1.0 / total)).astype(bf16)
            out = contract(probs, values, 1, 0)
            o_ref[rows, cols] = jnp.where(mine, out, o_ref[rows, cols])
            log_ref[rows, :] = jnp.where(lane == head, top + jnp.log2(total), log_ref[rows, :])

        over_blocks(block, tokens, step)

    over_heads(one_head, 0, HEADS, unroll)


def feed_kernel(
    o_ref, x0_ref, out_ref, near_ref, far_ref, vec_ref, dy_ref,
    y_ref, do_ref, dx1_ref, up_grad, down_grad, out_grad, sums_ref, up_ref, down_ref, up_wide, down_wide,
):
    unpack((near_ref, far_ref), EARLY, (up_wide, down_wide), layout(256, LATE)[1])
    up_ref[...] = up_wide[...].astype(bf16)
    down_ref[...] = down_wide[...].astype(bf16)
    o = o_ref[...].astype(bf16)
    x1 = x0_ref[...] + (contract(o, out_ref[...], 1, 0) + vec_ref[17:18, :])
    unit, inverse = norm_parts(x1)
    h2 = (unit * vec_ref[18:19, :] + vec_ref[19:20, :]).astype(bf16)
    dy_low = dy_ref[...]
    dy = dy_low.astype(f32)
    dyt = turned(dy_low)
    h2t = turned(h2)
    y = x1 + vec_ref[20:21, :]
    dh2 = jnp.zeros_like(y)
    for col in range(FF // 256):
        cols = slice(col * 256, col * 256 + 256)
        u = contract(h2, up_ref[:, cols], 1, 0) + vec_ref[21 + col : 22 + col, :]
        phi_sum = 0.5 * (1.0 + lax.erf(u * (2.0**-0.5)))
        density = jnp.exp(-0.5 * u * u) * ((2.0 * math.pi) ** -0.5)
        g = (u * phi_sum).astype(bf16)
        y = y + contract(g, down_ref[cols, :], 1, 0)
        down_grad[:, cols] = contract(dyt, g, 1, 0)
        du = (contract(dy_low, down_ref[cols, :], 1, 1) * (phi_sum + u * density)).astype(bf16)
        up_grad[:, cols] = contract(h2t, du, 1, 0)
        sums_ref[21 + col : 22 + col, :] = col_sum(du.astype(f32))
        dh2 = dh2 + contract(du, up_ref[:, cols], 1, 1)
    y_ref[...] = y.astype(bf16)
    back, gain_sum, bias_sum = norm_back(dh2, unit, inverse, vec_ref[18:19, :])
    dx1 = dy + back
    dx1_ref[...] = dx1
    da = dx1.astype(bf16)
    do_ref[...] = contract(da, out_ref[...], 1, 1).astype(bf16)
    out_grad[...] = contract(turned(o), da, 1, 0)
    sums_ref[0:17, :] = jnp.zeros((17, 256), f32)
    sums_ref[17:18, :] = col_sum(da.astype(f32))
    sums_ref[18:19, :] = gain_sum
    sums_ref[19:20, :] = bias_sum
    sums_ref[20:21, :] = col_sum(dy)


def rotate(left_turned, grad, right):
    half = contract(left_turned, grad.astype(bf16), 1, 0).astype(bf16)
    return contract(half, right, 1, 0)


def rotate_turned(grad_turned, left, right):
    half = contract(grad_turned.astype(bf16), left, 1, 0).astype(bf16)
    return contract(turned(half), right, 1, 0)


def share_out(keep_ref, send_ref, parts, mats):
    half = keep_ref.shape[0]
    for ref, base in ((keep_ref, 0), (send_ref, half)):

        def body(block, ref=ref, base=base):
            collect(ref, block, parts, mats, source(block + base))

        each_block(half, body)


def early_turn_kernel(up_grad, down_grad, turned_ref, narrow_ref, wide_ref, keep_ref, send_ref, up, down):
    up[...] = rotate(turned_ref[3], up_grad[...], wide_ref[0])
    down[...] = rotate_turned(down_grad[...], wide_ref[1], narrow_ref[6])
    share_out(keep_ref, send_ref, layout(256, EARLY)[0], (up, down))


def middle_turn_kernel(query_left, query_right, out_grad, turned_ref, narrow_ref, query_ref, out_ref):
    query_grad = jnp.concatenate([query_left[...], query_right[...]], axis=1)
    query_ref[...] = rotate(turned_ref[0], query_grad, narrow_ref[1])
    out_ref[...] = rotate(turned_ref[2], out_grad[...], narrow_ref[4])


def attend_back_kernel(
    step, unroll, group, q_ref, k_ref, v_ref, mask_ref, o_ref, log_ref, g_ref, h1_ref,
    dq_ref, keep_ref, send_ref, query_grad, bias_ref, dq_wide, dkv, ps, dss, qt, gt,
):
    tokens = q_ref.shape[0]
    scale = 32**-0.5
    lane = lax.broadcasted_iota(jnp.int32, (1, 128), 1)
    mask = mask_ref[...]
    cols = slice(group * 128, group * 128 + 128)
    qt[...] = turned(q_ref[:, cols])
    gt[...] = turned(g_ref[:, cols])

    def one_head(head):
        mine = lane // 32 == head
        keys = jnp.where(mine, k_ref[:, cols], 0)
        values = jnp.where(mine, v_ref[:, cols], 0)

        def block(start):
            rows = pl.ds(start, step)
            grad = g_ref[rows, cols]
            inner = jnp.sum(jnp.where(mine, grad.astype(f32) * o_ref[rows, cols], 0.0), axis=1, keepdims=True)
            if isinstance(head, int):
                log = log_ref[rows, group * 4 + head : group * 4 + head + 1]
            else:
                log = jnp.sum(jnp.where(lane == head + group * 4, log_ref[rows, :], 0.0), axis=1, keepdims=True)
            scores = contract(q_ref[rows, cols], keys, 1, 1)
            probs = jnp.exp2(scores * (scale * LOG2E) + mask - log)
            grad_scores = (probs * (contract(grad, values, 1, 1) - inner)).astype(bf16)
            ps[rows, :] = probs.astype(bf16)
            dss[rows, :] = grad_scores
            out = contract(grad_scores, keys, 1, 0) * scale
            dq_wide[rows, :] = jnp.where(mine, out, dq_wide[rows, :])

        over_blocks(block, tokens, step)
        dkv[head_rows(head), :] = contract(qt[head_rows(head), :], dss[...], 1, 0) * scale
        dkv[head_rows(head, 128), :] = contract(gt[head_rows(head), :], ps[...], 1, 0)

    over_heads(one_head, 0, 4, unroll)
    dq = dq_wide[...].astype(bf16)
    dq_ref[...] = dq
    bias_ref[...] = col_sum(dq.astype(f32))
    half = keep_ref.shape[0]
    keep_ref[...] = dkv[:, 0:half].T
    send_ref[...] = dkv[:, half:].T
    query_grad[...] = contract(turned(h1_ref[...]), dq, 1, 0)


def total_of(refs):
    total = refs[0][...]
    for ref in refs[1:]:
        total = total + ref[...].astype(f32)
    return total


def split_kernel(count, terms, *refs):
    total = total_of(refs[:terms])
    rows = total.shape[0] // count
    refs[terms][...] = total[:rows]
    for index in range(1, count):
        refs[terms + index][...] = total[index * rows : (index + 1) * rows].astype(bf16)


def split_sum(terms, count, after=()):
    rows = terms[0].shape[0] // count
    tail = terms[0].shape[1:]
    outs = [((rows,) + tail, f32)] + [((rows,) + tail, bf16)] * (count - 1)
    return run("split_sum", functools.partial(split_kernel, count, len(terms)), outs, terms, micros=0.6, after=after)


def split_heads_kernel(count, left_keep, left_got, right_keep, right_got, *outs):
    rows = outs[0].shape[0]
    for index in range(count):
        at = slice(index * rows, (index + 1) * rows)
        left = left_keep[at, :] + left_got[at, :]
        right = right_keep[at, :] + right_got[at, :]
        parts = (left[:, 0:128], right[:, 0:128], left[:, 128:256], right[:, 128:256])
        for place, part in enumerate(parts):
            cols = slice(place * 128, place * 128 + 128)
            outs[index][:, cols] = part if index == 0 else part.astype(bf16)


def pair_total(values):
    while len(values) > 1:
        values = [a + b for a, b in zip(values[::2], values[1::2])]
    return values[0]


def two_parts(value):
    high = value.astype(bf16)
    return high, (value - high.astype(f32)).astype(bf16)


def split_with_vectors_kernel(count, terms, first, early, *refs):
    vec_terms = 2 if first else 1
    early_refs = refs[terms + vec_terms : terms + vec_terms + early]
    outs = refs[terms + vec_terms + early :]
    rows = refs[0].shape[0]
    if first:
        total = total_of(refs[:terms])
        vec = refs[terms][...] + refs[terms + 1][...]
    else:
        total = refs[0][...]
        for ref in refs[1:terms]:
            total = total + ref[0:rows, :].astype(f32)
        vec = pair_total([refs[terms][...]] + [vector_part(ref, rows) for ref in refs[1:terms]])
    rows = total.shape[0] // count
    outs[0][...] = total[:rows]
    high, rest = two_parts(vec)
    outs[1][...] = high.astype(f32) + rest.astype(f32)
    sends = outs[2:]
    if early:
        early_total = total_of(early_refs)
        more = early_total.shape[0] // count
        outs[2][...] = early_total[:more]
        sends = outs[3:]
    for index, ref in enumerate(sends, 1):
        ref[0:rows, :] = total[index * rows : (index + 1) * rows].astype(bf16)
        ref[rows : rows + 32, :] = high
        ref[rows + 32 : rows + 64, :] = rest
        if early:
            ref[rows + 64 :, :] = early_total[index * more : (index + 1) * more].astype(bf16)


def vector_part(ref, rows):
    return ref[rows : rows + 32, :].astype(f32) + ref[rows + 32 : rows + 64, :].astype(f32)


def split_with_vectors(terms, vec_terms, early_terms, count, first, after=()):
    rows = terms[0].shape[0] // count
    width = terms[0].shape[1]
    more = early_terms[0].shape[0] // count if early_terms else 0
    outs = [((rows, width), f32), ((32, width), f32)]
    outs += [((more, width), f32)] if early_terms else []
    outs += [((rows + 64 + more, width), bf16)] * (count - 1)
    body = functools.partial(split_with_vectors_kernel, count, len(terms), first, len(early_terms))
    args = list(terms) + list(vec_terms) + list(early_terms)
    found = run("split_with_vectors", body, outs, args, micros=0.6, after=after)
    return found[: len(outs) - count + 1], found[len(outs) - count + 1 :]


def row_parts():
    return [("row", stride, size) for stride, size in rel_digits()[1:]]


def one_by_one(groups):
    return [(axis, stride << bit, 2) for axis, stride, size in groups for bit in reversed(range(size.bit_length() - 1))]


def side_by_side(x, groups):
    for axis, stride, size in groups:
        x = jnp.concatenate([x] + [swap(x, axis, j * stride) for j in range(1, size)], axis=0)
    return x


def keys_back_kernel(
    terms, *refs
):
    (kn_ref, c_ref, vec_ref, keyval_ref, blocks_ref, turned_ref, narrow_ref, pair_ref, wide_ref, query, out,
     keep_ref, send_ref, dc_ref, sums_ref, reduce, keyval) = refs[terms:]
    dkv = total_of(refs[:terms])
    high, rest = two_parts(dkv)
    dkn = contract(high, keyval_ref[...], 1, 1) + contract(rest, keyval_ref[...], 1, 1)
    unit, inverse = norm_parts(c_ref[...])
    back, gain_sum, bias_sum = norm_back(dkn, unit, inverse, vec_ref[14:15, :])
    dc = back.astype(bf16)
    dc_ref[...] = dc
    knt = turned(kn_ref[...])
    keyval[...] = rotate(turned_ref[1], contract(knt, high, 1, 0) + contract(knt, rest, 1, 0), pair_ref[...])
    reduce[...] = rotate_turned(contract(turned(dc), blocks_ref[...], 1, 0), wide_ref[2], narrow_ref[7])
    share_out(keep_ref, send_ref, layout(256, LATE)[0], (reduce, keyval, query, out))
    sums_ref[0:1, :] = col_sum(dc.astype(f32))
    sums_ref[1:2, :] = gain_sum
    sums_ref[2:3, :] = bias_sum
    sums_ref[3:4, :] = col_sum(dkv[:, 256:512])


def cells_back_kernel(
    tile_rows, cols, size_ref, dq_left, dq_right, dc_ref, query_ref, reduce_ref, x0_ref, dx1_ref, vec_ref, tile_ref, up_ref, down_ref,
    feed_sums, key_sums, left_sum, right_sum, dx0_ref, head_ref, tail_ref, sums_ref, frame,
):
    tokens = x0_ref.shape[0]
    dh1 = contract(dq_left[...], query_ref[:, 0:128], 1, 1) + contract(dq_right[...], query_ref[:, 128:256], 1, 1)
    for corner in range(4):
        pick = picked_cells((tokens, dc_ref.shape[0]), 0, size_ref, corner, tile_rows, cols)
        placed = contract(pick, dc_ref[...], 1, 0).astype(bf16)
        dh1 = dh1 + contract(placed, reduce_ref[corner * 256 : corner * 256 + 256, :], 1, 1)
    unit, inverse = norm_parts(x0_ref[...])
    back, gain_sum, bias_sum = norm_back(dh1, unit, inverse, vec_ref[10:11, :])
    dx0 = dx1_ref[...] + back
    dx0_ref[...] = dx0
    head_ref[...] = dx0[0:64].astype(bf16)
    tail_ref[...] = dx0[tokens - 64 :].astype(bf16)
    sums_ref[0:25, :] = feed_sums[...]
    sums_ref[25:32, :] = jnp.zeros((7, 256), f32)
    moved = shifted_frame(frame, tile_ref, up_ref, down_ref)
    grid = dx0.reshape(tile_rows, cols, 256)
    for tap in range(9):
        product = moved[tap % 3][tap // 3 : tap // 3 + tile_rows] * grid
        sums_ref[tap : tap + 1, :] = col_sum(product.reshape(tokens, 256))
    sums_ref[9:10, :] = col_sum(dx0)
    sums_ref[10:11, :] = gain_sum
    sums_ref[11:12, :] = bias_sum
    sums_ref[12:13, 0:128] = left_sum[...]
    sums_ref[12:13, 128:256] = right_sum[...]
    sums_ref[13:17, :] = key_sums[...]


def input_grad_kernel(tile_rows, dx0_ref, up_ref, down_ref, vec_ref, out_ref, token, frame):
    token[...] = jnp.zeros_like(token)
    moved = shifted_frame(frame, dx0_ref, up_ref, down_ref)
    total = moved[1][1:-1]
    for tap in range(9):
        down, right = 2 - tap // 3, 2 - tap % 3
        total = total + vec_ref[tap : tap + 1, :] * moved[right][down : down + tile_rows]
    out_ref[...] = total.reshape(out_ref.shape)


def moments_of(total, first, second, moment_ref, square_ref):
    moment = BETA * first + (1.0 - BETA) * total
    square = BETA * second + (1.0 - BETA) * total * total
    moment_ref[...] = moment
    square_ref[...] = square
    return moment * (1.0 / CORRECTION) / (jnp.sqrt(square * (1.0 / CORRECTION)) + ADAM_EPS)


def adam_kernel(terms, *refs):
    (own_vec, own_early, first_ref, second_ref, vec_ref, vec_first, vec_second, vec_ema,
     moment_ref, square_ref, step_ref, vec_out, vec_first_out, vec_second_out, vec_ema_out) = refs[terms:]
    rows = refs[0].shape[0]
    late, early = refs[0][...], own_early[...]
    for ref in refs[1:terms]:
        late = late + ref[0:rows, :].astype(f32)
        early = early + ref[rows + 64 :, :].astype(f32)
    for total, at in ((late, slice(0, rows)), (early, slice(rows, rows + early.shape[0]))):
        step = moments_of(total, first_ref[at, :], second_ref[at, :], moment_ref.at[at, :], square_ref.at[at, :])
        step_ref[at, :] = step.astype(bf16)
    vec = pair_total([own_vec[...]] + [vector_part(ref, rows) for ref in refs[1:terms]])
    vec = vec[0 : vec_ref.shape[0]]
    new = vec_ref[...] - VECTOR_RATE * moments_of(vec, vec_first[...], vec_second[...], vec_first_out, vec_second_out)
    vec_out[...] = new
    vec_ema_out[...] = EMA_KEEP * vec_ema[...] + (1.0 - EMA_KEEP) * new


def step_sides(width, chunks, own_narrow, own_wide):
    lefts = {0: (own_narrow, 0), 1: (own_narrow, 1), 2: (own_narrow, 2), 3: (own_narrow, 3), 4: (own_wide, 0), 5: (own_wide, 1)}
    found = []
    values = chunks[...].astype(f32)
    for j, first, rows, blocks in both_groups(width):
        left_ref, index = lefts[j]
        half = left_ref.shape[2] // 2
        left = left_ref[index][:, 0:half].astype(bf16)
        sides = []
        for col in range(blocks):
            part = values[:, first + col * rows : first + (col + 1) * rows, :]
            sides.append(contract(left, part.reshape(half, width).astype(bf16), 1, 0))
        found.append(sides)
    return found


def both_groups(width):
    late, count = layout(width, LATE)
    return late + [(j, first + count, rows, blocks) for j, first, rows, blocks in layout(width, EARLY)[0]]


def near_kernel(width, chunks, own_narrow, own_wide, keep_ref, send_ref):
    for (j, first, rows, blocks), sides in zip(both_groups(width), step_sides(width, chunks, own_narrow, own_wide)):
        pad = sides[0].shape[0] // 2
        for col, side in enumerate(sides):
            at = slice(first + col * rows, first + (col + 1) * rows)
            keep_ref[at, :] = side[0:rows]
            send_ref[at, :] = side[pad : pad + rows]


def finish_kernel(
    width, keep_ref, got_ref, narrow_ref, pair_ref, wide_ref, weights_ref, ema_ref, weights_out, ema_out, chunk
):
    rights = {0: narrow_ref.at[1], 1: pair_ref, 2: narrow_ref.at[4], 3: wide_ref.at[0], 4: narrow_ref.at[6], 5: narrow_ref.at[7]}
    sides = keep_ref[...] + got_ref[...]
    for j, first, rows, blocks in both_groups(width):
        parts = [sides[first + col * rows : first + (col + 1) * rows] for col in range(blocks)]
        side = parts[0] if blocks == 1 else jnp.concatenate(parts, axis=1)
        if rows < 8:
            side = jnp.concatenate([side, jnp.zeros((8 - rows, side.shape[1]), f32)], axis=0)
        full = contract(side.astype(bf16), rights[j][...], 1, 1)
        for col in range(blocks):
            at = slice(first + col * rows, first + (col + 1) * rows)
            old = weights_ref[at, :]
            piece = full[0:rows, col * width : (col + 1) * width]
            chunk[at, :] = old - MATRIX_RATES[j] * (piece + WEIGHT_DECAY * old)
    from_chunk(chunk, weights_out, width)
    chunk[...] = EMA_KEEP * ema_ref[...] + (1.0 - EMA_KEEP) * chunk[...]
    from_chunk(chunk, ema_out, width)


def packed_moments_kernel(width, moment_ref, square_ref, first_out, second_out):
    from_chunk(moment_ref, first_out, width)
    from_chunk(square_ref, second_out, width)


def on_device(
    patches,
    cotangent,
    image_sizes,
    weights,
    first_moment,
    second_moment,
    weight_ema,
    vectors,
    vec_first,
    vec_second,
    vec_ema,
    basis_narrow,
    basis_pair,
    basis_wide,
):
    _, rows, cols, width = patches.shape
    tokens = rows * cols
    shards = device_count()
    tile = patches.reshape(tokens, width)
    dy = cotangent.reshape(tokens, width)
    per = weights.shape[1]
    late_rows, early_rows = layout(width, LATE)[1], layout(width, EARLY)[1]
    chunk = late_rows + early_rows
    ranks = lax.axis_size("row")
    own_keys = tokens // 4
    keys = own_keys * ranks
    frame = ((rows + 2, cols + 16, width), f32)
    img_part = ("img", 1, lax.axis_size("img"))
    xy_parts = row_parts()

    def border(head, tail):
        up = lax.ppermute(tail, "row", [(i, i + 1) for i in range(ranks - 1)])
        return up, lax.ppermute(head, "row", [(i + 1, i) for i in range(ranks - 1)])

    gather_groups = xy_parts[::-1]
    lines = lax.axis_size("img")

    (packed,) = run(
        "pack",
        functools.partial(pack_kernel, width),
        [((chunk, width), bf16)],
        [weights],
        scratch=[((chunk, width), f32)],
    )
    line = join([packed[None]] + [swap(packed, "img", j)[None] for j in range(1, lines)])
    up_halo, down_halo = border(tile[:64], tile[tokens - 64 :])
    x0, h1, mask, vec, sizes = run(
        "front",
        functools.partial(front_kernel, rows, cols),
        [((tokens, width), f32), ((tokens, width), bf16), ((1, keys), f32), (vectors.shape, f32), ((8, 128), jnp.int32)],
        [image_sizes, tile, up_halo, down_halo, vectors],
        scratch=[frame],
        scalars=(0,),
        micros=1.3,
        after=[line],
    )
    wide, wide_done = run(
        "wide_bases",
        wide_bases_kernel,
        [((3, FF, FF), bf16), ((8, 128), f32)],
        [basis_wide],
        scratch=[((12, width, FF), f32)],
        micros=6.0,
        mib=48,
        raw=(0,),
        sems=12,
        after=[line],
    )
    all_near = line
    for axis, stride, size in gather_groups:
        pieces = [all_near] + [swap(all_near, axis, j * stride) for j in range(1, size)]
        all_near = join(pieces, after=[wide_done, vec])
    all_far = swap(all_near, "row", 1)
    w_reduce, w_keyval, w_query, w_out, blocks, c, kn, own_kv = run(
        "keys",
        functools.partial(keys_kernel, rows, cols),
        [
            ((4 * width, width), bf16),
            ((width, 2 * width), bf16),
            ((width, width), bf16),
            ((width, width), bf16),
            ((own_keys, 4 * width), bf16),
            ((own_keys, width), f32),
            ((own_keys, width), bf16),
            ((own_keys, 2 * width), bf16),
        ],
        [sizes, h1, vec, all_near, all_far],
        scratch=[((4 * width, width), f32), ((width, 2 * width), f32), ((width, width), f32), ((width, width), f32)],
        micros=1.5,
    )
    narrow, narrow_turned, pair, own_narrow = run(
        "narrow_bases",
        narrow_bases_kernel,
        [((8, width, width), bf16), ((4, width, width), bf16), ((2 * width, 2 * width), bf16), ((4, 32, width), f32)],
        [basis_narrow, basis_pair],
        scratch=[((2 * width, 128), f32)],
        micros=1.5,
        after=[own_kv],
    )
    kv_near = side_by_side(own_kv, gather_groups)
    kv_far = swap(kv_near, "row", 1)

    unroll = keys <= 1024
    step = tokens if unroll else 32
    q, k, v, o, log = run(
        "attend",
        functools.partial(attend_kernel, step, unroll),
        [((tokens, width), bf16), ((keys, width), bf16), ((keys, width), bf16), ((tokens, width), f32), ((tokens, 128), f32)],
        [h1, w_query, vec, kv_near, kv_far, mask],
        mib=8 if unroll else 44,
        micros=8.0,
        after=[own_narrow],
    )
    y, do, dx1, up_grad, down_grad, out_grad, feed_sums = run(
        "feed",
        feed_kernel,
        [
            ((tokens, width), bf16),
            ((tokens, width), bf16),
            ((tokens, width), f32),
            ((width, FF), f32),
            ((width, FF), f32),
            ((width, width), f32),
            (vectors.shape, f32),
        ],
        [o, x0, w_out, all_near, all_far, vec, dy],
        scratch=[((width, FF), bf16), ((FF, width), bf16), ((width, FF), f32), ((FF, width), f32)],
        mib=12,
        micros=3.5,
    )
    half = (shards // 2, early_rows, width)
    early_keep, early_send = run(
        "early_turn",
        early_turn_kernel,
        [(half, f32), (half, f32)],
        [up_grad, down_grad, narrow_turned, narrow, wide],
        scratch=[((width, FF), f32), ((FF, width), f32)],
        mib=10,
        micros=2.0,
    )

    def back(group, after):
        return run(
            "attend_back",
            functools.partial(attend_back_kernel, step, unroll, group),
            [
                ((tokens, 128), bf16),
                ((keys // 2, width), f32),
                ((keys // 2, width), f32),
                ((width, 128), f32),
                ((1, 128), f32),
            ],
            [q, k, v, mask, o, log, do, h1],
            scratch=[
                ((tokens, 128), f32),
                ((width, keys), f32),
                ((tokens, keys), bf16),
                ((tokens, keys), bf16),
                ((128, tokens), bf16),
                ((128, tokens), bf16),
            ],
            mib=14 if unroll else 60,
            micros=5.0,
            after=after,
        )

    pairs = one_by_one(xy_parts + [img_part])
    place = 0

    def early_pair(after=()):
        nonlocal early_terms, place
        keep, send = split_sum(early_terms, 2, after=after)
        early_terms = [keep, swap(send, *pairs[place][:2])]
        place += 1
        return keep

    early_terms = [early_keep, swap(early_send, "row", 1)]
    dq_left, left_keep, left_send, query_left, left_sum = back(0, [early_keep])
    token = early_pair([query_left])
    left_got = swap(left_send, "row", 1)
    dq_right, right_keep, right_send, query_right, right_sum = back(1, [token])
    right_got = swap(right_send, "row", 1)
    axis, stride, size = xy_parts[0]
    dkv_keep, *dkv_sends = run(
        "split_heads",
        functools.partial(split_heads_kernel, size),
        [((keys // 2 // size, 2 * width), f32)] + [((keys // 2 // size, 2 * width), bf16)] * (size - 1),
        [left_keep, left_got, right_keep, right_got],
        micros=0.8,
    )
    token = early_pair([dkv_keep])
    old_chunk, ema_chunk, first_chunk, second_chunk = run(
        "moments",
        functools.partial(moments_kernel, width),
        [((chunk, width), f32)] * 4,
        [jnp.concatenate([weights, weight_ema, first_moment, second_moment], axis=0)],
        after=[dkv_keep],
    )
    dkv_terms = [dkv_keep] + [swap(x, axis, j * stride) for j, x in enumerate(dkv_sends, 1)]
    for axis, stride, size in xy_parts[1:]:
        keep, *sends = split_sum(dkv_terms, size)
        dkv_terms = [keep] + [swap(x, axis, j * stride) for j, x in enumerate(sends, 1)]
    query_turn, out_turn = run(
        "middle_turn",
        middle_turn_kernel,
        [((width, width), f32), ((width, width), f32)],
        [query_left, query_right, out_grad, narrow_turned, narrow],
        micros=0.7,
        after=[dkv_keep],
    )
    half = (shards // 2, late_rows, width)
    late_keep, late_send, dc, key_sums = run(
        "keys_back",
        functools.partial(keys_back_kernel, len(dkv_terms)),
        [(half, f32), (half, f32), ((own_keys, width), bf16), ((4, width), f32)],
        list(dkv_terms) + [kn, c, vec, w_keyval, blocks, narrow_turned, narrow, pair, wide, query_turn, out_turn],
        scratch=[((4 * width, width), f32), ((width, 2 * width), f32)],
        micros=2.0,
        after=[token, old_chunk],
    )
    late_got = swap(late_send, "row", 1)
    dx0, head, tail, vec_grads = run(
        "cells_back",
        functools.partial(cells_back_kernel, rows, cols),
        [((tokens, width), f32), ((64, width), bf16), ((64, width), bf16), ((32, width), f32)],
        [
            sizes, dq_left, dq_right, dc, w_query, w_reduce, x0, dx1, vec, tile, up_halo, down_halo,
            feed_sums, key_sums, left_sum, right_sum,
        ],
        scratch=[frame],
        micros=2.0,
    )
    vec_terms = [vec_grads, swap(vec_grads, "row", 1)]
    grad_up, grad_down = border(head, tail)
    while place < len(pairs) - (lines.bit_length() - 1):
        early_pair([dc])
    late_terms = [late_keep.reshape(-1, width), late_got.reshape(-1, width)]
    early_keep, early_got = [t.reshape(-1, width) for t in early_terms]
    parts = xy_parts + [img_part]
    for index, (axis, stride, size) in enumerate(parts):
        riders = [early_keep, early_got] if index == len(parts) - 1 else []
        keeps, sends = split_with_vectors(late_terms, vec_terms, riders, size, index == 0, [dx0])
        late_terms = [keeps[0]] + [swap(x, axis, j * stride) for j, x in enumerate(sends, 1)]
        vec_terms = [keeps[1]]
    moments, squares, step, new_vectors, vec_moment, vec_square, new_vec_ema = run(
        "adam",
        functools.partial(adam_kernel, len(late_terms)),
        [((chunk, width), f32), ((chunk, width), f32), ((chunk, width), bf16)] + [(vectors.shape, f32)] * 4,
        late_terms + vec_terms + [keeps[2], first_chunk, second_chunk, vec, vec_first, vec_second, vec_ema],
        micros=0.8,
    )
    step_near = join([step[None]] + [swap(step, "img", j)[None] for j in range(1, lines)])
    (own_wide,) = run(
        "own_wide",
        own_wide_kernel,
        [((2, 2 * max(16, FF // shards), FF), f32)],
        [wide],
        scratch=[((2 * FF, 128), f32)],
        micros=1.5,
        after=[step_near],
    )
    grad_input, input_done = run(
        "input_grad",
        functools.partial(input_grad_kernel, rows),
        [((tokens, width), f32), ((8, 128), f32)],
        [dx0, grad_up, grad_down, vec],
        scratch=[frame],
        micros=1.5,
        after=[own_wide],
    )
    for axis, stride, size in gather_groups:
        pieces = [step_near] + [swap(step_near, axis, j * stride) for j in range(1, size)]
        step_near = join(pieces, [input_done])
    side_keep, side_send = run(
        "near",
        functools.partial(near_kernel, width),
        [((chunk, width), f32), ((chunk, width), f32)],
        [step_near, own_narrow, own_wide],
        micros=2.0,
    )
    side_got = swap(side_send, "row", 1)
    new_first, new_second = run(
        "packed_moments",
        functools.partial(packed_moments_kernel, width),
        [((1, per), f32), ((1, per), f32)],
        [moments, squares],
        after=[side_keep],
    )
    new_weights, new_ema = run(
        "finish",
        functools.partial(finish_kernel, width),
        [((1, per), f32)] * 2,
        [side_keep, side_got, narrow, pair, wide, old_chunk, ema_chunk],
        scratch=[((chunk, width), f32)],
        micros=1.5,
    )
    return (
        y.reshape(patches.shape),
        grad_input.reshape(patches.shape),
        new_weights,
        new_first,
        new_second,
        new_ema,
        new_vectors,
        vec_moment,
        vec_square,
        new_vec_ema,
    )


def solution(mesh):
    tiles = P("img", "row", None, None)
    packed = P(("img", "row"), None)
    return jax.shard_map(
        on_device,
        mesh=mesh,
        in_specs=(tiles, tiles, P("img", None)) + (packed,) * 4 + (P(),) * 7,
        out_specs=(tiles, tiles) + (packed,) * 4 + (P(),) * 4,
        check_vma=False,
    )
```

```python
import functools
import math

import jax
import jax.numpy as jnp
from jax import lax
from jax.experimental import pallas as pl
from jax.experimental.pallas import tpu as pltpu
from jax.sharding import PartitionSpec as P

HEADS = 8
FF = 1024
STEP = 5

NORM_EPS = 1e-05
ADAM_EPS = 1e-08
BETA = 0.5
WEIGHT_DECAY = 0.05
EMA_KEEP = 0.75
VECTOR_RATE = 0.06
MATRIX_RATES = (0.04, 0.02, 0.25, 0.02, 0.01, 0.01)
CORRECTION = 1.0 - BETA**STEP
LOG2E = math.log2(math.e)
f32 = jnp.float32
bf16 = jnp.bfloat16
LATE = (5, 1, 0, 2)
EARLY = (3, 4)


def matrix_shapes(width, hidden):
    return (
        (width, width),
        (width, 2 * width),
        (width, width),
        (width, hidden),
        (hidden, width),
        (4 * width, width),
    )


def contract(a, b, ca, cb, **kw):
    return lax.dot_general(
        a, b, (((ca,), (cb,)), ((), ())), preferred_element_type=f32, **kw
    )


def swap(x, axis, step):
    count = lax.axis_size(axis)
    return lax.ppermute(x, axis, [(i, i ^ step) for i in range(count)])


def row_groups():
    left = lax.axis_size("row") // 2
    groups, stride = [(1, 2)], 2
    while left > 1:
        size = 4 if left % 4 == 0 else 2
        groups.append((stride, size))
        left //= size
        stride *= size
    return groups


def rel_digits():
    groups = row_groups()
    return [groups[0]] + groups[1:][::-1]


def source(block):
    sizes = lax.axis_size("img")
    img, rest = block % sizes, block // sizes
    rel = 0
    for stride, size in reversed(rel_digits()):
        rel = rel + (rest % size) * stride
        rest = rest // size
    row = lax.axis_index("row") ^ rel
    return (lax.axis_index("img") ^ img) * lax.axis_size("row") + row


def device_count():
    return lax.axis_size("img") * lax.axis_size("row")


def run(name, body, outs, args, scratch=(), mib=6, scalars=(), micros=1.0, after=(), raw=(), sems=0):
    count = len(args)

    def without(*refs):
        body(*refs[:count], *refs[count + len(after) :])

    space = {index: pltpu.SMEM for index in scalars} | {index: pltpu.HBM for index in raw}
    specs = [pl.BlockSpec(memory_space=space.get(index, pltpu.VMEM)) for index in range(count)]
    return pl.pallas_call(
        without,
        out_shape=tuple(jax.ShapeDtypeStruct(shape, dtype) for shape, dtype in outs),
        in_specs=specs + [pl.BlockSpec(memory_space=pl.ANY)] * len(after),
        out_specs=tuple(pl.BlockSpec(memory_space=pltpu.VMEM) for _ in outs),
        scratch_shapes=[pltpu.VMEM(shape, dtype) for shape, dtype in scratch]
        + ([pltpu.SemaphoreType.DMA((sems,))] if sems else []),
        compiler_params=pltpu.CompilerParams(vmem_limit_bytes=mib * 2**20),
        cost_estimate=pl.CostEstimate(flops=0, bytes_accessed=int(micros * 3.6e6), transcendentals=0),
        name=name,
    )(*args, *after)


def each_block(count, body):
    if count <= 32:
        for index in range(count):
            body(index)
    else:

        def step(index, carry):
            body(index)
            return carry

        lax.fori_loop(0, count, step, 0)


def put_rows(ref, start, cols, value):
    count = value.shape[0]
    if count % 8 == 0:
        ref[pl.ds(pl.multiple_of(start, 8), count), cols] = value
    else:
        for row in range(count):
            ref[pl.ds(start + row, 1), cols] = value[row : row + 1]


def get_rows(ref, start, count, cols):
    if count % 8 == 0:
        return ref[pl.ds(pl.multiple_of(start, 8), count), cols]
    return jnp.concatenate([ref[pl.ds(start + row, 1), cols] for row in range(count)], axis=0)


def layout(width, group):
    dims = matrix_shapes(width, FF)
    found, start = [], 0
    for j in group:
        rows = dims[j][0] // device_count()
        blocks = dims[j][1] // width
        found.append((j, start, rows, blocks))
        start += rows * blocks
    return found, start


def packed_starts(width):
    dims = matrix_shapes(width, FF)
    starts, start = [], 0
    for m, n in dims:
        starts.append(start)
        start += m * n // device_count()
    return starts


def spread(block, parts, mats, start_of):
    for (j, first, rows, blocks), ref in zip(parts, mats):
        for col in range(blocks):
            piece = block[first + col * rows : first + (col + 1) * rows]
            put_rows(ref, start_of * rows, slice(col * 256, col * 256 + 256), piece)


def collect(out_ref, index, parts, mats, start_of):
    for (j, first, rows, blocks), ref in zip(parts, mats):
        for col in range(blocks):
            piece = get_rows(ref, start_of * rows, rows, slice(col * 256, col * 256 + 256))
            out_ref[index, first + col * rows : first + (col + 1) * rows, :] = piece


def norm_parts(values):
    centred = values - jnp.mean(values, axis=-1, keepdims=True)
    inverse = lax.rsqrt(jnp.mean(centred * centred, axis=-1, keepdims=True) + NORM_EPS)
    return centred * inverse, inverse


def norm_back(grad, unit, inverse, gain):
    grad_unit = grad * gain
    back = grad_unit - jnp.mean(grad_unit, axis=-1, keepdims=True)
    back = back - unit * jnp.mean(grad_unit * unit, axis=-1, keepdims=True)
    gain_sum = jnp.sum(grad * unit, axis=0, keepdims=True)
    return back * inverse, gain_sum, jnp.sum(grad, axis=0, keepdims=True)


def turned(value):
    return value.astype(f32).T.astype(bf16)


def col_sum(value):
    return jnp.sum(value, axis=0, keepdims=True)


def pack_kernel(width, w_ref, out_ref, chunk):
    to_chunk(w_ref, chunk, width)
    out_ref[...] = chunk[...].astype(bf16)


def to_chunk(flat_ref, out_ref, width, index=0):
    dims, starts, base = matrix_shapes(width, FF), packed_starts(width), 0
    for group in (LATE, EARLY):
        parts, count = layout(width, group)
        for j, first, rows, blocks in parts:
            for col in range(blocks):
                for row in range(rows):
                    at = starts[j] + row * dims[j][1] + col * width
                    place = base + first + col * rows + row
                    out_ref[place : place + 1, :] = flat_ref[index : index + 1, at : at + width]
        base += count


def from_chunk(values, out_ref, width):
    dims, starts = matrix_shapes(width, FF), packed_starts(width)
    for j, first, rows, blocks in both_groups(width):
        for col in range(blocks):
            for row in range(rows):
                at = starts[j] + row * dims[j][1] + col * width
                place = first + col * rows + row
                out_ref[0:1, at : at + width] = values[place : place + 1, :]


def moments_kernel(width, rows_ref, *outs):
    for index, ref in enumerate(outs):
        to_chunk(rows_ref, ref, width, index)


def left_block(matrix_ref, out_ref):
    lines, ranks = lax.axis_size("img"), lax.axis_size("row")
    size = matrix_ref.shape[0]
    rows = size // (lines * ranks)
    img, row = lax.axis_index("img"), lax.axis_index("row")

    def one_hot(count, axis, start_of):
        shape = (count * rows, size) if axis == 0 else (size, count * rows)
        place = lax.broadcasted_iota(jnp.int32, tuple(n if d == axis else 1 for d, n in enumerate(shape)), axis)
        block = place >> (rows.bit_length() - 1)
        target = start_of(block) * rows + (place & (rows - 1))
        return (lax.broadcasted_iota(jnp.int32, shape, 1 - axis) == target).astype(f32).astype(bf16)

    def owner(block):
        rel = jnp.zeros_like(block)
        for stride, count in reversed(rel_digits()):
            rel = rel + (block & (count - 1)) * stride
            block = block >> (count.bit_length() - 1)
        return img * ranks + (rel ^ row)

    mine = contract(one_hot(ranks, 0, owner), matrix_ref[...], 1, 0).astype(bf16)
    out_ref[...] = contract(mine, one_hot(lines, 1, lambda block: (block ^ img) * ranks + row), 1, 0)


def narrow_bases_kernel(narrow_ref, pair_ref, narrow_out, turned_out, pair_out, own_ref):
    narrow_out[...] = narrow_ref[...].astype(bf16)
    pair_out[...] = pair_ref[...].astype(bf16)
    for index, j in enumerate((0, 2, 3, 5)):
        turned_out[index] = narrow_ref[j].T.astype(bf16)
        left_block(narrow_out.at[j], own_ref.at[index])


def own_wide_kernel(wide_ref, own_ref):
    for index in range(2):
        left_block(wide_ref.at[index + 1], own_ref.at[index])


def wide_bases_kernel(wide_ref, wide_out, token, buffer, sems):
    count, size = wide_ref.shape[0], wide_ref.shape[1]
    rows, depth = buffer.shape[1], buffer.shape[0]
    each = size // rows
    total = count * each

    def copy(index):
        at = wide_ref.at[index // each, pl.ds(index % each * rows, rows)]
        return pltpu.make_async_copy(at, buffer.at[index % depth], sems.at[index % depth])

    for index in range(depth):
        copy(index).start()
    for index in range(total):
        copy(index).wait()
        first = index % each * rows
        wide_out[index // each, first : first + rows, :] = buffer[index % depth].astype(bf16)
        if index + depth < total:
            copy(index + depth).start()
    token[...] = jnp.zeros_like(token)


def join_kernel(*refs):
    start = 0
    for ref in refs[:-1]:
        refs[-1][start : start + ref.shape[0]] = ref[...]
        start += ref.shape[0]


def join(pieces, after=()):
    shape = (sum(x.shape[0] for x in pieces),) + pieces[0].shape[1:]
    return run("join", join_kernel, [(shape, pieces[0].dtype)], list(pieces), micros=0.4, after=after)[0]


def unpack(pieces, group, mats, base=0):
    parts = [(j, first + base, rows, blocks) for j, first, rows, blocks in layout(256, group)[0]]
    done = 0
    for piece in pieces:

        def body(block, piece=piece, done=done):
            spread(piece[block].astype(f32), parts, mats, source(block + done))

        each_block(piece.shape[0], body)
        done += piece.shape[0]


def shifted_frame(frame_ref, tile_ref, up_ref, down_ref):
    rows, cols, width = frame_ref.shape[0] - 2, 56, 256
    frame_ref[...] = jnp.zeros_like(frame_ref)
    frame_ref[0, 8 : 8 + cols, :] = up_ref[...].astype(f32)[-cols:]
    frame_ref[1 : 1 + rows, 8 : 8 + cols, :] = tile_ref[...].astype(f32).reshape(rows, cols, width)
    frame_ref[rows + 1, 8 : 8 + cols, :] = down_ref[...].astype(f32)[:cols]
    return [frame_ref[:, 7 + shift : 7 + shift + cols, :] for shift in range(3)]


def front_kernel(tile_rows, cols, size_ref, tile_ref, up_ref, down_ref, vec_ref, x0_ref, h1_ref, mask_ref, vec_out, size_out, frame):
    rows = frame.shape[0] - 2
    vec_out[...] = vec_ref[...]
    size_out[...] = jnp.where(lax.broadcasted_iota(jnp.int32, size_out.shape, 0) == 0, size_ref[0, 0], size_ref[0, 1])
    moved = shifted_frame(frame, tile_ref, up_ref, down_ref)
    total = moved[1][1:-1] + vec_ref[9:10, :]
    for tap in range(9):
        total = total + vec_ref[tap : tap + 1, :] * moved[tap % 3][tap // 3 : tap // 3 + rows]
    x0 = total.reshape(x0_ref.shape)
    x0_ref[...] = x0
    unit, _ = norm_parts(x0)
    h1_ref[...] = (unit * vec_ref[10:11, :] + vec_ref[11:12, :]).astype(bf16)
    half = cols // 2
    own = tile_rows // 2 * half
    key = lax.broadcasted_iota(jnp.int32, mask_ref.shape, 1)
    block = jnp.zeros_like(key)
    for start in range(own, mask_ref.shape[1], own):
        block = block + (key >= start).astype(jnp.int32)
    key = key - block * own
    row = jnp.zeros_like(key)
    for start in range(half, own, half):
        row = row + (key >= start).astype(jnp.int32)
    col = key - row * half
    rel = jnp.zeros_like(key)
    for stride, size in reversed(rel_digits()):
        rel = rel + (block & (size - 1)) * stride
        block = block >> (size.bit_length() - 1)
    row = row + (rel ^ lax.axis_index("row")) * (tile_rows // 2)
    inside = (2 * row < size_ref[0, 0]) & (2 * col < size_ref[0, 1])
    mask_ref[...] = jnp.where(inside, 0.0, -1e30)


def picked_cells(shape, cell_axis, size_ref, corner, tile_rows, cols):
    half = cols // 2
    key_shape = tuple(1 if axis == cell_axis else n for axis, n in enumerate(shape))
    key = lax.broadcasted_iota(jnp.int32, key_shape, 1 - cell_axis)
    row = jnp.zeros_like(key)
    for step in range(1, tile_rows // 2):
        row = row + (key >= step * half).astype(jnp.int32)
    col = 2 * (key - row * half) + corner % 2
    row = 2 * row + corner // 2
    inside = (row + lax.axis_index("row") * tile_rows < size_ref[0:1, 0:1]) & (col < size_ref[1:2, 0:1])
    target = jnp.where(inside, row * cols + col, -1)
    cell = lax.broadcasted_iota(jnp.int32, shape, cell_axis)
    return (cell == target).astype(f32).astype(bf16)


def keys_kernel(
    tile_rows, cols, size_ref, h1_ref, vec_ref, near_ref, far_ref,
    reduce_ref, keyval_ref, query_ref, out_ref, blocks_ref, c_ref, kn_ref, kv_ref,
    reduce_wide, keyval_wide, query_wide, out_wide,
):
    unpack((near_ref, far_ref), LATE, (reduce_wide, keyval_wide, query_wide, out_wide))
    reduce_ref[...] = reduce_wide[...].astype(bf16)
    keyval_ref[...] = keyval_wide[...].astype(bf16)
    query_ref[...] = query_wide[...].astype(bf16)
    out_ref[...] = out_wide[...].astype(bf16)
    keys = c_ref.shape[0]
    for corner in range(4):
        pick = picked_cells((keys, h1_ref.shape[0]), 1, size_ref, corner, tile_rows, cols)
        blocks_ref[:, corner * 256 : corner * 256 + 256] = contract(pick, h1_ref[...], 1, 0).astype(bf16)
    c = contract(blocks_ref[...], reduce_ref[...], 1, 0) + vec_ref[13:14, :]
    c_ref[...] = c
    unit, _ = norm_parts(c)
    kn = (unit * vec_ref[14:15, :] + vec_ref[15:16, :]).astype(bf16)
    kn_ref[...] = kn
    kv = contract(kn, keyval_ref[...], 1, 0)
    kv_ref[:, 0:256] = kv[:, 0:256].astype(bf16)
    kv_ref[:, 256:512] = (kv[:, 256:512] + vec_ref[16:17, :]).astype(bf16)


def over_heads(body, first, last, unroll):
    if unroll:
        for head in range(first, last):
            body(head)
    else:

        def step(head, carry):
            body(head)
            return carry

        lax.fori_loop(first, last, step, 0)


def over_blocks(block, tokens, step):
    if tokens == step:
        block(0)
    else:

        def go(index, carry):
            block(pl.multiple_of(index * step, step))
            return carry

        lax.fori_loop(0, tokens // step, go, 0)


def head_columns(head):
    group = head // 4
    if isinstance(head, int):
        return slice(group * 128, group * 128 + 128)
    return pl.ds(pl.multiple_of(group * 128, 128), 128)


def head_rows(head, base=0):
    if isinstance(head, int):
        return slice(base + head * 32, base + head * 32 + 32)
    return pl.ds(pl.multiple_of(base + head * 32, 32), 32)


def attend_kernel(
    step, unroll, h1_ref, query_ref, vec_ref, near_ref, far_ref, mask_ref, q_ref, k_ref, v_ref, o_ref, log_ref
):
    tokens = h1_ref.shape[0]
    half = near_ref.shape[0]
    for start, ref in ((0, near_ref), (half, far_ref)):
        k_ref[start : start + half, :] = ref[:, 0:256]
        v_ref[start : start + half, :] = ref[:, 256:512]
    q_ref[...] = (contract(h1_ref[...], query_ref[...], 1, 0) + vec_ref[12:13, :]).astype(bf16)
    scale = 32**-0.5 * LOG2E
    lane = lax.broadcasted_iota(jnp.int32, (1, 128), 1)
    mask = mask_ref[...]

    def one_head(head):
        cols = head_columns(head)
        mine = lane // 32 == head % 4
        keys = jnp.where(mine, k_ref[:, cols], 0)
        ones = jnp.where(lane // 32 == (head + 2) % 4, 1.0, 0.0).astype(bf16)
        values = jnp.where(mine, v_ref[:, cols], ones)

        def block(start):
            rows = pl.ds(start, step)
            scores = contract(q_ref[rows, cols], keys, 1, 1) * scale + mask
            top = jnp.max(scores, axis=1, keepdims=True)
            out = contract(jnp.exp2(scores - top).astype(bf16), values, 1, 0)
            if isinstance(head, int):
                total = out[:, (head + 2) % 4 * 32 : (head + 2) % 4 * 32 + 1]
            else:
                total = jnp.sum(jnp.where(lane == (head + 2) % 4 * 32, out, 0.0), axis=1, keepdims=True)
            o_ref[rows, cols] = jnp.where(mine, out * (1.0 / total), o_ref[rows, cols])
            log_ref[rows, :] = jnp.where(lane == head, top + jnp.log2(total), log_ref[rows, :])

        over_blocks(block, tokens, step)

    over_heads(one_head, 0, HEADS, unroll)


def feed_kernel(
    o_ref, x0_ref, out_ref, near_ref, far_ref, vec_ref, dy_ref,
    y_ref, do_ref, dx1_ref, up_grad, down_grad, out_grad, sums_ref, up_ref, down_ref, up_wide, down_wide,
):
    unpack((near_ref, far_ref), EARLY, (up_wide, down_wide), layout(256, LATE)[1])
    up_ref[...] = up_wide[...].astype(bf16)
    down_ref[...] = down_wide[...].astype(bf16)
    o = o_ref[...].astype(bf16)
    x1 = x0_ref[...] + (contract(o, out_ref[...], 1, 0) + vec_ref[17:18, :])
    unit, inverse = norm_parts(x1)
    h2 = (unit * vec_ref[18:19, :] + vec_ref[19:20, :]).astype(bf16)
    dy_low = dy_ref[...]
    dy = dy_low.astype(f32)
    dyt = turned(dy_low)
    h2t = turned(h2)
    y = x1 + vec_ref[20:21, :]
    dh2 = jnp.zeros_like(y)
    for col in range(FF // 256):
        cols = slice(col * 256, col * 256 + 256)
        u = contract(h2, up_ref[:, cols], 1, 0) + vec_ref[21 + col : 22 + col, :]
        phi_sum = 0.5 * (1.0 + lax.erf(u * (2.0**-0.5)))
        density = jnp.exp(-0.5 * u * u) * ((2.0 * math.pi) ** -0.5)
        g = (u * phi_sum).astype(bf16)
        y = y + contract(g, down_ref[cols, :], 1, 0)
        down_grad[:, cols] = contract(dyt, g, 1, 0)
        du = (contract(dy_low, down_ref[cols, :], 1, 1) * (phi_sum + u * density)).astype(bf16)
        up_grad[:, cols] = contract(h2t, du, 1, 0)
        sums_ref[21 + col : 22 + col, :] = col_sum(du.astype(f32))
        dh2 = dh2 + contract(du, up_ref[:, cols], 1, 1)
    y_ref[...] = y.astype(bf16)
    back, gain_sum, bias_sum = norm_back(dh2, unit, inverse, vec_ref[18:19, :])
    dx1 = dy + back
    dx1_ref[...] = dx1
    da = dx1.astype(bf16)
    do_ref[...] = contract(da, out_ref[...], 1, 1).astype(bf16)
    out_grad[...] = contract(turned(o), da, 1, 0)
    sums_ref[0:17, :] = jnp.zeros((17, 256), f32)
    sums_ref[17:18, :] = col_sum(da.astype(f32))
    sums_ref[18:19, :] = gain_sum
    sums_ref[19:20, :] = bias_sum
    sums_ref[20:21, :] = col_sum(dy)


def rotate(left_turned, grad, right):
    half = contract(left_turned, grad.astype(bf16), 1, 0).astype(bf16)
    return contract(half, right, 1, 0)


def rotate_turned(grad_turned, left, right):
    half = contract(grad_turned.astype(bf16), left, 1, 0).astype(bf16)
    return contract(turned(half), right, 1, 0)


def share_out(keep_ref, send_ref, parts, mats):
    half = keep_ref.shape[0]
    for ref, base in ((keep_ref, 0), (send_ref, half)):

        def body(block, ref=ref, base=base):
            collect(ref, block, parts, mats, source(block + base))

        each_block(half, body)


def early_turn_kernel(up_grad, down_grad, turned_ref, narrow_ref, wide_ref, keep_ref, send_ref, up, down):
    up[...] = rotate(turned_ref[3], up_grad[...], wide_ref[0])
    down[...] = rotate_turned(down_grad[...], wide_ref[1], narrow_ref[6])
    share_out(keep_ref, send_ref, layout(256, EARLY)[0], (up, down))


def middle_turn_kernel(query_left, query_right, out_grad, turned_ref, narrow_ref, query_ref, out_ref):
    query_grad = jnp.concatenate([query_left[...], query_right[...]], axis=1)
    query_ref[...] = rotate(turned_ref[0], query_grad, narrow_ref[1])
    out_ref[...] = rotate(turned_ref[2], out_grad[...], narrow_ref[4])


def attend_back_kernel(
    step, unroll, group, q_ref, k_ref, v_ref, mask_ref, o_ref, log_ref, g_ref, h1_ref,
    dq_ref, keep_ref, send_ref, query_grad, bias_ref, dq_wide, dkv, ps, dss, qt, gt,
):
    tokens = q_ref.shape[0]
    scale = 32**-0.5
    lane = lax.broadcasted_iota(jnp.int32, (1, 128), 1)
    mask = mask_ref[...]
    cols = slice(group * 128, group * 128 + 128)
    qt[...] = turned(q_ref[:, cols])
    gt[...] = turned(g_ref[:, cols])

    def one_head(head):
        mine = lane // 32 == head
        keys = jnp.where(mine, k_ref[:, cols], 0)
        values = jnp.where(mine, v_ref[:, cols], 0)

        def block(start):
            rows = pl.ds(start, step)
            grad = g_ref[rows, cols]
            inner = jnp.sum(jnp.where(mine, grad.astype(f32) * o_ref[rows, cols], 0.0), axis=1, keepdims=True)
            if isinstance(head, int):
                log = log_ref[rows, group * 4 + head : group * 4 + head + 1]
            else:
                log = jnp.sum(jnp.where(lane == head + group * 4, log_ref[rows, :], 0.0), axis=1, keepdims=True)
            scores = contract(q_ref[rows, cols], keys, 1, 1)
            probs = jnp.exp2(scores * (scale * LOG2E) + mask - log)
            grad_scores = (probs * (contract(grad, values, 1, 1) - inner)).astype(bf16)
            ps[rows, :] = probs.astype(bf16)
            dss[rows, :] = grad_scores
            out = contract(grad_scores, keys, 1, 0) * scale
            dq_wide[rows, :] = jnp.where(mine, out, dq_wide[rows, :])

        over_blocks(block, tokens, step)
        dkv[head_rows(head), :] = contract(qt[head_rows(head), :], dss[...], 1, 0) * scale
        dkv[head_rows(head, 128), :] = contract(gt[head_rows(head), :], ps[...], 1, 0)

    over_heads(one_head, 0, 4, unroll)
    dq = dq_wide[...].astype(bf16)
    dq_ref[...] = dq
    bias_ref[...] = col_sum(dq.astype(f32))
    half = keep_ref.shape[0]
    keep_ref[...] = dkv[:, 0:half].T
    send_ref[...] = dkv[:, half:].T
    query_grad[...] = contract(turned(h1_ref[...]), dq, 1, 0)


def total_of(refs):
    total = refs[0][...]
    for ref in refs[1:]:
        total = total + ref[...].astype(f32)
    return total


def split_kernel(count, terms, *refs):
    total = total_of(refs[:terms])
    rows = total.shape[0] // count
    refs[terms][...] = total[:rows]
    for index in range(1, count):
        refs[terms + index][...] = total[index * rows : (index + 1) * rows].astype(bf16)


def split_sum(terms, count, after=()):
    rows = terms[0].shape[0] // count
    tail = terms[0].shape[1:]
    outs = [((rows,) + tail, f32)] + [((rows,) + tail, bf16)] * (count - 1)
    return run("split_sum", functools.partial(split_kernel, count, len(terms)), outs, terms, micros=0.6, after=after)


def split_heads_kernel(count, left_keep, left_got, right_keep, right_got, *outs):
    rows = outs[0].shape[0]
    for index in range(count):
        at = slice(index * rows, (index + 1) * rows)
        left = left_keep[at, :] + left_got[at, :]
        right = right_keep[at, :] + right_got[at, :]
        parts = (left[:, 0:128], right[:, 0:128], left[:, 128:256], right[:, 128:256])
        for place, part in enumerate(parts):
            cols = slice(place * 128, place * 128 + 128)
            outs[index][:, cols] = part if index == 0 else part.astype(bf16)


def pair_total(values):
    while len(values) > 1:
        values = [a + b for a, b in zip(values[::2], values[1::2])]
    return values[0]


def two_parts(value):
    high = value.astype(bf16)
    return high, (value - high.astype(f32)).astype(bf16)


def sum_three(keeps, pieces):
    late, vec, early = [ref[...] for ref in keeps]
    rows, more = late.shape[0], vec.shape[0]
    vecs = [vec]
    for ref in pieces:
        late = late + ref[0:rows, :].astype(f32)
        vecs.append(ref[rows : rows + more, :].astype(f32))
        early = early + ref[rows + more :, :].astype(f32)
    return late, pair_total(vecs), early


def split_three_kernel(count, pieces, first, *refs):
    if first:
        late, vec, early = [refs[k][...] + refs[k + 1][...] for k in (0, 2, 4)]
        outs = refs[6:]
    else:
        late, vec, early = sum_three(refs[:3], refs[3 : 3 + pieces])
        outs = refs[3 + pieces :]
    rows, more, rest = late.shape[0] // count, vec.shape[0], early.shape[0] // count
    low = vec.astype(bf16)
    outs[0][...] = late[:rows]
    outs[1][...] = low.astype(f32)
    outs[2][...] = early[:rest]
    for index in range(1, count):
        ref = outs[2 + index]
        ref[0:rows, :] = late[index * rows : (index + 1) * rows].astype(bf16)
        ref[rows : rows + more, :] = low
        ref[rows + more :, :] = early[index * rest : (index + 1) * rest].astype(bf16)


def split_three(args, count, first, after=()):
    late, vec, early = args[0:6:2] if first else args[0:3]
    rows, more, rest, width = late.shape[0] // count, vec.shape[0], early.shape[0] // count, late.shape[1]
    outs = [((rows, width), f32), ((more, width), f32), ((rest, width), f32)]
    outs += [((rows + more + rest, width), bf16)] * (count - 1)
    body = functools.partial(split_three_kernel, count, len(args) - 3, first)
    found = run("split_three", body, outs, list(args), micros=0.6, after=after)
    return list(found[:3]), found[3:]


def row_parts():
    return [("row", stride, size) for stride, size in rel_digits()[1:]]


def one_by_one(groups):
    return [(axis, stride << bit, 2) for axis, stride, size in groups for bit in reversed(range(size.bit_length() - 1))]


def side_by_side(x, groups):
    for axis, stride, size in groups:
        x = jnp.concatenate([x] + [swap(x, axis, j * stride) for j in range(1, size)], axis=0)
    return x


def keys_back_kernel(
    terms, *refs
):
    (kn_ref, c_ref, vec_ref, keyval_ref, blocks_ref, turned_ref, narrow_ref, pair_ref, wide_ref, query, out,
     keep_ref, send_ref, dc_ref, sums_ref, reduce, keyval) = refs[terms:]
    dkv = total_of(refs[:terms])
    high, rest = two_parts(dkv)
    dkn = contract(high, keyval_ref[...], 1, 1) + contract(rest, keyval_ref[...], 1, 1)
    unit, inverse = norm_parts(c_ref[...])
    back, gain_sum, bias_sum = norm_back(dkn, unit, inverse, vec_ref[14:15, :])
    dc = back.astype(bf16)
    dc_ref[...] = dc
    knt = turned(kn_ref[...])
    keyval[...] = rotate(turned_ref[1], contract(knt, high, 1, 0) + contract(knt, rest, 1, 0), pair_ref[...])
    reduce[...] = rotate_turned(contract(turned(dc), blocks_ref[...], 1, 0), wide_ref[2], narrow_ref[7])
    share_out(keep_ref, send_ref, layout(256, LATE)[0], (reduce, keyval, query, out))
    sums_ref[0:1, :] = col_sum(dc.astype(f32))
    sums_ref[1:2, :] = gain_sum
    sums_ref[2:3, :] = bias_sum
    sums_ref[3:4, :] = col_sum(dkv[:, 256:512])


def cells_back_kernel(
    tile_rows, cols, size_ref, dq_left, dq_right, dc_ref, query_ref, reduce_ref, x0_ref, dx1_ref, vec_ref, tile_ref, up_ref, down_ref,
    feed_sums, key_sums, left_sum, right_sum, dx0_ref, head_ref, tail_ref, sums_ref, frame,
):
    tokens = x0_ref.shape[0]
    dh1 = contract(dq_left[...], query_ref[:, 0:128], 1, 1) + contract(dq_right[...], query_ref[:, 128:256], 1, 1)
    for corner in range(4):
        pick = picked_cells((tokens, dc_ref.shape[0]), 0, size_ref, corner, tile_rows, cols)
        placed = contract(pick, dc_ref[...], 1, 0).astype(bf16)
        dh1 = dh1 + contract(placed, reduce_ref[corner * 256 : corner * 256 + 256, :], 1, 1)
    unit, inverse = norm_parts(x0_ref[...])
    back, gain_sum, bias_sum = norm_back(dh1, unit, inverse, vec_ref[10:11, :])
    dx0 = dx1_ref[...] + back
    dx0_ref[...] = dx0
    head_ref[...] = dx0[0:64].astype(bf16)
    tail_ref[...] = dx0[tokens - 64 :].astype(bf16)
    sums_ref[0:25, :] = feed_sums[...]
    sums_ref[25:32, :] = jnp.zeros((7, 256), f32)
    moved = shifted_frame(frame, tile_ref, up_ref, down_ref)
    grid = dx0.reshape(tile_rows, cols, 256)
    for tap in range(9):
        product = moved[tap % 3][tap // 3 : tap // 3 + tile_rows] * grid
        sums_ref[tap : tap + 1, :] = col_sum(product.reshape(tokens, 256))
    sums_ref[9:10, :] = col_sum(dx0)
    sums_ref[10:11, :] = gain_sum
    sums_ref[11:12, :] = bias_sum
    sums_ref[12:13, 0:128] = left_sum[...]
    sums_ref[12:13, 128:256] = right_sum[...]
    sums_ref[13:17, :] = key_sums[...]


def input_grad_kernel(tile_rows, dx0_ref, up_ref, down_ref, vec_ref, out_ref, token, frame):
    token[...] = jnp.zeros_like(token)
    moved = shifted_frame(frame, dx0_ref, up_ref, down_ref)
    total = moved[1][1:-1]
    for tap in range(9):
        down, right = 2 - tap // 3, 2 - tap % 3
        total = total + vec_ref[tap : tap + 1, :] * moved[right][down : down + tile_rows]
    out_ref[...] = total.reshape(out_ref.shape)


def moments_of(total, first, second, moment_ref, square_ref):
    moment = BETA * first + (1.0 - BETA) * total
    square = BETA * second + (1.0 - BETA) * total * total
    moment_ref[...] = moment
    square_ref[...] = square
    return moment * (1.0 / CORRECTION) / (jnp.sqrt(square * (1.0 / CORRECTION)) + ADAM_EPS)


def adam_kernel(terms, *refs):
    (first_ref, second_ref, vec_ref, vec_first, vec_second, vec_ema,
     moment_ref, square_ref, step_ref, vec_out, vec_first_out, vec_second_out, vec_ema_out) = refs[terms:]
    late, vec, early = sum_three(refs[:3], refs[3:terms])
    rows = late.shape[0]
    for total, at in ((late, slice(0, rows)), (early, slice(rows, rows + early.shape[0]))):
        step = moments_of(total, first_ref[at, :], second_ref[at, :], moment_ref.at[at, :], square_ref.at[at, :])
        step_ref[at, :] = step.astype(bf16)
    vec = vec[0 : vec_ref.shape[0]]
    new = vec_ref[...] - VECTOR_RATE * moments_of(vec, vec_first[...], vec_second[...], vec_first_out, vec_second_out)
    vec_out[...] = new
    vec_ema_out[...] = EMA_KEEP * vec_ema[...] + (1.0 - EMA_KEEP) * new


def both_groups(width):
    late, count = layout(width, LATE)
    return late + [(j, first + count, rows, blocks) for j, first, rows, blocks in layout(width, EARLY)[0]]


def products_kernel(width, chunks, own_narrow, own_wide, keep_ref, send_ref):
    lefts = {0: (own_narrow, 0), 1: (own_narrow, 1), 2: (own_narrow, 2), 3: (own_narrow, 3), 4: (own_wide, 0), 5: (own_wide, 1)}
    half = keep_ref.shape[0]
    values = chunks[...].astype(f32)
    for j, first, rows, blocks in both_groups(width):
        left = lefts[j][0][lefts[j][1]].astype(bf16)
        for col in range(blocks):
            at = slice(first + col * rows, first + (col + 1) * rows)
            part = values[:, at, :].reshape(left.shape[1], width).astype(bf16)
            side = contract(left, part, 1, 0).reshape(2 * half, rows, width)
            keep_ref[:, at, :] = side[:half]
            send_ref[:, at, :] = side[half:]


def finish_kernel(
    width, terms, *refs
):
    narrow_ref, pair_ref, wide_ref, weights_ref, ema_ref, weights_out, ema_out, chunk = refs[terms:]
    rights = {0: narrow_ref.at[1], 1: pair_ref, 2: narrow_ref.at[4], 3: wide_ref.at[0], 4: narrow_ref.at[6], 5: narrow_ref.at[7]}
    sides = total_of(refs[:terms])
    for j, first, rows, blocks in both_groups(width):
        parts = [sides[first + col * rows : first + (col + 1) * rows] for col in range(blocks)]
        side = parts[0] if blocks == 1 else jnp.concatenate(parts, axis=1)
        if rows < 8:
            side = jnp.concatenate([side, jnp.zeros((8 - rows, side.shape[1]), f32)], axis=0)
        full = contract(side.astype(bf16), rights[j][...], 1, 1)
        for col in range(blocks):
            at = slice(first + col * rows, first + (col + 1) * rows)
            old = weights_ref[at, :]
            piece = full[0:rows, col * width : (col + 1) * width]
            chunk[at, :] = old - MATRIX_RATES[j] * (piece + WEIGHT_DECAY * old)
    from_chunk(chunk, weights_out, width)
    chunk[...] = EMA_KEEP * ema_ref[...] + (1.0 - EMA_KEEP) * chunk[...]
    from_chunk(chunk, ema_out, width)


def packed_moments_kernel(width, moment_ref, square_ref, first_out, second_out, token):
    token[...] = jnp.zeros_like(token)
    from_chunk(moment_ref, first_out, width)
    from_chunk(square_ref, second_out, width)


def on_device(
    patches,
    cotangent,
    image_sizes,
    weights,
    first_moment,
    second_moment,
    weight_ema,
    vectors,
    vec_first,
    vec_second,
    vec_ema,
    basis_narrow,
    basis_pair,
    basis_wide,
):
    _, rows, cols, width = patches.shape
    tokens = rows * cols
    shards = device_count()
    tile = patches.reshape(tokens, width)
    dy = cotangent.reshape(tokens, width)
    per = weights.shape[1]
    late_rows, early_rows = layout(width, LATE)[1], layout(width, EARLY)[1]
    chunk = late_rows + early_rows
    ranks = lax.axis_size("row")
    own_keys = tokens // 4
    keys = own_keys * ranks
    frame = ((rows + 2, cols + 16, width), f32)
    img_part = ("img", 1, lax.axis_size("img"))
    xy_parts = row_parts()

    def border(head, tail):
        up = lax.ppermute(tail, "row", [(i, i + 1) for i in range(ranks - 1)])
        return up, lax.ppermute(head, "row", [(i + 1, i) for i in range(ranks - 1)])

    gather_groups = xy_parts[::-1]
    lines = lax.axis_size("img")

    (packed,) = run(
        "pack",
        functools.partial(pack_kernel, width),
        [((chunk, width), bf16)],
        [weights],
        scratch=[((chunk, width), f32)],
    )
    line = join([packed[None]] + [swap(packed, "img", j)[None] for j in range(1, lines)])
    up_halo, down_halo = border(tile[:64], tile[tokens - 64 :])
    x0, h1, mask, vec, sizes = run(
        "front",
        functools.partial(front_kernel, rows, cols),
        [((tokens, width), f32), ((tokens, width), bf16), ((1, keys), f32), (vectors.shape, f32), ((8, 128), jnp.int32)],
        [image_sizes, tile, up_halo, down_halo, vectors],
        scratch=[frame],
        scalars=(0,),
        micros=1.3,
        after=[line],
    )
    wide, wide_done = run(
        "wide_bases",
        wide_bases_kernel,
        [((3, FF, FF), bf16), ((8, 128), f32)],
        [basis_wide],
        scratch=[((12, width, FF), f32)],
        micros=6.0,
        mib=48,
        raw=(0,),
        sems=12,
        after=[line],
    )
    all_near = line
    for axis, stride, size in gather_groups:
        pieces = [all_near] + [swap(all_near, axis, j * stride) for j in range(1, size)]
        all_near = join(pieces, after=[wide_done, vec])
    all_far = swap(all_near, "row", 1)
    w_reduce, w_keyval, w_query, w_out, blocks, c, kn, own_kv = run(
        "keys",
        functools.partial(keys_kernel, rows, cols),
        [
            ((4 * width, width), bf16),
            ((width, 2 * width), bf16),
            ((width, width), bf16),
            ((width, width), bf16),
            ((own_keys, 4 * width), bf16),
            ((own_keys, width), f32),
            ((own_keys, width), bf16),
            ((own_keys, 2 * width), bf16),
        ],
        [sizes, h1, vec, all_near, all_far],
        scratch=[((4 * width, width), f32), ((width, 2 * width), f32), ((width, width), f32), ((width, width), f32)],
        micros=1.5,
    )
    narrow, narrow_turned, pair, own_narrow = run(
        "narrow_bases",
        narrow_bases_kernel,
        [
            ((8, width, width), bf16),
            ((4, width, width), bf16),
            ((2 * width, 2 * width), bf16),
            ((4, width // lines, width // ranks), f32),
        ],
        [basis_narrow, basis_pair],
        micros=1.5,
        after=[own_kv],
    )
    kv_near = side_by_side(own_kv, gather_groups)
    kv_far = swap(kv_near, "row", 1)

    unroll = keys <= 1024
    step = tokens if unroll else 32
    q, k, v, o, log = run(
        "attend",
        functools.partial(attend_kernel, step, unroll),
        [((tokens, width), bf16), ((keys, width), bf16), ((keys, width), bf16), ((tokens, width), f32), ((tokens, 128), f32)],
        [h1, w_query, vec, kv_near, kv_far, mask],
        mib=8 if unroll else 44,
        micros=8.0,
        after=[own_narrow],
    )
    y, do, dx1, up_grad, down_grad, out_grad, feed_sums = run(
        "feed",
        feed_kernel,
        [
            ((tokens, width), bf16),
            ((tokens, width), bf16),
            ((tokens, width), f32),
            ((width, FF), f32),
            ((width, FF), f32),
            ((width, width), f32),
            (vectors.shape, f32),
        ],
        [o, x0, w_out, all_near, all_far, vec, dy],
        scratch=[((width, FF), bf16), ((FF, width), bf16), ((width, FF), f32), ((FF, width), f32)],
        mib=12,
        micros=3.5,
    )
    def back(group, after):
        return run(
            "attend_back",
            functools.partial(attend_back_kernel, step, unroll, group),
            [
                ((tokens, 128), bf16),
                ((keys // 2, width), f32),
                ((keys // 2, width), f32),
                ((width, 128), f32),
                ((1, 128), f32),
            ],
            [q, k, v, mask, o, log, do, h1],
            scratch=[
                ((tokens, 128), f32),
                ((width, keys), f32),
                ((tokens, keys), bf16),
                ((tokens, keys), bf16),
                ((128, tokens), bf16),
                ((128, tokens), bf16),
            ],
            mib=14 if unroll else 60,
            micros=5.0,
            after=after,
        )

    dq_left, left_keep, left_send, query_left, left_sum = back(0, [dx1])
    left_got = swap(left_send, "row", 1)
    dq_right, right_keep, right_send, query_right, right_sum = back(1, [query_left])
    right_got = swap(right_send, "row", 1)
    half = (shards // 2, early_rows, width)
    early_keep, early_send = run(
        "early_turn",
        early_turn_kernel,
        [(half, f32), (half, f32)],
        [up_grad, down_grad, narrow_turned, narrow, wide],
        scratch=[((width, FF), f32), ((FF, width), f32)],
        mib=10,
        micros=2.0,
        after=[query_right],
    )
    early_got = swap(early_send, "row", 1)
    axis, stride, size = xy_parts[0]
    dkv_keep, *sends = run(
        "split_heads",
        functools.partial(split_heads_kernel, size),
        [((keys // 2 // size, 2 * width), f32)] + [((keys // 2 // size, 2 * width), bf16)] * (size - 1),
        [left_keep, left_got, right_keep, right_got],
        micros=0.8,
        after=[early_keep],
    )
    dkv_terms = [dkv_keep] + [swap(x, axis, j * stride) for j, x in enumerate(sends, 1)]
    for axis, stride, size in xy_parts[1:]:
        keep, *sends = split_sum(dkv_terms, size)
        dkv_terms = [keep] + [swap(x, axis, j * stride) for j, x in enumerate(sends, 1)]
    old_chunk, ema_chunk, first_chunk, second_chunk = run(
        "moments",
        functools.partial(moments_kernel, width),
        [((chunk, width), f32)] * 4,
        [jnp.concatenate([weights, weight_ema, first_moment, second_moment], axis=0)],
        after=[dkv_keep],
    )
    query_turn, out_turn = run(
        "middle_turn",
        middle_turn_kernel,
        [((width, width), f32), ((width, width), f32)],
        [query_left, query_right, out_grad, narrow_turned, narrow],
        micros=0.7,
        after=[dkv_keep],
    )
    half = (shards // 2, late_rows, width)
    late_keep, late_send, dc, key_sums = run(
        "keys_back",
        functools.partial(keys_back_kernel, len(dkv_terms)),
        [(half, f32), (half, f32), ((own_keys, width), bf16), ((4, width), f32)],
        list(dkv_terms) + [kn, c, vec, w_keyval, blocks, narrow_turned, narrow, pair, wide, query_turn, out_turn],
        scratch=[((4 * width, width), f32), ((width, 2 * width), f32)],
        micros=2.0,
        after=[old_chunk],
    )
    late_got = swap(late_send, "row", 1)
    dx0, head, tail, vec_grads = run(
        "cells_back",
        functools.partial(cells_back_kernel, rows, cols),
        [((tokens, width), f32), ((64, width), bf16), ((64, width), bf16), ((32, width), f32)],
        [
            sizes, dq_left, dq_right, dc, w_query, w_reduce, x0, dx1, vec, tile, up_halo, down_halo,
            feed_sums, key_sums, left_sum, right_sum,
        ],
        scratch=[frame],
        micros=2.0,
    )
    grad_up, grad_down = border(head, tail)
    args = [late_keep, late_got, vec_grads, swap(vec_grads, "row", 1), early_keep, early_got]
    args = [x.reshape(-1, width) for x in args]
    for index, (axis, stride, size) in enumerate(xy_parts + [img_part]):
        keeps, sends = split_three(args, size, index == 0, [grad_up, grad_down] if index else [])
        args = keeps + [swap(x, axis, j * stride) for j, x in enumerate(sends, 1)]
    grad_input, input_done = run(
        "input_grad",
        functools.partial(input_grad_kernel, rows),
        [((tokens, width), f32), ((8, 128), f32)],
        [dx0, grad_up, grad_down, vec],
        scratch=[frame],
        micros=1.5,
        after=[keeps[1]],
    )
    moments, squares, step, new_vectors, vec_moment, vec_square, new_vec_ema = run(
        "adam",
        functools.partial(adam_kernel, len(args)),
        [((chunk, width), f32), ((chunk, width), f32), ((chunk, width), bf16)] + [(vectors.shape, f32)] * 4,
        args + [first_chunk, second_chunk, vec, vec_first, vec_second, vec_ema],
        micros=0.8,
        after=[input_done],
    )
    (own_wide,) = run(
        "own_wide",
        own_wide_kernel,
        [((2, FF // lines, FF // ranks), f32)],
        [wide],
        micros=1.5,
        after=[step],
    )
    new_first, new_second, packed_done = run(
        "packed_moments",
        functools.partial(packed_moments_kernel, width),
        [((1, per), f32), ((1, per), f32), ((8, 128), f32)],
        [moments, squares],
        after=[own_wide],
    )
    steps = join([step[None]] + [swap(step, "img", j)[None] for j in range(1, lines)], [packed_done])
    half = (ranks // 2, chunk, width)
    keep, send = run(
        "products",
        functools.partial(products_kernel, width),
        [(half, f32), (half, f32)],
        [steps, own_narrow, own_wide],
        micros=1.0,
    )
    terms = [keep.reshape(-1, width), swap(send, "row", 1).reshape(-1, width)]
    for index, (axis, stride, size) in enumerate(xy_parts):
        part, *sends = split_sum(terms, size)
        terms = [part] + [swap(x, axis, j * stride) for j, x in enumerate(sends, 1)]
    new_weights, new_ema = run(
        "finish",
        functools.partial(finish_kernel, width, len(terms)),
        [((1, per), f32)] * 2,
        list(terms) + [narrow, pair, wide, old_chunk, ema_chunk],
        scratch=[((chunk, width), f32)],
        micros=1.5,
    )
    return (
        y.reshape(patches.shape),
        grad_input.reshape(patches.shape),
        new_weights,
        new_first,
        new_second,
        new_ema,
        new_vectors,
        vec_moment,
        vec_square,
        new_vec_ema,
    )


def solution(mesh):
    tiles = P("img", "row", None, None)
    packed = P(("img", "row"), None)
    return jax.shard_map(
        on_device,
        mesh=mesh,
        in_specs=(tiles, tiles, P("img", None)) + (packed,) * 4 + (P(),) * 7,
        out_specs=(tiles, tiles) + (packed,) * 4 + (P(),) * 4,
        check_vma=False,
    )
```

```python
import functools
import math

import jax
import jax.numpy as jnp
from jax import lax
from jax.experimental import pallas as pl
from jax.experimental.pallas import tpu as pltpu
from jax.sharding import PartitionSpec as P

HEADS = 8
FF = 1024
STEP = 5

NORM_EPS = 1e-05
ADAM_EPS = 1e-08
BETA = 0.5
WEIGHT_DECAY = 0.05
EMA_KEEP = 0.75
VECTOR_RATE = 0.06
MATRIX_RATES = (0.04, 0.02, 0.25, 0.02, 0.01, 0.01)
CORRECTION = 1.0 - BETA**STEP
LOG2E = math.log2(math.e)
f32 = jnp.float32
bf16 = jnp.bfloat16
LATE = (5, 1, 0, 2)
EARLY = (3, 4)


def matrix_shapes(width, hidden):
    return (
        (width, width),
        (width, 2 * width),
        (width, width),
        (width, hidden),
        (hidden, width),
        (4 * width, width),
    )


def contract(a, b, ca, cb, **kw):
    return lax.dot_general(
        a, b, (((ca,), (cb,)), ((), ())), preferred_element_type=f32, **kw
    )


def swap(x, axis, step):
    count = lax.axis_size(axis)
    return lax.ppermute(x, axis, [(i, i ^ step) for i in range(count)])


def row_groups():
    left = lax.axis_size("row") // 2
    groups, stride = [(1, 2)], 2
    while left > 1:
        size = 4 if left % 4 == 0 else 2
        groups.append((stride, size))
        left //= size
        stride *= size
    return groups


def rel_digits():
    groups = row_groups()
    return [groups[0]] + groups[1:][::-1]


def source(block):
    sizes = lax.axis_size("img")
    img, rest = block % sizes, block // sizes
    rel = 0
    for stride, size in reversed(rel_digits()):
        rel = rel + (rest % size) * stride
        rest = rest // size
    row = lax.axis_index("row") ^ rel
    return (lax.axis_index("img") ^ img) * lax.axis_size("row") + row


def device_count():
    return lax.axis_size("img") * lax.axis_size("row")


def run(name, body, outs, args, scratch=(), mib=6, scalars=(), micros=1.0, after=(), raw=(), sems=0):
    count = len(args)

    def without(*refs):
        body(*refs[:count], *refs[count + len(after) :])

    space = {index: pltpu.SMEM for index in scalars} | {index: pltpu.HBM for index in raw}
    specs = [pl.BlockSpec(memory_space=space.get(index, pltpu.VMEM)) for index in range(count)]
    return pl.pallas_call(
        without,
        out_shape=tuple(jax.ShapeDtypeStruct(shape, dtype) for shape, dtype in outs),
        in_specs=specs + [pl.BlockSpec(memory_space=pl.ANY)] * len(after),
        out_specs=tuple(pl.BlockSpec(memory_space=pltpu.VMEM) for _ in outs),
        scratch_shapes=[pltpu.VMEM(shape, dtype) for shape, dtype in scratch]
        + ([pltpu.SemaphoreType.DMA((sems,))] if sems else []),
        compiler_params=pltpu.CompilerParams(vmem_limit_bytes=mib * 2**20),
        cost_estimate=pl.CostEstimate(flops=0, bytes_accessed=int(micros * 3.6e6), transcendentals=0),
        name=name,
    )(*args, *after)


def each_block(count, body):
    if count <= 32:
        for index in range(count):
            body(index)
    else:

        def step(index, carry):
            body(index)
            return carry

        lax.fori_loop(0, count, step, 0)


def put_rows(ref, start, cols, value):
    count = value.shape[0]
    if count % 8 == 0:
        ref[pl.ds(pl.multiple_of(start, 8), count), cols] = value
    else:
        for row in range(count):
            ref[pl.ds(start + row, 1), cols] = value[row : row + 1]


def get_rows(ref, start, count, cols):
    if count % 8 == 0:
        return ref[pl.ds(pl.multiple_of(start, 8), count), cols]
    return jnp.concatenate([ref[pl.ds(start + row, 1), cols] for row in range(count)], axis=0)


def layout(width, group):
    dims = matrix_shapes(width, FF)
    found, start = [], 0
    for j in group:
        rows = dims[j][0] // device_count()
        blocks = dims[j][1] // width
        found.append((j, start, rows, blocks))
        start += rows * blocks
    return found, start


def packed_starts(width):
    dims = matrix_shapes(width, FF)
    starts, start = [], 0
    for m, n in dims:
        starts.append(start)
        start += m * n // device_count()
    return starts


def spread(block, parts, mats, start_of):
    for (j, first, rows, blocks), ref in zip(parts, mats):
        for col in range(blocks):
            piece = block[first + col * rows : first + (col + 1) * rows]
            put_rows(ref, start_of * rows, slice(col * 256, col * 256 + 256), piece)


def collect(out_ref, index, parts, mats, start_of):
    for (j, first, rows, blocks), ref in zip(parts, mats):
        for col in range(blocks):
            piece = get_rows(ref, start_of * rows, rows, slice(col * 256, col * 256 + 256))
            out_ref[index, first + col * rows : first + (col + 1) * rows, :] = piece


def norm_parts(values):
    centred = values - jnp.mean(values, axis=-1, keepdims=True)
    inverse = lax.rsqrt(jnp.mean(centred * centred, axis=-1, keepdims=True) + NORM_EPS)
    return centred * inverse, inverse


def norm_back(grad, unit, inverse, gain):
    grad_unit = grad * gain
    back = grad_unit - jnp.mean(grad_unit, axis=-1, keepdims=True)
    back = back - unit * jnp.mean(grad_unit * unit, axis=-1, keepdims=True)
    gain_sum = jnp.sum(grad * unit, axis=0, keepdims=True)
    return back * inverse, gain_sum, jnp.sum(grad, axis=0, keepdims=True)


def turned(value):
    return value.astype(f32).T.astype(bf16)


def col_sum(value):
    return jnp.sum(value, axis=0, keepdims=True)


def pack_kernel(width, w_ref, out_ref, chunk):
    to_chunk(w_ref, chunk, width)
    out_ref[...] = chunk[...].astype(bf16)


def to_chunk(flat_ref, out_ref, width, index=0):
    dims, starts, base = matrix_shapes(width, FF), packed_starts(width), 0
    for group in (LATE, EARLY):
        parts, count = layout(width, group)
        for j, first, rows, blocks in parts:
            for col in range(blocks):
                for row in range(rows):
                    at = starts[j] + row * dims[j][1] + col * width
                    place = base + first + col * rows + row
                    out_ref[place : place + 1, :] = flat_ref[index : index + 1, at : at + width]
        base += count


def from_chunk(values, out_ref, width):
    dims, starts = matrix_shapes(width, FF), packed_starts(width)
    for j, first, rows, blocks in both_groups(width):
        for col in range(blocks):
            for row in range(rows):
                at = starts[j] + row * dims[j][1] + col * width
                place = first + col * rows + row
                out_ref[0:1, at : at + width] = values[place : place + 1, :]


def moments_kernel(width, rows_ref, *outs):
    for index, ref in enumerate(outs):
        to_chunk(rows_ref, ref, width, index)


def left_block(matrix_ref, out_ref):
    lines, ranks = lax.axis_size("img"), lax.axis_size("row")
    size = matrix_ref.shape[0]
    rows = size // (lines * ranks)
    img, row = lax.axis_index("img"), lax.axis_index("row")

    def one_hot(count, axis, start_of):
        shape = (count * rows, size) if axis == 0 else (size, count * rows)
        place = lax.broadcasted_iota(jnp.int32, tuple(n if d == axis else 1 for d, n in enumerate(shape)), axis)
        block = place >> (rows.bit_length() - 1)
        target = start_of(block) * rows + (place & (rows - 1))
        return (lax.broadcasted_iota(jnp.int32, shape, 1 - axis) == target).astype(f32).astype(bf16)

    def owner(block):
        rel = jnp.zeros_like(block)
        for stride, count in reversed(rel_digits()):
            rel = rel + (block & (count - 1)) * stride
            block = block >> (count.bit_length() - 1)
        return img * ranks + (rel ^ row)

    mine = contract(one_hot(ranks, 0, owner), matrix_ref[...], 1, 0).astype(bf16)
    out_ref[...] = contract(mine, one_hot(lines, 1, lambda block: (block ^ img) * ranks + row), 1, 0)


def narrow_bases_kernel(narrow_ref, pair_ref, narrow_out, turned_out, pair_out, own_ref):
    narrow_out[...] = narrow_ref[...].astype(bf16)
    pair_out[...] = pair_ref[...].astype(bf16)
    for index, j in enumerate((0, 2, 3, 5)):
        turned_out[index] = narrow_ref[j].T.astype(bf16)
        left_block(narrow_out.at[j], own_ref.at[index])


def own_wide_kernel(wide_ref, own_ref):
    for index in range(2):
        left_block(wide_ref.at[index + 1], own_ref.at[index])


def wide_bases_kernel(wide_ref, wide_out, token):
    for index in range(wide_ref.shape[0]):
        wide_out[index] = wide_ref[index].astype(bf16)
    token[...] = jnp.zeros_like(token)


def join_kernel(*refs):
    start = 0
    for ref in refs[-2::-1]:
        refs[-1][start : start + ref.shape[0]] = ref[...]
        start += ref.shape[0]


def join(pieces, after=()):
    shape = (sum(x.shape[0] for x in pieces),) + pieces[0].shape[1:]
    return run("join", join_kernel, [(shape, pieces[0].dtype)], list(pieces)[::-1], micros=0.4, after=after)[0]


def unpack(pieces, group, mats, base=0):
    parts = [(j, first + base, rows, blocks) for j, first, rows, blocks in layout(256, group)[0]]
    done = 0
    for piece in pieces:

        def body(block, piece=piece, done=done):
            spread(piece[block].astype(f32), parts, mats, source(block + done))

        each_block(piece.shape[0], body)
        done += piece.shape[0]


def shifted_frame(frame_ref, tile_ref, up_ref, down_ref):
    rows, cols, width = frame_ref.shape[0] - 2, 56, 256
    frame_ref[...] = jnp.zeros_like(frame_ref)
    frame_ref[0, 8 : 8 + cols, :] = up_ref[...].astype(f32)[-cols:]
    frame_ref[1 : 1 + rows, 8 : 8 + cols, :] = tile_ref[...].astype(f32).reshape(rows, cols, width)
    frame_ref[rows + 1, 8 : 8 + cols, :] = down_ref[...].astype(f32)[:cols]
    return [frame_ref[:, 7 + shift : 7 + shift + cols, :] for shift in range(3)]


def front_kernel(tile_rows, cols, size_ref, tile_ref, up_ref, down_ref, vec_ref, x0_ref, h1_ref, mask_ref, vec_out, size_out, frame):
    rows = frame.shape[0] - 2
    vec_out[...] = vec_ref[...]
    size_out[...] = jnp.where(lax.broadcasted_iota(jnp.int32, size_out.shape, 0) == 0, size_ref[0, 0], size_ref[0, 1])
    moved = shifted_frame(frame, tile_ref, up_ref, down_ref)
    total = moved[1][1:-1] + vec_ref[9:10, :]
    for tap in range(9):
        total = total + vec_ref[tap : tap + 1, :] * moved[tap % 3][tap // 3 : tap // 3 + rows]
    x0 = total.reshape(x0_ref.shape)
    x0_ref[...] = x0
    unit, _ = norm_parts(x0)
    h1_ref[...] = (unit * vec_ref[10:11, :] + vec_ref[11:12, :]).astype(bf16)
    half = cols // 2
    own = tile_rows // 2 * half
    key = lax.broadcasted_iota(jnp.int32, mask_ref.shape, 1)
    block = jnp.zeros_like(key)
    for start in range(own, mask_ref.shape[1], own):
        block = block + (key >= start).astype(jnp.int32)
    key = key - block * own
    row = jnp.zeros_like(key)
    for start in range(half, own, half):
        row = row + (key >= start).astype(jnp.int32)
    col = key - row * half
    rel = jnp.zeros_like(key)
    for stride, size in reversed(rel_digits()):
        rel = rel + (block & (size - 1)) * stride
        block = block >> (size.bit_length() - 1)
    row = row + (rel ^ lax.axis_index("row")) * (tile_rows // 2)
    inside = (2 * row < size_ref[0, 0]) & (2 * col < size_ref[0, 1])
    mask_ref[...] = jnp.where(inside, 0.0, -1e30)


def picked_cells(shape, cell_axis, size_ref, corner, tile_rows, cols):
    half = cols // 2
    key_shape = tuple(1 if axis == cell_axis else n for axis, n in enumerate(shape))
    key = lax.broadcasted_iota(jnp.int32, key_shape, 1 - cell_axis)
    row = jnp.zeros_like(key)
    for step in range(1, tile_rows // 2):
        row = row + (key >= step * half).astype(jnp.int32)
    col = 2 * (key - row * half) + corner % 2
    row = 2 * row + corner // 2
    inside = (row + lax.axis_index("row") * tile_rows < size_ref[0:1, 0:1]) & (col < size_ref[1:2, 0:1])
    target = jnp.where(inside, row * cols + col, -1)
    cell = lax.broadcasted_iota(jnp.int32, shape, cell_axis)
    return (cell == target).astype(f32).astype(bf16)


def keys_kernel(
    tile_rows, cols, size_ref, h1_ref, vec_ref, near_ref, far_ref,
    reduce_ref, keyval_ref, query_ref, out_ref, blocks_ref, c_ref, kn_ref, kv_ref,
    reduce_wide, keyval_wide, query_wide, out_wide,
):
    unpack((near_ref, far_ref), LATE, (reduce_wide, keyval_wide, query_wide, out_wide))
    reduce_ref[...] = reduce_wide[...].astype(bf16)
    keyval_ref[...] = keyval_wide[...].astype(bf16)
    query_ref[...] = query_wide[...].astype(bf16)
    out_ref[...] = out_wide[...].astype(bf16)
    keys = c_ref.shape[0]
    for corner in range(4):
        pick = picked_cells((keys, h1_ref.shape[0]), 1, size_ref, corner, tile_rows, cols)
        blocks_ref[:, corner * 256 : corner * 256 + 256] = contract(pick, h1_ref[...], 1, 0).astype(bf16)
    c = contract(blocks_ref[...], reduce_ref[...], 1, 0) + vec_ref[13:14, :]
    c_ref[...] = c
    unit, _ = norm_parts(c)
    kn = (unit * vec_ref[14:15, :] + vec_ref[15:16, :]).astype(bf16)
    kn_ref[...] = kn
    kv = contract(kn, keyval_ref[...], 1, 0)
    kv_ref[:, 0:256] = kv[:, 0:256].astype(bf16)
    kv_ref[:, 256:512] = (kv[:, 256:512] + vec_ref[16:17, :]).astype(bf16)


def over_heads(body, first, last, unroll):
    if unroll:
        for head in range(first, last):
            body(head)
    else:

        def step(head, carry):
            body(head)
            return carry

        lax.fori_loop(first, last, step, 0)


def over_blocks(block, tokens, step):
    if tokens == step:
        block(0)
    else:

        def go(index, carry):
            block(pl.multiple_of(index * step, step))
            return carry

        lax.fori_loop(0, tokens // step, go, 0)


def head_columns(head):
    group = head // 4
    if isinstance(head, int):
        return slice(group * 128, group * 128 + 128)
    return pl.ds(pl.multiple_of(group * 128, 128), 128)


def head_rows(head, base=0):
    if isinstance(head, int):
        return slice(base + head * 32, base + head * 32 + 32)
    return pl.ds(pl.multiple_of(base + head * 32, 32), 32)


def attend_kernel(
    step, unroll, h1_ref, query_ref, vec_ref, near_ref, far_ref, mask_ref, q_ref, k_ref, v_ref, o_ref, stat_ref, *kept
):
    tokens = h1_ref.shape[0]
    half = near_ref.shape[0]
    for start, ref in ((0, near_ref), (half, far_ref)):
        k_ref[start : start + half, :] = ref[:, 0:256]
        v_ref[start : start + half, :] = ref[:, 256:512]
    q_ref[...] = (contract(h1_ref[...], query_ref[...], 1, 0) + vec_ref[12:13, :]).astype(bf16)
    scale = 32**-0.5 * LOG2E
    lane = lax.broadcasted_iota(jnp.int32, (1, 128), 1)
    mask = mask_ref[...]

    def one_head(head):
        cols = head_columns(head)
        mine = lane // 32 == head % 4
        keys = jnp.where(mine, k_ref[:, cols], 0)
        ones = jnp.where(lane // 32 == (head + 2) % 4, 1.0, 0.0).astype(bf16)
        values = jnp.where(mine, v_ref[:, cols], ones)

        def block(start):
            rows = pl.ds(start, step)
            scores = contract(q_ref[rows, cols], keys, 1, 1) * scale + mask
            top = jnp.max(scores, axis=1, keepdims=True)
            exponent = jnp.exp2(scores - top).astype(bf16)
            if kept:
                kept[0][head] = exponent
            out = contract(exponent, values, 1, 0)
            if isinstance(head, int):
                total = out[:, (head + 2) % 4 * 32 : (head + 2) % 4 * 32 + 1]
            else:
                total = jnp.sum(jnp.where(lane == (head + 2) % 4 * 32, out, 0.0), axis=1, keepdims=True)
            inverse = 1.0 / total
            o_ref[rows, cols] = jnp.where(mine, out * inverse, o_ref[rows, cols])
            stat = inverse if kept else top + jnp.log2(total)
            stat_ref[rows, :] = jnp.where(lane == head, stat, stat_ref[rows, :])

        over_blocks(block, tokens, step)

    over_heads(one_head, 0, HEADS, unroll)


def feed_kernel(
    o_ref, x0_ref, out_ref, near_ref, far_ref, vec_ref, dy_ref,
    y_ref, do_ref, dx1_ref, up_grad, down_grad, out_grad, sums_ref, up_ref, down_ref, up_wide, down_wide,
):
    unpack((near_ref, far_ref), EARLY, (up_wide, down_wide), layout(256, LATE)[1])
    up_ref[...] = up_wide[...].astype(bf16)
    down_ref[...] = down_wide[...].astype(bf16)
    o = o_ref[...].astype(bf16)
    x1 = x0_ref[...] + (contract(o, out_ref[...], 1, 0) + vec_ref[17:18, :])
    unit, inverse = norm_parts(x1)
    h2 = (unit * vec_ref[18:19, :] + vec_ref[19:20, :]).astype(bf16)
    dy_low = dy_ref[...]
    dy = dy_low.astype(f32)
    dyt = turned(dy_low)
    h2t = turned(h2)
    y = x1 + vec_ref[20:21, :]
    dh2 = jnp.zeros_like(y)
    for col in range(FF // 256):
        cols = slice(col * 256, col * 256 + 256)
        u = contract(h2, up_ref[:, cols], 1, 0) + vec_ref[21 + col : 22 + col, :]
        phi_sum = 0.5 * (1.0 + lax.erf(u * (2.0**-0.5)))
        density = jnp.exp(-0.5 * u * u) * ((2.0 * math.pi) ** -0.5)
        g = (u * phi_sum).astype(bf16)
        y = y + contract(g, down_ref[cols, :], 1, 0)
        down_grad[:, cols] = contract(dyt, g, 1, 0)
        du = (contract(dy_low, down_ref[cols, :], 1, 1) * (phi_sum + u * density)).astype(bf16)
        up_grad[:, cols] = contract(h2t, du, 1, 0)
        sums_ref[21 + col : 22 + col, :] = col_sum(du.astype(f32))
        dh2 = dh2 + contract(du, up_ref[:, cols], 1, 1)
    y_ref[...] = y.astype(bf16)
    back, gain_sum, bias_sum = norm_back(dh2, unit, inverse, vec_ref[18:19, :])
    dx1 = dy + back
    dx1_ref[...] = dx1
    da = dx1.astype(bf16)
    do_ref[...] = contract(da, out_ref[...], 1, 1).astype(bf16)
    out_grad[...] = contract(turned(o), da, 1, 0)
    sums_ref[0:17, :] = jnp.zeros((17, 256), f32)
    sums_ref[17:18, :] = col_sum(da.astype(f32))
    sums_ref[18:19, :] = gain_sum
    sums_ref[19:20, :] = bias_sum
    sums_ref[20:21, :] = col_sum(dy)


def rotate(left_turned, grad, right):
    half = contract(left_turned, grad.astype(bf16), 1, 0).astype(bf16)
    return contract(half, right, 1, 0)


def rotate_turned(grad_turned, left, right):
    half = contract(grad_turned.astype(bf16), left, 1, 0).astype(bf16)
    return contract(turned(half), right, 1, 0)


def share_out(keep_ref, send_ref, parts, mats):
    half = keep_ref.shape[0]
    for ref, base in ((keep_ref, 0), (send_ref, half)):

        def body(block, ref=ref, base=base):
            collect(ref, block, parts, mats, source(block + base))

        each_block(half, body)


def early_turn_kernel(up_grad, down_grad, turned_ref, narrow_ref, wide_ref, keep_ref, send_ref, up, down):
    up[...] = rotate(turned_ref[3], up_grad[...], wide_ref[0])
    down[...] = rotate_turned(down_grad[...], wide_ref[1], narrow_ref[6])
    share_out(keep_ref, send_ref, layout(256, EARLY)[0], (up, down))


def middle_turn_kernel(query_left, query_right, out_grad, turned_ref, narrow_ref, query_ref, out_ref):
    query_grad = jnp.concatenate([query_left[...], query_right[...]], axis=1)
    query_ref[...] = rotate(turned_ref[0], query_grad, narrow_ref[1])
    out_ref[...] = rotate(turned_ref[2], out_grad[...], narrow_ref[4])


def back_outputs(dq_wide, dkv, h1_ref, dq_ref, keep_ref, send_ref, query_grad, bias_ref):
    dq = dq_wide[...].astype(bf16)
    dq_ref[...] = dq
    bias_ref[...] = col_sum(dq.astype(f32))
    half = keep_ref.shape[0]
    keep_ref[...] = dkv[:, 0:half].T
    send_ref[...] = dkv[:, half:].T
    query_grad[...] = contract(turned(h1_ref[...]), dq, 1, 0)


def inner_sum(grad, out, mine):
    return jnp.sum(jnp.where(mine, grad.astype(f32) * out, 0.0), axis=1, keepdims=True)


def attend_back_kept_kernel(
    group, q_ref, k_ref, v_ref, o_ref, stat_ref, kept_ref, g_ref, h1_ref,
    dq_ref, keep_ref, send_ref, query_grad, bias_ref, dq_wide, dkv, dss, qt, gt,
):
    scale = 32**-0.5
    lane = lax.broadcasted_iota(jnp.int32, (1, 128), 1)
    cols = slice(group * 128, group * 128 + 128)
    grad = g_ref[:, cols]
    stats = [stat_ref[:, group * 4 + head : group * 4 + head + 1] for head in range(4)]
    spread_stats = stats[3]
    for head in range(3):
        spread_stats = jnp.where(lane // 32 == head, stats[head], spread_stats)
    qt[...] = turned(q_ref[:, cols])
    gt[...] = (grad.astype(f32) * spread_stats).T.astype(bf16)
    for head in range(4):
        mine = lane // 32 == head
        keys = jnp.where(mine, k_ref[:, cols], 0)
        values = jnp.where(mine, v_ref[:, cols], 0)
        inner = inner_sum(grad, o_ref[:, cols], mine)
        exponent = kept_ref[group * 4 + head]
        slope = (contract(grad, values, 1, 1) - inner) * stats[head]
        dss[...] = (exponent.astype(f32) * slope).astype(bf16)
        out = contract(dss[...], keys, 1, 0) * scale
        dq_wide[...] = jnp.where(mine, out, dq_wide[...])
        dkv[head_rows(head), :] = contract(qt[head_rows(head), :], dss[...], 1, 0) * scale
        dkv[head_rows(head, 128), :] = contract(gt[head_rows(head), :], exponent, 1, 0)
    back_outputs(dq_wide, dkv, h1_ref, dq_ref, keep_ref, send_ref, query_grad, bias_ref)


def attend_back_kernel(
    step, group, q_ref, k_ref, v_ref, mask_ref, o_ref, stat_ref, g_ref, h1_ref,
    dq_ref, keep_ref, send_ref, query_grad, bias_ref, dq_wide, dkv, ps, dss, qt, gt,
):
    tokens = q_ref.shape[0]
    scale = 32**-0.5
    lane = lax.broadcasted_iota(jnp.int32, (1, 128), 1)
    mask = mask_ref[...]
    cols = slice(group * 128, group * 128 + 128)
    qt[...] = turned(q_ref[:, cols])
    gt[...] = turned(g_ref[:, cols])

    def one_head(head):
        mine = lane // 32 == head
        keys = jnp.where(mine, k_ref[:, cols], 0)
        values = jnp.where(mine, v_ref[:, cols], 0)

        def block(start):
            rows = pl.ds(start, step)
            grad = g_ref[rows, cols]
            inner = inner_sum(grad, o_ref[rows, cols], mine)
            log = jnp.sum(jnp.where(lane == head + group * 4, stat_ref[rows, :], 0.0), axis=1, keepdims=True)
            scores = contract(q_ref[rows, cols], keys, 1, 1)
            probs = jnp.exp2(scores * (scale * LOG2E) + mask - log)
            grad_scores = (probs * (contract(grad, values, 1, 1) - inner)).astype(bf16)
            ps[rows, :] = probs.astype(bf16)
            dss[rows, :] = grad_scores
            out = contract(grad_scores, keys, 1, 0) * scale
            dq_wide[rows, :] = jnp.where(mine, out, dq_wide[rows, :])

        over_blocks(block, tokens, step)
        dkv[head_rows(head), :] = contract(qt[head_rows(head), :], dss[...], 1, 0) * scale
        dkv[head_rows(head, 128), :] = contract(gt[head_rows(head), :], ps[...], 1, 0)

    over_heads(one_head, 0, 4, False)
    back_outputs(dq_wide, dkv, h1_ref, dq_ref, keep_ref, send_ref, query_grad, bias_ref)


def total_of(refs):
    total = refs[0][...]
    for ref in refs[1:]:
        total = total + ref[...].astype(f32)
    return total


def split_kernel(count, terms, *refs):
    total = total_of(refs[:terms])
    rows = total.shape[0] // count
    refs[terms][...] = total[:rows]
    for index in range(1, count):
        refs[terms + index][...] = total[index * rows : (index + 1) * rows].astype(bf16)


def split_sum(terms, count, after=()):
    rows = terms[0].shape[0] // count
    tail = terms[0].shape[1:]
    outs = [((rows,) + tail, f32)] + [((rows,) + tail, bf16)] * (count - 1)
    return run("split_sum", functools.partial(split_kernel, count, len(terms)), outs, terms, micros=0.6, after=after)


def split_heads_kernel(count, left_keep, left_got, right_keep, right_got, *outs):
    rows = outs[0].shape[0]
    for index in range(count):
        at = slice(index * rows, (index + 1) * rows)
        left = left_keep[at, :] + left_got[at, :]
        right = right_keep[at, :] + right_got[at, :]
        parts = (left[:, 0:128], right[:, 0:128], left[:, 128:256], right[:, 128:256])
        for place, part in enumerate(parts):
            cols = slice(place * 128, place * 128 + 128)
            outs[index][:, cols] = part if index == 0 else part.astype(bf16)


def pair_total(values):
    while len(values) > 1:
        values = [a + b for a, b in zip(values[::2], values[1::2])]
    return values[0]


def two_parts(value):
    high = value.astype(bf16)
    return high, (value - high.astype(f32)).astype(bf16)


def sum_three(keeps, pieces):
    late, vec, early = [ref[...] for ref in keeps]
    rows, more = late.shape[0], vec.shape[0]
    vecs = [vec]
    for ref in pieces:
        late = late + ref[0:rows, :].astype(f32)
        vecs.append(ref[rows : rows + more, :].astype(f32))
        early = early + ref[rows + more :, :].astype(f32)
    return late, pair_total(vecs), early


def split_three_kernel(count, pieces, first, *refs):
    if first:
        late, vec, early = [refs[k][...] + refs[k + 1][...] for k in (0, 2, 4)]
        outs = refs[6:]
    else:
        late, vec, early = sum_three(refs[:3], refs[3 : 3 + pieces])
        outs = refs[3 + pieces :]
    rows, more, rest = late.shape[0] // count, vec.shape[0], early.shape[0] // count
    low = vec.astype(bf16)
    outs[0][...] = late[:rows]
    outs[1][...] = low.astype(f32)
    outs[2][...] = early[:rest]
    for index in range(1, count):
        ref = outs[2 + index]
        ref[0:rows, :] = late[index * rows : (index + 1) * rows].astype(bf16)
        ref[rows : rows + more, :] = low
        ref[rows + more :, :] = early[index * rest : (index + 1) * rest].astype(bf16)


def split_three(args, count, first, after=()):
    late, vec, early = args[0:6:2] if first else args[0:3]
    rows, more, rest, width = late.shape[0] // count, vec.shape[0], early.shape[0] // count, late.shape[1]
    outs = [((rows, width), f32), ((more, width), f32), ((rest, width), f32)]
    outs += [((rows + more + rest, width), bf16)] * (count - 1)
    body = functools.partial(split_three_kernel, count, len(args) - 3, first)
    found = run("split_three", body, outs, list(args), micros=0.6, after=after)
    return list(found[:3]), found[3:]


def row_parts():
    return [("row", stride, size) for stride, size in rel_digits()[1:]]


def one_by_one(groups):
    return [(axis, stride << bit, 2) for axis, stride, size in groups for bit in reversed(range(size.bit_length() - 1))]


def side_by_side(x, groups):
    for axis, stride, size in groups:
        x = jnp.concatenate([x] + [swap(x, axis, j * stride) for j in range(1, size)], axis=0)
    return x


def keys_back_kernel(
    terms, *refs
):
    (kn_ref, c_ref, vec_ref, keyval_ref, blocks_ref, turned_ref, narrow_ref, pair_ref, wide_ref, query, out,
     keep_ref, send_ref, dc_ref, sums_ref, reduce, keyval) = refs[terms:]
    dkv = total_of(refs[:terms])
    high, rest = two_parts(dkv)
    dkn = contract(high, keyval_ref[...], 1, 1) + contract(rest, keyval_ref[...], 1, 1)
    unit, inverse = norm_parts(c_ref[...])
    back, gain_sum, bias_sum = norm_back(dkn, unit, inverse, vec_ref[14:15, :])
    dc = back.astype(bf16)
    dc_ref[...] = dc
    knt = turned(kn_ref[...])
    keyval[...] = rotate(turned_ref[1], contract(knt, high, 1, 0) + contract(knt, rest, 1, 0), pair_ref[...])
    reduce[...] = rotate_turned(contract(turned(dc), blocks_ref[...], 1, 0), wide_ref[2], narrow_ref[7])
    share_out(keep_ref, send_ref, layout(256, LATE)[0], (reduce, keyval, query, out))
    sums_ref[0:1, :] = col_sum(dc.astype(f32))
    sums_ref[1:2, :] = gain_sum
    sums_ref[2:3, :] = bias_sum
    sums_ref[3:4, :] = col_sum(dkv[:, 256:512])


def cells_back_kernel(
    tile_rows, cols, size_ref, dq_left, dq_right, dc_ref, query_ref, reduce_ref, x0_ref, dx1_ref, vec_ref, tile_ref, up_ref, down_ref,
    feed_sums, key_sums, left_sum, right_sum, dx0_ref, head_ref, tail_ref, sums_ref, frame,
):
    tokens = x0_ref.shape[0]
    dh1 = contract(dq_left[...], query_ref[:, 0:128], 1, 1) + contract(dq_right[...], query_ref[:, 128:256], 1, 1)
    for corner in range(4):
        pick = picked_cells((tokens, dc_ref.shape[0]), 0, size_ref, corner, tile_rows, cols)
        placed = contract(pick, dc_ref[...], 1, 0).astype(bf16)
        dh1 = dh1 + contract(placed, reduce_ref[corner * 256 : corner * 256 + 256, :], 1, 1)
    unit, inverse = norm_parts(x0_ref[...])
    back, gain_sum, bias_sum = norm_back(dh1, unit, inverse, vec_ref[10:11, :])
    dx0 = dx1_ref[...] + back
    dx0_ref[...] = dx0
    head_ref[...] = dx0[0:64].astype(bf16)
    tail_ref[...] = dx0[tokens - 64 :].astype(bf16)
    sums_ref[0:25, :] = feed_sums[...]
    sums_ref[25:32, :] = jnp.zeros((7, 256), f32)
    moved = shifted_frame(frame, tile_ref, up_ref, down_ref)
    grid = dx0.reshape(tile_rows, cols, 256)
    for tap in range(9):
        product = moved[tap % 3][tap // 3 : tap // 3 + tile_rows] * grid
        sums_ref[tap : tap + 1, :] = col_sum(product.reshape(tokens, 256))
    sums_ref[9:10, :] = col_sum(dx0)
    sums_ref[10:11, :] = gain_sum
    sums_ref[11:12, :] = bias_sum
    sums_ref[12:13, 0:128] = left_sum[...]
    sums_ref[12:13, 128:256] = right_sum[...]
    sums_ref[13:17, :] = key_sums[...]


def input_grad_kernel(tile_rows, dx0_ref, up_ref, down_ref, vec_ref, out_ref, token, frame):
    token[...] = jnp.zeros_like(token)
    moved = shifted_frame(frame, dx0_ref, up_ref, down_ref)
    total = moved[1][1:-1]
    for tap in range(9):
        down, right = 2 - tap // 3, 2 - tap % 3
        total = total + vec_ref[tap : tap + 1, :] * moved[right][down : down + tile_rows]
    out_ref[...] = total.reshape(out_ref.shape)


def moments_of(total, first, second, moment_ref, square_ref):
    moment = BETA * first + (1.0 - BETA) * total
    square = BETA * second + (1.0 - BETA) * total * total
    moment_ref[...] = moment
    square_ref[...] = square
    return moment * (1.0 / CORRECTION) / (jnp.sqrt(square * (1.0 / CORRECTION)) + ADAM_EPS)


def adam_kernel(terms, *refs):
    (first_ref, second_ref, vec_ref, vec_first, vec_second, vec_ema,
     moment_ref, square_ref, step_ref, vec_out, vec_first_out, vec_second_out, vec_ema_out) = refs[terms:]
    late, vec, early = sum_three(refs[:3], refs[3:terms])
    rows = late.shape[0]
    for total, at in ((late, slice(0, rows)), (early, slice(rows, rows + early.shape[0]))):
        step = moments_of(total, first_ref[at, :], second_ref[at, :], moment_ref.at[at, :], square_ref.at[at, :])
        step_ref[at, :] = step.astype(bf16)
    vec = vec[0 : vec_ref.shape[0]]
    new = vec_ref[...] - VECTOR_RATE * moments_of(vec, vec_first[...], vec_second[...], vec_first_out, vec_second_out)
    vec_out[...] = new
    vec_ema_out[...] = EMA_KEEP * vec_ema[...] + (1.0 - EMA_KEEP) * new


def both_groups(width):
    late, count = layout(width, LATE)
    return late + [(j, first + count, rows, blocks) for j, first, rows, blocks in layout(width, EARLY)[0]]


def products_kernel(width, chunks, own_narrow, own_wide, keep_ref, send_ref):
    lefts = {0: (own_narrow, 0), 1: (own_narrow, 1), 2: (own_narrow, 2), 3: (own_narrow, 3), 4: (own_wide, 0), 5: (own_wide, 1)}
    half = keep_ref.shape[0]
    values = chunks[...].astype(f32)
    for j, first, rows, blocks in both_groups(width):
        left = lefts[j][0][lefts[j][1]].astype(bf16)
        for col in range(blocks):
            at = slice(first + col * rows, first + (col + 1) * rows)
            part = values[:, at, :].reshape(left.shape[1], width).astype(bf16)
            side = contract(left, part, 1, 0).reshape(2 * half, rows, width)
            keep_ref[:, at, :] = side[:half]
            send_ref[:, at, :] = side[half:]


def finish_kernel(
    width, terms, *refs
):
    narrow_ref, pair_ref, wide_ref, weights_ref, ema_ref, weights_out, ema_out, chunk = refs[terms:]
    rights = {0: narrow_ref.at[1], 1: pair_ref, 2: narrow_ref.at[4], 3: wide_ref.at[0], 4: narrow_ref.at[6], 5: narrow_ref.at[7]}
    sides = total_of(refs[:terms])
    for j, first, rows, blocks in both_groups(width):
        parts = [sides[first + col * rows : first + (col + 1) * rows] for col in range(blocks)]
        side = parts[0] if blocks == 1 else jnp.concatenate(parts, axis=1)
        if rows < 8:
            side = jnp.concatenate([side, jnp.zeros((8 - rows, side.shape[1]), f32)], axis=0)
        full = contract(side.astype(bf16), rights[j][...], 1, 1)
        for col in range(blocks):
            at = slice(first + col * rows, first + (col + 1) * rows)
            old = weights_ref[at, :]
            piece = full[0:rows, col * width : (col + 1) * width]
            chunk[at, :] = old - MATRIX_RATES[j] * (piece + WEIGHT_DECAY * old)
    from_chunk(chunk, weights_out, width)
    chunk[...] = EMA_KEEP * ema_ref[...] + (1.0 - EMA_KEEP) * chunk[...]
    from_chunk(chunk, ema_out, width)


def packed_moments_kernel(width, moment_ref, square_ref, first_out, second_out, token):
    token[...] = jnp.zeros_like(token)
    from_chunk(moment_ref, first_out, width)
    from_chunk(square_ref, second_out, width)


def on_device(
    patches,
    cotangent,
    image_sizes,
    weights,
    first_moment,
    second_moment,
    weight_ema,
    vectors,
    vec_first,
    vec_second,
    vec_ema,
    basis_narrow,
    basis_pair,
    basis_wide,
):
    _, rows, cols, width = patches.shape
    tokens = rows * cols
    shards = device_count()
    tile = patches.reshape(tokens, width)
    dy = cotangent.reshape(tokens, width)
    per = weights.shape[1]
    late_rows, early_rows = layout(width, LATE)[1], layout(width, EARLY)[1]
    chunk = late_rows + early_rows
    ranks = lax.axis_size("row")
    own_keys = tokens // 4
    keys = own_keys * ranks
    frame = ((rows + 2, cols + 16, width), f32)
    img_part = ("img", 1, lax.axis_size("img"))
    xy_parts = row_parts()

    def border(head, tail):
        up = lax.ppermute(tail, "row", [(i, i + 1) for i in range(ranks - 1)])
        return up, lax.ppermute(head, "row", [(i + 1, i) for i in range(ranks - 1)])

    gather_groups = xy_parts[::-1]
    lines = lax.axis_size("img")

    (packed,) = run(
        "pack",
        functools.partial(pack_kernel, width),
        [((chunk, width), bf16)],
        [weights],
        scratch=[((chunk, width), f32)],
    )
    line = join([packed[None]] + [swap(packed, "img", j)[None] for j in range(1, lines)])
    up_halo, down_halo = border(tile[:64], tile[tokens - 64 :])
    x0, h1, mask, vec, sizes = run(
        "front",
        functools.partial(front_kernel, rows, cols),
        [((tokens, width), f32), ((tokens, width), bf16), ((1, keys), f32), (vectors.shape, f32), ((8, 128), jnp.int32)],
        [image_sizes, tile, up_halo, down_halo, vectors],
        scratch=[frame],
        scalars=(0,),
        micros=1.3,
        after=[line],
    )
    wide, wide_done = run(
        "wide_bases",
        wide_bases_kernel,
        [((3, FF, FF), bf16), ((8, 128), f32)],
        [basis_wide],
        micros=6.0,
        after=[line],
    )
    all_near = line
    for axis, stride, size in gather_groups:
        pieces = [all_near] + [swap(all_near, axis, j * stride) for j in range(1, size)]
        all_near = join(pieces, after=[wide_done, vec])
    all_far = swap(all_near, "row", 1)
    w_reduce, w_keyval, w_query, w_out, blocks, c, kn, own_kv = run(
        "keys",
        functools.partial(keys_kernel, rows, cols),
        [
            ((4 * width, width), bf16),
            ((width, 2 * width), bf16),
            ((width, width), bf16),
            ((width, width), bf16),
            ((own_keys, 4 * width), bf16),
            ((own_keys, width), f32),
            ((own_keys, width), bf16),
            ((own_keys, 2 * width), bf16),
        ],
        [sizes, h1, vec, all_near, all_far],
        scratch=[((4 * width, width), f32), ((width, 2 * width), f32), ((width, width), f32), ((width, width), f32)],
        micros=1.5,
    )
    narrow, narrow_turned, pair, own_narrow = run(
        "narrow_bases",
        narrow_bases_kernel,
        [
            ((8, width, width), bf16),
            ((4, width, width), bf16),
            ((2 * width, 2 * width), bf16),
            ((4, width // lines, width // ranks), f32),
        ],
        [basis_narrow, basis_pair],
        micros=1.5,
        after=[own_kv],
    )
    kv_near = side_by_side(own_kv, gather_groups)
    kv_far = swap(kv_near, "row", 1)

    unroll = keys <= 1024
    step = tokens if unroll else 32
    q, k, v, o, stat, *kept = run(
        "attend",
        functools.partial(attend_kernel, step, unroll),
        [((tokens, width), bf16), ((keys, width), bf16), ((keys, width), bf16), ((tokens, width), f32), ((tokens, 128), f32)]
        + ([((HEADS, tokens, keys), bf16)] if unroll else []),
        [h1, w_query, vec, kv_near, kv_far, mask],
        mib=8 if unroll else 44,
        micros=8.0,
        after=[own_narrow],
    )
    y, do, dx1, up_grad, down_grad, out_grad, feed_sums = run(
        "feed",
        feed_kernel,
        [
            ((tokens, width), bf16),
            ((tokens, width), bf16),
            ((tokens, width), f32),
            ((width, FF), f32),
            ((width, FF), f32),
            ((width, width), f32),
            (vectors.shape, f32),
        ],
        [o, x0, w_out, all_near, all_far, vec, dy],
        scratch=[((width, FF), bf16), ((FF, width), bf16), ((width, FF), f32), ((FF, width), f32)],
        mib=12,
        micros=3.5,
    )
    def back(group, after):
        if kept:
            body, args, more = functools.partial(attend_back_kept_kernel, group), [q, k, v, o, stat, kept[0]], []
        else:
            body, args = functools.partial(attend_back_kernel, step, group), [q, k, v, mask, o, stat]
            more = [((tokens, keys), bf16)]
        return run(
            "attend_back",
            body,
            [
                ((tokens, 128), bf16),
                ((keys // 2, width), f32),
                ((keys // 2, width), f32),
                ((width, 128), f32),
                ((1, 128), f32),
            ],
            args + [do, h1],
            scratch=[((tokens, 128), f32), ((width, keys), f32)]
            + more
            + [((tokens, keys), bf16), ((128, tokens), bf16), ((128, tokens), bf16)],
            mib=14 if kept else 60,
            micros=5.0,
            after=after,
        )

    dq_left, left_keep, left_send, query_left, left_sum = back(0, [dx1])
    left_got = swap(left_send, "row", 1)
    dq_right, right_keep, right_send, query_right, right_sum = back(1, [query_left])
    right_got = swap(right_send, "row", 1)
    half = (shards // 2, early_rows, width)
    early_keep, early_send = run(
        "early_turn",
        early_turn_kernel,
        [(half, f32), (half, f32)],
        [up_grad, down_grad, narrow_turned, narrow, wide],
        scratch=[((width, FF), f32), ((FF, width), f32)],
        mib=10,
        micros=2.0,
        after=[query_right],
    )
    early_got = swap(early_send, "row", 1)
    axis, stride, size = xy_parts[0]
    dkv_keep, *sends = run(
        "split_heads",
        functools.partial(split_heads_kernel, size),
        [((keys // 2 // size, 2 * width), f32)] + [((keys // 2 // size, 2 * width), bf16)] * (size - 1),
        [left_keep, left_got, right_keep, right_got],
        micros=0.8,
        after=[early_keep],
    )
    dkv_terms = [dkv_keep] + [swap(x, axis, j * stride) for j, x in enumerate(sends, 1)]
    for axis, stride, size in xy_parts[1:]:
        keep, *sends = split_sum(dkv_terms, size)
        dkv_terms = [keep] + [swap(x, axis, j * stride) for j, x in enumerate(sends, 1)]
    old_chunk, ema_chunk, first_chunk, second_chunk = run(
        "moments",
        functools.partial(moments_kernel, width),
        [((chunk, width), f32)] * 4,
        [jnp.concatenate([weights, weight_ema, first_moment, second_moment], axis=0)],
        after=[dkv_keep],
    )
    query_turn, out_turn = run(
        "middle_turn",
        middle_turn_kernel,
        [((width, width), f32), ((width, width), f32)],
        [query_left, query_right, out_grad, narrow_turned, narrow],
        micros=0.7,
        after=[dkv_keep],
    )
    half = (shards // 2, late_rows, width)
    late_keep, late_send, dc, key_sums = run(
        "keys_back",
        functools.partial(keys_back_kernel, len(dkv_terms)),
        [(half, f32), (half, f32), ((own_keys, width), bf16), ((4, width), f32)],
        list(dkv_terms) + [kn, c, vec, w_keyval, blocks, narrow_turned, narrow, pair, wide, query_turn, out_turn],
        scratch=[((4 * width, width), f32), ((width, 2 * width), f32)],
        micros=2.0,
        after=[old_chunk],
    )
    late_got = swap(late_send, "row", 1)
    dx0, head, tail, vec_grads = run(
        "cells_back",
        functools.partial(cells_back_kernel, rows, cols),
        [((tokens, width), f32), ((64, width), bf16), ((64, width), bf16), ((32, width), f32)],
        [
            sizes, dq_left, dq_right, dc, w_query, w_reduce, x0, dx1, vec, tile, up_halo, down_halo,
            feed_sums, key_sums, left_sum, right_sum,
        ],
        scratch=[frame],
        micros=2.0,
    )
    grad_up, grad_down = border(head, tail)
    args = [late_keep, late_got, vec_grads, swap(vec_grads, "row", 1), early_keep, early_got]
    args = [x.reshape(-1, width) for x in args]
    for index, (axis, stride, size) in enumerate(xy_parts + [img_part]):
        keeps, sends = split_three(args, size, index == 0, [grad_up, grad_down] if index else [])
        args = keeps + [swap(x, axis, j * stride) for j, x in enumerate(sends, 1)]
    grad_input, input_done = run(
        "input_grad",
        functools.partial(input_grad_kernel, rows),
        [((tokens, width), f32), ((8, 128), f32)],
        [dx0, grad_up, grad_down, vec],
        scratch=[frame],
        micros=1.5,
        after=[keeps[1]],
    )
    moments, squares, step, new_vectors, vec_moment, vec_square, new_vec_ema = run(
        "adam",
        functools.partial(adam_kernel, len(args)),
        [((chunk, width), f32), ((chunk, width), f32), ((chunk, width), bf16)] + [(vectors.shape, f32)] * 4,
        args + [first_chunk, second_chunk, vec, vec_first, vec_second, vec_ema],
        micros=0.8,
        after=[input_done],
    )
    (own_wide,) = run(
        "own_wide",
        own_wide_kernel,
        [((2, FF // lines, FF // ranks), f32)],
        [wide],
        micros=1.5,
        after=[step],
    )
    new_first, new_second, packed_done = run(
        "packed_moments",
        functools.partial(packed_moments_kernel, width),
        [((1, per), f32), ((1, per), f32), ((8, 128), f32)],
        [moments, squares],
        after=[own_wide],
    )
    steps = join([step[None]] + [swap(step, "img", j)[None] for j in range(1, lines)], [packed_done])
    half = (ranks // 2, chunk, width)
    keep, send = run(
        "products",
        functools.partial(products_kernel, width),
        [(half, f32), (half, f32)],
        [steps, own_narrow, own_wide],
        micros=1.0,
    )
    terms = [keep.reshape(-1, width), swap(send, "row", 1).reshape(-1, width)]
    for index, (axis, stride, size) in enumerate(xy_parts):
        part, *sends = split_sum(terms, size)
        terms = [part] + [swap(x, axis, j * stride) for j, x in enumerate(sends, 1)]
    new_weights, new_ema = run(
        "finish",
        functools.partial(finish_kernel, width, len(terms)),
        [((1, per), f32)] * 2,
        list(terms) + [narrow, pair, wide, old_chunk, ema_chunk],
        scratch=[((chunk, width), f32)],
        micros=1.5,
    )
    return (
        y.reshape(patches.shape),
        grad_input.reshape(patches.shape),
        new_weights,
        new_first,
        new_second,
        new_ema,
        new_vectors,
        vec_moment,
        vec_square,
        new_vec_ema,
    )


def solution(mesh):
    tiles = P("img", "row", None, None)
    packed = P(("img", "row"), None)
    return jax.shard_map(
        on_device,
        mesh=mesh,
        in_specs=(tiles, tiles, P("img", None)) + (packed,) * 4 + (P(),) * 7,
        out_specs=(tiles, tiles) + (packed,) * 4 + (P(),) * 4,
        check_vma=False,
    )
```

```python
import functools
import math

import jax
import jax.numpy as jnp
from jax import lax
from jax.experimental import pallas as pl
from jax.experimental.pallas import tpu as pltpu
from jax.sharding import PartitionSpec as P

HEADS = 8
FF = 1024
STEP = 5

NORM_EPS = 1e-05
ADAM_EPS = 1e-08
BETA = 0.5
WEIGHT_DECAY = 0.05
EMA_KEEP = 0.75
VECTOR_RATE = 0.06
MATRIX_RATES = (0.04, 0.02, 0.25, 0.02, 0.01, 0.01)
CORRECTION = 1.0 - BETA**STEP
LOG2E = math.log2(math.e)
f32 = jnp.float32
bf16 = jnp.bfloat16
LATE = (5, 1, 0, 2)
EARLY = (3, 4)


def matrix_shapes(width, hidden):
    return (
        (width, width),
        (width, 2 * width),
        (width, width),
        (width, hidden),
        (hidden, width),
        (4 * width, width),
    )


def contract(a, b, ca, cb, **kw):
    return lax.dot_general(
        a, b, (((ca,), (cb,)), ((), ())), preferred_element_type=f32, **kw
    )


def swap(x, axis, step):
    count = lax.axis_size(axis)
    return lax.ppermute(x, axis, [(i, i ^ step) for i in range(count)])


def row_groups():
    left = lax.axis_size("row") // 2
    groups, stride = [(1, 2)], 2
    while left > 1:
        size = 4 if left % 4 == 0 else 2
        groups.append((stride, size))
        left //= size
        stride *= size
    return groups


def rel_digits():
    groups = row_groups()
    return [groups[0]] + groups[1:][::-1]


def source(block):
    sizes = lax.axis_size("img")
    img, rest = block % sizes, block // sizes
    rel = 0
    for stride, size in reversed(rel_digits()):
        rel = rel + (rest % size) * stride
        rest = rest // size
    row = lax.axis_index("row") ^ rel
    return (lax.axis_index("img") ^ img) * lax.axis_size("row") + row


def device_count():
    return lax.axis_size("img") * lax.axis_size("row")


def run(name, body, outs, args, scratch=(), mib=6, scalars=(), micros=1.0, after=(), raw=(), sems=0):
    count = len(args)

    def without(*refs):
        body(*refs[:count], *refs[count + len(after) :])

    space = {index: pltpu.SMEM for index in scalars} | {index: pltpu.HBM for index in raw}
    specs = [pl.BlockSpec(memory_space=space.get(index, pltpu.VMEM)) for index in range(count)]
    return pl.pallas_call(
        without,
        out_shape=tuple(jax.ShapeDtypeStruct(shape, dtype) for shape, dtype in outs),
        in_specs=specs + [pl.BlockSpec(memory_space=pl.ANY)] * len(after),
        out_specs=tuple(pl.BlockSpec(memory_space=pltpu.VMEM) for _ in outs),
        scratch_shapes=[pltpu.VMEM(shape, dtype) for shape, dtype in scratch]
        + ([pltpu.SemaphoreType.DMA((sems,))] if sems else []),
        compiler_params=pltpu.CompilerParams(vmem_limit_bytes=mib * 2**20),
        cost_estimate=pl.CostEstimate(flops=0, bytes_accessed=int(micros * 3.6e6), transcendentals=0),
        name=name,
    )(*args, *after)


def each_block(count, body):
    if count <= 32:
        for index in range(count):
            body(index)
    else:

        def step(index, carry):
            body(index)
            return carry

        lax.fori_loop(0, count, step, 0)


def put_rows(ref, start, cols, value):
    count = value.shape[0]
    if count % 8 == 0:
        ref[pl.ds(pl.multiple_of(start, 8), count), cols] = value
    else:
        for row in range(count):
            ref[pl.ds(start + row, 1), cols] = value[row : row + 1]


def get_rows(ref, start, count, cols):
    if count % 8 == 0:
        return ref[pl.ds(pl.multiple_of(start, 8), count), cols]
    return jnp.concatenate([ref[pl.ds(start + row, 1), cols] for row in range(count)], axis=0)


def layout(width, group):
    dims = matrix_shapes(width, FF)
    found, start = [], 0
    for j in group:
        rows = dims[j][0] // device_count()
        blocks = dims[j][1] // width
        found.append((j, start, rows, blocks))
        start += rows * blocks
    return found, start


def packed_starts(width):
    dims = matrix_shapes(width, FF)
    starts, start = [], 0
    for m, n in dims:
        starts.append(start)
        start += m * n // device_count()
    return starts


def spread(block, parts, mats, start_of):
    for (j, first, rows, blocks), ref in zip(parts, mats):
        for col in range(blocks):
            piece = block[first + col * rows : first + (col + 1) * rows]
            put_rows(ref, start_of * rows, slice(col * 256, col * 256 + 256), piece)


def collect(out_ref, index, parts, mats, start_of):
    for (j, first, rows, blocks), ref in zip(parts, mats):
        for col in range(blocks):
            piece = get_rows(ref, start_of * rows, rows, slice(col * 256, col * 256 + 256))
            out_ref[index, first + col * rows : first + (col + 1) * rows, :] = piece


def norm_parts(values):
    centred = values - jnp.mean(values, axis=-1, keepdims=True)
    inverse = lax.rsqrt(jnp.mean(centred * centred, axis=-1, keepdims=True) + NORM_EPS)
    return centred * inverse, inverse


def norm_back(grad, unit, inverse, gain):
    grad_unit = grad * gain
    back = grad_unit - jnp.mean(grad_unit, axis=-1, keepdims=True)
    back = back - unit * jnp.mean(grad_unit * unit, axis=-1, keepdims=True)
    gain_sum = jnp.sum(grad * unit, axis=0, keepdims=True)
    return back * inverse, gain_sum, jnp.sum(grad, axis=0, keepdims=True)


def turned(value):
    return value.astype(f32).T.astype(bf16)


def col_sum(value):
    return jnp.sum(value, axis=0, keepdims=True)


def pack_kernel(width, w_ref, out_ref, chunk):
    to_chunk(w_ref, chunk, width)
    out_ref[...] = chunk[...].astype(bf16)


def to_chunk(flat_ref, out_ref, width, index=0):
    dims, starts, base = matrix_shapes(width, FF), packed_starts(width), 0
    for group in (LATE, EARLY):
        parts, count = layout(width, group)
        for j, first, rows, blocks in parts:
            for col in range(blocks):
                for row in range(rows):
                    at = starts[j] + row * dims[j][1] + col * width
                    place = base + first + col * rows + row
                    out_ref[place : place + 1, :] = flat_ref[index : index + 1, at : at + width]
        base += count


def from_chunk(values, out_ref, width):
    dims, starts = matrix_shapes(width, FF), packed_starts(width)
    for j, first, rows, blocks in both_groups(width):
        for col in range(blocks):
            for row in range(rows):
                at = starts[j] + row * dims[j][1] + col * width
                place = first + col * rows + row
                out_ref[0:1, at : at + width] = values[place : place + 1, :]


def moments_kernel(width, rows_ref, *outs):
    for index, ref in enumerate(outs):
        to_chunk(rows_ref, ref, width, index)


def left_block(matrix_ref, out_ref):
    lines, ranks = lax.axis_size("img"), lax.axis_size("row")
    size = matrix_ref.shape[0]
    rows = size // (lines * ranks)
    img, row = lax.axis_index("img"), lax.axis_index("row")

    def one_hot(count, axis, start_of):
        shape = (count * rows, size) if axis == 0 else (size, count * rows)
        place = lax.broadcasted_iota(jnp.int32, tuple(n if d == axis else 1 for d, n in enumerate(shape)), axis)
        block = place >> (rows.bit_length() - 1)
        target = start_of(block) * rows + (place & (rows - 1))
        return (lax.broadcasted_iota(jnp.int32, shape, 1 - axis) == target).astype(f32).astype(bf16)

    def owner(block):
        rel = jnp.zeros_like(block)
        for stride, count in reversed(rel_digits()):
            rel = rel + (block & (count - 1)) * stride
            block = block >> (count.bit_length() - 1)
        return img * ranks + (rel ^ row)

    mine = contract(one_hot(ranks, 0, owner), matrix_ref[...], 1, 0).astype(bf16)
    out_ref[...] = contract(mine, one_hot(lines, 1, lambda block: (block ^ img) * ranks + row), 1, 0)


def narrow_bases_kernel(narrow_ref, pair_ref, narrow_out, turned_out, pair_out, own_ref):
    narrow_out[...] = narrow_ref[...].astype(bf16)
    pair_out[...] = pair_ref[...].astype(bf16)
    for index, j in enumerate((0, 2, 3, 5)):
        turned_out[index] = narrow_ref[j].T.astype(bf16)
        left_block(narrow_out.at[j], own_ref.at[index])


def own_wide_kernel(wide_ref, own_ref):
    for index in range(2):
        left_block(wide_ref.at[index + 1], own_ref.at[index])


def wide_bases_kernel(wide_ref, wide_out, token):
    for index in range(wide_ref.shape[0]):
        wide_out[index] = wide_ref[index].astype(bf16)
    token[...] = jnp.zeros_like(token)


def join_kernel(*refs):
    start = 0
    for ref in refs[-2::-1]:
        refs[-1][start : start + ref.shape[0]] = ref[...]
        start += ref.shape[0]


def join(pieces, after=()):
    shape = (sum(x.shape[0] for x in pieces),) + pieces[0].shape[1:]
    return run("join", join_kernel, [(shape, pieces[0].dtype)], list(pieces)[::-1], micros=0.4, after=after)[0]


def unpack(pieces, group, mats, base=0):
    parts = [(j, first + base, rows, blocks) for j, first, rows, blocks in layout(256, group)[0]]
    done = 0
    for piece in pieces:

        def body(block, piece=piece, done=done):
            spread(piece[block].astype(f32), parts, mats, source(block + done))

        each_block(piece.shape[0], body)
        done += piece.shape[0]


def shifted_frame(frame_ref, tile_ref, up_ref, down_ref):
    rows, cols, width = frame_ref.shape[0] - 2, 56, 256
    frame_ref[...] = jnp.zeros_like(frame_ref)
    frame_ref[0, 8 : 8 + cols, :] = up_ref[...].astype(f32)[-cols:]
    frame_ref[1 : 1 + rows, 8 : 8 + cols, :] = tile_ref[...].astype(f32).reshape(rows, cols, width)
    frame_ref[rows + 1, 8 : 8 + cols, :] = down_ref[...].astype(f32)[:cols]
    return [frame_ref[:, 7 + shift : 7 + shift + cols, :] for shift in range(3)]


def front_kernel(tile_rows, cols, size_ref, tile_ref, up_ref, down_ref, vec_ref, x0_ref, h1_ref, mask_ref, vec_out, size_out, frame):
    rows = frame.shape[0] - 2
    vec_out[...] = vec_ref[...]
    size_out[...] = jnp.where(lax.broadcasted_iota(jnp.int32, size_out.shape, 0) == 0, size_ref[0, 0], size_ref[0, 1])
    moved = shifted_frame(frame, tile_ref, up_ref, down_ref)
    total = moved[1][1:-1] + vec_ref[9:10, :]
    for tap in range(9):
        total = total + vec_ref[tap : tap + 1, :] * moved[tap % 3][tap // 3 : tap // 3 + rows]
    x0 = total.reshape(x0_ref.shape)
    x0_ref[...] = x0
    unit, _ = norm_parts(x0)
    h1_ref[...] = (unit * vec_ref[10:11, :] + vec_ref[11:12, :]).astype(bf16)
    half = cols // 2
    own = tile_rows // 2 * half
    key = lax.broadcasted_iota(jnp.int32, mask_ref.shape, 1)
    block = jnp.zeros_like(key)
    for start in range(own, mask_ref.shape[1], own):
        block = block + (key >= start).astype(jnp.int32)
    key = key - block * own
    row = jnp.zeros_like(key)
    for start in range(half, own, half):
        row = row + (key >= start).astype(jnp.int32)
    col = key - row * half
    rel = jnp.zeros_like(key)
    for stride, size in reversed(rel_digits()):
        rel = rel + (block & (size - 1)) * stride
        block = block >> (size.bit_length() - 1)
    row = row + (rel ^ lax.axis_index("row")) * (tile_rows // 2)
    inside = (2 * row < size_ref[0, 0]) & (2 * col < size_ref[0, 1])
    mask_ref[...] = jnp.where(inside, 0.0, -1e30)


def picked_cells(shape, cell_axis, size_ref, corner, tile_rows, cols):
    half = cols // 2
    key_shape = tuple(1 if axis == cell_axis else n for axis, n in enumerate(shape))
    key = lax.broadcasted_iota(jnp.int32, key_shape, 1 - cell_axis)
    row = jnp.zeros_like(key)
    for step in range(1, tile_rows // 2):
        row = row + (key >= step * half).astype(jnp.int32)
    col = 2 * (key - row * half) + corner % 2
    row = 2 * row + corner // 2
    inside = (row + lax.axis_index("row") * tile_rows < size_ref[0:1, 0:1]) & (col < size_ref[1:2, 0:1])
    target = jnp.where(inside, row * cols + col, -1)
    cell = lax.broadcasted_iota(jnp.int32, shape, cell_axis)
    return (cell == target).astype(f32).astype(bf16)


def keys_kernel(
    tile_rows, cols, size_ref, h1_ref, vec_ref, near_ref, far_ref,
    reduce_ref, keyval_ref, query_ref, out_ref, blocks_ref, c_ref, kn_ref,
    reduce_wide, keyval_wide, query_wide, out_wide,
):
    unpack((near_ref, far_ref), LATE, (reduce_wide, keyval_wide, query_wide, out_wide))
    reduce_ref[...] = reduce_wide[...].astype(bf16)
    keyval_ref[...] = keyval_wide[...].astype(bf16)
    query_ref[...] = query_wide[...].astype(bf16)
    out_ref[...] = out_wide[...].astype(bf16)
    keys = c_ref.shape[0]
    for corner in range(4):
        pick = picked_cells((keys, h1_ref.shape[0]), 1, size_ref, corner, tile_rows, cols)
        blocks_ref[:, corner * 256 : corner * 256 + 256] = contract(pick, h1_ref[...], 1, 0).astype(bf16)
    c = contract(blocks_ref[...], reduce_ref[...], 1, 0) + vec_ref[13:14, :]
    c_ref[...] = c
    unit, _ = norm_parts(c)
    kn = (unit * vec_ref[14:15, :] + vec_ref[15:16, :]).astype(bf16)
    kn_ref[...] = kn


def over_heads(body, first, last, unroll):
    if unroll:
        for head in range(first, last):
            body(head)
    else:

        def step(head, carry):
            body(head)
            return carry

        lax.fori_loop(first, last, step, 0)


def over_blocks(block, tokens, step):
    if tokens == step:
        block(0)
    else:

        def go(index, carry):
            block(pl.multiple_of(index * step, step))
            return carry

        lax.fori_loop(0, tokens // step, go, 0)


def head_columns(head):
    group = head // 4
    if isinstance(head, int):
        return slice(group * 128, group * 128 + 128)
    return pl.ds(pl.multiple_of(group * 128, 128), 128)


def head_rows(head, base=0):
    if isinstance(head, int):
        return slice(base + head * 32, base + head * 32 + 32)
    return pl.ds(pl.multiple_of(base + head * 32, 32), 32)


def attend_kernel(
    step, unroll, h1_ref, query_ref, keyval_ref, vec_ref, near_ref, far_ref, mask_ref,
    kn_ref, q_ref, k_ref, v_ref, o_ref, stat_ref, *kept
):
    tokens = h1_ref.shape[0]
    half = near_ref.shape[0]
    kn_ref[0:half, :] = near_ref[...]
    kn_ref[half:, :] = far_ref[...]
    k_ref[...] = contract(kn_ref[...], keyval_ref[:, 0:256], 1, 0).astype(bf16)
    v_ref[...] = (contract(kn_ref[...], keyval_ref[:, 256:512], 1, 0) + vec_ref[16:17, :]).astype(bf16)
    q_ref[...] = (contract(h1_ref[...], query_ref[...], 1, 0) + vec_ref[12:13, :]).astype(bf16)
    scale = 32**-0.5 * LOG2E
    lane = lax.broadcasted_iota(jnp.int32, (1, 128), 1)
    mask = mask_ref[...]

    def one_head(head):
        cols = head_columns(head)
        mine = lane // 32 == head % 4
        keys = jnp.where(mine, k_ref[:, cols], 0)
        ones = jnp.where(lane // 32 == (head + 2) % 4, 1.0, 0.0).astype(bf16)
        values = jnp.where(mine, v_ref[:, cols], ones)

        def block(start):
            rows = pl.ds(start, step)
            scores = contract(q_ref[rows, cols], keys, 1, 1) * scale + mask
            top = jnp.max(scores, axis=1, keepdims=True)
            exponent = jnp.exp2(scores - top).astype(bf16)
            if kept:
                kept[0][head] = exponent
            out = contract(exponent, values, 1, 0)
            if isinstance(head, int):
                total = out[:, (head + 2) % 4 * 32 : (head + 2) % 4 * 32 + 1]
            else:
                total = jnp.sum(jnp.where(lane == (head + 2) % 4 * 32, out, 0.0), axis=1, keepdims=True)
            inverse = 1.0 / total
            o_ref[rows, cols] = jnp.where(mine, out * inverse, o_ref[rows, cols])
            stat = inverse if kept else top + jnp.log2(total)
            stat_ref[rows, :] = jnp.where(lane == head, stat, stat_ref[rows, :])

        over_blocks(block, tokens, step)

    over_heads(one_head, 0, HEADS, unroll)


def feed_kernel(
    o_ref, x0_ref, out_ref, near_ref, far_ref, vec_ref, dy_ref,
    y_ref, do_ref, dx1_ref, up_grad, down_grad, out_grad, sums_ref, up_ref, down_ref, up_wide, down_wide,
):
    unpack((near_ref, far_ref), EARLY, (up_wide, down_wide), layout(256, LATE)[1])
    up_ref[...] = up_wide[...].astype(bf16)
    down_ref[...] = down_wide[...].astype(bf16)
    o = o_ref[...].astype(bf16)
    x1 = x0_ref[...] + (contract(o, out_ref[...], 1, 0) + vec_ref[17:18, :])
    unit, inverse = norm_parts(x1)
    h2 = (unit * vec_ref[18:19, :] + vec_ref[19:20, :]).astype(bf16)
    dy_low = dy_ref[...]
    dy = dy_low.astype(f32)
    dyt = turned(dy_low)
    h2t = turned(h2)
    y = x1 + vec_ref[20:21, :]
    dh2 = jnp.zeros_like(y)
    for col in range(FF // 256):
        cols = slice(col * 256, col * 256 + 256)
        u = contract(h2, up_ref[:, cols], 1, 0) + vec_ref[21 + col : 22 + col, :]
        phi_sum = 0.5 * (1.0 + lax.erf(u * (2.0**-0.5)))
        density = jnp.exp(-0.5 * u * u) * ((2.0 * math.pi) ** -0.5)
        g = (u * phi_sum).astype(bf16)
        y = y + contract(g, down_ref[cols, :], 1, 0)
        down_grad[:, cols] = contract(dyt, g, 1, 0)
        du = (contract(dy_low, down_ref[cols, :], 1, 1) * (phi_sum + u * density)).astype(bf16)
        up_grad[:, cols] = contract(h2t, du, 1, 0)
        sums_ref[21 + col : 22 + col, :] = col_sum(du.astype(f32))
        dh2 = dh2 + contract(du, up_ref[:, cols], 1, 1)
    y_ref[...] = y.astype(bf16)
    back, gain_sum, bias_sum = norm_back(dh2, unit, inverse, vec_ref[18:19, :])
    dx1 = dy + back
    dx1_ref[...] = dx1
    da = dx1.astype(bf16)
    do_ref[...] = contract(da, out_ref[...], 1, 1).astype(bf16)
    out_grad[...] = contract(turned(o), da, 1, 0)
    sums_ref[0:17, :] = jnp.zeros((17, 256), f32)
    sums_ref[17:18, :] = col_sum(da.astype(f32))
    sums_ref[18:19, :] = gain_sum
    sums_ref[19:20, :] = bias_sum
    sums_ref[20:21, :] = col_sum(dy)


def rotate(left_turned, grad, right):
    half = contract(left_turned, grad.astype(bf16), 1, 0).astype(bf16)
    return contract(half, right, 1, 0)


def rotate_turned(grad_turned, left, right):
    half = contract(grad_turned.astype(bf16), left, 1, 0).astype(bf16)
    return contract(turned(half), right, 1, 0)


def share_out(keep_ref, send_ref, parts, mats):
    half = keep_ref.shape[0]
    for ref, base in ((keep_ref, 0), (send_ref, half)):

        def body(block, ref=ref, base=base):
            collect(ref, block, parts, mats, source(block + base))

        each_block(half, body)


def early_turn_kernel(up_grad, down_grad, turned_ref, narrow_ref, wide_ref, keep_ref, send_ref, up, down):
    up[...] = rotate(turned_ref[3], up_grad[...], wide_ref[0])
    down[...] = rotate_turned(down_grad[...], wide_ref[1], narrow_ref[6])
    share_out(keep_ref, send_ref, layout(256, EARLY)[0], (up, down))


def middle_turn_kernel(
    h1_ref, dq_left, dq_right, out_grad, kn_ref, dkv_left, dkv_right, turned_ref, narrow_ref, pair_ref,
    query_ref, out_ref, keyval_ref, sums_ref, grad,
):
    dq = jnp.concatenate([dq_left[...], dq_right[...]], axis=1)
    query_ref[...] = rotate(turned_ref[0], contract(turned(h1_ref[...]), dq, 1, 0), narrow_ref[1])
    out_ref[...] = rotate(turned_ref[2], out_grad[...], narrow_ref[4])
    sums_ref[0:1, :] = col_sum(dq.astype(f32))
    sums_ref[2:8, :] = jnp.zeros((6, 256), f32)
    ones = jnp.ones((8, kn_ref.shape[0]), bf16)
    for group, ref in enumerate((dkv_left, dkv_right)):
        high, rest = two_parts(ref[...])
        found = contract(high, kn_ref[...], 1, 0) + contract(rest, kn_ref[...], 1, 0)
        grad[group * 128 : group * 128 + 128, :] = found[0:128]
        grad[256 + group * 128 : 256 + group * 128 + 128, :] = found[128:256]
        sums = contract(ones, high[128:256, :], 1, 1) + contract(ones, rest[128:256, :], 1, 1)
        sums_ref[1:2, group * 128 : group * 128 + 128] = sums[0:1]
    keyval_ref[...] = rotate_turned(grad[...], narrow_ref[2], pair_ref[...])


def back_outputs(group, dq_wide, dkv, keyval_ref, earlier, dq_ref, outs):
    dq_ref[...] = dq_wide[...].astype(bf16)
    keys = dkv.shape[1]
    span = keys if keys <= 1024 else keys // 8
    for start in range(0, keys, span):
        at = slice(start, start + span)
        high, rest = two_parts(dkv[:, at])
        total = earlier[0][:, at] if earlier else None
        for base, first in ((0, group * 128), (128, 256 + group * 128)):
            matrix = keyval_ref[:, first : first + 128]
            for part in (high, rest):
                term = contract(matrix, part[base : base + 128, :], 1, 0)
                total = term if total is None else total + term
        half = keys // 2
        if not earlier:
            outs[0][:, at] = total
        elif span == keys:
            outs[0][...] = total[:, 0:half].T
            outs[1][...] = total[:, half:].T
        else:
            outs[start // half][start % half : start % half + span, :] = total.T


def inner_sum(grad, out, mine):
    return jnp.sum(jnp.where(mine, grad.astype(f32) * out, 0.0), axis=1, keepdims=True)


def attend_back_kept_kernel(
    group, q_ref, k_ref, v_ref, o_ref, stat_ref, kept_ref, g_ref, keyval_ref, *refs
):
    earlier, (dq_ref, dkv, *outs), (dq_wide, dss, qt, gt) = refs[:group], refs[group:-4], refs[-4:]
    scale = 32**-0.5
    lane = lax.broadcasted_iota(jnp.int32, (1, 128), 1)
    cols = slice(group * 128, group * 128 + 128)
    grad = g_ref[:, cols]
    stats = [stat_ref[:, group * 4 + head : group * 4 + head + 1] for head in range(4)]
    spread_stats = stats[3]
    for head in range(3):
        spread_stats = jnp.where(lane // 32 == head, stats[head], spread_stats)
    qt[...] = turned(q_ref[:, cols])
    gt[...] = (grad.astype(f32) * spread_stats).T.astype(bf16)
    for head in range(4):
        mine = lane // 32 == head
        keys = jnp.where(mine, k_ref[:, cols], 0)
        values = jnp.where(mine, v_ref[:, cols], 0)
        inner = inner_sum(grad, o_ref[:, cols], mine)
        exponent = kept_ref[group * 4 + head]
        slope = (contract(grad, values, 1, 1) - inner) * stats[head]
        dss[...] = (exponent.astype(f32) * slope).astype(bf16)
        out = contract(dss[...], keys, 1, 0) * scale
        dq_wide[...] = jnp.where(mine, out, dq_wide[...])
        dkv[head_rows(head), :] = contract(qt[head_rows(head), :], dss[...], 1, 0) * scale
        dkv[head_rows(head, 128), :] = contract(gt[head_rows(head), :], exponent, 1, 0)
    back_outputs(group, dq_wide, dkv, keyval_ref, earlier, dq_ref, outs)


def attend_back_kernel(
    step, group, q_ref, k_ref, v_ref, mask_ref, o_ref, stat_ref, g_ref, keyval_ref, *refs
):
    earlier, (dq_ref, dkv, *outs), (dq_wide, ps, dss, qt, gt) = refs[:group], refs[group:-5], refs[-5:]
    tokens = q_ref.shape[0]
    scale = 32**-0.5
    lane = lax.broadcasted_iota(jnp.int32, (1, 128), 1)
    mask = mask_ref[...]
    cols = slice(group * 128, group * 128 + 128)
    qt[...] = turned(q_ref[:, cols])
    gt[...] = turned(g_ref[:, cols])

    def one_head(head):
        mine = lane // 32 == head
        keys = jnp.where(mine, k_ref[:, cols], 0)
        values = jnp.where(mine, v_ref[:, cols], 0)

        def block(start):
            rows = pl.ds(start, step)
            grad = g_ref[rows, cols]
            inner = inner_sum(grad, o_ref[rows, cols], mine)
            log = jnp.sum(jnp.where(lane == head + group * 4, stat_ref[rows, :], 0.0), axis=1, keepdims=True)
            scores = contract(q_ref[rows, cols], keys, 1, 1)
            probs = jnp.exp2(scores * (scale * LOG2E) + mask - log)
            grad_scores = (probs * (contract(grad, values, 1, 1) - inner)).astype(bf16)
            ps[rows, :] = probs.astype(bf16)
            dss[rows, :] = grad_scores
            out = contract(grad_scores, keys, 1, 0) * scale
            dq_wide[rows, :] = jnp.where(mine, out, dq_wide[rows, :])

        over_blocks(block, tokens, step)
        dkv[head_rows(head), :] = contract(qt[head_rows(head), :], dss[...], 1, 0) * scale
        dkv[head_rows(head, 128), :] = contract(gt[head_rows(head), :], ps[...], 1, 0)

    over_heads(one_head, 0, 4, False)
    back_outputs(group, dq_wide, dkv, keyval_ref, earlier, dq_ref, outs)


def total_of(refs):
    total = refs[0][...]
    for ref in refs[1:]:
        total = total + ref[...].astype(f32)
    return total


def split_kernel(count, terms, *refs):
    total = total_of(refs[:terms])
    rows = total.shape[0] // count
    refs[terms][...] = total[:rows]
    for index in range(1, count):
        refs[terms + index][...] = total[index * rows : (index + 1) * rows].astype(bf16)


def split_sum(terms, count, after=()):
    rows = terms[0].shape[0] // count
    tail = terms[0].shape[1:]
    outs = [((rows,) + tail, f32)] + [((rows,) + tail, bf16)] * (count - 1)
    return run("split_sum", functools.partial(split_kernel, count, len(terms)), outs, terms, micros=0.6, after=after)


def pair_total(values):
    while len(values) > 1:
        values = [a + b for a, b in zip(values[::2], values[1::2])]
    return values[0]


def two_parts(value):
    high = value.astype(bf16)
    return high, (value - high.astype(f32)).astype(bf16)


def sum_three(keeps, pieces):
    late, vec, early = [ref[...] for ref in keeps]
    rows, more = late.shape[0], vec.shape[0]
    vecs = [vec]
    for ref in pieces:
        late = late + ref[0:rows, :].astype(f32)
        vecs.append(ref[rows : rows + more, :].astype(f32))
        early = early + ref[rows + more :, :].astype(f32)
    return late, pair_total(vecs), early


def split_three_kernel(count, pieces, first, *refs):
    if first:
        late, vec, early = [refs[k][...] + refs[k + 1][...] for k in (0, 2, 4)]
        outs = refs[6:]
    else:
        late, vec, early = sum_three(refs[:3], refs[3 : 3 + pieces])
        outs = refs[3 + pieces :]
    rows, more, rest = late.shape[0] // count, vec.shape[0], early.shape[0] // count
    low = vec.astype(bf16)
    outs[0][...] = late[:rows]
    outs[1][...] = low.astype(f32)
    outs[2][...] = early[:rest]
    for index in range(1, count):
        ref = outs[2 + index]
        ref[0:rows, :] = late[index * rows : (index + 1) * rows].astype(bf16)
        ref[rows : rows + more, :] = low
        ref[rows + more :, :] = early[index * rest : (index + 1) * rest].astype(bf16)


def split_three(args, count, first, after=()):
    late, vec, early = args[0:6:2] if first else args[0:3]
    rows, more, rest, width = late.shape[0] // count, vec.shape[0], early.shape[0] // count, late.shape[1]
    outs = [((rows, width), f32), ((more, width), f32), ((rest, width), f32)]
    outs += [((rows + more + rest, width), bf16)] * (count - 1)
    body = functools.partial(split_three_kernel, count, len(args) - 3, first)
    found = run("split_three", body, outs, list(args), micros=0.6, after=after)
    return list(found[:3]), found[3:]


def row_parts():
    return [("row", stride, size) for stride, size in rel_digits()[1:]]


def one_by_one(groups):
    return [(axis, stride << bit, 2) for axis, stride, size in groups for bit in reversed(range(size.bit_length() - 1))]


def side_by_side(x, groups):
    for axis, stride, size in groups:
        x = jnp.concatenate([x] + [swap(x, axis, j * stride) for j in range(1, size)], axis=0)
    return x


def keys_back_kernel(terms, *refs):
    (c_ref, vec_ref, blocks_ref, narrow_ref, wide_ref, query, out, keyval,
     keep_ref, send_ref, dc_ref, sums_ref, reduce) = refs[terms:]
    dkn = total_of(refs[:terms])
    unit, inverse = norm_parts(c_ref[...])
    back, gain_sum, bias_sum = norm_back(dkn, unit, inverse, vec_ref[14:15, :])
    dc = back.astype(bf16)
    dc_ref[...] = dc
    reduce[...] = rotate_turned(contract(turned(dc), blocks_ref[...], 1, 0), wide_ref[2], narrow_ref[7])
    share_out(keep_ref, send_ref, layout(256, LATE)[0], (reduce, keyval, query, out))
    sums_ref[0:1, :] = col_sum(dc.astype(f32))
    sums_ref[1:2, :] = gain_sum
    sums_ref[2:3, :] = bias_sum


def cells_back_kernel(
    tile_rows, cols, size_ref, dq_left, dq_right, dc_ref, query_ref, reduce_ref, x0_ref, dx1_ref, vec_ref, tile_ref, up_ref, down_ref,
    feed_sums, key_sums, query_sums, dx0_ref, head_ref, tail_ref, sums_ref, frame,
):
    tokens = x0_ref.shape[0]
    dh1 = contract(dq_left[...], query_ref[:, 0:128], 1, 1) + contract(dq_right[...], query_ref[:, 128:256], 1, 1)
    for corner in range(4):
        pick = picked_cells((tokens, dc_ref.shape[0]), 0, size_ref, corner, tile_rows, cols)
        placed = contract(pick, dc_ref[...], 1, 0).astype(bf16)
        dh1 = dh1 + contract(placed, reduce_ref[corner * 256 : corner * 256 + 256, :], 1, 1)
    unit, inverse = norm_parts(x0_ref[...])
    back, gain_sum, bias_sum = norm_back(dh1, unit, inverse, vec_ref[10:11, :])
    dx0 = dx1_ref[...] + back
    dx0_ref[...] = dx0
    head_ref[...] = dx0[0:64].astype(bf16)
    tail_ref[...] = dx0[tokens - 64 :].astype(bf16)
    sums_ref[0:25, :] = feed_sums[...]
    sums_ref[25:32, :] = jnp.zeros((7, 256), f32)
    moved = shifted_frame(frame, tile_ref, up_ref, down_ref)
    grid = dx0.reshape(tile_rows, cols, 256)
    for tap in range(9):
        product = moved[tap % 3][tap // 3 : tap // 3 + tile_rows] * grid
        sums_ref[tap : tap + 1, :] = col_sum(product.reshape(tokens, 256))
    sums_ref[9:10, :] = col_sum(dx0)
    sums_ref[10:11, :] = gain_sum
    sums_ref[11:12, :] = bias_sum
    sums_ref[12:13, :] = query_sums[0:1, :]
    sums_ref[13:16, :] = key_sums[...]
    sums_ref[16:17, :] = query_sums[1:2, :]


def input_grad_kernel(tile_rows, dx0_ref, up_ref, down_ref, vec_ref, out_ref, token, frame):
    token[...] = jnp.zeros_like(token)
    moved = shifted_frame(frame, dx0_ref, up_ref, down_ref)
    total = moved[1][1:-1]
    for tap in range(9):
        down, right = 2 - tap // 3, 2 - tap % 3
        total = total + vec_ref[tap : tap + 1, :] * moved[right][down : down + tile_rows]
    out_ref[...] = total.reshape(out_ref.shape)


def moments_of(total, first, second, moment_ref, square_ref):
    moment = BETA * first + (1.0 - BETA) * total
    square = BETA * second + (1.0 - BETA) * total * total
    moment_ref[...] = moment
    square_ref[...] = square
    return moment * (1.0 / CORRECTION) / (jnp.sqrt(square * (1.0 / CORRECTION)) + ADAM_EPS)


def adam_kernel(terms, *refs):
    (first_ref, second_ref, vec_ref, vec_first, vec_second, vec_ema,
     moment_ref, square_ref, step_ref, vec_out, vec_first_out, vec_second_out, vec_ema_out) = refs[terms:]
    late, vec, early = sum_three(refs[:3], refs[3:terms])
    rows = late.shape[0]
    for total, at in ((late, slice(0, rows)), (early, slice(rows, rows + early.shape[0]))):
        step = moments_of(total, first_ref[at, :], second_ref[at, :], moment_ref.at[at, :], square_ref.at[at, :])
        step_ref[at, :] = step.astype(bf16)
    vec = vec[0 : vec_ref.shape[0]]
    new = vec_ref[...] - VECTOR_RATE * moments_of(vec, vec_first[...], vec_second[...], vec_first_out, vec_second_out)
    vec_out[...] = new
    vec_ema_out[...] = EMA_KEEP * vec_ema[...] + (1.0 - EMA_KEEP) * new


def both_groups(width):
    late, count = layout(width, LATE)
    return late + [(j, first + count, rows, blocks) for j, first, rows, blocks in layout(width, EARLY)[0]]


def products_kernel(width, chunks, own_narrow, own_wide, keep_ref, send_ref):
    lefts = {0: (own_narrow, 0), 1: (own_narrow, 1), 2: (own_narrow, 2), 3: (own_narrow, 3), 4: (own_wide, 0), 5: (own_wide, 1)}
    half = keep_ref.shape[0]
    values = chunks[...].astype(f32)
    for j, first, rows, blocks in both_groups(width):
        left = lefts[j][0][lefts[j][1]].astype(bf16)
        for col in range(blocks):
            at = slice(first + col * rows, first + (col + 1) * rows)
            part = values[:, at, :].reshape(left.shape[1], width).astype(bf16)
            side = contract(left, part, 1, 0).reshape(2 * half, rows, width)
            keep_ref[:, at, :] = side[:half]
            send_ref[:, at, :] = side[half:]


def finish_kernel(
    width, terms, *refs
):
    narrow_ref, pair_ref, wide_ref, weights_ref, ema_ref, weights_out, ema_out, chunk = refs[terms:]
    rights = {0: narrow_ref.at[1], 1: pair_ref, 2: narrow_ref.at[4], 3: wide_ref.at[0], 4: narrow_ref.at[6], 5: narrow_ref.at[7]}
    sides = total_of(refs[:terms])
    for j, first, rows, blocks in both_groups(width):
        parts = [sides[first + col * rows : first + (col + 1) * rows] for col in range(blocks)]
        side = parts[0] if blocks == 1 else jnp.concatenate(parts, axis=1)
        if rows < 8:
            side = jnp.concatenate([side, jnp.zeros((8 - rows, side.shape[1]), f32)], axis=0)
        full = contract(side.astype(bf16), rights[j][...], 1, 1)
        for col in range(blocks):
            at = slice(first + col * rows, first + (col + 1) * rows)
            old = weights_ref[at, :]
            piece = full[0:rows, col * width : (col + 1) * width]
            chunk[at, :] = old - MATRIX_RATES[j] * (piece + WEIGHT_DECAY * old)
    from_chunk(chunk, weights_out, width)
    chunk[...] = EMA_KEEP * ema_ref[...] + (1.0 - EMA_KEEP) * chunk[...]
    from_chunk(chunk, ema_out, width)


def packed_moments_kernel(width, moment_ref, square_ref, first_out, second_out, token):
    token[...] = jnp.zeros_like(token)
    from_chunk(moment_ref, first_out, width)
    from_chunk(square_ref, second_out, width)


def on_device(
    patches,
    cotangent,
    image_sizes,
    weights,
    first_moment,
    second_moment,
    weight_ema,
    vectors,
    vec_first,
    vec_second,
    vec_ema,
    basis_narrow,
    basis_pair,
    basis_wide,
):
    _, rows, cols, width = patches.shape
    tokens = rows * cols
    shards = device_count()
    tile = patches.reshape(tokens, width)
    dy = cotangent.reshape(tokens, width)
    per = weights.shape[1]
    late_rows, early_rows = layout(width, LATE)[1], layout(width, EARLY)[1]
    chunk = late_rows + early_rows
    ranks = lax.axis_size("row")
    own_keys = tokens // 4
    keys = own_keys * ranks
    frame = ((rows + 2, cols + 16, width), f32)
    img_part = ("img", 1, lax.axis_size("img"))
    xy_parts = row_parts()

    def border(head, tail):
        up = lax.ppermute(tail, "row", [(i, i + 1) for i in range(ranks - 1)])
        return up, lax.ppermute(head, "row", [(i + 1, i) for i in range(ranks - 1)])

    gather_groups = xy_parts[::-1]
    lines = lax.axis_size("img")

    (packed,) = run(
        "pack",
        functools.partial(pack_kernel, width),
        [((chunk, width), bf16)],
        [weights],
        scratch=[((chunk, width), f32)],
    )
    line = join([packed[None]] + [swap(packed, "img", j)[None] for j in range(1, lines)])
    up_halo, down_halo = border(tile[:64], tile[tokens - 64 :])
    x0, h1, mask, vec, sizes = run(
        "front",
        functools.partial(front_kernel, rows, cols),
        [((tokens, width), f32), ((tokens, width), bf16), ((1, keys), f32), (vectors.shape, f32), ((8, 128), jnp.int32)],
        [image_sizes, tile, up_halo, down_halo, vectors],
        scratch=[frame],
        scalars=(0,),
        micros=1.3,
        after=[line],
    )
    wide, wide_done = run(
        "wide_bases",
        wide_bases_kernel,
        [((3, FF, FF), bf16), ((8, 128), f32)],
        [basis_wide],
        micros=6.0,
        after=[line],
    )
    all_near = line
    for axis, stride, size in gather_groups:
        pieces = [all_near] + [swap(all_near, axis, j * stride) for j in range(1, size)]
        all_near = join(pieces, after=[wide_done, vec])
    all_far = swap(all_near, "row", 1)
    w_reduce, w_keyval, w_query, w_out, blocks, c, kn = run(
        "keys",
        functools.partial(keys_kernel, rows, cols),
        [
            ((4 * width, width), bf16),
            ((width, 2 * width), bf16),
            ((width, width), bf16),
            ((width, width), bf16),
            ((own_keys, 4 * width), bf16),
            ((own_keys, width), f32),
            ((own_keys, width), bf16),
        ],
        [sizes, h1, vec, all_near, all_far],
        scratch=[((4 * width, width), f32), ((width, 2 * width), f32), ((width, width), f32), ((width, width), f32)],
        micros=1.5,
    )
    narrow, narrow_turned, pair, own_narrow = run(
        "narrow_bases",
        narrow_bases_kernel,
        [
            ((8, width, width), bf16),
            ((4, width, width), bf16),
            ((2 * width, 2 * width), bf16),
            ((4, width // lines, width // ranks), f32),
        ],
        [basis_narrow, basis_pair],
        micros=1.5,
        after=[kn],
    )
    kn_near = side_by_side(kn, gather_groups)
    kn_far = swap(kn_near, "row", 1)

    unroll = keys <= 1024
    step = tokens if unroll else 32
    kn_all, q, k, v, o, stat, *kept = run(
        "attend",
        functools.partial(attend_kernel, step, unroll),
        [((keys, width), bf16), ((tokens, width), bf16), ((keys, width), bf16), ((keys, width), bf16)]
        + [((tokens, width), f32), ((tokens, 128), f32)]
        + ([((HEADS, tokens, keys), bf16)] if unroll else []),
        [h1, w_query, w_keyval, vec, kn_near, kn_far, mask],
        mib=8 if unroll else 44,
        micros=8.0,
        after=[own_narrow],
    )
    y, do, dx1, up_grad, down_grad, out_grad, feed_sums = run(
        "feed",
        feed_kernel,
        [
            ((tokens, width), bf16),
            ((tokens, width), bf16),
            ((tokens, width), f32),
            ((width, FF), f32),
            ((width, FF), f32),
            ((width, width), f32),
            (vectors.shape, f32),
        ],
        [o, x0, w_out, all_near, all_far, vec, dy],
        scratch=[((width, FF), bf16), ((FF, width), bf16), ((width, FF), f32), ((FF, width), f32)],
        mib=12,
        micros=3.5,
    )
    def back(group, earlier):
        if kept:
            body, args, more = functools.partial(attend_back_kept_kernel, group), [q, k, v, o, stat, kept[0]], []
        else:
            body, args = functools.partial(attend_back_kernel, step, group), [q, k, v, mask, o, stat]
            more = [((tokens, keys), bf16)]
        halves = [((keys // 2, width), f32)] * 2 if earlier else [((width, keys), f32)]
        return run(
            "attend_back",
            body,
            [((tokens, 128), bf16), ((width, keys), f32)] + halves,
            args + [do, w_keyval] + earlier,
            scratch=[((tokens, 128), f32)]
            + more
            + [((tokens, keys), bf16), ((128, tokens), bf16), ((128, tokens), bf16)],
            mib=14 if kept else 60,
            micros=5.0,
            after=[dx1],
        )

    dq_left, dkv_left, dkn_left = back(0, [])
    dq_right, dkv_right, dkn_keep, dkn_send = back(1, [dkn_left])
    dkn_got = swap(dkn_send, "row", 1)
    half = (shards // 2, early_rows, width)
    early_keep, early_send = run(
        "early_turn",
        early_turn_kernel,
        [(half, f32), (half, f32)],
        [up_grad, down_grad, narrow_turned, narrow, wide],
        scratch=[((width, FF), f32), ((FF, width), f32)],
        mib=10,
        micros=2.0,
        after=[dq_right],
    )
    early_got = swap(early_send, "row", 1)
    dkn_terms = [dkn_keep, dkn_got]
    for axis, stride, size in xy_parts:
        part, *sends = split_sum(dkn_terms, size, [early_keep])
        dkn_terms = [part] + [swap(x, axis, j * stride) for j, x in enumerate(sends, 1)]
    old_chunk, ema_chunk, first_chunk, second_chunk = run(
        "moments",
        functools.partial(moments_kernel, width),
        [((chunk, width), f32)] * 4,
        [jnp.concatenate([weights, weight_ema, first_moment, second_moment], axis=0)],
        after=[part],
    )
    query_turn, out_turn, keyval_turn, query_sums = run(
        "middle_turn",
        middle_turn_kernel,
        [((width, width), f32), ((width, width), f32), ((width, 2 * width), f32), ((8, width), f32)],
        [h1, dq_left, dq_right, out_grad, kn_all, dkv_left, dkv_right, narrow_turned, narrow, pair],
        scratch=[((2 * width, width), f32)],
        micros=1.5,
        mib=12 if kept else 40,
        after=[part],
    )
    half = (shards // 2, late_rows, width)
    late_keep, late_send, dc, key_sums = run(
        "keys_back",
        functools.partial(keys_back_kernel, len(dkn_terms)),
        [(half, f32), (half, f32), ((own_keys, width), bf16), ((3, width), f32)],
        list(dkn_terms) + [c, vec, blocks, narrow, wide, query_turn, out_turn, keyval_turn],
        scratch=[((4 * width, width), f32)],
        micros=2.0,
        after=[old_chunk],
    )
    late_got = swap(late_send, "row", 1)
    dx0, head, tail, vec_grads = run(
        "cells_back",
        functools.partial(cells_back_kernel, rows, cols),
        [((tokens, width), f32), ((64, width), bf16), ((64, width), bf16), ((32, width), f32)],
        [
            sizes, dq_left, dq_right, dc, w_query, w_reduce, x0, dx1, vec, tile, up_halo, down_halo,
            feed_sums, key_sums, query_sums,
        ],
        scratch=[frame],
        micros=2.0,
    )
    grad_up, grad_down = border(head, tail)
    args = [late_keep, late_got, vec_grads, swap(vec_grads, "row", 1), early_keep, early_got]
    args = [x.reshape(-1, width) for x in args]
    for index, (axis, stride, size) in enumerate(xy_parts + [img_part]):
        keeps, sends = split_three(args, size, index == 0, [grad_up, grad_down] if index else [])
        args = keeps + [swap(x, axis, j * stride) for j, x in enumerate(sends, 1)]
    grad_input, input_done = run(
        "input_grad",
        functools.partial(input_grad_kernel, rows),
        [((tokens, width), f32), ((8, 128), f32)],
        [dx0, grad_up, grad_down, vec],
        scratch=[frame],
        micros=1.5,
        after=[keeps[1]],
    )
    moments, squares, step, new_vectors, vec_moment, vec_square, new_vec_ema = run(
        "adam",
        functools.partial(adam_kernel, len(args)),
        [((chunk, width), f32), ((chunk, width), f32), ((chunk, width), bf16)] + [(vectors.shape, f32)] * 4,
        args + [first_chunk, second_chunk, vec, vec_first, vec_second, vec_ema],
        micros=0.8,
        after=[input_done],
    )
    (own_wide,) = run(
        "own_wide",
        own_wide_kernel,
        [((2, FF // lines, FF // ranks), f32)],
        [wide],
        micros=1.5,
        after=[step],
    )
    new_first, new_second, packed_done = run(
        "packed_moments",
        functools.partial(packed_moments_kernel, width),
        [((1, per), f32), ((1, per), f32), ((8, 128), f32)],
        [moments, squares],
        after=[own_wide],
    )
    steps = join([step[None]] + [swap(step, "img", j)[None] for j in range(1, lines)], [packed_done])
    half = (ranks // 2, chunk, width)
    keep, send = run(
        "products",
        functools.partial(products_kernel, width),
        [(half, f32), (half, f32)],
        [steps, own_narrow, own_wide],
        micros=1.0,
    )
    terms = [keep.reshape(-1, width), swap(send, "row", 1).reshape(-1, width)]
    for index, (axis, stride, size) in enumerate(xy_parts):
        part, *sends = split_sum(terms, size)
        terms = [part] + [swap(x, axis, j * stride) for j, x in enumerate(sends, 1)]
    new_weights, new_ema = run(
        "finish",
        functools.partial(finish_kernel, width, len(terms)),
        [((1, per), f32)] * 2,
        list(terms) + [narrow, pair, wide, old_chunk, ema_chunk],
        scratch=[((chunk, width), f32)],
        micros=1.5,
    )
    return (
        y.reshape(patches.shape),
        grad_input.reshape(patches.shape),
        new_weights,
        new_first,
        new_second,
        new_ema,
        new_vectors,
        vec_moment,
        vec_square,
        new_vec_ema,
    )


def solution(mesh):
    tiles = P("img", "row", None, None)
    packed = P(("img", "row"), None)
    return jax.shard_map(
        on_device,
        mesh=mesh,
        in_specs=(tiles, tiles, P("img", None)) + (packed,) * 4 + (P(),) * 7,
        out_specs=(tiles, tiles) + (packed,) * 4 + (P(),) * 4,
        check_vma=False,
    )
```

```python
import functools
import math

import jax
import jax.numpy as jnp
from jax import lax
from jax.experimental import pallas as pl
from jax.experimental.pallas import tpu as pltpu
from jax.sharding import PartitionSpec as P

HEADS = 8
FF = 1024
STEP = 5

NORM_EPS = 1e-05
ADAM_EPS = 1e-08
BETA = 0.5
WEIGHT_DECAY = 0.05
EMA_KEEP = 0.75
VECTOR_RATE = 0.06
MATRIX_RATES = (0.04, 0.02, 0.25, 0.02, 0.01, 0.01)
CORRECTION = 1.0 - BETA**STEP
LOG2E = math.log2(math.e)
f32 = jnp.float32
bf16 = jnp.bfloat16
LATE = (5, 1, 0, 2)
EARLY = (3, 4)


def matrix_shapes(width, hidden):
    return (
        (width, width),
        (width, 2 * width),
        (width, width),
        (width, hidden),
        (hidden, width),
        (4 * width, width),
    )


def contract(a, b, ca, cb, **kw):
    return lax.dot_general(
        a, b, (((ca,), (cb,)), ((), ())), preferred_element_type=f32, **kw
    )


def swap(x, axis, step):
    count = lax.axis_size(axis)
    return lax.ppermute(x, axis, [(i, i ^ step) for i in range(count)])


def row_groups():
    left = lax.axis_size("row") // 2
    groups, stride = [(1, 2)], 2
    while left > 1:
        size = 4 if left % 4 == 0 else 2
        groups.append((stride, size))
        left //= size
        stride *= size
    return groups


def rel_digits():
    groups = row_groups()
    return [groups[0]] + groups[1:][::-1]


def source(block):
    sizes = lax.axis_size("img")
    img, rest = block % sizes, block // sizes
    rel = 0
    for stride, size in reversed(rel_digits()):
        rel = rel + (rest % size) * stride
        rest = rest // size
    row = lax.axis_index("row") ^ rel
    return (lax.axis_index("img") ^ img) * lax.axis_size("row") + row


def device_count():
    return lax.axis_size("img") * lax.axis_size("row")


def run(name, body, outs, args, scratch=(), mib=6, scalars=(), micros=1.0, after=(), raw=(), sems=0):
    count = len(args)

    def without(*refs):
        body(*refs[:count], *refs[count + len(after) :])

    space = {index: pltpu.SMEM for index in scalars} | {index: pltpu.HBM for index in raw}
    specs = [pl.BlockSpec(memory_space=space.get(index, pltpu.VMEM)) for index in range(count)]
    return pl.pallas_call(
        without,
        out_shape=tuple(jax.ShapeDtypeStruct(shape, dtype) for shape, dtype in outs),
        in_specs=specs + [pl.BlockSpec(memory_space=pl.ANY)] * len(after),
        out_specs=tuple(pl.BlockSpec(memory_space=pltpu.VMEM) for _ in outs),
        scratch_shapes=[pltpu.VMEM(shape, dtype) for shape, dtype in scratch]
        + ([pltpu.SemaphoreType.DMA((sems,))] if sems else []),
        compiler_params=pltpu.CompilerParams(vmem_limit_bytes=mib * 2**20),
        cost_estimate=pl.CostEstimate(flops=0, bytes_accessed=int(micros * 3.6e6), transcendentals=0),
        name=name,
    )(*args, *after)


def each_block(count, body):
    if count <= 32:
        for index in range(count):
            body(index)
    else:

        def step(index, carry):
            body(index)
            return carry

        lax.fori_loop(0, count, step, 0)


def put_rows(ref, start, cols, value):
    count = value.shape[0]
    if count % 8 == 0:
        ref[pl.ds(pl.multiple_of(start, 8), count), cols] = value
    else:
        for row in range(count):
            ref[pl.ds(start + row, 1), cols] = value[row : row + 1]


def get_rows(ref, start, count, cols):
    if count % 8 == 0:
        return ref[pl.ds(pl.multiple_of(start, 8), count), cols]
    return jnp.concatenate([ref[pl.ds(start + row, 1), cols] for row in range(count)], axis=0)


def layout(width, group):
    dims = matrix_shapes(width, FF)
    found, start = [], 0
    for j in group:
        rows = dims[j][0] // device_count()
        blocks = dims[j][1] // width
        found.append((j, start, rows, blocks))
        start += rows * blocks
    return found, start


def packed_starts(width):
    dims = matrix_shapes(width, FF)
    starts, start = [], 0
    for m, n in dims:
        starts.append(start)
        start += m * n // device_count()
    return starts


def spread(block, parts, mats, start_of):
    for (j, first, rows, blocks), ref in zip(parts, mats):
        for col in range(blocks):
            piece = block[first + col * rows : first + (col + 1) * rows]
            put_rows(ref, start_of * rows, slice(col * 256, col * 256 + 256), piece)


def collect(out_ref, index, parts, mats, start_of):
    for (j, first, rows, blocks), ref in zip(parts, mats):
        for col in range(blocks):
            piece = get_rows(ref, start_of * rows, rows, slice(col * 256, col * 256 + 256))
            out_ref[index, first + col * rows : first + (col + 1) * rows, :] = piece


def norm_parts(values):
    centred = values - jnp.mean(values, axis=-1, keepdims=True)
    inverse = lax.rsqrt(jnp.mean(centred * centred, axis=-1, keepdims=True) + NORM_EPS)
    return centred * inverse, inverse


def norm_back(grad, unit, inverse, gain):
    grad_unit = grad * gain
    back = grad_unit - jnp.mean(grad_unit, axis=-1, keepdims=True)
    back = back - unit * jnp.mean(grad_unit * unit, axis=-1, keepdims=True)
    gain_sum = jnp.sum(grad * unit, axis=0, keepdims=True)
    return back * inverse, gain_sum, jnp.sum(grad, axis=0, keepdims=True)


def turned(value):
    return value.astype(f32).T.astype(bf16)


def col_sum(value):
    return jnp.sum(value, axis=0, keepdims=True)


def pack_kernel(width, w_ref, out_ref, chunk):
    to_chunk(w_ref, chunk, width)
    out_ref[...] = chunk[...].astype(bf16)


def to_chunk(flat_ref, out_ref, width, index=0):
    dims, starts, base = matrix_shapes(width, FF), packed_starts(width), 0
    for group in (LATE, EARLY):
        parts, count = layout(width, group)
        for j, first, rows, blocks in parts:
            for col in range(blocks):
                for row in range(rows):
                    at = starts[j] + row * dims[j][1] + col * width
                    place = base + first + col * rows + row
                    out_ref[place : place + 1, :] = flat_ref[index : index + 1, at : at + width]
        base += count


def from_chunk(values, out_ref, width):
    dims, starts = matrix_shapes(width, FF), packed_starts(width)
    for j, first, rows, blocks in both_groups(width):
        for col in range(blocks):
            for row in range(rows):
                at = starts[j] + row * dims[j][1] + col * width
                place = first + col * rows + row
                out_ref[0:1, at : at + width] = values[place : place + 1, :]


def moments_kernel(width, rows_ref, *outs):
    for index, ref in enumerate(outs):
        to_chunk(rows_ref, ref, width, index)


def left_block(matrix_ref, out_ref):
    lines, ranks = lax.axis_size("img"), lax.axis_size("row")
    size = matrix_ref.shape[0]
    rows = size // (lines * ranks)
    img, row = lax.axis_index("img"), lax.axis_index("row")

    def one_hot(count, axis, start_of):
        shape = (count * rows, size) if axis == 0 else (size, count * rows)
        place = lax.broadcasted_iota(jnp.int32, tuple(n if d == axis else 1 for d, n in enumerate(shape)), axis)
        block = place >> (rows.bit_length() - 1)
        target = start_of(block) * rows + (place & (rows - 1))
        return (lax.broadcasted_iota(jnp.int32, shape, 1 - axis) == target).astype(f32).astype(bf16)

    def owner(block):
        rel = jnp.zeros_like(block)
        for stride, count in reversed(rel_digits()):
            rel = rel + (block & (count - 1)) * stride
            block = block >> (count.bit_length() - 1)
        return img * ranks + (rel ^ row)

    mine = contract(one_hot(ranks, 0, owner), matrix_ref[...], 1, 0).astype(bf16)
    out_ref[...] = contract(mine, one_hot(lines, 1, lambda block: (block ^ img) * ranks + row), 1, 0)


def narrow_bases_kernel(narrow_ref, pair_ref, narrow_out, turned_out, pair_out, own_ref):
    narrow_out[...] = narrow_ref[...].astype(bf16)
    pair_out[...] = pair_ref[...].astype(bf16)
    for index, j in enumerate((0, 2, 3, 5)):
        turned_out[index] = narrow_ref[j].T.astype(bf16)
        left_block(narrow_out.at[j], own_ref.at[index])


def own_wide_kernel(wide_ref, own_ref):
    for index in range(2):
        left_block(wide_ref.at[index + 1], own_ref.at[index])


def wide_bases_kernel(wide_ref, wide_out, token):
    for index in range(wide_ref.shape[0]):
        wide_out[index] = wide_ref[index].astype(bf16)
    token[...] = jnp.zeros_like(token)


def join_kernel(*refs):
    start = 0
    for ref in refs[-2::-1]:
        refs[-1][start : start + ref.shape[0]] = ref[...]
        start += ref.shape[0]


def join(pieces, after=()):
    shape = (sum(x.shape[0] for x in pieces),) + pieces[0].shape[1:]
    return run("join", join_kernel, [(shape, pieces[0].dtype)], list(pieces)[::-1], micros=0.4, after=after)[0]


def unpack(pieces, group, mats, base=0):
    parts = [(j, first + base, rows, blocks) for j, first, rows, blocks in layout(256, group)[0]]
    done = 0
    for piece in pieces:

        def body(block, piece=piece, done=done):
            spread(piece[block].astype(f32), parts, mats, source(block + done))

        each_block(piece.shape[0], body)
        done += piece.shape[0]


def shifted_frame(frame_ref, tile_ref, up_ref, down_ref):
    rows, cols, width = frame_ref.shape[0] - 2, 56, 256
    frame_ref[...] = jnp.zeros_like(frame_ref)
    frame_ref[0, 8 : 8 + cols, :] = up_ref[...].astype(f32)[-cols:]
    frame_ref[1 : 1 + rows, 8 : 8 + cols, :] = tile_ref[...].astype(f32).reshape(rows, cols, width)
    frame_ref[rows + 1, 8 : 8 + cols, :] = down_ref[...].astype(f32)[:cols]
    return [frame_ref[:, 7 + shift : 7 + shift + cols, :] for shift in range(3)]


def front_kernel(tile_rows, cols, size_ref, tile_ref, up_ref, down_ref, vec_ref, x0_ref, h1_ref, mask_ref, vec_out, size_out, frame):
    rows = frame.shape[0] - 2
    vec_out[...] = vec_ref[...]
    size_out[...] = jnp.where(lax.broadcasted_iota(jnp.int32, size_out.shape, 0) == 0, size_ref[0, 0], size_ref[0, 1])
    moved = shifted_frame(frame, tile_ref, up_ref, down_ref)
    total = moved[1][1:-1] + vec_ref[9:10, :]
    for tap in range(9):
        total = total + vec_ref[tap : tap + 1, :] * moved[tap % 3][tap // 3 : tap // 3 + rows]
    x0 = total.reshape(x0_ref.shape)
    x0_ref[...] = x0
    unit, _ = norm_parts(x0)
    h1_ref[...] = (unit * vec_ref[10:11, :] + vec_ref[11:12, :]).astype(bf16)
    half = cols // 2
    own = tile_rows // 2 * half
    key = lax.broadcasted_iota(jnp.int32, mask_ref.shape, 1)
    block = jnp.zeros_like(key)
    for start in range(own, mask_ref.shape[1], own):
        block = block + (key >= start).astype(jnp.int32)
    key = key - block * own
    row = jnp.zeros_like(key)
    for start in range(half, own, half):
        row = row + (key >= start).astype(jnp.int32)
    col = key - row * half
    rel = jnp.zeros_like(key)
    for stride, size in reversed(rel_digits()):
        rel = rel + (block & (size - 1)) * stride
        block = block >> (size.bit_length() - 1)
    row = row + (rel ^ lax.axis_index("row")) * (tile_rows // 2)
    inside = (2 * row < size_ref[0, 0]) & (2 * col < size_ref[0, 1])
    mask_ref[...] = jnp.where(inside, 0.0, -1e30)


def picked_cells(shape, cell_axis, size_ref, corner, tile_rows, cols):
    half = cols // 2
    key_shape = tuple(1 if axis == cell_axis else n for axis, n in enumerate(shape))
    key = lax.broadcasted_iota(jnp.int32, key_shape, 1 - cell_axis)
    row = jnp.zeros_like(key)
    for step in range(1, tile_rows // 2):
        row = row + (key >= step * half).astype(jnp.int32)
    col = 2 * (key - row * half) + corner % 2
    row = 2 * row + corner // 2
    inside = (row + lax.axis_index("row") * tile_rows < size_ref[0:1, 0:1]) & (col < size_ref[1:2, 0:1])
    target = jnp.where(inside, row * cols + col, -1)
    cell = lax.broadcasted_iota(jnp.int32, shape, cell_axis)
    return (cell == target).astype(f32).astype(bf16)


def keys_kernel(
    tile_rows, cols, size_ref, h1_ref, vec_ref, near_ref, far_ref,
    reduce_ref, keyval_ref, query_ref, out_ref, blocks_ref, c_ref, kn_ref,
    reduce_wide, keyval_wide, query_wide, out_wide,
):
    unpack((near_ref, far_ref), LATE, (reduce_wide, keyval_wide, query_wide, out_wide))
    reduce_ref[...] = reduce_wide[...].astype(bf16)
    keyval_ref[...] = keyval_wide[...].astype(bf16)
    query_ref[...] = query_wide[...].astype(bf16)
    out_ref[...] = out_wide[...].astype(bf16)
    keys = c_ref.shape[0]
    for corner in range(4):
        pick = picked_cells((keys, h1_ref.shape[0]), 1, size_ref, corner, tile_rows, cols)
        blocks_ref[:, corner * 256 : corner * 256 + 256] = contract(pick, h1_ref[...], 1, 0).astype(bf16)
    c = contract(blocks_ref[...], reduce_ref[...], 1, 0) + vec_ref[13:14, :]
    c_ref[...] = c
    unit, _ = norm_parts(c)
    kn = (unit * vec_ref[14:15, :] + vec_ref[15:16, :]).astype(bf16)
    kn_ref[...] = kn


def over_heads(body, first, last, unroll):
    if unroll:
        for head in range(first, last):
            body(head)
    else:

        def step(head, carry):
            body(head)
            return carry

        lax.fori_loop(first, last, step, 0)


def over_blocks(block, tokens, step):
    if tokens == step:
        block(0)
    else:

        def go(index, carry):
            block(pl.multiple_of(index * step, step))
            return carry

        lax.fori_loop(0, tokens // step, go, 0)


def head_columns(head):
    group = head // 4
    if isinstance(head, int):
        return slice(group * 128, group * 128 + 128)
    return pl.ds(pl.multiple_of(group * 128, 128), 128)


def head_rows(head, base=0):
    if isinstance(head, int):
        return slice(base + head * 32, base + head * 32 + 32)
    return pl.ds(pl.multiple_of(base + head * 32, 32), 32)


def attend_kernel(
    step, unroll, h1_ref, query_ref, keyval_ref, vec_ref, near_ref, far_ref, mask_ref,
    kn_ref, q_ref, k_ref, v_ref, o_ref, stat_ref, *kept
):
    tokens = h1_ref.shape[0]
    half = near_ref.shape[0]
    kn_ref[0:half, :] = near_ref[...]
    kn_ref[half:, :] = far_ref[...]
    k_ref[...] = contract(kn_ref[...], keyval_ref[:, 0:256], 1, 0).astype(bf16)
    v_ref[...] = (contract(kn_ref[...], keyval_ref[:, 256:512], 1, 0) + vec_ref[16:17, :]).astype(bf16)
    q_ref[...] = (contract(h1_ref[...], query_ref[...], 1, 0) + vec_ref[12:13, :]).astype(bf16)
    scale = 32**-0.5 * LOG2E
    lane = lax.broadcasted_iota(jnp.int32, (1, 128), 1)
    mask = mask_ref[...]

    def one_head(head):
        cols = head_columns(head)
        mine = lane // 32 == head % 4
        keys = jnp.where(mine, k_ref[:, cols], 0)
        ones = jnp.where(lane // 32 == (head + 2) % 4, 1.0, 0.0).astype(bf16)
        values = jnp.where(mine, v_ref[:, cols], ones)

        def block(start):
            rows = pl.ds(start, step)
            scores = contract(q_ref[rows, cols], keys, 1, 1) * scale + mask
            top = jnp.max(scores, axis=1, keepdims=True)
            exponent = jnp.exp2(scores - top).astype(bf16)
            if kept:
                kept[0][head] = exponent
            out = contract(exponent, values, 1, 0)
            if isinstance(head, int):
                total = out[:, (head + 2) % 4 * 32 : (head + 2) % 4 * 32 + 1]
            else:
                total = jnp.sum(jnp.where(lane == (head + 2) % 4 * 32, out, 0.0), axis=1, keepdims=True)
            inverse = 1.0 / total
            o_ref[rows, cols] = jnp.where(mine, out * inverse, o_ref[rows, cols])
            stat = inverse if kept else top + jnp.log2(total)
            stat_ref[rows, :] = jnp.where(lane == head, stat, stat_ref[rows, :])

        over_blocks(block, tokens, step)

    over_heads(one_head, 0, HEADS, unroll)


def feed_kernel(
    o_ref, x0_ref, out_ref, near_ref, far_ref, vec_ref, dy_ref,
    y_ref, do_ref, dx1_ref, up_grad, down_grad, out_grad, sums_ref, up_ref, down_ref, up_wide, down_wide,
):
    unpack((near_ref, far_ref), EARLY, (up_wide, down_wide), layout(256, LATE)[1])
    up_ref[...] = up_wide[...].astype(bf16)
    down_ref[...] = down_wide[...].astype(bf16)
    o = o_ref[...].astype(bf16)
    x1 = x0_ref[...] + (contract(o, out_ref[...], 1, 0) + vec_ref[17:18, :])
    unit, inverse = norm_parts(x1)
    h2 = (unit * vec_ref[18:19, :] + vec_ref[19:20, :]).astype(bf16)
    dy_low = dy_ref[...]
    dy = dy_low.astype(f32)
    dyt = turned(dy_low)
    h2t = turned(h2)
    y = x1 + vec_ref[20:21, :]
    dh2 = jnp.zeros_like(y)
    for col in range(FF // 256):
        cols = slice(col * 256, col * 256 + 256)
        u = contract(h2, up_ref[:, cols], 1, 0) + vec_ref[21 + col : 22 + col, :]
        phi_sum = 0.5 * (1.0 + lax.erf(u * (2.0**-0.5)))
        density = jnp.exp(-0.5 * u * u) * ((2.0 * math.pi) ** -0.5)
        g = (u * phi_sum).astype(bf16)
        y = y + contract(g, down_ref[cols, :], 1, 0)
        down_grad[:, cols] = contract(dyt, g, 1, 0)
        du = (contract(dy_low, down_ref[cols, :], 1, 1) * (phi_sum + u * density)).astype(bf16)
        up_grad[:, cols] = contract(h2t, du, 1, 0)
        sums_ref[21 + col : 22 + col, :] = col_sum(du.astype(f32))
        dh2 = dh2 + contract(du, up_ref[:, cols], 1, 1)
    y_ref[...] = y.astype(bf16)
    back, gain_sum, bias_sum = norm_back(dh2, unit, inverse, vec_ref[18:19, :])
    dx1 = dy + back
    dx1_ref[...] = dx1
    da = dx1.astype(bf16)
    do_ref[...] = contract(da, out_ref[...], 1, 1).astype(bf16)
    out_grad[...] = contract(turned(o), da, 1, 0)
    sums_ref[0:17, :] = jnp.zeros((17, 256), f32)
    sums_ref[17:18, :] = col_sum(da.astype(f32))
    sums_ref[18:19, :] = gain_sum
    sums_ref[19:20, :] = bias_sum
    sums_ref[20:21, :] = col_sum(dy)


def rotate(left_turned, grad, right):
    half = contract(left_turned, grad.astype(bf16), 1, 0).astype(bf16)
    return contract(half, right, 1, 0)


def rotate_turned(grad_turned, left, right):
    half = contract(grad_turned.astype(bf16), left, 1, 0).astype(bf16)
    return contract(turned(half), right, 1, 0)


def share_out(keep_ref, send_ref, parts, mats):
    half = keep_ref.shape[0]
    for ref, base in ((keep_ref, 0), (send_ref, half)):

        def body(block, ref=ref, base=base):
            collect(ref, block, parts, mats, source(block + base))

        each_block(half, body)


def early_turn_kernel(up_grad, down_grad, turned_ref, narrow_ref, wide_ref, keep_ref, send_ref, up, down):
    up[...] = rotate(turned_ref[3], up_grad[...], wide_ref[0])
    down[...] = rotate_turned(down_grad[...], wide_ref[1], narrow_ref[6])
    share_out(keep_ref, send_ref, layout(256, EARLY)[0], (up, down))


def middle_turn_kernel(
    h1_ref, dq_ref, out_grad, kn_ref, dkv_ref, turned_ref, narrow_ref, pair_ref, query_ref, out_ref, keyval_ref, sums_ref
):
    dq = dq_ref[...]
    query_ref[...] = rotate(turned_ref[0], contract(turned(h1_ref[...]), dq, 1, 0), narrow_ref[1])
    out_ref[...] = rotate(turned_ref[2], out_grad[...], narrow_ref[4])
    sums_ref[0:1, :] = col_sum(dq.astype(f32))
    sums_ref[2:8, :] = jnp.zeros((6, 256), f32)
    high, rest = two_parts(dkv_ref[...])
    ones = jnp.ones((8, kn_ref.shape[0]), bf16)
    sums = contract(ones, high[256:512, :], 1, 1) + contract(ones, rest[256:512, :], 1, 1)
    sums_ref[1:2, :] = sums[0:1]
    grad = contract(high, kn_ref[...], 1, 0) + contract(rest, kn_ref[...], 1, 0)
    keyval_ref[...] = rotate_turned(grad, narrow_ref[2], pair_ref[...])


def back_outputs(dq_wide, dkv, keyval_ref, dq_ref, keep_ref, send_ref):
    dq_ref[...] = dq_wide[...].astype(bf16)
    keys = dkv.shape[1]
    half = keys // 2
    span = keys if keys <= 1024 else keys // 8
    for start in range(0, keys, span):
        high, rest = two_parts(dkv[:, start : start + span])
        total = contract(keyval_ref[...], high, 1, 0) + contract(keyval_ref[...], rest, 1, 0)
        if span == keys:
            keep_ref[...] = total[:, 0:half].T
            send_ref[...] = total[:, half:].T
        else:
            out = (keep_ref, send_ref)[start // half]
            out[start % half : start % half + span, :] = total.T


def inner_sum(grad, out, mine):
    return jnp.sum(jnp.where(mine, grad.astype(f32) * out, 0.0), axis=1, keepdims=True)


def attend_back_kept_kernel(
    q_ref, k_ref, v_ref, o_ref, stat_ref, kept_ref, g_ref, keyval_ref,
    dq_ref, dkv, keep_ref, send_ref, dq_wide, dss, qt, gt,
):
    scale = 32**-0.5
    width = q_ref.shape[1]
    lane = lax.broadcasted_iota(jnp.int32, (1, 128), 1)
    qt[...] = turned(q_ref[...])
    for group in range(2):
        cols = slice(group * 128, group * 128 + 128)
        grad = g_ref[:, cols]
        stats = [stat_ref[:, group * 4 + head : group * 4 + head + 1] for head in range(4)]
        spread_stats = stats[3]
        for head in range(3):
            spread_stats = jnp.where(lane // 32 == head, stats[head], spread_stats)
        gt[cols, :] = (grad.astype(f32) * spread_stats).T.astype(bf16)
        for head in range(4):
            mine = lane // 32 == head
            keys = jnp.where(mine, k_ref[:, cols], 0)
            values = jnp.where(mine, v_ref[:, cols], 0)
            inner = inner_sum(grad, o_ref[:, cols], mine)
            rows = head_rows(group * 4 + head)
            exponent = kept_ref[group * 4 + head]
            slope = (contract(grad, values, 1, 1) - inner) * stats[head]
            dss[...] = (exponent.astype(f32) * slope).astype(bf16)
            out = contract(dss[...], keys, 1, 0) * scale
            dq_wide[:, cols] = jnp.where(mine, out, dq_wide[:, cols])
            dkv[rows, :] = contract(qt[rows, :], dss[...], 1, 0) * scale
            dkv[head_rows(group * 4 + head, width), :] = contract(gt[rows, :], exponent, 1, 0)
    back_outputs(dq_wide, dkv, keyval_ref, dq_ref, keep_ref, send_ref)


def attend_back_kernel(
    step, q_ref, k_ref, v_ref, mask_ref, o_ref, stat_ref, g_ref, keyval_ref,
    dq_ref, dkv, keep_ref, send_ref, dq_wide, dss, qt, gt, ps,
):
    tokens, width = q_ref.shape
    scale = 32**-0.5
    lane = lax.broadcasted_iota(jnp.int32, (1, 128), 1)
    mask = mask_ref[...]
    qt[...] = turned(q_ref[...])
    gt[...] = turned(g_ref[...])

    def one_head(head):
        cols = head_columns(head)
        mine = lane // 32 == head % 4
        keys = jnp.where(mine, k_ref[:, cols], 0)
        values = jnp.where(mine, v_ref[:, cols], 0)

        def block(start):
            rows = pl.ds(start, step)
            grad = g_ref[rows, cols]
            inner = inner_sum(grad, o_ref[rows, cols], mine)
            log = jnp.sum(jnp.where(lane == head, stat_ref[rows, :], 0.0), axis=1, keepdims=True)
            scores = contract(q_ref[rows, cols], keys, 1, 1)
            probs = jnp.exp2(scores * (scale * LOG2E) + mask - log)
            grad_scores = (probs * (contract(grad, values, 1, 1) - inner)).astype(bf16)
            ps[rows, :] = probs.astype(bf16)
            dss[rows, :] = grad_scores
            out = contract(grad_scores, keys, 1, 0) * scale
            dq_wide[rows, cols] = jnp.where(mine, out, dq_wide[rows, cols])

        over_blocks(block, tokens, step)
        dkv[head_rows(head), :] = contract(qt[head_rows(head), :], dss[...], 1, 0) * scale
        dkv[head_rows(head, width), :] = contract(gt[head_rows(head), :], ps[...], 1, 0)

    over_heads(one_head, 0, HEADS, False)
    back_outputs(dq_wide, dkv, keyval_ref, dq_ref, keep_ref, send_ref)


def total_of(refs):
    total = refs[0][...]
    for ref in refs[1:]:
        total = total + ref[...].astype(f32)
    return total


def split_kernel(count, terms, *refs):
    total = total_of(refs[:terms])
    rows = total.shape[0] // count
    refs[terms][...] = total[:rows]
    for index in range(1, count):
        refs[terms + index][...] = total[index * rows : (index + 1) * rows].astype(bf16)


def split_sum(terms, count, after=()):
    rows = terms[0].shape[0] // count
    tail = terms[0].shape[1:]
    outs = [((rows,) + tail, f32)] + [((rows,) + tail, bf16)] * (count - 1)
    return run("split_sum", functools.partial(split_kernel, count, len(terms)), outs, terms, micros=0.6, after=after)


def pair_total(values):
    while len(values) > 1:
        values = [a + b for a, b in zip(values[::2], values[1::2])]
    return values[0]


def two_parts(value):
    high = value.astype(bf16)
    return high, (value - high.astype(f32)).astype(bf16)


def sum_three(keeps, pieces):
    late, vec, early = [ref[...] for ref in keeps]
    rows, more = late.shape[0], vec.shape[0]
    vecs = [vec]
    for ref in pieces:
        late = late + ref[0:rows, :].astype(f32)
        vecs.append(ref[rows : rows + more, :].astype(f32))
        early = early + ref[rows + more :, :].astype(f32)
    return late, pair_total(vecs), early


def split_three_kernel(count, pieces, first, *refs):
    if first:
        late, vec, early = [refs[k][...] + refs[k + 1][...] for k in (0, 2, 4)]
        outs = refs[6:]
    else:
        late, vec, early = sum_three(refs[:3], refs[3 : 3 + pieces])
        outs = refs[3 + pieces :]
    rows, more, rest = late.shape[0] // count, vec.shape[0], early.shape[0] // count
    low = vec.astype(bf16)
    outs[0][...] = late[:rows]
    outs[1][...] = low.astype(f32)
    outs[2][...] = early[:rest]
    for index in range(1, count):
        ref = outs[2 + index]
        ref[0:rows, :] = late[index * rows : (index + 1) * rows].astype(bf16)
        ref[rows : rows + more, :] = low
        ref[rows + more :, :] = early[index * rest : (index + 1) * rest].astype(bf16)


def split_three(args, count, first, after=()):
    late, vec, early = args[0:6:2] if first else args[0:3]
    rows, more, rest, width = late.shape[0] // count, vec.shape[0], early.shape[0] // count, late.shape[1]
    outs = [((rows, width), f32), ((more, width), f32), ((rest, width), f32)]
    outs += [((rows + more + rest, width), bf16)] * (count - 1)
    body = functools.partial(split_three_kernel, count, len(args) - 3, first)
    found = run("split_three", body, outs, list(args), micros=0.6, after=after)
    return list(found[:3]), found[3:]


def row_parts():
    return [("row", stride, size) for stride, size in rel_digits()[1:]]


def one_by_one(groups):
    return [(axis, stride << bit, 2) for axis, stride, size in groups for bit in reversed(range(size.bit_length() - 1))]


def side_by_side(x, groups):
    for axis, stride, size in groups:
        x = jnp.concatenate([x] + [swap(x, axis, j * stride) for j in range(1, size)], axis=0)
    return x


def keys_back_kernel(terms, *refs):
    (c_ref, vec_ref, blocks_ref, narrow_ref, wide_ref, query, out, keyval,
     keep_ref, send_ref, dc_ref, sums_ref, reduce) = refs[terms:]
    dkn = total_of(refs[:terms])
    unit, inverse = norm_parts(c_ref[...])
    back, gain_sum, bias_sum = norm_back(dkn, unit, inverse, vec_ref[14:15, :])
    dc = back.astype(bf16)
    dc_ref[...] = dc
    reduce[...] = rotate_turned(contract(turned(dc), blocks_ref[...], 1, 0), wide_ref[2], narrow_ref[7])
    share_out(keep_ref, send_ref, layout(256, LATE)[0], (reduce, keyval, query, out))
    sums_ref[0:1, :] = col_sum(dc.astype(f32))
    sums_ref[1:2, :] = gain_sum
    sums_ref[2:3, :] = bias_sum


def cells_back_kernel(
    tile_rows, cols, size_ref, dq_ref, dc_ref, query_ref, reduce_ref, x0_ref, dx1_ref, vec_ref, tile_ref, up_ref, down_ref,
    feed_sums, key_sums, query_sums, dx0_ref, head_ref, tail_ref, sums_ref, frame,
):
    tokens = x0_ref.shape[0]
    dh1 = contract(dq_ref[...], query_ref[...], 1, 1)
    for corner in range(4):
        pick = picked_cells((tokens, dc_ref.shape[0]), 0, size_ref, corner, tile_rows, cols)
        placed = contract(pick, dc_ref[...], 1, 0).astype(bf16)
        dh1 = dh1 + contract(placed, reduce_ref[corner * 256 : corner * 256 + 256, :], 1, 1)
    unit, inverse = norm_parts(x0_ref[...])
    back, gain_sum, bias_sum = norm_back(dh1, unit, inverse, vec_ref[10:11, :])
    dx0 = dx1_ref[...] + back
    dx0_ref[...] = dx0
    head_ref[...] = dx0[0:64].astype(bf16)
    tail_ref[...] = dx0[tokens - 64 :].astype(bf16)
    sums_ref[0:25, :] = feed_sums[...]
    sums_ref[25:32, :] = jnp.zeros((7, 256), f32)
    moved = shifted_frame(frame, tile_ref, up_ref, down_ref)
    grid = dx0.reshape(tile_rows, cols, 256)
    for tap in range(9):
        product = moved[tap % 3][tap // 3 : tap // 3 + tile_rows] * grid
        sums_ref[tap : tap + 1, :] = col_sum(product.reshape(tokens, 256))
    sums_ref[9:10, :] = col_sum(dx0)
    sums_ref[10:11, :] = gain_sum
    sums_ref[11:12, :] = bias_sum
    sums_ref[12:13, :] = query_sums[0:1, :]
    sums_ref[13:16, :] = key_sums[...]
    sums_ref[16:17, :] = query_sums[1:2, :]


def input_grad_kernel(tile_rows, dx0_ref, up_ref, down_ref, vec_ref, out_ref, token, frame):
    token[...] = jnp.zeros_like(token)
    moved = shifted_frame(frame, dx0_ref, up_ref, down_ref)
    total = moved[1][1:-1]
    for tap in range(9):
        down, right = 2 - tap // 3, 2 - tap % 3
        total = total + vec_ref[tap : tap + 1, :] * moved[right][down : down + tile_rows]
    out_ref[...] = total.reshape(out_ref.shape)


def moments_of(total, first, second, moment_ref, square_ref):
    moment = BETA * first + (1.0 - BETA) * total
    square = BETA * second + (1.0 - BETA) * total * total
    moment_ref[...] = moment
    square_ref[...] = square
    return moment * (1.0 / CORRECTION) / (jnp.sqrt(square * (1.0 / CORRECTION)) + ADAM_EPS)


def adam_kernel(terms, *refs):
    (first_ref, second_ref, vec_ref, vec_first, vec_second, vec_ema,
     moment_ref, square_ref, step_ref, vec_out, vec_first_out, vec_second_out, vec_ema_out) = refs[terms:]
    late, vec, early = sum_three(refs[:3], refs[3:terms])
    rows = late.shape[0]
    for total, at in ((late, slice(0, rows)), (early, slice(rows, rows + early.shape[0]))):
        step = moments_of(total, first_ref[at, :], second_ref[at, :], moment_ref.at[at, :], square_ref.at[at, :])
        step_ref[at, :] = step.astype(bf16)
    vec = vec[0 : vec_ref.shape[0]]
    new = vec_ref[...] - VECTOR_RATE * moments_of(vec, vec_first[...], vec_second[...], vec_first_out, vec_second_out)
    vec_out[...] = new
    vec_ema_out[...] = EMA_KEEP * vec_ema[...] + (1.0 - EMA_KEEP) * new


def both_groups(width):
    late, count = layout(width, LATE)
    return late + [(j, first + count, rows, blocks) for j, first, rows, blocks in layout(width, EARLY)[0]]


def products_kernel(width, chunks, own_narrow, own_wide, keep_ref, send_ref, whole):
    lefts = {0: (own_narrow, 0), 1: (own_narrow, 1), 2: (own_narrow, 2), 3: (own_narrow, 3), 4: (own_wide, 0), 5: (own_wide, 1)}
    half = keep_ref.shape[0]
    values = chunks[...].astype(f32)
    for j, first, rows, blocks in both_groups(width):
        left = lefts[j][0][lefts[j][1]].astype(bf16)
        for col in range(blocks):
            at = slice(first + col * rows, first + (col + 1) * rows)
            part = values[:, at, :].reshape(left.shape[1], width).astype(bf16)
            side = contract(left, part, 1, 0).reshape(2 * half, rows, width)
            keep_ref[:, at, :] = side[:half]
            whole[:, at, :] = side[half:]
    send_ref[...] = whole[...].astype(bf16)


def finish_kernel(
    width, terms, *refs
):
    narrow_ref, pair_ref, wide_ref, weights_ref, ema_ref, weights_out, ema_out, chunk = refs[terms:]
    rights = {0: narrow_ref.at[1], 1: pair_ref, 2: narrow_ref.at[4], 3: wide_ref.at[0], 4: narrow_ref.at[6], 5: narrow_ref.at[7]}
    sides = total_of(refs[:terms])
    for j, first, rows, blocks in both_groups(width):
        parts = [sides[first + col * rows : first + (col + 1) * rows] for col in range(blocks)]
        side = parts[0] if blocks == 1 else jnp.concatenate(parts, axis=1)
        if rows < 8:
            side = jnp.concatenate([side, jnp.zeros((8 - rows, side.shape[1]), f32)], axis=0)
        full = contract(side.astype(bf16), rights[j][...], 1, 1)
        for col in range(blocks):
            at = slice(first + col * rows, first + (col + 1) * rows)
            old = weights_ref[at, :]
            piece = full[0:rows, col * width : (col + 1) * width]
            chunk[at, :] = old - MATRIX_RATES[j] * (piece + WEIGHT_DECAY * old)
    from_chunk(chunk, weights_out, width)
    chunk[...] = EMA_KEEP * ema_ref[...] + (1.0 - EMA_KEEP) * chunk[...]
    from_chunk(chunk, ema_out, width)


def packed_moments_kernel(width, moment_ref, square_ref, first_out, second_out, token):
    token[...] = jnp.zeros_like(token)
    from_chunk(moment_ref, first_out, width)
    from_chunk(square_ref, second_out, width)


def on_device(
    patches,
    cotangent,
    image_sizes,
    weights,
    first_moment,
    second_moment,
    weight_ema,
    vectors,
    vec_first,
    vec_second,
    vec_ema,
    basis_narrow,
    basis_pair,
    basis_wide,
):
    _, rows, cols, width = patches.shape
    tokens = rows * cols
    shards = device_count()
    tile = patches.reshape(tokens, width)
    dy = cotangent.reshape(tokens, width)
    per = weights.shape[1]
    late_rows, early_rows = layout(width, LATE)[1], layout(width, EARLY)[1]
    chunk = late_rows + early_rows
    ranks = lax.axis_size("row")
    own_keys = tokens // 4
    keys = own_keys * ranks
    frame = ((rows + 2, cols + 16, width), f32)
    img_part = ("img", 1, lax.axis_size("img"))
    xy_parts = row_parts()

    def border(head, tail):
        up = lax.ppermute(tail, "row", [(i, i + 1) for i in range(ranks - 1)])
        return up, lax.ppermute(head, "row", [(i + 1, i) for i in range(ranks - 1)])

    gather_groups = xy_parts[::-1]
    lines = lax.axis_size("img")

    (packed,) = run(
        "pack",
        functools.partial(pack_kernel, width),
        [((chunk, width), bf16)],
        [weights],
        scratch=[((chunk, width), f32)],
    )
    line = join([packed[None]] + [swap(packed, "img", j)[None] for j in range(1, lines)])
    up_halo, down_halo = border(tile[:64], tile[tokens - 64 :])
    x0, h1, mask, vec, sizes = run(
        "front",
        functools.partial(front_kernel, rows, cols),
        [((tokens, width), f32), ((tokens, width), bf16), ((1, keys), f32), (vectors.shape, f32), ((8, 128), jnp.int32)],
        [image_sizes, tile, up_halo, down_halo, vectors],
        scratch=[frame],
        scalars=(0,),
        micros=1.3,
        after=[line],
    )
    wide, wide_done = run(
        "wide_bases",
        wide_bases_kernel,
        [((3, FF, FF), bf16), ((8, 128), f32)],
        [basis_wide],
        micros=6.0,
        after=[line],
    )
    all_near = line
    for axis, stride, size in gather_groups:
        pieces = [all_near] + [swap(all_near, axis, j * stride) for j in range(1, size)]
        all_near = join(pieces, after=[wide_done, vec])
    all_far = swap(all_near, "row", 1)
    w_reduce, w_keyval, w_query, w_out, blocks, c, kn = run(
        "keys",
        functools.partial(keys_kernel, rows, cols),
        [
            ((4 * width, width), bf16),
            ((width, 2 * width), bf16),
            ((width, width), bf16),
            ((width, width), bf16),
            ((own_keys, 4 * width), bf16),
            ((own_keys, width), f32),
            ((own_keys, width), bf16),
        ],
        [sizes, h1, vec, all_near, all_far],
        scratch=[((4 * width, width), f32), ((width, 2 * width), f32), ((width, width), f32), ((width, width), f32)],
        micros=1.5,
    )
    narrow, narrow_turned, pair, own_narrow = run(
        "narrow_bases",
        narrow_bases_kernel,
        [
            ((8, width, width), bf16),
            ((4, width, width), bf16),
            ((2 * width, 2 * width), bf16),
            ((4, width // lines, width // ranks), f32),
        ],
        [basis_narrow, basis_pair],
        micros=1.5,
        after=[kn],
    )
    kn_near = side_by_side(kn, gather_groups)
    kn_far = swap(kn_near, "row", 1)

    unroll = keys <= 1024
    step = tokens if unroll else 32
    kn_all, q, k, v, o, stat, *kept = run(
        "attend",
        functools.partial(attend_kernel, step, unroll),
        [((keys, width), bf16), ((tokens, width), bf16), ((keys, width), bf16), ((keys, width), bf16)]
        + [((tokens, width), f32), ((tokens, 128), f32)]
        + ([((HEADS, tokens, keys), bf16)] if unroll else []),
        [h1, w_query, w_keyval, vec, kn_near, kn_far, mask],
        mib=8 if unroll else 44,
        micros=8.0,
        after=[own_narrow],
    )
    y, do, dx1, up_grad, down_grad, out_grad, feed_sums = run(
        "feed",
        feed_kernel,
        [
            ((tokens, width), bf16),
            ((tokens, width), bf16),
            ((tokens, width), f32),
            ((width, FF), f32),
            ((width, FF), f32),
            ((width, width), f32),
            (vectors.shape, f32),
        ],
        [o, x0, w_out, all_near, all_far, vec, dy],
        scratch=[((width, FF), bf16), ((FF, width), bf16), ((width, FF), f32), ((FF, width), f32)],
        mib=12,
        micros=3.5,
    )
    if kept:
        body, args, more = attend_back_kept_kernel, [q, k, v, o, stat, kept[0]], []
    else:
        body, args = functools.partial(attend_back_kernel, step), [q, k, v, mask, o, stat]
        more = [((tokens, keys), bf16)]
    dq, dkv, dkn_keep, dkn_send = run(
        "attend_back",
        body,
        [((tokens, width), bf16), ((2 * width, keys), f32), ((keys // 2, width), f32), ((keys // 2, width), f32)],
        args + [do, w_keyval],
        scratch=[((tokens, width), f32), ((tokens, keys), bf16), ((width, tokens), bf16), ((width, tokens), bf16)] + more,
        mib=16 if kept else 60,
        micros=8.0,
    )
    dkn_got = swap(dkn_send, "row", 1)
    half = (shards // 2, early_rows, width)
    early_keep, early_send = run(
        "early_turn",
        early_turn_kernel,
        [(half, f32), (half, f32)],
        [up_grad, down_grad, narrow_turned, narrow, wide],
        scratch=[((width, FF), f32), ((FF, width), f32)],
        mib=10,
        micros=2.0,
        after=[dq],
    )
    early_got = swap(early_send, "row", 1)
    dkn_terms = [dkn_keep, dkn_got]
    for axis, stride, size in xy_parts:
        part, *sends = split_sum(dkn_terms, size, [early_keep])
        dkn_terms = [part] + [swap(x, axis, j * stride) for j, x in enumerate(sends, 1)][::-1]
    old_chunk, ema_chunk, first_chunk, second_chunk = run(
        "moments",
        functools.partial(moments_kernel, width),
        [((chunk, width), f32)] * 4,
        [jnp.concatenate([weights, weight_ema, first_moment, second_moment], axis=0)],
        after=[part],
    )
    query_turn, out_turn, keyval_turn, query_sums = run(
        "middle_turn",
        middle_turn_kernel,
        [((width, width), f32), ((width, width), f32), ((width, 2 * width), f32), ((8, width), f32)],
        [h1, dq, out_grad, kn_all, dkv, narrow_turned, narrow, pair],
        micros=1.5,
        mib=12 if kept else 40,
        after=[part],
    )
    half = (shards // 2, late_rows, width)
    late_keep, late_send, dc, key_sums = run(
        "keys_back",
        functools.partial(keys_back_kernel, len(dkn_terms)),
        [(half, f32), (half, f32), ((own_keys, width), bf16), ((3, width), f32)],
        list(dkn_terms) + [c, vec, blocks, narrow, wide, query_turn, out_turn, keyval_turn],
        scratch=[((4 * width, width), f32)],
        micros=2.0,
        after=[old_chunk],
    )
    late_got = swap(late_send, "row", 1)
    dx0, head, tail, vec_grads = run(
        "cells_back",
        functools.partial(cells_back_kernel, rows, cols),
        [((tokens, width), f32), ((64, width), bf16), ((64, width), bf16), ((32, width), f32)],
        [
            sizes, dq, dc, w_query, w_reduce, x0, dx1, vec, tile, up_halo, down_halo,
            feed_sums, key_sums, query_sums,
        ],
        scratch=[frame],
        micros=2.0,
    )
    grad_up, grad_down = border(head, tail)
    args = [late_keep, late_got, vec_grads, swap(vec_grads, "row", 1), early_keep, early_got]
    args = [x.reshape(-1, width) for x in args]
    for index, (axis, stride, size) in enumerate(xy_parts + [img_part]):
        keeps, sends = split_three(args, size, index == 0, [grad_up, grad_down] if index else [])
        args = keeps + [swap(x, axis, j * stride) for j, x in enumerate(sends, 1)]
    grad_input, input_done = run(
        "input_grad",
        functools.partial(input_grad_kernel, rows),
        [((tokens, width), f32), ((8, 128), f32)],
        [dx0, grad_up, grad_down, vec],
        scratch=[frame],
        micros=1.5,
        after=[keeps[1]],
    )
    moments, squares, step, new_vectors, vec_moment, vec_square, new_vec_ema = run(
        "adam",
        functools.partial(adam_kernel, len(args)),
        [((chunk, width), f32), ((chunk, width), f32), ((chunk, width), bf16)] + [(vectors.shape, f32)] * 4,
        args + [first_chunk, second_chunk, vec, vec_first, vec_second, vec_ema],
        micros=0.8,
        after=[input_done],
    )
    (own_wide,) = run(
        "own_wide",
        own_wide_kernel,
        [((2, FF // lines, FF // ranks), f32)],
        [wide],
        micros=1.5,
        after=[step],
    )
    new_first, new_second, packed_done = run(
        "packed_moments",
        functools.partial(packed_moments_kernel, width),
        [((1, per), f32), ((1, per), f32), ((8, 128), f32)],
        [moments, squares],
        after=[own_wide],
    )
    steps = join([step[None]] + [swap(step, "img", j)[None] for j in range(1, lines)], [packed_done])
    half = (ranks // 2, chunk, width)
    keep, send = run(
        "products",
        functools.partial(products_kernel, width),
        [(half, f32), (half, bf16)],
        [steps, own_narrow, own_wide],
        scratch=[(half, f32)],
        micros=1.0,
    )
    terms = [keep.reshape(-1, width), swap(send, "row", 1).reshape(-1, width)]
    for index, (axis, stride, size) in enumerate(xy_parts):
        part, *sends = split_sum(terms, size)
        terms = [part] + [swap(x, axis, j * stride) for j, x in enumerate(sends, 1)]
    new_weights, new_ema = run(
        "finish",
        functools.partial(finish_kernel, width, len(terms)),
        [((1, per), f32)] * 2,
        list(terms) + [narrow, pair, wide, old_chunk, ema_chunk],
        scratch=[((chunk, width), f32)],
        micros=1.5,
    )
    return (
        y.reshape(patches.shape),
        grad_input.reshape(patches.shape),
        new_weights,
        new_first,
        new_second,
        new_ema,
        new_vectors,
        vec_moment,
        vec_square,
        new_vec_ema,
    )


def solution(mesh):
    tiles = P("img", "row", None, None)
    packed = P(("img", "row"), None)
    return jax.shard_map(
        on_device,
        mesh=mesh,
        in_specs=(tiles, tiles, P("img", None)) + (packed,) * 4 + (P(),) * 7,
        out_specs=(tiles, tiles) + (packed,) * 4 + (P(),) * 4,
        check_vma=False,
    )
```

```python
import functools
import math

import jax
import jax.numpy as jnp
from jax import lax
from jax.experimental import pallas as pl
from jax.experimental.pallas import tpu as pltpu
from jax.sharding import PartitionSpec as P

HEADS = 8
FF = 1024
STEP = 5

NORM_EPS = 1e-05
ADAM_EPS = 1e-08
BETA = 0.5
WEIGHT_DECAY = 0.05
EMA_KEEP = 0.75
VECTOR_RATE = 0.06
MATRIX_RATES = (0.04, 0.02, 0.25, 0.02, 0.01, 0.01)
CORRECTION = 1.0 - BETA**STEP
LOG2E = math.log2(math.e)
f32 = jnp.float32
bf16 = jnp.bfloat16
LATE = (5, 1, 0, 2)
EARLY = (3, 4)


def matrix_shapes(width, hidden):
    return (
        (width, width),
        (width, 2 * width),
        (width, width),
        (width, hidden),
        (hidden, width),
        (4 * width, width),
    )


def contract(a, b, ca, cb, **kw):
    return lax.dot_general(
        a, b, (((ca,), (cb,)), ((), ())), preferred_element_type=f32, **kw
    )


def swap(x, axis, step):
    count = lax.axis_size(axis)
    return lax.ppermute(x, axis, [(i, i ^ step) for i in range(count)])


def row_groups():
    left = lax.axis_size("row") // 2
    groups, stride = [(1, 2)], 2
    while left > 1:
        size = 4 if left % 4 == 0 else 2
        groups.append((stride, size))
        left //= size
        stride *= size
    return groups


def rel_digits():
    groups = row_groups()
    return [groups[0]] + groups[1:][::-1]


def source(block):
    sizes = lax.axis_size("img")
    img, rest = block % sizes, block // sizes
    rel = 0
    for stride, size in reversed(rel_digits()):
        rel = rel + (rest % size) * stride
        rest = rest // size
    row = lax.axis_index("row") ^ rel
    return (lax.axis_index("img") ^ img) * lax.axis_size("row") + row


def device_count():
    return lax.axis_size("img") * lax.axis_size("row")


def run(name, body, outs, args, scratch=(), mib=6, scalars=(), micros=1.0, after=(), raw=(), sems=0):
    count = len(args)

    def without(*refs):
        body(*refs[:count], *refs[count + len(after) :])

    space = {index: pltpu.SMEM for index in scalars} | {index: pltpu.HBM for index in raw}
    specs = [pl.BlockSpec(memory_space=space.get(index, pltpu.VMEM)) for index in range(count)]
    return pl.pallas_call(
        without,
        out_shape=tuple(jax.ShapeDtypeStruct(shape, dtype) for shape, dtype in outs),
        in_specs=specs + [pl.BlockSpec(memory_space=pl.ANY)] * len(after),
        out_specs=tuple(pl.BlockSpec(memory_space=pltpu.VMEM) for _ in outs),
        scratch_shapes=[pltpu.VMEM(shape, dtype) for shape, dtype in scratch]
        + ([pltpu.SemaphoreType.DMA((sems,))] if sems else []),
        compiler_params=pltpu.CompilerParams(vmem_limit_bytes=mib * 2**20),
        cost_estimate=pl.CostEstimate(flops=0, bytes_accessed=int(micros * 3.6e6), transcendentals=0),
        name=name,
    )(*args, *after)


def each_block(count, body):
    if count <= 32:
        for index in range(count):
            body(index)
    else:

        def step(index, carry):
            body(index)
            return carry

        lax.fori_loop(0, count, step, 0)


def put_rows(ref, start, cols, value):
    count = value.shape[0]
    if count % 8 == 0:
        ref[pl.ds(pl.multiple_of(start, 8), count), cols] = value
    else:
        for row in range(count):
            ref[pl.ds(start + row, 1), cols] = value[row : row + 1]


def get_rows(ref, start, count, cols):
    if count % 8 == 0:
        return ref[pl.ds(pl.multiple_of(start, 8), count), cols]
    return jnp.concatenate([ref[pl.ds(start + row, 1), cols] for row in range(count)], axis=0)


def layout(width, group):
    dims = matrix_shapes(width, FF)
    found, start = [], 0
    for j in group:
        rows = dims[j][0] // device_count()
        blocks = dims[j][1] // width
        found.append((j, start, rows, blocks))
        start += rows * blocks
    return found, start


def packed_starts(width):
    dims = matrix_shapes(width, FF)
    starts, start = [], 0
    for m, n in dims:
        starts.append(start)
        start += m * n // device_count()
    return starts


def spread(block, parts, mats, start_of):
    for (j, first, rows, blocks), ref in zip(parts, mats):
        for col in range(blocks):
            piece = block[first + col * rows : first + (col + 1) * rows]
            put_rows(ref, start_of * rows, slice(col * 256, col * 256 + 256), piece)


def collect(out_ref, index, parts, mats, start_of):
    for (j, first, rows, blocks), ref in zip(parts, mats):
        for col in range(blocks):
            piece = get_rows(ref, start_of * rows, rows, slice(col * 256, col * 256 + 256))
            out_ref[index, first + col * rows : first + (col + 1) * rows, :] = piece


def norm_parts(values):
    centred = values - jnp.mean(values, axis=-1, keepdims=True)
    inverse = lax.rsqrt(jnp.mean(centred * centred, axis=-1, keepdims=True) + NORM_EPS)
    return centred * inverse, inverse


def norm_back(grad, unit, inverse, gain):
    grad_unit = grad * gain
    back = grad_unit - jnp.mean(grad_unit, axis=-1, keepdims=True)
    back = back - unit * jnp.mean(grad_unit * unit, axis=-1, keepdims=True)
    gain_sum = jnp.sum(grad * unit, axis=0, keepdims=True)
    return back * inverse, gain_sum, jnp.sum(grad, axis=0, keepdims=True)


def turned(value):
    return value.astype(f32).T.astype(bf16)


def col_sum(value):
    return jnp.sum(value, axis=0, keepdims=True)


def pack_kernel(width, w_ref, out_ref, chunk):
    to_chunk(w_ref, chunk, width)
    out_ref[...] = chunk[...].astype(bf16)


def to_chunk(flat_ref, out_ref, width, index=0):
    dims, starts, base = matrix_shapes(width, FF), packed_starts(width), 0
    for group in (LATE, EARLY):
        parts, count = layout(width, group)
        for j, first, rows, blocks in parts:
            for col in range(blocks):
                for row in range(rows):
                    at = starts[j] + row * dims[j][1] + col * width
                    place = base + first + col * rows + row
                    out_ref[place : place + 1, :] = flat_ref[index : index + 1, at : at + width]
        base += count


def from_chunk(values, out_ref, width):
    dims, starts = matrix_shapes(width, FF), packed_starts(width)
    for j, first, rows, blocks in both_groups(width):
        for col in range(blocks):
            for row in range(rows):
                at = starts[j] + row * dims[j][1] + col * width
                place = first + col * rows + row
                out_ref[0:1, at : at + width] = values[place : place + 1, :]


def moments_kernel(width, rows_ref, *outs):
    for index, ref in enumerate(outs):
        to_chunk(rows_ref, ref, width, index)


def left_block(matrix_ref, out_ref):
    lines, ranks = lax.axis_size("img"), lax.axis_size("row")
    size = matrix_ref.shape[0]
    rows = size // (lines * ranks)
    img, row = lax.axis_index("img"), lax.axis_index("row")

    def one_hot(count, axis, start_of):
        shape = (count * rows, size) if axis == 0 else (size, count * rows)
        place = lax.broadcasted_iota(jnp.int32, tuple(n if d == axis else 1 for d, n in enumerate(shape)), axis)
        block = place >> (rows.bit_length() - 1)
        target = start_of(block) * rows + (place & (rows - 1))
        return (lax.broadcasted_iota(jnp.int32, shape, 1 - axis) == target).astype(f32).astype(bf16)

    def owner(block):
        rel = jnp.zeros_like(block)
        for stride, count in reversed(rel_digits()):
            rel = rel + (block & (count - 1)) * stride
            block = block >> (count.bit_length() - 1)
        return img * ranks + (rel ^ row)

    mine = contract(one_hot(ranks, 0, owner), matrix_ref[...], 1, 0).astype(bf16)
    out_ref[...] = contract(mine, one_hot(lines, 1, lambda block: (block ^ img) * ranks + row), 1, 0)


def narrow_bases_kernel(narrow_ref, pair_ref, narrow_out, turned_out, pair_out, own_ref):
    narrow_out[...] = narrow_ref[...].astype(bf16)
    pair_out[...] = pair_ref[...].astype(bf16)
    for index, j in enumerate((0, 2, 3, 5)):
        turned_out[index] = narrow_ref[j].T.astype(bf16)
        left_block(narrow_out.at[j], own_ref.at[index])


def own_wide_kernel(wide_ref, own_ref):
    for index in range(2):
        left_block(wide_ref.at[index + 1], own_ref.at[index])


def wide_bases_kernel(wide_ref, wide_out, token):
    for index in range(wide_ref.shape[0]):
        wide_out[index] = wide_ref[index].astype(bf16)
    token[...] = jnp.zeros_like(token)


def join_kernel(*refs):
    start = 0
    for ref in refs[-2::-1]:
        refs[-1][start : start + ref.shape[0]] = ref[...]
        start += ref.shape[0]


def join_apart_kernel(rows, *refs):
    first, second = refs[-2:]
    start = 0
    for ref in refs[-3::-1]:
        first[start : start + ref.shape[0]] = ref[:, 0:rows]
        second[start : start + ref.shape[0]] = ref[:, rows:]
        start += ref.shape[0]


def join_apart(pieces, rows, after):
    count, all_rows, width = sum(x.shape[0] for x in pieces), pieces[0].shape[1], pieces[0].shape[2]
    outs = [((count, rows, width), bf16), ((count, all_rows - rows, width), bf16)]
    return run("join", functools.partial(join_apart_kernel, rows), outs, list(pieces)[::-1], micros=0.4, after=after)


def join(pieces, after=()):
    shape = (sum(x.shape[0] for x in pieces),) + pieces[0].shape[1:]
    return run("join", join_kernel, [(shape, pieces[0].dtype)], list(pieces)[::-1], micros=0.4, after=after)[0]


def unpack(pieces, group, mats):
    parts, start = [], min(part[1] for part in both_groups(256) if part[0] in group)
    for j in group:
        parts += [(j, first - start, rows, blocks) for k, first, rows, blocks in both_groups(256) if k == j]
    done = 0
    for piece in pieces:

        def body(block, piece=piece, done=done):
            spread(piece[block].astype(f32), parts, mats, source(block + done))

        each_block(piece.shape[0], body)
        done += piece.shape[0]


def weights_kernel(group, near_ref, far_ref, *refs):
    count = len(group)
    unpack((near_ref, far_ref), group, refs[count:])
    for out_ref, ref in zip(refs[:count], refs[count:]):
        out_ref[...] = ref[...].astype(bf16)


def shifted_frame(frame_ref, tile_ref, up_ref, down_ref):
    rows, cols, width = frame_ref.shape[0] - 2, 56, 256
    frame_ref[...] = jnp.zeros_like(frame_ref)
    frame_ref[0, 8 : 8 + cols, :] = up_ref[...].astype(f32)[-cols:]
    frame_ref[1 : 1 + rows, 8 : 8 + cols, :] = tile_ref[...].astype(f32).reshape(rows, cols, width)
    frame_ref[rows + 1, 8 : 8 + cols, :] = down_ref[...].astype(f32)[:cols]
    return [frame_ref[:, 7 + shift : 7 + shift + cols, :] for shift in range(3)]


def front_kernel(tile_rows, cols, size_ref, tile_ref, up_ref, down_ref, vec_ref, x0_ref, h1_ref, mask_ref, vec_out, size_out, frame):
    rows = frame.shape[0] - 2
    vec_out[...] = vec_ref[...]
    size_out[...] = jnp.where(lax.broadcasted_iota(jnp.int32, size_out.shape, 0) == 0, size_ref[0, 0], size_ref[0, 1])
    moved = shifted_frame(frame, tile_ref, up_ref, down_ref)
    total = moved[1][1:-1] + vec_ref[9:10, :]
    for tap in range(9):
        total = total + vec_ref[tap : tap + 1, :] * moved[tap % 3][tap // 3 : tap // 3 + rows]
    x0 = total.reshape(x0_ref.shape)
    x0_ref[...] = x0
    unit, _ = norm_parts(x0)
    h1_ref[...] = (unit * vec_ref[10:11, :] + vec_ref[11:12, :]).astype(bf16)
    half = cols // 2
    own = tile_rows // 2 * half
    key = lax.broadcasted_iota(jnp.int32, mask_ref.shape, 1)
    block = jnp.zeros_like(key)
    for start in range(own, mask_ref.shape[1], own):
        block = block + (key >= start).astype(jnp.int32)
    key = key - block * own
    row = jnp.zeros_like(key)
    for start in range(half, own, half):
        row = row + (key >= start).astype(jnp.int32)
    col = key - row * half
    rel = jnp.zeros_like(key)
    for stride, size in reversed(rel_digits()):
        rel = rel + (block & (size - 1)) * stride
        block = block >> (size.bit_length() - 1)
    row = row + (rel ^ lax.axis_index("row")) * (tile_rows // 2)
    inside = (2 * row < size_ref[0, 0]) & (2 * col < size_ref[0, 1])
    mask_ref[...] = jnp.where(inside, 0.0, -1e30)


def picked_cells(shape, cell_axis, size_ref, corner, tile_rows, cols):
    half = cols // 2
    key_shape = tuple(1 if axis == cell_axis else n for axis, n in enumerate(shape))
    key = lax.broadcasted_iota(jnp.int32, key_shape, 1 - cell_axis)
    row = jnp.zeros_like(key)
    for step in range(1, tile_rows // 2):
        row = row + (key >= step * half).astype(jnp.int32)
    col = 2 * (key - row * half) + corner % 2
    row = 2 * row + corner // 2
    inside = (row + lax.axis_index("row") * tile_rows < size_ref[0:1, 0:1]) & (col < size_ref[1:2, 0:1])
    target = jnp.where(inside, row * cols + col, -1)
    cell = lax.broadcasted_iota(jnp.int32, shape, cell_axis)
    return (cell == target).astype(f32).astype(bf16)


def keys_kernel(
    tile_rows, cols, size_ref, h1_ref, vec_ref, near_ref, far_ref,
    reduce_ref, blocks_ref, c_ref, kn_ref, reduce_wide,
):
    unpack((near_ref, far_ref), (5,), (reduce_wide,))
    reduce_ref[...] = reduce_wide[...].astype(bf16)
    keys = c_ref.shape[0]
    for corner in range(4):
        pick = picked_cells((keys, h1_ref.shape[0]), 1, size_ref, corner, tile_rows, cols)
        blocks_ref[:, corner * 256 : corner * 256 + 256] = contract(pick, h1_ref[...], 1, 0).astype(bf16)
    c = contract(blocks_ref[...], reduce_ref[...], 1, 0) + vec_ref[13:14, :]
    c_ref[...] = c
    unit, _ = norm_parts(c)
    kn = (unit * vec_ref[14:15, :] + vec_ref[15:16, :]).astype(bf16)
    kn_ref[...] = kn


def over_heads(body, first, last, unroll):
    if unroll:
        for head in range(first, last):
            body(head)
    else:

        def step(head, carry):
            body(head)
            return carry

        lax.fori_loop(first, last, step, 0)


def over_blocks(block, tokens, step):
    if tokens == step:
        block(0)
    else:

        def go(index, carry):
            block(pl.multiple_of(index * step, step))
            return carry

        lax.fori_loop(0, tokens // step, go, 0)


def head_columns(head):
    group = head // 4
    if isinstance(head, int):
        return slice(group * 128, group * 128 + 128)
    return pl.ds(pl.multiple_of(group * 128, 128), 128)


def head_rows(head, base=0):
    if isinstance(head, int):
        return slice(base + head * 32, base + head * 32 + 32)
    return pl.ds(pl.multiple_of(base + head * 32, 32), 32)


def attend_kernel(
    step, unroll, h1_ref, query_ref, keyval_ref, vec_ref, near_ref, far_ref, mask_ref,
    kn_ref, q_ref, k_ref, v_ref, o_ref, stat_ref, *kept
):
    tokens = h1_ref.shape[0]
    half = near_ref.shape[0]
    kn_ref[0:half, :] = near_ref[...]
    kn_ref[half:, :] = far_ref[...]
    k_ref[...] = contract(kn_ref[...], keyval_ref[:, 0:256], 1, 0).astype(bf16)
    v_ref[...] = (contract(kn_ref[...], keyval_ref[:, 256:512], 1, 0) + vec_ref[16:17, :]).astype(bf16)
    q_ref[...] = (contract(h1_ref[...], query_ref[...], 1, 0) + vec_ref[12:13, :]).astype(bf16)
    scale = 32**-0.5 * LOG2E
    lane = lax.broadcasted_iota(jnp.int32, (1, 128), 1)
    mask = mask_ref[...]

    def one_head(head):
        cols = head_columns(head)
        mine = lane // 32 == head % 4
        keys = jnp.where(mine, k_ref[:, cols], 0)
        ones = jnp.where(lane // 32 == (head + 2) % 4, 1.0, 0.0).astype(bf16)
        values = jnp.where(mine, v_ref[:, cols], ones)

        def block(start):
            rows = pl.ds(start, step)
            scores = contract(q_ref[rows, cols], keys, 1, 1) * scale + mask
            top = jnp.max(scores, axis=1, keepdims=True)
            exponent = jnp.exp2(scores - top).astype(bf16)
            if kept:
                kept[0][head] = exponent
            out = contract(exponent, values, 1, 0)
            if isinstance(head, int):
                total = out[:, (head + 2) % 4 * 32 : (head + 2) % 4 * 32 + 1]
            else:
                total = jnp.sum(jnp.where(lane == (head + 2) % 4 * 32, out, 0.0), axis=1, keepdims=True)
            inverse = 1.0 / total
            o_ref[rows, cols] = jnp.where(mine, out * inverse, o_ref[rows, cols])
            stat = inverse if kept else top + jnp.log2(total)
            stat_ref[rows, :] = jnp.where(lane == head, stat, stat_ref[rows, :])

        over_blocks(block, tokens, step)

    over_heads(one_head, 0, HEADS, unroll)


def feed_kernel(
    o_ref, x0_ref, out_ref, up_ref, down_ref, vec_ref, dy_ref,
    y_ref, do_ref, dx1_ref, up_grad, down_grad, out_grad, sums_ref,
):
    o = o_ref[...].astype(bf16)
    x1 = x0_ref[...] + (contract(o, out_ref[...], 1, 0) + vec_ref[17:18, :])
    unit, inverse = norm_parts(x1)
    h2 = (unit * vec_ref[18:19, :] + vec_ref[19:20, :]).astype(bf16)
    dy_low = dy_ref[...]
    dy = dy_low.astype(f32)
    dyt = turned(dy_low)
    h2t = turned(h2)
    y = x1 + vec_ref[20:21, :]
    dh2 = jnp.zeros_like(y)
    for col in range(FF // 256):
        cols = slice(col * 256, col * 256 + 256)
        u = contract(h2, up_ref[:, cols], 1, 0) + vec_ref[21 + col : 22 + col, :]
        phi_sum = 0.5 * (1.0 + lax.erf(u * (2.0**-0.5)))
        density = jnp.exp(-0.5 * u * u) * ((2.0 * math.pi) ** -0.5)
        g = (u * phi_sum).astype(bf16)
        y = y + contract(g, down_ref[cols, :], 1, 0)
        down_grad[:, cols] = contract(dyt, g, 1, 0)
        du = (contract(dy_low, down_ref[cols, :], 1, 1) * (phi_sum + u * density)).astype(bf16)
        up_grad[:, cols] = contract(h2t, du, 1, 0)
        sums_ref[21 + col : 22 + col, :] = col_sum(du.astype(f32))
        dh2 = dh2 + contract(du, up_ref[:, cols], 1, 1)
    y_ref[...] = y.astype(bf16)
    back, gain_sum, bias_sum = norm_back(dh2, unit, inverse, vec_ref[18:19, :])
    dx1 = dy + back
    dx1_ref[...] = dx1
    da = dx1.astype(bf16)
    do_ref[...] = contract(da, out_ref[...], 1, 1).astype(bf16)
    out_grad[...] = contract(turned(o), da, 1, 0)
    sums_ref[0:17, :] = jnp.zeros((17, 256), f32)
    sums_ref[17:18, :] = col_sum(da.astype(f32))
    sums_ref[18:19, :] = gain_sum
    sums_ref[19:20, :] = bias_sum
    sums_ref[20:21, :] = col_sum(dy)


def rotate(left_turned, grad, right):
    half = contract(left_turned, grad.astype(bf16), 1, 0).astype(bf16)
    return contract(half, right, 1, 0)


def rotate_turned(grad_turned, left, right):
    half = contract(grad_turned.astype(bf16), left, 1, 0).astype(bf16)
    return contract(turned(half), right, 1, 0)


def share_out(keep_ref, send_ref, parts, mats):
    half = keep_ref.shape[0]
    for ref, base in ((keep_ref, 0), (send_ref, half)):

        def body(block, ref=ref, base=base):
            collect(ref, block, parts, mats, source(block + base))

        each_block(half, body)


def early_turn_kernel(up_grad, down_grad, turned_ref, narrow_ref, wide_ref, keep_ref, send_ref, up, down):
    up[...] = rotate(turned_ref[3], up_grad[...], wide_ref[0])
    down[...] = rotate_turned(down_grad[...], wide_ref[1], narrow_ref[6])
    share_out(keep_ref, send_ref, layout(256, EARLY)[0], (up, down))


def middle_turn_kernel(
    h1_ref, dq_ref, out_grad, kn_ref, dkv_ref, turned_ref, narrow_ref, pair_ref, query_ref, out_ref, keyval_ref, sums_ref
):
    dq = dq_ref[...]
    query_ref[...] = rotate(turned_ref[0], contract(turned(h1_ref[...]), dq, 1, 0), narrow_ref[1])
    out_ref[...] = rotate(turned_ref[2], out_grad[...], narrow_ref[4])
    sums_ref[0:1, :] = col_sum(dq.astype(f32))
    sums_ref[2:8, :] = jnp.zeros((6, 256), f32)
    high, rest = two_parts(dkv_ref[...])
    ones = jnp.ones((8, kn_ref.shape[0]), bf16)
    sums = contract(ones, high[256:512, :], 1, 1) + contract(ones, rest[256:512, :], 1, 1)
    sums_ref[1:2, :] = sums[0:1]
    grad = contract(high, kn_ref[...], 1, 0) + contract(rest, kn_ref[...], 1, 0)
    keyval_ref[...] = rotate_turned(grad, narrow_ref[2], pair_ref[...])


def back_outputs(dq_wide, dkv, keyval_ref, dq_ref, keep_ref, send_ref):
    dq_ref[...] = dq_wide[...].astype(bf16)
    keys = dkv.shape[1]
    half = keys // 2
    span = keys if keys <= 1024 else keys // 8
    for start in range(0, keys, span):
        high, rest = two_parts(dkv[:, start : start + span])
        total = contract(keyval_ref[...], high, 1, 0) + contract(keyval_ref[...], rest, 1, 0)
        if span == keys:
            keep_ref[...] = total[:, 0:half].T
            send_ref[...] = total[:, half:].T
        else:
            out = (keep_ref, send_ref)[start // half]
            out[start % half : start % half + span, :] = total.T


def inner_sum(grad, out, mine):
    return jnp.sum(jnp.where(mine, grad.astype(f32) * out, 0.0), axis=1, keepdims=True)


def attend_back_kept_kernel(
    q_ref, k_ref, v_ref, o_ref, stat_ref, kept_ref, g_ref, keyval_ref,
    dq_ref, dkv, keep_ref, send_ref, dq_wide, dss, qt, gt,
):
    scale = 32**-0.5
    width = q_ref.shape[1]
    lane = lax.broadcasted_iota(jnp.int32, (1, 128), 1)
    qt[...] = turned(q_ref[...])
    for group in range(2):
        cols = slice(group * 128, group * 128 + 128)
        grad = g_ref[:, cols]
        stats = [stat_ref[:, group * 4 + head : group * 4 + head + 1] for head in range(4)]
        spread_stats = stats[3]
        for head in range(3):
            spread_stats = jnp.where(lane // 32 == head, stats[head], spread_stats)
        gt[cols, :] = (grad.astype(f32) * spread_stats).T.astype(bf16)
        for head in range(4):
            mine = lane // 32 == head
            keys = jnp.where(mine, k_ref[:, cols], 0)
            values = jnp.where(mine, v_ref[:, cols], 0)
            inner = inner_sum(grad, o_ref[:, cols], mine)
            rows = head_rows(group * 4 + head)
            exponent = kept_ref[group * 4 + head]
            slope = (contract(grad, values, 1, 1) - inner) * stats[head]
            dss[...] = (exponent.astype(f32) * slope).astype(bf16)
            out = contract(dss[...], keys, 1, 0) * scale
            dq_wide[:, cols] = jnp.where(mine, out, dq_wide[:, cols])
            dkv[rows, :] = contract(qt[rows, :], dss[...], 1, 0) * scale
            dkv[head_rows(group * 4 + head, width), :] = contract(gt[rows, :], exponent, 1, 0)
    back_outputs(dq_wide, dkv, keyval_ref, dq_ref, keep_ref, send_ref)


def attend_back_kernel(
    step, q_ref, k_ref, v_ref, mask_ref, o_ref, stat_ref, g_ref, keyval_ref,
    dq_ref, dkv, keep_ref, send_ref, dq_wide, dss, qt, gt, ps,
):
    tokens, width = q_ref.shape
    scale = 32**-0.5
    lane = lax.broadcasted_iota(jnp.int32, (1, 128), 1)
    mask = mask_ref[...]
    qt[...] = turned(q_ref[...])
    gt[...] = turned(g_ref[...])

    def one_head(head):
        cols = head_columns(head)
        mine = lane // 32 == head % 4
        keys = jnp.where(mine, k_ref[:, cols], 0)
        values = jnp.where(mine, v_ref[:, cols], 0)

        def block(start):
            rows = pl.ds(start, step)
            grad = g_ref[rows, cols]
            inner = inner_sum(grad, o_ref[rows, cols], mine)
            log = jnp.sum(jnp.where(lane == head, stat_ref[rows, :], 0.0), axis=1, keepdims=True)
            scores = contract(q_ref[rows, cols], keys, 1, 1)
            probs = jnp.exp2(scores * (scale * LOG2E) + mask - log)
            grad_scores = (probs * (contract(grad, values, 1, 1) - inner)).astype(bf16)
            ps[rows, :] = probs.astype(bf16)
            dss[rows, :] = grad_scores
            out = contract(grad_scores, keys, 1, 0) * scale
            dq_wide[rows, cols] = jnp.where(mine, out, dq_wide[rows, cols])

        over_blocks(block, tokens, step)
        dkv[head_rows(head), :] = contract(qt[head_rows(head), :], dss[...], 1, 0) * scale
        dkv[head_rows(head, width), :] = contract(gt[head_rows(head), :], ps[...], 1, 0)

    over_heads(one_head, 0, HEADS, False)
    back_outputs(dq_wide, dkv, keyval_ref, dq_ref, keep_ref, send_ref)


def total_of(refs):
    total = refs[0][...]
    for ref in refs[1:]:
        total = total + ref[...].astype(f32)
    return total


def split_kernel(count, terms, *refs):
    total = total_of(refs[:terms])
    rows = total.shape[0] // count
    refs[terms][...] = total[:rows]
    for index in range(1, count):
        refs[terms + index][...] = total[index * rows : (index + 1) * rows].astype(bf16)


def split_sum(terms, count, after=()):
    rows = terms[0].shape[0] // count
    tail = terms[0].shape[1:]
    outs = [((rows,) + tail, f32)] + [((rows,) + tail, bf16)] * (count - 1)
    return run("split_sum", functools.partial(split_kernel, count, len(terms)), outs, terms, micros=0.6, after=after)


def pair_total(values):
    while len(values) > 1:
        values = [a + b for a, b in zip(values[::2], values[1::2])]
    return values[0]


def two_parts(value):
    high = value.astype(bf16)
    return high, (value - high.astype(f32)).astype(bf16)


def sum_three(keeps, pieces):
    late, vec, early = [ref[...] for ref in keeps]
    rows, more = late.shape[0], vec.shape[0]
    vecs = [vec]
    for ref in pieces:
        late = late + ref[0:rows, :].astype(f32)
        vecs.append(ref[rows : rows + more, :].astype(f32))
        early = early + ref[rows + more :, :].astype(f32)
    return late, pair_total(vecs), early


def split_three_kernel(count, pieces, first, *refs):
    if first:
        late, vec, early = [refs[k][...] + refs[k + 1][...] for k in (0, 2, 4)]
        outs = refs[6:]
    else:
        late, vec, early = sum_three(refs[:3], refs[3 : 3 + pieces])
        outs = refs[3 + pieces :]
    rows, more, rest = late.shape[0] // count, vec.shape[0], early.shape[0] // count
    low = vec.astype(bf16)
    outs[0][...] = late[:rows]
    outs[1][...] = low.astype(f32)
    outs[2][...] = early[:rest]
    for index in range(1, count):
        ref = outs[2 + index]
        ref[0:rows, :] = late[index * rows : (index + 1) * rows].astype(bf16)
        ref[rows : rows + more, :] = low
        ref[rows + more :, :] = early[index * rest : (index + 1) * rest].astype(bf16)


def split_three(args, count, first, after=()):
    late, vec, early = args[0:6:2] if first else args[0:3]
    rows, more, rest, width = late.shape[0] // count, vec.shape[0], early.shape[0] // count, late.shape[1]
    outs = [((rows, width), f32), ((more, width), f32), ((rest, width), f32)]
    outs += [((rows + more + rest, width), bf16)] * (count - 1)
    body = functools.partial(split_three_kernel, count, len(args) - 3, first)
    found = run("split_three", body, outs, list(args), micros=0.6, after=after)
    return list(found[:3]), found[3:]


def row_parts():
    return [("row", stride, size) for stride, size in rel_digits()[1:]]


def one_by_one(groups):
    return [(axis, stride << bit, 2) for axis, stride, size in groups for bit in reversed(range(size.bit_length() - 1))]


def side_by_side(x, groups):
    for axis, stride, size in groups:
        x = jnp.concatenate([x] + [swap(x, axis, j * stride) for j in range(1, size)], axis=0)
    return x


def keys_back_kernel(terms, *refs):
    (c_ref, vec_ref, blocks_ref, narrow_ref, wide_ref, query, out, keyval,
     keep_ref, send_ref, dc_ref, sums_ref, reduce) = refs[terms:]
    dkn = total_of(refs[:terms])
    unit, inverse = norm_parts(c_ref[...])
    back, gain_sum, bias_sum = norm_back(dkn, unit, inverse, vec_ref[14:15, :])
    dc = back.astype(bf16)
    dc_ref[...] = dc
    reduce[...] = rotate_turned(contract(turned(dc), blocks_ref[...], 1, 0), wide_ref[2], narrow_ref[7])
    share_out(keep_ref, send_ref, layout(256, LATE)[0], (reduce, keyval, query, out))
    sums_ref[0:1, :] = col_sum(dc.astype(f32))
    sums_ref[1:2, :] = gain_sum
    sums_ref[2:3, :] = bias_sum


def cells_back_kernel(
    tile_rows, cols, size_ref, dq_ref, dc_ref, query_ref, reduce_ref, x0_ref, dx1_ref, vec_ref, tile_ref, up_ref, down_ref,
    feed_sums, key_sums, query_sums, dx0_ref, head_ref, tail_ref, sums_ref, frame,
):
    tokens = x0_ref.shape[0]
    dh1 = contract(dq_ref[...], query_ref[...], 1, 1)
    for corner in range(4):
        pick = picked_cells((tokens, dc_ref.shape[0]), 0, size_ref, corner, tile_rows, cols)
        placed = contract(pick, dc_ref[...], 1, 0).astype(bf16)
        dh1 = dh1 + contract(placed, reduce_ref[corner * 256 : corner * 256 + 256, :], 1, 1)
    unit, inverse = norm_parts(x0_ref[...])
    back, gain_sum, bias_sum = norm_back(dh1, unit, inverse, vec_ref[10:11, :])
    dx0 = dx1_ref[...] + back
    dx0_ref[...] = dx0
    head_ref[...] = dx0[0:64].astype(bf16)
    tail_ref[...] = dx0[tokens - 64 :].astype(bf16)
    sums_ref[0:25, :] = feed_sums[...]
    sums_ref[25:32, :] = jnp.zeros((7, 256), f32)
    moved = shifted_frame(frame, tile_ref, up_ref, down_ref)
    grid = dx0.reshape(tile_rows, cols, 256)
    for tap in range(9):
        product = moved[tap % 3][tap // 3 : tap // 3 + tile_rows] * grid
        sums_ref[tap : tap + 1, :] = col_sum(product.reshape(tokens, 256))
    sums_ref[9:10, :] = col_sum(dx0)
    sums_ref[10:11, :] = gain_sum
    sums_ref[11:12, :] = bias_sum
    sums_ref[12:13, :] = query_sums[0:1, :]
    sums_ref[13:16, :] = key_sums[...]
    sums_ref[16:17, :] = query_sums[1:2, :]


def input_grad_kernel(tile_rows, dx0_ref, up_ref, down_ref, vec_ref, out_ref, token, frame):
    token[...] = jnp.zeros_like(token)
    moved = shifted_frame(frame, dx0_ref, up_ref, down_ref)
    total = moved[1][1:-1]
    for tap in range(9):
        down, right = 2 - tap // 3, 2 - tap % 3
        total = total + vec_ref[tap : tap + 1, :] * moved[right][down : down + tile_rows]
    out_ref[...] = total.reshape(out_ref.shape)


def moments_of(total, first, second, moment_ref, square_ref):
    moment = BETA * first + (1.0 - BETA) * total
    square = BETA * second + (1.0 - BETA) * total * total
    moment_ref[...] = moment
    square_ref[...] = square
    return moment * (1.0 / CORRECTION) / (jnp.sqrt(square * (1.0 / CORRECTION)) + ADAM_EPS)


def adam_kernel(terms, *refs):
    (first_ref, second_ref, vec_ref, vec_first, vec_second, vec_ema,
     moment_ref, square_ref, step_ref, vec_out, vec_first_out, vec_second_out, vec_ema_out) = refs[terms:]
    late, vec, early = sum_three(refs[:3], refs[3:terms])
    rows = late.shape[0]
    for total, at in ((late, slice(0, rows)), (early, slice(rows, rows + early.shape[0]))):
        step = moments_of(total, first_ref[at, :], second_ref[at, :], moment_ref.at[at, :], square_ref.at[at, :])
        step_ref[at, :] = step.astype(bf16)
    vec = vec[0 : vec_ref.shape[0]]
    new = vec_ref[...] - VECTOR_RATE * moments_of(vec, vec_first[...], vec_second[...], vec_first_out, vec_second_out)
    vec_out[...] = new
    vec_ema_out[...] = EMA_KEEP * vec_ema[...] + (1.0 - EMA_KEEP) * new


def both_groups(width):
    late, count = layout(width, LATE)
    return late + [(j, first + count, rows, blocks) for j, first, rows, blocks in layout(width, EARLY)[0]]


def products_kernel(width, chunks, own_narrow, own_wide, keep_ref, send_ref, whole):
    lefts = {0: (own_narrow, 0), 1: (own_narrow, 1), 2: (own_narrow, 2), 3: (own_narrow, 3), 4: (own_wide, 0), 5: (own_wide, 1)}
    half = keep_ref.shape[0]
    values = chunks[...].astype(f32)
    for j, first, rows, blocks in both_groups(width):
        left = lefts[j][0][lefts[j][1]].astype(bf16)
        for col in range(blocks):
            at = slice(first + col * rows, first + (col + 1) * rows)
            part = values[:, at, :].reshape(left.shape[1], width).astype(bf16)
            side = contract(left, part, 1, 0).reshape(2 * half, rows, width)
            keep_ref[:, at, :] = side[:half]
            whole[:, at, :] = side[half:]
    send_ref[...] = whole[...].astype(bf16)


def finish_kernel(
    width, terms, *refs
):
    narrow_ref, pair_ref, wide_ref, weights_ref, ema_ref, weights_out, ema_out, chunk = refs[terms:]
    rights = {0: narrow_ref.at[1], 1: pair_ref, 2: narrow_ref.at[4], 3: wide_ref.at[0], 4: narrow_ref.at[6], 5: narrow_ref.at[7]}
    sides = total_of(refs[:terms])
    for j, first, rows, blocks in both_groups(width):
        parts = [sides[first + col * rows : first + (col + 1) * rows] for col in range(blocks)]
        side = parts[0] if blocks == 1 else jnp.concatenate(parts, axis=1)
        if rows < 8:
            side = jnp.concatenate([side, jnp.zeros((8 - rows, side.shape[1]), f32)], axis=0)
        full = contract(side.astype(bf16), rights[j][...], 1, 1)
        for col in range(blocks):
            at = slice(first + col * rows, first + (col + 1) * rows)
            old = weights_ref[at, :]
            piece = full[0:rows, col * width : (col + 1) * width]
            chunk[at, :] = old - MATRIX_RATES[j] * (piece + WEIGHT_DECAY * old)
    from_chunk(chunk, weights_out, width)
    chunk[...] = EMA_KEEP * ema_ref[...] + (1.0 - EMA_KEEP) * chunk[...]
    from_chunk(chunk, ema_out, width)


def packed_moments_kernel(width, moment_ref, square_ref, first_out, second_out, token):
    token[...] = jnp.zeros_like(token)
    from_chunk(moment_ref, first_out, width)
    from_chunk(square_ref, second_out, width)


def on_device(
    patches,
    cotangent,
    image_sizes,
    weights,
    first_moment,
    second_moment,
    weight_ema,
    vectors,
    vec_first,
    vec_second,
    vec_ema,
    basis_narrow,
    basis_pair,
    basis_wide,
):
    _, rows, cols, width = patches.shape
    tokens = rows * cols
    shards = device_count()
    tile = patches.reshape(tokens, width)
    dy = cotangent.reshape(tokens, width)
    per = weights.shape[1]
    late_rows, early_rows = layout(width, LATE)[1], layout(width, EARLY)[1]
    chunk = late_rows + early_rows
    ranks = lax.axis_size("row")
    own_keys = tokens // 4
    keys = own_keys * ranks
    frame = ((rows + 2, cols + 16, width), f32)
    img_part = ("img", 1, lax.axis_size("img"))
    xy_parts = row_parts()

    def border(head, tail):
        up = lax.ppermute(tail, "row", [(i, i + 1) for i in range(ranks - 1)])
        return up, lax.ppermute(head, "row", [(i + 1, i) for i in range(ranks - 1)])

    gather_groups = xy_parts[::-1]
    lines = lax.axis_size("img")

    (packed,) = run(
        "pack",
        functools.partial(pack_kernel, width),
        [((chunk, width), bf16)],
        [weights],
        scratch=[((chunk, width), f32)],
    )
    line = join([packed[None]] + [swap(packed, "img", j)[None] for j in range(1, lines)])
    up_halo, down_halo = border(tile[:64], tile[tokens - 64 :])
    x0, h1, mask, vec, sizes = run(
        "front",
        functools.partial(front_kernel, rows, cols),
        [((tokens, width), f32), ((tokens, width), bf16), ((1, keys), f32), (vectors.shape, f32), ((8, 128), jnp.int32)],
        [image_sizes, tile, up_halo, down_halo, vectors],
        scratch=[frame],
        scalars=(0,),
        micros=1.3,
        after=[line],
    )
    wide, wide_done = run(
        "wide_bases",
        wide_bases_kernel,
        [((3, FF, FF), bf16), ((8, 128), f32)],
        [basis_wide],
        micros=6.0,
        after=[line],
    )
    all_near = line
    for axis, stride, size in gather_groups:
        pieces = [all_near] + [swap(all_near, axis, j * stride) for j in range(1, size)]
        if stride * size == ranks:
            near, rest_near = join_apart(pieces, width * 4 // shards, [wide_done, vec])
        else:
            all_near = join(pieces, after=[wide_done, vec])
    far, rest_far = swap(near, "row", 1), swap(rest_near, "row", 1)
    w_reduce, blocks, c, kn = run(
        "keys",
        functools.partial(keys_kernel, rows, cols),
        [
            ((4 * width, width), bf16),
            ((own_keys, 4 * width), bf16),
            ((own_keys, width), f32),
            ((own_keys, width), bf16),
        ],
        [sizes, h1, vec, near, far],
        scratch=[((4 * width, width), f32)],
        micros=1.5,
    )
    narrow, narrow_turned, pair, own_narrow = run(
        "narrow_bases",
        narrow_bases_kernel,
        [
            ((8, width, width), bf16),
            ((4, width, width), bf16),
            ((2 * width, 2 * width), bf16),
            ((4, width // lines, width // ranks), f32),
        ],
        [basis_narrow, basis_pair],
        micros=1.5,
        after=[kn],
    )
    group = (1, 0, 2, 3, 4)
    w_keyval, w_query, w_out, w_up, w_down = run(
        "weights",
        functools.partial(weights_kernel, group),
        [(matrix_shapes(width, FF)[j], bf16) for j in group],
        [rest_near, rest_far],
        scratch=[(matrix_shapes(width, FF)[j], f32) for j in group],
        micros=1.0,
        after=[kn],
    )
    kn_near = side_by_side(kn, gather_groups)
    kn_far = swap(kn_near, "row", 1)

    unroll = keys <= 1024
    step = tokens if unroll else 32
    kn_all, q, k, v, o, stat, *kept = run(
        "attend",
        functools.partial(attend_kernel, step, unroll),
        [((keys, width), bf16), ((tokens, width), bf16), ((keys, width), bf16), ((keys, width), bf16)]
        + [((tokens, width), f32), ((tokens, 128), f32)]
        + ([((HEADS, tokens, keys), bf16)] if unroll else []),
        [h1, w_query, w_keyval, vec, kn_near, kn_far, mask],
        mib=8 if unroll else 44,
        micros=8.0,
        after=[own_narrow],
    )
    y, do, dx1, up_grad, down_grad, out_grad, feed_sums = run(
        "feed",
        feed_kernel,
        [
            ((tokens, width), bf16),
            ((tokens, width), bf16),
            ((tokens, width), f32),
            ((width, FF), f32),
            ((width, FF), f32),
            ((width, width), f32),
            (vectors.shape, f32),
        ],
        [o, x0, w_out, w_up, w_down, vec, dy],
        mib=12,
        micros=3.5,
    )
    if kept:
        body, args, more = attend_back_kept_kernel, [q, k, v, o, stat, kept[0]], []
    else:
        body, args = functools.partial(attend_back_kernel, step), [q, k, v, mask, o, stat]
        more = [((tokens, keys), bf16)]
    dq, dkv, dkn_keep, dkn_send = run(
        "attend_back",
        body,
        [((tokens, width), bf16), ((2 * width, keys), f32), ((keys // 2, width), f32), ((keys // 2, width), f32)],
        args + [do, w_keyval],
        scratch=[((tokens, width), f32), ((tokens, keys), bf16), ((width, tokens), bf16), ((width, tokens), bf16)] + more,
        mib=16 if kept else 60,
        micros=8.0,
    )
    dkn_got = swap(dkn_send, "row", 1)
    half = (shards // 2, early_rows, width)
    early_keep, early_send = run(
        "early_turn",
        early_turn_kernel,
        [(half, f32), (half, f32)],
        [up_grad, down_grad, narrow_turned, narrow, wide],
        scratch=[((width, FF), f32), ((FF, width), f32)],
        mib=10,
        micros=2.0,
        after=[dq],
    )
    early_got = swap(early_send, "row", 1)
    dkn_terms = [dkn_keep, dkn_got]
    for axis, stride, size in xy_parts:
        part, *sends = split_sum(dkn_terms, size, [early_keep])
        dkn_terms = [part] + [swap(x, axis, j * stride) for j, x in enumerate(sends, 1)][::-1]
    old_chunk, ema_chunk, first_chunk, second_chunk = run(
        "moments",
        functools.partial(moments_kernel, width),
        [((chunk, width), f32)] * 4,
        [jnp.concatenate([weights, weight_ema, first_moment, second_moment], axis=0)],
        after=[part],
    )
    query_turn, out_turn, keyval_turn, query_sums = run(
        "middle_turn",
        middle_turn_kernel,
        [((width, width), f32), ((width, width), f32), ((width, 2 * width), f32), ((8, width), f32)],
        [h1, dq, out_grad, kn_all, dkv, narrow_turned, narrow, pair],
        micros=1.5,
        mib=12 if kept else 40,
        after=[part],
    )
    half = (shards // 2, late_rows, width)
    late_keep, late_send, dc, key_sums = run(
        "keys_back",
        functools.partial(keys_back_kernel, len(dkn_terms)),
        [(half, f32), (half, f32), ((own_keys, width), bf16), ((3, width), f32)],
        list(dkn_terms) + [c, vec, blocks, narrow, wide, query_turn, out_turn, keyval_turn],
        scratch=[((4 * width, width), f32)],
        micros=2.0,
        after=[old_chunk],
    )
    late_got = swap(late_send, "row", 1)
    dx0, head, tail, vec_grads = run(
        "cells_back",
        functools.partial(cells_back_kernel, rows, cols),
        [((tokens, width), f32), ((64, width), bf16), ((64, width), bf16), ((32, width), f32)],
        [
            sizes, dq, dc, w_query, w_reduce, x0, dx1, vec, tile, up_halo, down_halo,
            feed_sums, key_sums, query_sums,
        ],
        scratch=[frame],
        micros=2.0,
    )
    grad_up, grad_down = border(head, tail)
    args = [late_keep, late_got, vec_grads, swap(vec_grads, "row", 1), early_keep, early_got]
    args = [x.reshape(-1, width) for x in args]
    for index, (axis, stride, size) in enumerate(xy_parts + [img_part]):
        keeps, sends = split_three(args, size, index == 0, [grad_up, grad_down] if index else [])
        args = keeps + [swap(x, axis, j * stride) for j, x in enumerate(sends, 1)]
    grad_input, input_done = run(
        "input_grad",
        functools.partial(input_grad_kernel, rows),
        [((tokens, width), f32), ((8, 128), f32)],
        [dx0, grad_up, grad_down, vec],
        scratch=[frame],
        micros=1.5,
        after=[keeps[1]],
    )
    moments, squares, step, new_vectors, vec_moment, vec_square, new_vec_ema = run(
        "adam",
        functools.partial(adam_kernel, len(args)),
        [((chunk, width), f32), ((chunk, width), f32), ((chunk, width), bf16)] + [(vectors.shape, f32)] * 4,
        args + [first_chunk, second_chunk, vec, vec_first, vec_second, vec_ema],
        micros=0.8,
        after=[input_done],
    )
    (own_wide,) = run(
        "own_wide",
        own_wide_kernel,
        [((2, FF // lines, FF // ranks), f32)],
        [wide],
        micros=1.5,
        after=[step],
    )
    new_first, new_second, packed_done = run(
        "packed_moments",
        functools.partial(packed_moments_kernel, width),
        [((1, per), f32), ((1, per), f32), ((8, 128), f32)],
        [moments, squares],
        after=[own_wide],
    )
    steps = join([step[None]] + [swap(step, "img", j)[None] for j in range(1, lines)], [packed_done])
    half = (ranks // 2, chunk, width)
    keep, send = run(
        "products",
        functools.partial(products_kernel, width),
        [(half, f32), (half, bf16)],
        [steps, own_narrow, own_wide],
        scratch=[(half, f32)],
        micros=1.0,
    )
    terms = [keep.reshape(-1, width), swap(send, "row", 1).reshape(-1, width)]
    for index, (axis, stride, size) in enumerate(xy_parts):
        part, *sends = split_sum(terms, size)
        terms = [part] + [swap(x, axis, j * stride) for j, x in enumerate(sends, 1)]
    new_weights, new_ema = run(
        "finish",
        functools.partial(finish_kernel, width, len(terms)),
        [((1, per), f32)] * 2,
        list(terms) + [narrow, pair, wide, old_chunk, ema_chunk],
        scratch=[((chunk, width), f32)],
        micros=1.5,
    )
    return (
        y.reshape(patches.shape),
        grad_input.reshape(patches.shape),
        new_weights,
        new_first,
        new_second,
        new_ema,
        new_vectors,
        vec_moment,
        vec_square,
        new_vec_ema,
    )


def solution(mesh):
    tiles = P("img", "row", None, None)
    packed = P(("img", "row"), None)
    return jax.shard_map(
        on_device,
        mesh=mesh,
        in_specs=(tiles, tiles, P("img", None)) + (packed,) * 4 + (P(),) * 7,
        out_specs=(tiles, tiles) + (packed,) * 4 + (P(),) * 4,
        check_vma=False,
    )
```

```python
import functools
import math

import jax
import jax.numpy as jnp
from jax import lax
from jax.experimental import pallas as pl
from jax.experimental.pallas import tpu as pltpu
from jax.sharding import PartitionSpec as P

HEADS = 8
FF = 1024
STEP = 5

NORM_EPS = 1e-05
ADAM_EPS = 1e-08
BETA = 0.5
WEIGHT_DECAY = 0.05
EMA_KEEP = 0.75
VECTOR_RATE = 0.06
MATRIX_RATES = (0.04, 0.02, 0.25, 0.02, 0.01, 0.01)
CORRECTION = 1.0 - BETA**STEP
LOG2E = math.log2(math.e)
f32 = jnp.float32
bf16 = jnp.bfloat16
LATE = (5, 1, 0, 2)
EARLY = (3, 4)


def matrix_shapes(width, hidden):
    return (
        (width, width),
        (width, 2 * width),
        (width, width),
        (width, hidden),
        (hidden, width),
        (4 * width, width),
    )


def contract(a, b, ca, cb, **kw):
    return lax.dot_general(
        a, b, (((ca,), (cb,)), ((), ())), preferred_element_type=f32, **kw
    )


def swap(x, axis, step):
    count = lax.axis_size(axis)
    return lax.ppermute(x, axis, [(i, i ^ step) for i in range(count)])


def row_groups():
    left = lax.axis_size("row") // 2
    groups, stride = [(1, 2)], 2
    while left > 1:
        size = 4 if left % 4 == 0 else 2
        groups.append((stride, size))
        left //= size
        stride *= size
    return groups


def rel_digits():
    groups = row_groups()
    return [groups[0]] + groups[1:][::-1]


def source(block):
    sizes = lax.axis_size("img")
    img, rest = block % sizes, block // sizes
    rel = 0
    for stride, size in reversed(rel_digits()):
        rel = rel + (rest % size) * stride
        rest = rest // size
    row = lax.axis_index("row") ^ rel
    return (lax.axis_index("img") ^ img) * lax.axis_size("row") + row


def device_count():
    return lax.axis_size("img") * lax.axis_size("row")


def run(name, body, outs, args, scratch=(), mib=6, scalars=(), micros=1.0, after=(), raw=(), sems=0):
    count = len(args)

    def without(*refs):
        body(*refs[:count], *refs[count + len(after) :])

    space = {index: pltpu.SMEM for index in scalars} | {index: pltpu.HBM for index in raw}
    specs = [pl.BlockSpec(memory_space=space.get(index, pltpu.VMEM)) for index in range(count)]
    return pl.pallas_call(
        without,
        out_shape=tuple(jax.ShapeDtypeStruct(shape, dtype) for shape, dtype in outs),
        in_specs=specs + [pl.BlockSpec(memory_space=pl.ANY)] * len(after),
        out_specs=tuple(pl.BlockSpec(memory_space=pltpu.VMEM) for _ in outs),
        scratch_shapes=[pltpu.VMEM(shape, dtype) for shape, dtype in scratch]
        + ([pltpu.SemaphoreType.DMA((sems,))] if sems else []),
        compiler_params=pltpu.CompilerParams(vmem_limit_bytes=mib * 2**20),
        cost_estimate=pl.CostEstimate(flops=0, bytes_accessed=int(micros * 3.6e6), transcendentals=0),
        name=name,
    )(*args, *after)


def each_block(count, body):
    if count <= 32:
        for index in range(count):
            body(index)
    else:

        def step(index, carry):
            body(index)
            return carry

        lax.fori_loop(0, count, step, 0)


def put_rows(ref, start, cols, value):
    count = value.shape[0]
    if count % 8 == 0:
        ref[pl.ds(pl.multiple_of(start, 8), count), cols] = value
    else:
        for row in range(count):
            ref[pl.ds(start + row, 1), cols] = value[row : row + 1]


def get_rows(ref, start, count, cols):
    if count % 8 == 0:
        return ref[pl.ds(pl.multiple_of(start, 8), count), cols]
    return jnp.concatenate([ref[pl.ds(start + row, 1), cols] for row in range(count)], axis=0)


def layout(width, group):
    dims = matrix_shapes(width, FF)
    found, start = [], 0
    for j in group:
        rows = dims[j][0] // device_count()
        blocks = dims[j][1] // width
        found.append((j, start, rows, blocks))
        start += rows * blocks
    return found, start


def packed_starts(width):
    dims = matrix_shapes(width, FF)
    starts, start = [], 0
    for m, n in dims:
        starts.append(start)
        start += m * n // device_count()
    return starts


def spread(block, parts, mats, start_of):
    for (j, first, rows, blocks), ref in zip(parts, mats):
        for col in range(blocks):
            piece = block[first + col * rows : first + (col + 1) * rows]
            put_rows(ref, start_of * rows, slice(col * 256, col * 256 + 256), piece)


def collect(out_ref, index, parts, mats, start_of):
    for (j, first, rows, blocks), ref in zip(parts, mats):
        for col in range(blocks):
            piece = get_rows(ref, start_of * rows, rows, slice(col * 256, col * 256 + 256))
            out_ref[index, first + col * rows : first + (col + 1) * rows, :] = piece


def norm_parts(values):
    centred = values - jnp.mean(values, axis=-1, keepdims=True)
    inverse = lax.rsqrt(jnp.mean(centred * centred, axis=-1, keepdims=True) + NORM_EPS)
    return centred * inverse, inverse


def norm_back(grad, unit, inverse, gain):
    grad_unit = grad * gain
    back = grad_unit - jnp.mean(grad_unit, axis=-1, keepdims=True)
    back = back - unit * jnp.mean(grad_unit * unit, axis=-1, keepdims=True)
    gain_sum = jnp.sum(grad * unit, axis=0, keepdims=True)
    return back * inverse, gain_sum, jnp.sum(grad, axis=0, keepdims=True)


def turned(value):
    return value.astype(f32).T.astype(bf16)


def col_sum(value):
    return jnp.sum(value, axis=0, keepdims=True)


def pack_kernel(width, w_ref, out_ref, chunk):
    to_chunk(w_ref, chunk, width)
    out_ref[...] = chunk[...].astype(bf16)


def to_chunk(flat_ref, out_ref, width, index=0):
    dims, starts, base = matrix_shapes(width, FF), packed_starts(width), 0
    for group in (LATE, EARLY):
        parts, count = layout(width, group)
        for j, first, rows, blocks in parts:
            for col in range(blocks):
                for row in range(rows):
                    at = starts[j] + row * dims[j][1] + col * width
                    place = base + first + col * rows + row
                    out_ref[place : place + 1, :] = flat_ref[index : index + 1, at : at + width]
        base += count


def from_chunk(values, out_ref, width):
    dims, starts = matrix_shapes(width, FF), packed_starts(width)
    for j, first, rows, blocks in both_groups(width):
        for col in range(blocks):
            for row in range(rows):
                at = starts[j] + row * dims[j][1] + col * width
                place = first + col * rows + row
                out_ref[0:1, at : at + width] = values[place : place + 1, :]


def moments_kernel(width, rows_ref, *outs):
    for index, ref in enumerate(outs):
        to_chunk(rows_ref, ref, width, index)


def left_block(matrix_ref, out_ref):
    lines, ranks = lax.axis_size("img"), lax.axis_size("row")
    size = matrix_ref.shape[0]
    rows = size // (lines * ranks)
    img, row = lax.axis_index("img"), lax.axis_index("row")

    def one_hot(count, axis, start_of):
        shape = (count * rows, size) if axis == 0 else (size, count * rows)
        place = lax.broadcasted_iota(jnp.int32, tuple(n if d == axis else 1 for d, n in enumerate(shape)), axis)
        block = place >> (rows.bit_length() - 1)
        target = start_of(block) * rows + (place & (rows - 1))
        return (lax.broadcasted_iota(jnp.int32, shape, 1 - axis) == target).astype(f32).astype(bf16)

    def owner(block):
        rel = jnp.zeros_like(block)
        for stride, count in reversed(rel_digits()):
            rel = rel + (block & (count - 1)) * stride
            block = block >> (count.bit_length() - 1)
        return img * ranks + (rel ^ row)

    mine = contract(one_hot(ranks, 0, owner), matrix_ref[...], 1, 0).astype(bf16)
    out_ref[...] = contract(mine, one_hot(lines, 1, lambda block: (block ^ img) * ranks + row), 1, 0)


def narrow_bases_kernel(narrow_ref, pair_ref, narrow_out, turned_out, pair_out, own_ref):
    narrow_out[...] = narrow_ref[...].astype(bf16)
    pair_out[...] = pair_ref[...].astype(bf16)
    for index, j in enumerate((0, 2, 3, 5)):
        turned_out[index] = narrow_ref[j].T.astype(bf16)
        left_block(narrow_out.at[j], own_ref.at[index])


def own_wide_kernel(wide_ref, own_ref):
    for index in range(2):
        left_block(wide_ref.at[index + 1], own_ref.at[index])


def wide_bases_kernel(wide_ref, wide_out, token):
    for index in range(wide_ref.shape[0]):
        wide_out[index] = wide_ref[index].astype(bf16)
    token[...] = jnp.zeros_like(token)


def join_kernel(*refs):
    start = 0
    for ref in refs[-2::-1]:
        refs[-1][start : start + ref.shape[0]] = ref[...]
        start += ref.shape[0]


def join_apart_kernel(rows, *refs):
    first, second = refs[-2:]
    start = 0
    for ref in refs[-3::-1]:
        first[start : start + ref.shape[0]] = ref[:, 0:rows]
        second[start : start + ref.shape[0]] = ref[:, rows:]
        start += ref.shape[0]


def join_apart(pieces, rows, after):
    count, all_rows, width = sum(x.shape[0] for x in pieces), pieces[0].shape[1], pieces[0].shape[2]
    outs = [((count, rows, width), bf16), ((count, all_rows - rows, width), bf16)]
    return run("join", functools.partial(join_apart_kernel, rows), outs, list(pieces)[::-1], micros=0.4, after=after)


def join(pieces, after=()):
    shape = (sum(x.shape[0] for x in pieces),) + pieces[0].shape[1:]
    return run("join", join_kernel, [(shape, pieces[0].dtype)], list(pieces)[::-1], micros=0.4, after=after)[0]


def unpack(pieces, group, mats):
    parts, start = [], min(part[1] for part in both_groups(256) if part[0] in group)
    for j in group:
        parts += [(j, first - start, rows, blocks) for k, first, rows, blocks in both_groups(256) if k == j]
    done = 0
    for piece in pieces:

        def body(block, piece=piece, done=done):
            spread(piece[block].astype(f32), parts, mats, source(block + done))

        each_block(piece.shape[0], body)
        done += piece.shape[0]


def weights_kernel(group, near_ref, far_ref, *refs):
    count = len(group)
    unpack((near_ref, far_ref), group, refs[count:])
    for out_ref, ref in zip(refs[:count], refs[count:]):
        out_ref[...] = ref[...].astype(bf16)


def shifted_frame(frame_ref, tile_ref, up_ref, down_ref):
    rows, cols, width = frame_ref.shape[0] - 2, 56, 256
    frame_ref[...] = jnp.zeros_like(frame_ref)
    frame_ref[0, 8 : 8 + cols, :] = up_ref[...].astype(f32)[-cols:]
    frame_ref[1 : 1 + rows, 8 : 8 + cols, :] = tile_ref[...].astype(f32).reshape(rows, cols, width)
    frame_ref[rows + 1, 8 : 8 + cols, :] = down_ref[...].astype(f32)[:cols]
    return [frame_ref[:, 7 + shift : 7 + shift + cols, :] for shift in range(3)]


def front_kernel(tile_rows, cols, size_ref, tile_ref, up_ref, down_ref, vec_ref, x0_ref, h1_ref, mask_ref, vec_out, size_out, frame):
    rows = frame.shape[0] - 2
    vec_out[...] = vec_ref[...]
    size_out[...] = jnp.where(lax.broadcasted_iota(jnp.int32, size_out.shape, 0) == 0, size_ref[0, 0], size_ref[0, 1])
    moved = shifted_frame(frame, tile_ref, up_ref, down_ref)
    total = moved[1][1:-1] + vec_ref[9:10, :]
    for tap in range(9):
        total = total + vec_ref[tap : tap + 1, :] * moved[tap % 3][tap // 3 : tap // 3 + rows]
    x0 = total.reshape(x0_ref.shape)
    x0_ref[...] = x0
    unit, _ = norm_parts(x0)
    h1_ref[...] = (unit * vec_ref[10:11, :] + vec_ref[11:12, :]).astype(bf16)
    half = cols // 2
    own = tile_rows // 2 * half
    key = lax.broadcasted_iota(jnp.int32, mask_ref.shape, 1)
    block = jnp.zeros_like(key)
    for start in range(own, mask_ref.shape[1], own):
        block = block + (key >= start).astype(jnp.int32)
    key = key - block * own
    row = jnp.zeros_like(key)
    for start in range(half, own, half):
        row = row + (key >= start).astype(jnp.int32)
    col = key - row * half
    rel = jnp.zeros_like(key)
    for stride, size in reversed(rel_digits()):
        rel = rel + (block & (size - 1)) * stride
        block = block >> (size.bit_length() - 1)
    row = row + (rel ^ lax.axis_index("row")) * (tile_rows // 2)
    inside = (2 * row < size_ref[0, 0]) & (2 * col < size_ref[0, 1])
    mask_ref[...] = jnp.where(inside, 0.0, -1e30)


def picked_cells(shape, cell_axis, size_ref, corner, tile_rows, cols):
    half = cols // 2
    key_shape = tuple(1 if axis == cell_axis else n for axis, n in enumerate(shape))
    key = lax.broadcasted_iota(jnp.int32, key_shape, 1 - cell_axis)
    row = jnp.zeros_like(key)
    for step in range(1, tile_rows // 2):
        row = row + (key >= step * half).astype(jnp.int32)
    col = 2 * (key - row * half) + corner % 2
    row = 2 * row + corner // 2
    inside = (row + lax.axis_index("row") * tile_rows < size_ref[0:1, 0:1]) & (col < size_ref[1:2, 0:1])
    target = jnp.where(inside, row * cols + col, -1)
    cell = lax.broadcasted_iota(jnp.int32, shape, cell_axis)
    return (cell == target).astype(f32).astype(bf16)


def keys_kernel(
    tile_rows, cols, size_ref, h1_ref, vec_ref, near_ref, far_ref,
    reduce_ref, blocks_ref, c_ref, kn_ref, reduce_wide,
):
    unpack((near_ref, far_ref), (5,), (reduce_wide,))
    reduce_ref[...] = reduce_wide[...].astype(bf16)
    keys = c_ref.shape[0]
    for corner in range(4):
        pick = picked_cells((keys, h1_ref.shape[0]), 1, size_ref, corner, tile_rows, cols)
        blocks_ref[:, corner * 256 : corner * 256 + 256] = contract(pick, h1_ref[...], 1, 0).astype(bf16)
    c = contract(blocks_ref[...], reduce_ref[...], 1, 0) + vec_ref[13:14, :]
    c_ref[...] = c
    unit, _ = norm_parts(c)
    kn = (unit * vec_ref[14:15, :] + vec_ref[15:16, :]).astype(bf16)
    kn_ref[...] = kn


def over_heads(body, first, last, unroll):
    if unroll:
        for head in range(first, last):
            body(head)
    else:

        def step(head, carry):
            body(head)
            return carry

        lax.fori_loop(first, last, step, 0)


def over_blocks(block, tokens, step):
    if tokens == step:
        block(0)
    else:

        def go(index, carry):
            block(pl.multiple_of(index * step, step))
            return carry

        lax.fori_loop(0, tokens // step, go, 0)


def head_columns(head):
    group = head // 4
    if isinstance(head, int):
        return slice(group * 128, group * 128 + 128)
    return pl.ds(pl.multiple_of(group * 128, 128), 128)


def head_rows(head, base=0):
    if isinstance(head, int):
        return slice(base + head * 32, base + head * 32 + 32)
    return pl.ds(pl.multiple_of(base + head * 32, 32), 32)


def attend_kernel(
    step, unroll, h1_ref, query_ref, keyval_ref, vec_ref, near_ref, far_ref, mask_ref,
    kn_ref, q_ref, k_ref, v_ref, o_ref, stat_ref, *kept
):
    tokens = h1_ref.shape[0]
    half = near_ref.shape[0]
    kn_ref[0:half, :] = near_ref[...]
    kn_ref[half:, :] = far_ref[...]
    k_ref[...] = contract(kn_ref[...], keyval_ref[:, 0:256], 1, 0).astype(bf16)
    v_ref[...] = (contract(kn_ref[...], keyval_ref[:, 256:512], 1, 0) + vec_ref[16:17, :]).astype(bf16)
    q_ref[...] = (contract(h1_ref[...], query_ref[...], 1, 0) + vec_ref[12:13, :]).astype(bf16)
    scale = 32**-0.5 * LOG2E
    lane = lax.broadcasted_iota(jnp.int32, (1, 128), 1)
    mask = mask_ref[...]

    def one_head(head):
        cols = head_columns(head)
        mine = lane // 32 == head % 4
        keys = jnp.where(mine, k_ref[:, cols], 0)
        ones = jnp.where(lane // 32 == (head + 2) % 4, 1.0, 0.0).astype(bf16)
        values = jnp.where(mine, v_ref[:, cols], ones)

        def block(start):
            rows = pl.ds(start, step)
            scores = contract(q_ref[rows, cols], keys, 1, 1) * scale + mask
            top = jnp.max(scores, axis=1, keepdims=True)
            exponent = jnp.exp2(scores - top).astype(bf16)
            if kept:
                kept[0][head] = exponent
            out = contract(exponent, values, 1, 0)
            if isinstance(head, int):
                total = out[:, (head + 2) % 4 * 32 : (head + 2) % 4 * 32 + 1]
            else:
                total = jnp.sum(jnp.where(lane == (head + 2) % 4 * 32, out, 0.0), axis=1, keepdims=True)
            inverse = 1.0 / total
            o_ref[rows, cols] = jnp.where(mine, out * inverse, o_ref[rows, cols])
            stat = inverse if kept else top + jnp.log2(total)
            stat_ref[rows, :] = jnp.where(lane == head, stat, stat_ref[rows, :])

        over_blocks(block, tokens, step)

    over_heads(one_head, 0, HEADS, unroll)


def feed_kernel(
    o_ref, x0_ref, out_ref, up_ref, down_ref, vec_ref, dy_ref,
    y_ref, do_ref, dx1_ref, up_grad, down_grad, out_grad, sums_ref,
):
    o = o_ref[...].astype(bf16)
    x1 = x0_ref[...] + (contract(o, out_ref[...], 1, 0) + vec_ref[17:18, :])
    unit, inverse = norm_parts(x1)
    h2 = (unit * vec_ref[18:19, :] + vec_ref[19:20, :]).astype(bf16)
    dy_low = dy_ref[...]
    dy = dy_low.astype(f32)
    dyt = turned(dy_low)
    h2t = turned(h2)
    y = x1 + vec_ref[20:21, :]
    dh2 = jnp.zeros_like(y)
    for col in range(FF // 256):
        cols = slice(col * 256, col * 256 + 256)
        u = contract(h2, up_ref[:, cols], 1, 0) + vec_ref[21 + col : 22 + col, :]
        phi_sum = 0.5 * (1.0 + lax.erf(u * (2.0**-0.5)))
        density = jnp.exp(-0.5 * u * u) * ((2.0 * math.pi) ** -0.5)
        g = (u * phi_sum).astype(bf16)
        y = y + contract(g, down_ref[cols, :], 1, 0)
        down_grad[:, cols] = contract(dyt, g, 1, 0)
        du = (contract(dy_low, down_ref[cols, :], 1, 1) * (phi_sum + u * density)).astype(bf16)
        up_grad[:, cols] = contract(h2t, du, 1, 0)
        sums_ref[21 + col : 22 + col, :] = col_sum(du.astype(f32))
        dh2 = dh2 + contract(du, up_ref[:, cols], 1, 1)
    y_ref[...] = y.astype(bf16)
    back, gain_sum, bias_sum = norm_back(dh2, unit, inverse, vec_ref[18:19, :])
    dx1 = dy + back
    dx1_ref[...] = dx1
    da = dx1.astype(bf16)
    do_ref[...] = contract(da, out_ref[...], 1, 1).astype(bf16)
    out_grad[...] = contract(turned(o), da, 1, 0)
    sums_ref[0:17, :] = jnp.zeros((17, 256), f32)
    sums_ref[17:18, :] = col_sum(da.astype(f32))
    sums_ref[18:19, :] = gain_sum
    sums_ref[19:20, :] = bias_sum
    sums_ref[20:21, :] = col_sum(dy)


def rotate(left_turned, grad, right):
    half = contract(left_turned, grad.astype(bf16), 1, 0).astype(bf16)
    return contract(half, right, 1, 0)


def rotate_turned(grad_turned, left, right):
    half = contract(grad_turned.astype(bf16), left, 1, 0).astype(bf16)
    return contract(turned(half), right, 1, 0)


def share_out(keep_ref, send_ref, parts, mats):
    half = keep_ref.shape[0]
    for ref, base in ((keep_ref, 0), (send_ref, half)):

        def body(block, ref=ref, base=base):
            collect(ref, block, parts, mats, source(block + base))

        each_block(half, body)


def early_turn_kernel(up_grad, down_grad, turned_ref, narrow_ref, wide_ref, keep_ref, send_ref, up, down):
    up[...] = rotate(turned_ref[3], up_grad[...], wide_ref[0])
    down[...] = rotate_turned(down_grad[...], wide_ref[1], narrow_ref[6])
    share_out(keep_ref, send_ref, layout(256, EARLY)[0], (up, down))


def middle_turn_kernel(
    h1_ref, dq_ref, out_grad, kn_ref, dkv_ref, turned_ref, narrow_ref, pair_ref, query_ref, out_ref, keyval_ref, sums_ref
):
    dq = dq_ref[...]
    query_ref[...] = rotate(turned_ref[0], contract(turned(h1_ref[...]), dq, 1, 0), narrow_ref[1])
    out_ref[...] = rotate(turned_ref[2], out_grad[...], narrow_ref[4])
    sums_ref[0:1, :] = col_sum(dq.astype(f32))
    sums_ref[2:8, :] = jnp.zeros((6, 256), f32)
    high, rest = two_parts(dkv_ref[...])
    ones = jnp.ones((8, kn_ref.shape[0]), bf16)
    sums = contract(ones, high[256:512, :], 1, 1) + contract(ones, rest[256:512, :], 1, 1)
    sums_ref[1:2, :] = sums[0:1]
    grad = contract(high, kn_ref[...], 1, 0) + contract(rest, kn_ref[...], 1, 0)
    keyval_ref[...] = rotate_turned(grad, narrow_ref[2], pair_ref[...])


def back_outputs(dq_wide, dkv, keyval_ref, dq_ref, keep_ref, send_ref):
    dq_ref[...] = dq_wide[...].astype(bf16)
    keys = dkv.shape[1]
    half = keys // 2
    span = keys if keys <= 1024 else keys // 8
    for start in range(0, keys, span):
        high, rest = two_parts(dkv[:, start : start + span])
        total = contract(keyval_ref[...], high, 1, 0) + contract(keyval_ref[...], rest, 1, 0)
        if span == keys:
            keep_ref[...] = total[:, 0:half].T
            send_ref[...] = total[:, half:].T
        else:
            out = (keep_ref, send_ref)[start // half]
            out[start % half : start % half + span, :] = total.T


def inner_sum(grad, out, mine):
    return jnp.sum(jnp.where(mine, grad.astype(f32) * out, 0.0), axis=1, keepdims=True)


def attend_back_kept_kernel(
    q_ref, k_ref, v_ref, o_ref, stat_ref, kept_ref, g_ref, keyval_ref,
    dq_ref, dkv, keep_ref, send_ref, dq_wide, dss, qt, gt,
):
    scale = 32**-0.5
    width = q_ref.shape[1]
    lane = lax.broadcasted_iota(jnp.int32, (1, 128), 1)
    qt[...] = turned(q_ref[...])
    for group in range(2):
        cols = slice(group * 128, group * 128 + 128)
        grad = g_ref[:, cols]
        stats = [stat_ref[:, group * 4 + head : group * 4 + head + 1] for head in range(4)]
        spread_stats = stats[3]
        for head in range(3):
            spread_stats = jnp.where(lane // 32 == head, stats[head], spread_stats)
        gt[cols, :] = (grad.astype(f32) * spread_stats).T.astype(bf16)
        for head in range(4):
            mine = lane // 32 == head
            keys = jnp.where(mine, k_ref[:, cols], 0)
            values = jnp.where(mine, v_ref[:, cols], 0)
            inner = inner_sum(grad, o_ref[:, cols], mine)
            rows = head_rows(group * 4 + head)
            exponent = kept_ref[group * 4 + head]
            slope = (contract(grad, values, 1, 1) - inner) * stats[head]
            dss[...] = (exponent.astype(f32) * slope).astype(bf16)
            out = contract(dss[...], keys, 1, 0) * scale
            dq_wide[:, cols] = jnp.where(mine, out, dq_wide[:, cols])
            dkv[rows, :] = contract(qt[rows, :], dss[...], 1, 0) * scale
            dkv[head_rows(group * 4 + head, width), :] = contract(gt[rows, :], exponent, 1, 0)
    back_outputs(dq_wide, dkv, keyval_ref, dq_ref, keep_ref, send_ref)


def attend_back_kernel(
    step, q_ref, k_ref, v_ref, mask_ref, o_ref, stat_ref, g_ref, keyval_ref,
    dq_ref, dkv, keep_ref, send_ref, dq_wide, dss, qt, gt, ps,
):
    tokens, width = q_ref.shape
    scale = 32**-0.5
    lane = lax.broadcasted_iota(jnp.int32, (1, 128), 1)
    mask = mask_ref[...]
    qt[...] = turned(q_ref[...])
    gt[...] = turned(g_ref[...])

    def one_head(head):
        cols = head_columns(head)
        mine = lane // 32 == head % 4
        keys = jnp.where(mine, k_ref[:, cols], 0)
        values = jnp.where(mine, v_ref[:, cols], 0)

        def block(start):
            rows = pl.ds(start, step)
            grad = g_ref[rows, cols]
            inner = inner_sum(grad, o_ref[rows, cols], mine)
            log = jnp.sum(jnp.where(lane == head, stat_ref[rows, :], 0.0), axis=1, keepdims=True)
            scores = contract(q_ref[rows, cols], keys, 1, 1)
            probs = jnp.exp2(scores * (scale * LOG2E) + mask - log)
            grad_scores = (probs * (contract(grad, values, 1, 1) - inner)).astype(bf16)
            ps[rows, :] = probs.astype(bf16)
            dss[rows, :] = grad_scores
            out = contract(grad_scores, keys, 1, 0) * scale
            dq_wide[rows, cols] = jnp.where(mine, out, dq_wide[rows, cols])

        over_blocks(block, tokens, step)
        dkv[head_rows(head), :] = contract(qt[head_rows(head), :], dss[...], 1, 0) * scale
        dkv[head_rows(head, width), :] = contract(gt[head_rows(head), :], ps[...], 1, 0)

    over_heads(one_head, 0, HEADS, False)
    back_outputs(dq_wide, dkv, keyval_ref, dq_ref, keep_ref, send_ref)


def total_of(refs):
    total = refs[0][...]
    for ref in refs[1:]:
        total = total + ref[...].astype(f32)
    return total


def split_kernel(count, terms, *refs):
    total = total_of(refs[:terms])
    rows = total.shape[0] // count
    refs[terms][...] = total[:rows]
    for index in range(1, count):
        refs[terms + index][...] = total[index * rows : (index + 1) * rows].astype(bf16)


def split_sum(terms, count, after=()):
    rows = terms[0].shape[0] // count
    tail = terms[0].shape[1:]
    outs = [((rows,) + tail, f32)] + [((rows,) + tail, bf16)] * (count - 1)
    return run("split_sum", functools.partial(split_kernel, count, len(terms)), outs, terms, micros=0.6, after=after)


def pair_total(values):
    while len(values) > 1:
        values = [a + b for a, b in zip(values[::2], values[1::2])]
    return values[0]


def two_parts(value):
    high = value.astype(bf16)
    return high, (value - high.astype(f32)).astype(bf16)


def sum_three(keeps, pieces):
    late, vec, early = [ref[...] for ref in keeps]
    rows, more = late.shape[0], vec.shape[0]
    vecs = [vec]
    for ref in pieces:
        late = late + ref[0:rows, :].astype(f32)
        vecs.append(ref[rows : rows + more, :].astype(f32))
        early = early + ref[rows + more :, :].astype(f32)
    return late, pair_total(vecs), early


def split_three_kernel(count, pieces, first, *refs):
    if first:
        late, vec, early = [refs[k][...] + refs[k + 1][...] for k in (0, 2, 4)]
        outs = refs[6:]
    else:
        late, vec, early = sum_three(refs[:3], refs[3 : 3 + pieces])
        outs = refs[3 + pieces :]
    rows, more, rest = late.shape[0] // count, vec.shape[0], early.shape[0] // count
    low = vec.astype(bf16)
    outs[0][...] = late[:rows]
    outs[1][...] = low.astype(f32)
    outs[2][...] = early[:rest]
    for index in range(1, count):
        ref = outs[2 + index]
        ref[0:rows, :] = late[index * rows : (index + 1) * rows].astype(bf16)
        ref[rows : rows + more, :] = low
        ref[rows + more :, :] = early[index * rest : (index + 1) * rest].astype(bf16)


def split_three(args, count, first, after=()):
    late, vec, early = args[0:6:2] if first else args[0:3]
    rows, more, rest, width = late.shape[0] // count, vec.shape[0], early.shape[0] // count, late.shape[1]
    outs = [((rows, width), f32), ((more, width), f32), ((rest, width), f32)]
    outs += [((rows + more + rest, width), bf16)] * (count - 1)
    body = functools.partial(split_three_kernel, count, len(args) - 3, first)
    found = run("split_three", body, outs, list(args), micros=0.6, after=after)
    return list(found[:3]), found[3:]


def row_parts():
    return [("row", stride, size) for stride, size in rel_digits()[1:]]


def one_by_one(groups):
    return [(axis, stride << bit, 2) for axis, stride, size in groups for bit in reversed(range(size.bit_length() - 1))]


def side_by_side(x, groups):
    for axis, stride, size in groups:
        x = jnp.concatenate([x] + [swap(x, axis, j * stride) for j in range(1, size)], axis=0)
    return x


def keys_back_kernel(terms, *refs):
    (c_ref, vec_ref, blocks_ref, narrow_ref, wide_ref, query, out, keyval,
     keep_ref, send_ref, dc_ref, sums_ref, reduce) = refs[terms:]
    dkn = total_of(refs[:terms])
    unit, inverse = norm_parts(c_ref[...])
    back, gain_sum, bias_sum = norm_back(dkn, unit, inverse, vec_ref[14:15, :])
    dc = back.astype(bf16)
    dc_ref[...] = dc
    reduce[...] = rotate_turned(contract(turned(dc), blocks_ref[...], 1, 0), wide_ref[2], narrow_ref[7])
    share_out(keep_ref, send_ref, layout(256, LATE)[0], (reduce, keyval, query, out))
    sums_ref[0:1, :] = col_sum(dc.astype(f32))
    sums_ref[1:2, :] = gain_sum
    sums_ref[2:3, :] = bias_sum


def cells_back_kernel(
    tile_rows, cols, size_ref, dq_ref, dc_ref, query_ref, reduce_ref, x0_ref, dx1_ref, vec_ref, tile_ref, up_ref, down_ref,
    feed_sums, key_sums, query_sums, dx0_ref, head_ref, tail_ref, sums_ref, frame,
):
    tokens = x0_ref.shape[0]
    dh1 = contract(dq_ref[...], query_ref[...], 1, 1)
    for corner in range(4):
        pick = picked_cells((tokens, dc_ref.shape[0]), 0, size_ref, corner, tile_rows, cols)
        placed = contract(pick, dc_ref[...], 1, 0).astype(bf16)
        dh1 = dh1 + contract(placed, reduce_ref[corner * 256 : corner * 256 + 256, :], 1, 1)
    unit, inverse = norm_parts(x0_ref[...])
    back, gain_sum, bias_sum = norm_back(dh1, unit, inverse, vec_ref[10:11, :])
    dx0 = dx1_ref[...] + back
    dx0_ref[...] = dx0
    head_ref[...] = dx0[0:64].astype(bf16)
    tail_ref[...] = dx0[tokens - 64 :].astype(bf16)
    sums_ref[0:25, :] = feed_sums[...]
    sums_ref[25:32, :] = jnp.zeros((7, 256), f32)
    moved = shifted_frame(frame, tile_ref, up_ref, down_ref)
    grid = dx0.reshape(tile_rows, cols, 256)
    for tap in range(9):
        product = moved[tap % 3][tap // 3 : tap // 3 + tile_rows] * grid
        sums_ref[tap : tap + 1, :] = col_sum(product.reshape(tokens, 256))
    sums_ref[9:10, :] = col_sum(dx0)
    sums_ref[10:11, :] = gain_sum
    sums_ref[11:12, :] = bias_sum
    sums_ref[12:13, :] = query_sums[0:1, :]
    sums_ref[13:16, :] = key_sums[...]
    sums_ref[16:17, :] = query_sums[1:2, :]


def input_grad_kernel(tile_rows, dx0_ref, up_ref, down_ref, vec_ref, out_ref, token, frame):
    token[...] = jnp.zeros_like(token)
    moved = shifted_frame(frame, dx0_ref, up_ref, down_ref)
    total = moved[1][1:-1]
    for tap in range(9):
        down, right = 2 - tap // 3, 2 - tap % 3
        total = total + vec_ref[tap : tap + 1, :] * moved[right][down : down + tile_rows]
    out_ref[...] = total.reshape(out_ref.shape)


def moments_of(total, first, second, moment_ref, square_ref):
    moment = BETA * first + (1.0 - BETA) * total
    square = BETA * second + (1.0 - BETA) * total * total
    moment_ref[...] = moment
    square_ref[...] = square
    return moment * (1.0 / CORRECTION) / (jnp.sqrt(square * (1.0 / CORRECTION)) + ADAM_EPS)


def adam_kernel(terms, *refs):
    (first_ref, second_ref, vec_ref, vec_first, vec_second, vec_ema,
     moment_ref, square_ref, step_ref, vec_out, vec_first_out, vec_second_out, vec_ema_out) = refs[terms:]
    late, vec, early = sum_three(refs[:3], refs[3:terms])
    rows = late.shape[0]
    for total, at in ((late, slice(0, rows)), (early, slice(rows, rows + early.shape[0]))):
        step = moments_of(total, first_ref[at, :], second_ref[at, :], moment_ref.at[at, :], square_ref.at[at, :])
        step_ref[at, :] = step.astype(bf16)
    vec = vec[0 : vec_ref.shape[0]]
    new = vec_ref[...] - VECTOR_RATE * moments_of(vec, vec_first[...], vec_second[...], vec_first_out, vec_second_out)
    vec_out[...] = new
    vec_ema_out[...] = EMA_KEEP * vec_ema[...] + (1.0 - EMA_KEEP) * new


def both_groups(width):
    late, count = layout(width, LATE)
    return late + [(j, first + count, rows, blocks) for j, first, rows, blocks in layout(width, EARLY)[0]]


def products_kernel(width, chunks, own_narrow, own_wide, keep_ref, send_ref, whole):
    lefts = {0: (own_narrow, 0), 1: (own_narrow, 1), 2: (own_narrow, 2), 3: (own_narrow, 3), 4: (own_wide, 0), 5: (own_wide, 1)}
    half = keep_ref.shape[0]
    values = chunks[...].astype(f32)
    for j, first, rows, blocks in both_groups(width):
        left = lefts[j][0][lefts[j][1]].astype(bf16)
        for col in range(blocks):
            at = slice(first + col * rows, first + (col + 1) * rows)
            part = values[:, at, :].reshape(left.shape[1], width).astype(bf16)
            side = contract(left, part, 1, 0).reshape(2 * half, rows, width)
            keep_ref[:, at, :] = side[:half]
            whole[:, at, :] = side[half:]
    send_ref[...] = whole[...].astype(bf16)


def finish_kernel(
    width, terms, *refs
):
    narrow_ref, pair_ref, wide_ref, weights_ref, ema_ref, weights_out, ema_out, chunk = refs[terms:]
    rights = {0: narrow_ref.at[1], 1: pair_ref, 2: narrow_ref.at[4], 3: wide_ref.at[0], 4: narrow_ref.at[6], 5: narrow_ref.at[7]}
    sides = total_of(refs[:terms])
    for j, first, rows, blocks in both_groups(width):
        parts = [sides[first + col * rows : first + (col + 1) * rows] for col in range(blocks)]
        side = parts[0] if blocks == 1 else jnp.concatenate(parts, axis=1)
        if rows < 8:
            side = jnp.concatenate([side, jnp.zeros((8 - rows, side.shape[1]), f32)], axis=0)
        full = contract(side.astype(bf16), rights[j][...], 1, 1)
        for col in range(blocks):
            at = slice(first + col * rows, first + (col + 1) * rows)
            old = weights_ref[at, :]
            piece = full[0:rows, col * width : (col + 1) * width]
            chunk[at, :] = old - MATRIX_RATES[j] * (piece + WEIGHT_DECAY * old)
    from_chunk(chunk, weights_out, width)
    chunk[...] = EMA_KEEP * ema_ref[...] + (1.0 - EMA_KEEP) * chunk[...]
    from_chunk(chunk, ema_out, width)


def packed_moments_kernel(width, moment_ref, square_ref, first_out, second_out, token):
    token[...] = jnp.zeros_like(token)
    from_chunk(moment_ref, first_out, width)
    from_chunk(square_ref, second_out, width)


def on_device(
    patches,
    cotangent,
    image_sizes,
    weights,
    first_moment,
    second_moment,
    weight_ema,
    vectors,
    vec_first,
    vec_second,
    vec_ema,
    basis_narrow,
    basis_pair,
    basis_wide,
):
    _, rows, cols, width = patches.shape
    tokens = rows * cols
    shards = device_count()
    tile = patches.reshape(tokens, width)
    dy = cotangent.reshape(tokens, width)
    per = weights.shape[1]
    late_rows, early_rows = layout(width, LATE)[1], layout(width, EARLY)[1]
    chunk = late_rows + early_rows
    ranks = lax.axis_size("row")
    own_keys = tokens // 4
    keys = own_keys * ranks
    frame = ((rows + 2, cols + 16, width), f32)
    img_part = ("img", 1, lax.axis_size("img"))
    xy_parts = row_parts()

    def border(head, tail):
        up = lax.ppermute(tail, "row", [(i, i + 1) for i in range(ranks - 1)])
        return up, lax.ppermute(head, "row", [(i + 1, i) for i in range(ranks - 1)])

    gather_groups = xy_parts[::-1]
    lines = lax.axis_size("img")

    (packed,) = run(
        "pack",
        functools.partial(pack_kernel, width),
        [((chunk, width), bf16)],
        [weights],
        scratch=[((chunk, width), f32)],
    )
    line = join([packed[None]] + [swap(packed, "img", j)[None] for j in range(1, lines)])
    up_halo, down_halo = border(tile[:64], tile[tokens - 64 :])
    x0, h1, mask, vec, sizes = run(
        "front",
        functools.partial(front_kernel, rows, cols),
        [((tokens, width), f32), ((tokens, width), bf16), ((1, keys), f32), (vectors.shape, f32), ((8, 128), jnp.int32)],
        [image_sizes, tile, up_halo, down_halo, vectors],
        scratch=[frame],
        scalars=(0,),
        micros=1.3,
        after=[line],
    )
    wide, wide_done = run(
        "wide_bases",
        wide_bases_kernel,
        [((3, FF, FF), bf16), ((8, 128), f32)],
        [basis_wide],
        micros=6.0,
        after=[line],
    )
    all_near = line
    for axis, stride, size in gather_groups:
        pieces = [all_near] + [swap(all_near, axis, j * stride) for j in range(1, size)]
        if stride * size == ranks:
            near, rest_near = join_apart(pieces, width * 4 // shards, [wide_done, vec])
        else:
            all_near = join(pieces, after=[wide_done, vec])
    far, rest_far = swap(near, "row", 1), swap(rest_near, "row", 1)
    w_reduce, blocks, c, kn = run(
        "keys",
        functools.partial(keys_kernel, rows, cols),
        [
            ((4 * width, width), bf16),
            ((own_keys, 4 * width), bf16),
            ((own_keys, width), f32),
            ((own_keys, width), bf16),
        ],
        [sizes, h1, vec, near, far],
        scratch=[((4 * width, width), f32)],
        micros=1.5,
    )
    narrow, narrow_turned, pair, own_narrow = run(
        "narrow_bases",
        narrow_bases_kernel,
        [
            ((8, width, width), bf16),
            ((4, width, width), bf16),
            ((2 * width, 2 * width), bf16),
            ((4, width // lines, width // ranks), f32),
        ],
        [basis_narrow, basis_pair],
        micros=1.5,
        after=[kn],
    )
    old_chunk, ema_chunk, first_chunk, second_chunk = run(
        "moments",
        functools.partial(moments_kernel, width),
        [((chunk, width), f32)] * 4,
        [jnp.concatenate([weights, weight_ema, first_moment, second_moment], axis=0)],
        after=[kn],
    )
    group = (1, 0, 2, 3, 4)
    w_keyval, w_query, w_out, w_up, w_down = run(
        "weights",
        functools.partial(weights_kernel, group),
        [(matrix_shapes(width, FF)[j], bf16) for j in group],
        [rest_near, rest_far],
        scratch=[(matrix_shapes(width, FF)[j], f32) for j in group],
        micros=1.0,
        after=[kn],
    )
    kn_near = side_by_side(kn, gather_groups)
    kn_far = swap(kn_near, "row", 1)

    unroll = keys <= 1024
    step = tokens if unroll else 32
    kn_all, q, k, v, o, stat, *kept = run(
        "attend",
        functools.partial(attend_kernel, step, unroll),
        [((keys, width), bf16), ((tokens, width), bf16), ((keys, width), bf16), ((keys, width), bf16)]
        + [((tokens, width), f32), ((tokens, 128), f32)]
        + ([((HEADS, tokens, keys), bf16)] if unroll else []),
        [h1, w_query, w_keyval, vec, kn_near, kn_far, mask],
        mib=8 if unroll else 44,
        micros=8.0,
        after=[own_narrow, old_chunk],
    )
    y, do, dx1, up_grad, down_grad, out_grad, feed_sums = run(
        "feed",
        feed_kernel,
        [
            ((tokens, width), bf16),
            ((tokens, width), bf16),
            ((tokens, width), f32),
            ((width, FF), f32),
            ((width, FF), f32),
            ((width, width), f32),
            (vectors.shape, f32),
        ],
        [o, x0, w_out, w_up, w_down, vec, dy],
        mib=12,
        micros=3.5,
    )
    if kept:
        body, args, more = attend_back_kept_kernel, [q, k, v, o, stat, kept[0]], []
    else:
        body, args = functools.partial(attend_back_kernel, step), [q, k, v, mask, o, stat]
        more = [((tokens, keys), bf16)]
    dq, dkv, dkn_keep, dkn_send = run(
        "attend_back",
        body,
        [((tokens, width), bf16), ((2 * width, keys), f32), ((keys // 2, width), f32), ((keys // 2, width), f32)],
        args + [do, w_keyval],
        scratch=[((tokens, width), f32), ((tokens, keys), bf16), ((width, tokens), bf16), ((width, tokens), bf16)] + more,
        mib=16 if kept else 60,
        micros=8.0,
    )
    dkn_got = swap(dkn_send, "row", 1)
    half = (shards // 2, early_rows, width)
    early_keep, early_send = run(
        "early_turn",
        early_turn_kernel,
        [(half, f32), (half, f32)],
        [up_grad, down_grad, narrow_turned, narrow, wide],
        scratch=[((width, FF), f32), ((FF, width), f32)],
        mib=10,
        micros=2.0,
        after=[dq],
    )
    early_got = swap(early_send, "row", 1)
    dkn_terms = [dkn_keep, dkn_got]
    for axis, stride, size in xy_parts:
        part, *sends = split_sum(dkn_terms, size, [early_keep])
        dkn_terms = [part] + [swap(x, axis, j * stride) for j, x in enumerate(sends, 1)][::-1]
    query_turn, out_turn, keyval_turn, query_sums = run(
        "middle_turn",
        middle_turn_kernel,
        [((width, width), f32), ((width, width), f32), ((width, 2 * width), f32), ((8, width), f32)],
        [h1, dq, out_grad, kn_all, dkv, narrow_turned, narrow, pair],
        micros=1.5,
        mib=12 if kept else 40,
        after=[part],
    )
    half = (shards // 2, late_rows, width)
    late_keep, late_send, dc, key_sums = run(
        "keys_back",
        functools.partial(keys_back_kernel, len(dkn_terms)),
        [(half, f32), (half, f32), ((own_keys, width), bf16), ((3, width), f32)],
        list(dkn_terms) + [c, vec, blocks, narrow, wide, query_turn, out_turn, keyval_turn],
        scratch=[((4 * width, width), f32)],
        micros=2.0,
    )
    late_got = swap(late_send, "row", 1)
    dx0, head, tail, vec_grads = run(
        "cells_back",
        functools.partial(cells_back_kernel, rows, cols),
        [((tokens, width), f32), ((64, width), bf16), ((64, width), bf16), ((32, width), f32)],
        [
            sizes, dq, dc, w_query, w_reduce, x0, dx1, vec, tile, up_halo, down_halo,
            feed_sums, key_sums, query_sums,
        ],
        scratch=[frame],
        micros=2.0,
    )
    grad_up, grad_down = border(head, tail)
    args = [late_keep, late_got, vec_grads, swap(vec_grads, "row", 1), early_keep, early_got]
    args = [x.reshape(-1, width) for x in args]
    for index, (axis, stride, size) in enumerate(xy_parts + [img_part]):
        keeps, sends = split_three(args, size, index == 0, [grad_up, grad_down] if index else [])
        args = keeps + [swap(x, axis, j * stride) for j, x in enumerate(sends, 1)]
    grad_input, input_done = run(
        "input_grad",
        functools.partial(input_grad_kernel, rows),
        [((tokens, width), f32), ((8, 128), f32)],
        [dx0, grad_up, grad_down, vec],
        scratch=[frame],
        micros=1.5,
        after=[keeps[1]],
    )
    moments, squares, step, new_vectors, vec_moment, vec_square, new_vec_ema = run(
        "adam",
        functools.partial(adam_kernel, len(args)),
        [((chunk, width), f32), ((chunk, width), f32), ((chunk, width), bf16)] + [(vectors.shape, f32)] * 4,
        args + [first_chunk, second_chunk, vec, vec_first, vec_second, vec_ema],
        micros=0.8,
        after=[input_done],
    )
    (own_wide,) = run(
        "own_wide",
        own_wide_kernel,
        [((2, FF // lines, FF // ranks), f32)],
        [wide],
        micros=1.5,
        after=[step],
    )
    new_first, new_second, packed_done = run(
        "packed_moments",
        functools.partial(packed_moments_kernel, width),
        [((1, per), f32), ((1, per), f32), ((8, 128), f32)],
        [moments, squares],
        after=[own_wide],
    )
    steps = join([step[None]] + [swap(step, "img", j)[None] for j in range(1, lines)], [packed_done])
    half = (ranks // 2, chunk, width)
    keep, send = run(
        "products",
        functools.partial(products_kernel, width),
        [(half, f32), (half, bf16)],
        [steps, own_narrow, own_wide],
        scratch=[(half, f32)],
        micros=1.0,
    )
    terms = [keep.reshape(-1, width), swap(send, "row", 1).reshape(-1, width)]
    for index, (axis, stride, size) in enumerate(xy_parts):
        part, *sends = split_sum(terms, size)
        terms = [part] + [swap(x, axis, j * stride) for j, x in enumerate(sends, 1)]
    new_weights, new_ema = run(
        "finish",
        functools.partial(finish_kernel, width, len(terms)),
        [((1, per), f32)] * 2,
        list(terms) + [narrow, pair, wide, old_chunk, ema_chunk],
        scratch=[((chunk, width), f32)],
        micros=1.5,
    )
    return (
        y.reshape(patches.shape),
        grad_input.reshape(patches.shape),
        new_weights,
        new_first,
        new_second,
        new_ema,
        new_vectors,
        vec_moment,
        vec_square,
        new_vec_ema,
    )


def solution(mesh):
    tiles = P("img", "row", None, None)
    packed = P(("img", "row"), None)
    return jax.shard_map(
        on_device,
        mesh=mesh,
        in_specs=(tiles, tiles, P("img", None)) + (packed,) * 4 + (P(),) * 7,
        out_specs=(tiles, tiles) + (packed,) * 4 + (P(),) * 4,
        check_vma=False,
    )
```
